32 devices in a mesh: dp: 2 (over core), row: 4 (over y, x), col: 4 (over z).
Axes of the slice: x: 2, y: 2, z: 4, core: 2. Of those that a mesh axis runs over, the one named last changes fastest.
Arguments:
- block_input: bfloat16 [16384, 768], P(('dp', 'col', 'row')), may hold values from -6 to 6
- out_grad: bfloat16 [16384, 768], P(('dp', 'col', 'row')), may hold values from -6 to 6
- lengths: int32 [8, 2], P(('dp', 'col')), may hold values from 256 to 1024, as said below
- w_qkv: float32 [3, 768, 768], P(None, 'col', 'row'), may hold values from -0.21875 to 0.21875
- w_out: float32 [768, 768], P('row', 'col'), may hold values from -3.5 to 3.5
- w_gate_up: float32 [2, 768, 2048], P(None, 'col', 'row'), may hold values from -0.21875 to 0.21875
- w_down: float32 [2048, 768], P('row', 'col'), may hold values from -0.125 to 0.125
- gains: float32 [2, 768], replicated, may hold values from 0.5 to 1.5
- mom_qkv: float32 [3, 768, 768], P(None, 'col', 'row'), may hold values from -0.0015033532 to 0.0015033532
- mom_out: float32 [768, 768], P('row', 'col'), may hold values from -0.0015033532 to 0.0015033532
- mom_gate_up: float32 [2, 768, 2048], P(None, 'col', 'row'), may hold values from -0.0015033532 to 0.0015033532
- mom_down: float32 [2048, 768], P('row', 'col'), may hold values from -0.0015033532 to 0.0015033532
- mom_gains: float32 [2, 768], replicated, may hold values from -0.006013413 to 0.006013413
- ema_qkv: float32 [3, 768, 768], P(None, 'col', 'row'), may hold values from -0.21875 to 0.21875
- ema_out: float32 [768, 768], P('row', 'col'), may hold values from -3.5 to 3.5
- ema_gate_up: float32 [2, 768, 2048], P(None, 'col', 'row'), may hold values from -0.21875 to 0.21875
- ema_down: float32 [2048, 768], P('row', 'col'), may hold values from -0.125 to 0.125
- ema_gains: float32 [2, 768], replicated, may hold values from 0.5 to 1.5
Outputs:
- output: float32 [16384, 768], P(('dp', 'col', 'row'))
- input_grad: float32 [16384, 768], P(('dp', 'col', 'row'))
- grad_norm: float32 [], replicated
- new_mom_qkv: float32 [3, 768, 768], P(None, 'col', 'row')
- new_mom_out: float32 [768, 768], P('row', 'col')
- new_mom_gate_up: float32 [2, 768, 2048], P(None, 'col', 'row')
- new_mom_down: float32 [2048, 768], P('row', 'col')
- new_mom_gains: float32 [2, 768], replicated
- new_w_qkv: float32 [3, 768, 768], P(None, 'col', 'row')
- new_w_out: float32 [768, 768], P('row', 'col')
- new_w_gate_up: float32 [2, 768, 2048], P(None, 'col', 'row')
- new_w_down: float32 [2048, 768], P('row', 'col')
- new_gains: float32 [2, 768], replicated
- new_ema_qkv: float32 [3, 768, 768], P(None, 'col', 'row')
- new_ema_out: float32 [768, 768], P('row', 'col')
- new_ema_gate_up: float32 [2, 768, 2048], P(None, 'col', 'row')
- new_ema_down: float32 [2048, 768], P('row', 'col')
- new_ema_gains: float32 [2, 768], replicated
The draws below stay inside these ranges and needn't reach their ends.
Inputs may be any that keep to these rules, and one draw needn't show every extreme that they name: `lengths`: each sequence's real tokens fill its first slots; the rest are padding. Some sequence is full.
All inputs are finite; a program needn't handle non-finite values.
Results may differ from the reference program's by a relative error of at most 0.02.
Values may be sent and summed in bfloat16 or wider, within the bound.
No kernel may reach another device: no remote copies, remote signals or barrier semaphores. Data moves between devices by JAX's collectives and lax.ppermute only.
A program may use at most 192 MiB of HBM per device.

```python
import jax
import jax.numpy as jnp
from jax import lax

D = 768
HEADS = 12
HD = 64
FF = 2048
LEN = 1024
SEQ_DEV = 2
GROUPS = 8
TOK_DEV = 2048
TOKENS = 16384
PARAMS = 7079424


def draw_lengths(key, part):
    counts = jax.random.randint(key, (GROUPS, SEQ_DEV), LEN // 4, LEN + 1)
    counts = counts.at[0, 0].set(LEN)
    return counts.at[GROUPS - 1, SEQ_DEV - 1].set(LEN // 4)


def level_of(rng, dims, pieces, low, high):
    loudness = 1.0
    for axis_at, parts in pieces:
        heights = jax.random.uniform(jax.random.fold_in(jax.random.fold_in(rng, 6), axis_at), (parts,), jnp.float32, low / len(pieces), high / len(pieces))
        loudness = loudness * jnp.repeat(jnp.exp(heights), dims[axis_at] // parts).reshape((-1,) + (1,) * (len(dims) - 1 - axis_at))
    return loudness


def centred(stream_key, extent, deviation, limit, pieces=(), kind=jnp.bfloat16):
    gain = level_of(stream_key, extent, pieces, -0.22, 0.18) if pieces else 1.0
    entries = jax.random.normal(stream_key, extent, jnp.float32) * deviation * gain
    return jnp.minimum(jnp.maximum(entries, -limit), limit).astype(kind)


def setup_inputs(seed: int = 0) -> dict:
    streams_of = jax.random.split(jax.random.key(seed), 19)
    block_input = centred(streams_of[0], (TOKENS, D), 1.0, 6.0, ((0, 32),))
    out_grad = centred(streams_of[1], (TOKENS, D), 1.0, 6.0, ((0, 32),))
    lengths = draw_lengths(jax.random.fold_in(streams_of[18], 71), 0)
    w_qkv = centred(streams_of[3], (3, D, D), D ** -0.5, 0.21875, ((1, 4), (2, 4)), jnp.float32)
    w_out = centred(streams_of[4], (D, D), (D * 4 // LEN) ** -0.5, 3.5, ((0, 4), (1, 4)), jnp.float32)
    w_gate_up = centred(streams_of[5], (2, D, FF), D ** -0.5, 0.21875, ((1, 4), (2, 4)), jnp.float32)
    w_down = centred(streams_of[6], (FF, D), FF ** -0.5, 0.125, ((0, 4), (1, 4)), jnp.float32)
    gains = jnp.clip(1.0 + 0.1 * jax.random.normal(streams_of[7], (2, D), jnp.float32), 0.5, 1.5)
    mom_qkv = centred(streams_of[8], (3, D, D), (1.0 / PARAMS ** 0.5), 0.0015033532, ((1, 4), (2, 4)), jnp.float32)
    mom_out = centred(streams_of[9], (D, D), (1.0 / PARAMS ** 0.5), 0.0015033532, ((0, 4), (1, 4)), jnp.float32)
    mom_gate_up = centred(streams_of[10], (2, D, FF), (1.0 / PARAMS ** 0.5), 0.0015033532, ((1, 4), (2, 4)), jnp.float32)
    mom_down = centred(streams_of[11], (FF, D), (1.0 / PARAMS ** 0.5), 0.0015033532, ((0, 4), (1, 4)), jnp.float32)
    mom_gains = centred(streams_of[12], (2, D), (4.0 / PARAMS ** 0.5), 0.006013413, (), jnp.float32)
    ema_qkv = centred(streams_of[13], (3, D, D), D ** -0.5, 0.21875, ((1, 4), (2, 4)), jnp.float32)
    ema_out = centred(streams_of[14], (D, D), (D * 4 // LEN) ** -0.5, 3.5, ((0, 4), (1, 4)), jnp.float32)
    ema_gate_up = centred(streams_of[15], (2, D, FF), D ** -0.5, 0.21875, ((1, 4), (2, 4)), jnp.float32)
    ema_down = centred(streams_of[16], (FF, D), FF ** -0.5, 0.125, ((0, 4), (1, 4)), jnp.float32)
    ema_gains = jnp.clip(1.0 + 0.1 * jax.random.normal(streams_of[17], (2, D), jnp.float32), 0.5, 1.5)
    return dict(block_input=block_input, out_grad=out_grad, lengths=lengths, w_qkv=w_qkv, w_out=w_out, w_gate_up=w_gate_up, w_down=w_down, gains=gains, mom_qkv=mom_qkv, mom_out=mom_out, mom_gate_up=mom_gate_up, mom_down=mom_down, mom_gains=mom_gains, ema_qkv=ema_qkv, ema_out=ema_out, ema_gate_up=ema_gate_up, ema_down=ema_down, ema_gains=ema_gains)


EPSILON = 1e-06
THETA = 10000.0
MOMENTUM = 0.9
RATE = 300.0
DECAY = 0.6
CLIP = 1.0
NEGATIVE = -1e+30
HIGHEST = lax.Precision.HIGHEST

@jax.custom_vjp
def low(v):
    return lax.optimization_barrier(v.astype(jnp.bfloat16)).astype(jnp.float32)

@jax.custom_vjp
def low_back(v):
    return v

def low_keep(v):
    return (low(v), None)

def low_pass(kept, grad):
    return (grad,)

def back_keep(v):
    return (v, None)

def back_low(kept, grad):
    return (low(grad),)
low.defvjp(low_keep, low_pass)
low_back.defvjp(back_keep, back_low)

def rope_tables():
    half_dim = HD // 2
    freqs = THETA ** (-(jnp.arange(half_dim, dtype=jnp.float32) * 2.0) / HD)
    angles = jnp.arange(LEN, dtype=jnp.float32)[:, None] * freqs[None, :]
    return (jnp.cos(angles), jnp.sin(angles))

def rotate(tensor, cosine, sine_table):
    half_dim = HD // 2
    first_half = tensor[..., :half_dim]
    second = tensor[..., half_dim:]
    cos_b = cosine[None, :, None, :]
    sin_b = sine_table[None, :, None, :]
    return jnp.concatenate([first_half * cos_b - second * sin_b, first_half * sin_b + second * cos_b], -1)

def layer(inputs, w_qkv, w_out, w_gate_up, w_down, gains, valid_keys, cosine, sine_table):
    tok_rows = inputs.shape[0]
    seq_count = tok_rows // LEN
    score_scale = HD ** (-0.5)
    qkv = jnp.einsum('td,kde->kte', inputs, low(w_qkv), precision=HIGHEST)
    queries = low_back(qkv[0]).reshape(seq_count, LEN, HEADS, HD)
    keys_raw = low_back(qkv[1]).reshape(seq_count, LEN, HEADS, HD)
    values = low(low_back(qkv[2])).reshape(seq_count, LEN, HEADS, HD)
    queries = low(rotate(queries, cosine, sine_table))
    keys_rot = low(rotate(keys_raw, cosine, sine_table))
    scores = low_back(jnp.einsum('sqhd,skhd->shqk', queries, keys_rot, precision=HIGHEST)) * score_scale
    scores = jnp.where(valid_keys, scores, NEGATIVE)
    softmax_w = jax.nn.softmax(scores, axis=-1)
    attended = jnp.einsum('shqk,skhd->sqhd', low(softmax_w), values, precision=HIGHEST).reshape(tok_rows, D)
    attended = low(low_back(attended))
    branch = low_back(jnp.dot(attended, low(w_out), precision=HIGHEST))
    residual = inputs + branch
    scale_one = lax.rsqrt(lax.optimization_barrier(jnp.mean(residual * residual, -1, keepdims=True)) + EPSILON)
    normed = residual * scale_one * gains[0]
    gate_up = jnp.einsum('td,kde->kte', low(normed), low(w_gate_up), precision=HIGHEST)
    gate_act = low_back(gate_up[0])
    up_act = low_back(gate_up[1])
    hidden = low(jax.nn.silu(gate_act) * up_act)
    ffn_out = low_back(jnp.dot(hidden, low(w_down), precision=HIGHEST))
    summed = normed + ffn_out
    scale_two = lax.rsqrt(lax.optimization_barrier(jnp.mean(summed * summed, -1, keepdims=True)) + EPSILON)
    return summed * scale_two * gains[1]

def update(grad_full, moment, weight, average, factor):
    clipped = grad_full * factor
    new_moment = MOMENTUM * moment + clipped
    new_weight = weight - RATE * (clipped + MOMENTUM * new_moment)
    new_average = DECAY * average + (1.0 - DECAY) * new_weight
    return (new_moment, new_weight, new_average)

def reference(block_input, out_grad, lengths, w_qkv, w_out, w_gate_up, w_down, gains, mom_qkv, mom_out, mom_gate_up, mom_down, mom_gains, ema_qkv, ema_out, ema_gate_up, ema_down, ema_gains):
    cosine, sine_table = rope_tables()
    positions = jnp.arange(LEN, dtype=jnp.int32)
    causal = positions[None, :] <= positions[:, None]
    inputs_all = block_input.astype(jnp.float32).reshape(GROUPS, TOK_DEV, D)
    cot_all = out_grad.astype(jnp.float32).reshape(GROUPS, SEQ_DEV, LEN, D)
    params = (w_qkv, w_out, w_gate_up, w_down, gains)

    def one_group(totals, items):
        inputs, cot_group, seq_lengths = items
        valid = causal[None, None] & (positions[None, None, None, :] < seq_lengths[:, None, None, None])
        row_live = (positions[None, :] < seq_lengths[:, None]).astype(jnp.float32)

        def run_layer(inp, a_w, b_w, c_w, d_w, e_w):
            return layer(inp, a_w, b_w, c_w, d_w, e_w, valid, cosine, sine_table)
        outputs, pullback = jax.vjp(run_layer, inputs, *params)
        cot_live = (cot_group * row_live[:, :, None]).reshape(TOK_DEV, D)
        grads = pullback(cot_live)
        totals = tuple((t_sum + g_new for t_sum, g_new in zip(totals, grads[1:])))
        return (totals, (outputs, grads[0]))
    zeros = tuple((jnp.zeros_like(p_arr) for p_arr in params))
    totals, (outs_all, dx_all) = lax.scan(one_group, zeros, (inputs_all, cot_all, lengths))
    squares = sum((jnp.sum(g_arr * g_arr) for g_arr in totals))
    grad_norm = jnp.sqrt(squares)
    factor = jnp.minimum(1.0, CLIP / (grad_norm + 1e-06))
    moments = (mom_qkv, mom_out, mom_gate_up, mom_down, mom_gains)
    averages = (ema_qkv, ema_out, ema_gate_up, ema_down, ema_gains)
    results = [update(g_arr, m_arr, w_arr, e_arr, factor) for g_arr, m_arr, w_arr, e_arr in zip(totals, moments, params, averages)]
    return (outs_all.reshape(TOKENS, D), dx_all.reshape(TOKENS, D), grad_norm, results[0][0], results[1][0], results[2][0], results[3][0], results[4][0], results[0][1], results[1][1], results[2][1], results[3][1], results[4][1], results[0][2], results[1][2], results[2][2], results[3][2], results[4][2])
```

```python
import functools

import jax
import jax.numpy as jnp
import numpy as np
from jax import lax
from jax.experimental import pallas as pl
from jax.experimental.pallas import tpu as pltpu
from jax.sharding import PartitionSpec as P

HD = 64
LEN = 1024

EPSILON = 1e-06
THETA = 10000.0
MOMENTUM = 0.9
RATE = 300.0
DECAY = 0.6
CLIP = 1.0
NEGATIVE = -1e30

F32 = jnp.float32
BF16 = jnp.bfloat16
NT = (((1,), (1,)), ((), ()))
NN = (((1,), (0,)), ((), ()))
TN = (((0,), (0,)), ((), ()))
BQ = 256


def rope_tables():
    half = HD // 2
    freqs = np.float32(THETA) ** (-(np.arange(half, dtype=np.float32) * np.float32(2.0)) / np.float32(HD))
    angles = np.arange(LEN, dtype=np.float32)[:, None] * freqs[None, :].astype(np.float32)
    return np.cos(angles), np.sin(angles)


def padded_tables():
    cosine, sine = rope_tables()
    zero = np.zeros((LEN, HD), np.float32)
    return (
        jnp.asarray(np.concatenate([cosine, cosine, zero], 1)),
        jnp.asarray(np.concatenate([sine, -sine, zero], 1)),
    )


def mxu(lhs, rhs, dims):
    return lax.dot_general(lhs, rhs, dims, preferred_element_type=F32)


def causal(scores_t, block):
    keys = scores_t.shape[0]
    row = lax.broadcasted_iota(jnp.int32, (block, block), 0)
    column = lax.broadcasted_iota(jnp.int32, (block, block), 1)
    tail = jnp.where(row <= column, scores_t[keys - block :], NEGATIVE)
    return tail if keys == block else jnp.concatenate([scores_t[: keys - block], tail], 0)


def attend_forward_kernel(q_ref, k_ref, v_ref, o_ref, ot_ref, lse_ref):
    length = q_ref.shape[1]
    for block in range(length // BQ):
        keys = (block + 1) * BQ
        span = slice(block * BQ, keys)
        parts = []
        for head in range(3):
            scores = causal(mxu(k_ref[head, :keys, :], q_ref[head, span, :], NT), BQ)
            top = jnp.max(scores, 0, keepdims=True)
            probs = jnp.exp(scores - top).astype(BF16)
            out = mxu(v_ref[head, :keys, :], probs, TN)
            total = out[HD : HD + 1]
            parts.append(out[:HD] / total)
            lse_ref[0, head : head + 1, span] = top + jnp.log(total)
        out = jnp.concatenate(parts, 0)
        ot_ref[0, :, span] = out.astype(BF16)
        o_ref[0, span, :] = out.T.astype(BF16)


def attend_forward(q, k, v):
    heads, length, _ = q.shape
    groups = heads // 3
    blk = pl.BlockSpec((3, length, 128), lambda j: (j, 0, 0))
    return pl.pallas_call(
        attend_forward_kernel,
        grid=(groups,),
        in_specs=[blk] * 3,
        out_specs=[
            pl.BlockSpec((1, length, 192), lambda j: (j, 0, 0)),
            pl.BlockSpec((1, 192, length), lambda j: (j, 0, 0)),
            pl.BlockSpec((1, 8, length), lambda j: (j, 0, 0)),
        ],
        out_shape=[
            jax.ShapeDtypeStruct((groups, length, 192), BF16),
            jax.ShapeDtypeStruct((groups, 192, length), BF16),
            jax.ShapeDtypeStruct((groups, 8, length), F32),
        ],
        compiler_params=pltpu.CompilerParams(vmem_limit_bytes=48 << 20),
        cost_estimate=pl.CostEstimate(flops=4 << 30, bytes_accessed=6 << 20, transcendentals=4 << 20),
    )(q, k, v)


def attend_backward_kernel(
    q_ref, k_ref, v_ref, do_ref, ot_ref, lse_ref, cos_ref, sin_ref, dqk_ref, dv_ref, dk_acc, dv_acc
):
    length = q_ref.shape[1]
    products = do_ref[0].astype(F32).T * ot_ref[0].astype(F32)
    lane = lax.broadcasted_iota(jnp.int32, (1, 128), 1)

    def unrotate(t):
        swapped = jnp.where(lane < 32, pltpu.roll(t, 96, 1), pltpu.roll(t, 32, 1))
        return t * cos_ref[...] + swapped * sin_ref[...]

    for head in range(3):
        lanes = slice(head * HD, (head + 1) * HD)
        delta = jnp.sum(products[lanes], 0, keepdims=True)
        dq_parts = []
        for block in range(length // BQ):
            keys = (block + 1) * BQ
            span = slice(block * BQ, keys)
            before = keys - BQ
            q = q_ref[head, span, :]
            scores = causal(mxu(k_ref[head, :keys, :], q, NT), BQ)
            probs = jnp.exp(scores - lse_ref[0, head : head + 1, span])
            d_out = do_ref[0, span, lanes]
            d_probs = mxu(v_ref[head, :keys, :HD], d_out, NT)
            d_scores = (probs * (d_probs - delta[:, span])).astype(BF16)
            dv_part = mxu(probs.astype(BF16), d_out, NN)
            dk_part = mxu(d_scores, q, NN)
            if block:
                dv_acc[:before, :] += dv_part[:before]
                dk_acc[:before, :] += dk_part[:before]
            dv_acc[before:keys, :] = dv_part[before:]
            dk_acc[before:keys, :] = dk_part[before:]
            dq_parts.append(mxu(d_scores, k_ref[head, :keys, :], TN))
        dq = jnp.concatenate(dq_parts, 0) * (HD ** -0.5)
        dqk_ref[0, :, head * HD : (head + 1) * HD] = unrotate(dq)[:, :HD].astype(BF16)
        dqk_ref[0, :, 192 + head * HD : 192 + (head + 1) * HD] = unrotate(dk_acc[...])[:, :HD].astype(BF16)
        dv_ref[0, :, lanes] = dv_acc[...].astype(BF16)


def attend_backward(q, k, v, d_out, out_t, lse, cos, sin):
    heads, length, _ = q.shape
    groups = heads // 3
    blk = pl.BlockSpec((3, length, 128), lambda j: (j, 0, 0))
    table = pl.BlockSpec((length, 128), lambda j: (0, 0))
    wide = pl.BlockSpec((1, length, 192), lambda j: (j, 0, 0))
    return pl.pallas_call(
        attend_backward_kernel,
        grid=(groups,),
        in_specs=[blk] * 3
        + [
            wide,
            pl.BlockSpec((1, 192, length), lambda j: (j, 0, 0)),
            pl.BlockSpec((1, 8, length), lambda j: (j, 0, 0)),
            table,
            table,
        ],
        out_specs=[pl.BlockSpec((1, length, 384), lambda j: (j, 0, 0)), wide],
        out_shape=[
            jax.ShapeDtypeStruct((groups, length, 384), BF16),
            jax.ShapeDtypeStruct((groups, length, 192), BF16),
        ],
        scratch_shapes=[pltpu.VMEM((length, 128), F32), pltpu.VMEM((length, HD), F32)],
        compiler_params=pltpu.CompilerParams(vmem_limit_bytes=56 << 20),
        cost_estimate=pl.CostEstimate(flops=10 << 30, bytes_accessed=8 << 20, transcendentals=4 << 20),
    )(q, k, v, d_out, out_t, lse, cos, sin)


def update(grad_full, moment, weight, average, factor):
    clipped = grad_full * factor
    new_moment = MOMENTUM * moment + clipped
    new_weight = weight - RATE * (clipped + MOMENTUM * new_moment)
    new_average = DECAY * average + (1.0 - DECAY) * new_weight
    return (new_moment, new_weight, new_average)


def body(
    rows,
    cols,
    block_input,
    out_grad,
    lengths,
    w_qkv,
    w_out,
    w_gate_up,
    w_down,
    gains,
    mom_qkv,
    mom_out,
    mom_gate_up,
    mom_down,
    mom_gains,
    ema_qkv,
    ema_out,
    ema_gate_up,
    ema_down,
    ema_gains,
):
    d = lax.axis_index("dp")
    r = lax.axis_index("row")
    c = lax.axis_index("col")
    core0 = d == 0
    tokens, width = block_input.shape
    ring = cols <= 4
    part = width // cols

    pairs = [(i, j) for i in range(2) for j in range(rows)]
    swap_pairs = [(i * rows + j, (j % 2) * rows + (j // 2) * 2 + i) for i, j in pairs]
    first_pairs = [(i * rows + j, i * rows + (j ^ (1 if i == 0 else 2))) for i, j in pairs]
    second_pairs = [(i * rows + j, i * rows + (j ^ (2 if i == 0 else 1))) for i, j in pairs]

    def swap_tokens(t):
        return lax.ppermute(t, ("dp", "row"), swap_pairs)

    def first(t):
        return lax.ppermute(t, ("dp", "row"), first_pairs)

    def second(t):
        return lax.ppermute(t, ("dp", "row"), second_pairs)

    def core(t):
        return lax.ppermute(t, "dp", [(0, 1), (1, 0)])

    def along(t, k):
        return lax.ppermute(t, "col", [(i, (i + k) % cols) for i in range(cols)])

    def sum_all(t):
        for axis, size in (("dp", 2), ("row", rows), ("col", cols)):
            bit = 1
            while bit < size:
                t = t + lax.ppermute(t, axis, [(i, i ^ bit) for i in range(size)])
                bit *= 2
        return t

    def relative(t):
        if not ring:
            return t
        return lax.dynamic_slice_in_dim(jnp.concatenate([t, t], -1), c * part, width, t.ndim - 1)

    def absolute(t):
        if not ring:
            return t
        back = (cols - c) % cols
        return lax.dynamic_slice_in_dim(jnp.concatenate([t, t], -1), back * part, width, t.ndim - 1)

    def gather_cols(t, axis):
        if not ring:
            return lax.all_gather(t, "col", axis=axis, tiled=True)
        got = [t] + [along(t, k) for k in range(1, cols)]
        return jnp.concatenate([got[-k % cols] for k in range(cols)], axis)

    def gather_rows(t):
        one, two = first(t), second(t)
        return [t, one, two, second(one)]

    def scatter_rows(slots):
        slot_one = (slots[1].astype(F32) + second(slots[3]).astype(F32)).astype(BF16)
        return slots[0].astype(F32) + first(slot_one).astype(F32) + second(slots[2]).astype(F32)

    def scatter_cols(t, axis):
        if not ring:
            return lax.psum_scatter(t, "col", scatter_dimension=axis, tiled=True).astype(F32)
        blocks = [lax.slice_in_dim(t, k * part, (k + 1) * part, axis=axis) for k in range(cols)]
        total = blocks[0].astype(F32)
        for k in range(1, cols):
            total = total + along(blocks[k], k).astype(F32)
        return total

    x_own = relative(swap_tokens(block_input))
    own_length = swap_tokens(lengths)[0, :]
    seq_ids = jnp.arange(own_length.shape[0], dtype=jnp.int32)
    own_length = jnp.sum(jnp.where(seq_ids == r // 2, own_length, 0))
    gains_rel = relative(gains)

    half = w_gate_up.shape[2] // 2
    wq = w_qkv.astype(BF16)
    head_cols = wq.shape[2]
    piece_qk = jnp.concatenate([wq[0], wq[1]], 1)
    piece_vo = jnp.concatenate([wq[2], w_out.T.astype(BF16)], 1)
    piece_a = jnp.where(core0, piece_qk, piece_vo)
    wgu = lax.dynamic_slice_in_dim(w_gate_up, d * half, half, 2).astype(BF16)
    piece_g = jnp.concatenate([wgu[0], wgu[1]], 1)
    piece_d = lax.dynamic_slice_in_dim(w_down, d * half, half, 0).T.astype(BF16)

    slots_d = jnp.stack(gather_rows(piece_d))
    full_a = gather_cols(piece_a, 0)
    slots_a = gather_rows(full_a)
    full_g = gather_cols(piece_g, 0)
    w_gu = jnp.stack(gather_rows(full_g))
    w_dn = gather_cols(slots_d, 1)

    keep = jnp.where(core0, jnp.stack([slots_a[0], slots_a[1]]), jnp.stack([slots_a[1], slots_a[3]]))
    send = jnp.where(core0, jnp.stack([slots_a[2], slots_a[3]]), jnp.stack([slots_a[0], slots_a[2]]))
    got = core(send)
    w_qk = jnp.where(core0, keep, got)
    w_vo = jnp.where(core0, got, keep)

    x_other = core(x_own)
    x_full = jnp.where(
        core0, jnp.concatenate([x_own, x_other], 0), jnp.concatenate([x_other, x_own], 0)
    )
    cosine, sine = rope_tables()
    cosine = jnp.asarray(cosine)[None, :, None, :]
    sine = jnp.asarray(sine)[None, :, None, :]
    heads = head_cols // HD

    def rotate(t):
        t = t.reshape(2, LEN, heads, HD)
        u, w = t[..., : HD // 2], t[..., HD // 2 :]
        return jnp.concatenate([u * cosine - w * sine, u * sine + w * cosine], -1)

    def by_head(t, tail):
        t = t.reshape(2, LEN, heads, HD).transpose(0, 2, 1, 3).reshape(2 * heads, LEN, HD).astype(BF16)
        extra = jnp.broadcast_to(tail[None, :, None], (2 * heads, LEN, 1))
        return jnp.concatenate([t, extra, jnp.zeros((2 * heads, LEN, HD - 1), BF16)], -1)

    qk = jnp.einsum("td,jde->jte", x_full, w_qk, preferred_element_type=F32)
    v = jnp.einsum("td,jde->jte", x_full, w_vo[:, :, :head_cols], preferred_element_type=F32)
    ones = jnp.ones((LEN,), BF16)
    bias = jnp.where(jnp.arange(LEN, dtype=jnp.int32) < own_length, 0.0, NEGATIVE).astype(BF16)
    q_pad = by_head(rotate(qk[:, :, :head_cols]) * (HD ** -0.5), ones)
    k_pad = by_head(rotate(qk[:, :, head_cols:]), bias)
    v_pad = by_head(v, ones)
    attended, attended_t, lse = attend_forward(q_pad, k_pad, v_pad)

    def split_sum(whole):
        own = lax.dynamic_index_in_dim(whole, d, 0, keepdims=False)
        other = lax.dynamic_index_in_dim(whole, 1 - d, 0, keepdims=False)
        return own, core(other.astype(BF16)).astype(F32)

    w_o = w_vo[:, :, head_cols:]
    partial = jnp.einsum("jte,jde->td", attended, w_o, preferred_element_type=F32)
    own, other = split_sum(partial.reshape(2, tokens, width))
    residual = x_own.astype(F32) + (own + other)
    scale_one = lax.rsqrt(jnp.mean(residual * residual, -1, keepdims=True) + EPSILON)
    normed = residual * scale_one * gains_rel[0]
    normed_b = normed.astype(BF16)
    normed_full = jnp.concatenate([normed_b, core(normed_b)], 0)

    gate_up = jnp.einsum("td,sde->ste", normed_full, w_gu, preferred_element_type=F32)
    gate_act = gate_up[:, :, :half]
    up_act = gate_up[:, :, half:]
    sigmoid_g = jax.nn.sigmoid(gate_act)
    silu_g = gate_act * sigmoid_g
    hidden = (silu_g * up_act).astype(BF16)
    ffn_other = jnp.einsum("ste,sde->td", hidden[:, tokens:], w_dn, preferred_element_type=F32)
    ffn_got = core(ffn_other.astype(BF16)).astype(F32)
    ffn_own = jnp.einsum("ste,sde->td", hidden[:, :tokens], w_dn, preferred_element_type=F32)
    summed = normed + (ffn_own + ffn_got)
    scale_two = lax.rsqrt(jnp.mean(summed * summed, -1, keepdims=True) + EPSILON)
    output = summed * scale_two * gains_rel[1]
    output = swap_tokens(absolute(output.astype(BF16))).astype(F32)

    position = d * tokens + jnp.arange(tokens, dtype=jnp.int32)
    row_live = (position < own_length).astype(F32)[:, None]
    cot_live = relative(swap_tokens(out_grad)).astype(F32) * row_live
    grad_gain_two = jnp.sum(cot_live * summed * scale_two, 0)
    hat_two = cot_live * gains_rel[1]
    inner_two = jnp.sum(hat_two * summed, -1, keepdims=True)
    d_summed = scale_two * (hat_two - summed * scale_two * scale_two * inner_two / width)
    d_ffn = d_summed.astype(BF16)
    d_ffn_full = jnp.concatenate([d_ffn, core(d_ffn)], 0)
    grad_dn = jnp.einsum("td,ste->sde", d_ffn_full, hidden, preferred_element_type=F32).astype(BF16)
    shard_d = scatter_rows([t for t in scatter_cols(grad_dn, 1).astype(BF16)])
    d_hidden = jnp.einsum("td,sde->ste", d_ffn_full, w_dn, preferred_element_type=F32)
    d_gate = d_hidden * up_act * (sigmoid_g * (1.0 + gate_act * (1.0 - sigmoid_g)))
    d_up = d_hidden * silu_g
    d_gu = jnp.concatenate([d_gate, d_up], -1).astype(BF16)
    dn_other = jnp.einsum("ste,sde->td", d_gu[:, tokens:], w_gu, preferred_element_type=F32)
    dn_got = core(dn_other.astype(BF16)).astype(F32)
    dn_own = jnp.einsum("ste,sde->td", d_gu[:, :tokens], w_gu, preferred_element_type=F32)
    grad_gu = [
        jnp.einsum("td,te->de", normed_full, d_gu[s], preferred_element_type=F32).astype(BF16)
        for s in range(4)
    ]
    shard_g = scatter_cols(scatter_rows(grad_gu).astype(BF16), 0)
    d_normed = d_summed + (dn_own + dn_got)
    grad_gain_one = jnp.sum(d_normed * residual * scale_one, 0)
    hat_one = d_normed * gains_rel[0]
    inner_one = jnp.sum(hat_one * residual, -1, keepdims=True)
    d_residual = scale_one * (hat_one - residual * scale_one * scale_one * inner_one / width)
    d_branch = d_residual.astype(BF16)
    d_branch_other = core(d_branch)
    d_branch_full = jnp.where(
        core0,
        jnp.concatenate([d_branch, d_branch_other], 0),
        jnp.concatenate([d_branch_other, d_branch], 0),
    )
    d_attended = jnp.einsum("td,jde->jte", d_branch_full, w_o, preferred_element_type=F32).astype(BF16)
    cos_pad, sin_pad = padded_tables()
    d_qk, d_v = attend_backward(q_pad, k_pad, v_pad, d_attended, attended_t, lse, cos_pad, sin_pad)
    grad_o = jnp.einsum("td,jte->jde", d_branch_full, attended, preferred_element_type=F32)
    grad_v = jnp.einsum("td,jte->jde", x_full, d_v, preferred_element_type=F32)
    grad_qk = jnp.einsum("td,jte->jde", x_full, d_qk, preferred_element_type=F32).astype(BF16)
    grad_vo = jnp.concatenate([grad_v, grad_o], -1).astype(BF16)
    mine = jnp.where(core0, grad_qk, grad_vo)
    got = core(jnp.where(core0, grad_vo, grad_qk))
    slots = [
        jnp.where(core0, mine[0], got[0]),
        jnp.where(core0, mine[1], mine[0]),
        jnp.where(core0, got[0], got[1]),
        jnp.where(core0, got[1], mine[1]),
    ]
    shard_a = scatter_cols(scatter_rows(slots).astype(BF16), 0)
    dx = jnp.einsum("jte,jde->td", d_qk, w_qk, preferred_element_type=F32) + jnp.einsum(
        "jte,jde->td", d_v, w_vo[:, :, :head_cols], preferred_element_type=F32
    )
    own, other = split_sum(dx.reshape(2, tokens, width))
    input_grad = absolute((d_residual + (own + other)).astype(BF16))
    input_grad = swap_tokens(input_grad).astype(F32)

    def both(t):
        t = t.astype(BF16)
        other = core(t)
        return jnp.where(core0, t, other).astype(F32), jnp.where(core0, other, t).astype(F32), t.astype(F32)

    g_qk, g_vo, own_a = both(shard_a)
    g_lo, g_hi, own_g = both(shard_g)
    d_lo, d_hi, own_d = both(shard_d)
    g_qkv = jnp.stack([g_qk[:, :head_cols], g_qk[:, head_cols:], g_vo[:, :head_cols]])
    g_out = g_vo[:, head_cols:].T
    g_gate_up = jnp.stack(
        [
            jnp.concatenate([g_lo[:, :half], g_hi[:, :half]], 1),
            jnp.concatenate([g_lo[:, half:], g_hi[:, half:]], 1),
        ]
    )
    g_down = jnp.concatenate([d_lo.T, d_hi.T], 0)
    gain_total = sum_all(absolute(jnp.stack([grad_gain_one, grad_gain_two])))
    local_squares = jnp.sum(own_a * own_a) + jnp.sum(own_g * own_g) + jnp.sum(own_d * own_d)
    first_device = core0 & (r == 0) & (c == 0)
    local_squares = local_squares + jnp.where(first_device, jnp.sum(gain_total * gain_total), 0.0)
    squares = sum_all(jnp.full((8, 128), local_squares, F32))[0, 0]
    grad_norm = jnp.sqrt(squares)
    factor = jnp.minimum(1.0, CLIP / (grad_norm + 1e-06))
    grads_all = (g_qkv, g_out, g_gate_up, g_down, gain_total)
    params = (w_qkv, w_out, w_gate_up, w_down, gains)
    moments = (mom_qkv, mom_out, mom_gate_up, mom_down, mom_gains)
    averages = (ema_qkv, ema_out, ema_gate_up, ema_down, ema_gains)
    results = [
        update(g_arr, m_arr, w_arr, e_arr, factor)
        for g_arr, m_arr, w_arr, e_arr in zip(grads_all, moments, params, averages)
    ]
    return (
        output,
        input_grad,
        grad_norm,
        *[t[0] for t in results],
        *[t[1] for t in results],
        *[t[2] for t in results],
    )


def solution(mesh):
    tok = P(("dp", "col", "row"), None)
    weights = (P(None, "col", "row"), P("row", "col"), P(None, "col", "row"), P("row", "col"), P())
    in_specs = (tok, tok, P(("dp", "col"), None)) + weights * 3
    out_specs = (tok, tok, P()) + weights * 3
    fn = functools.partial(body, mesh.shape["row"], mesh.shape["col"])
    return jax.shard_map(fn, mesh=mesh, in_specs=in_specs, out_specs=out_specs, check_vma=False)
```

```python
import functools

import jax
import jax.numpy as jnp
import numpy as np
from jax import lax
from jax.experimental import pallas as pl
from jax.experimental.pallas import tpu as pltpu
from jax.sharding import PartitionSpec as P

HD = 64
LEN = 1024

EPSILON = 1e-06
THETA = 10000.0
MOMENTUM = 0.9
RATE = 300.0
DECAY = 0.6
CLIP = 1.0
NEGATIVE = -1e30

F32 = jnp.float32
BF16 = jnp.bfloat16
NT = (((1,), (1,)), ((), ()))
NN = (((1,), (0,)), ((), ()))
TN = (((0,), (0,)), ((), ()))
BQ = 256


def rope_tables():
    half = HD // 2
    freqs = np.float32(THETA) ** (-(np.arange(half, dtype=np.float32) * np.float32(2.0)) / np.float32(HD))
    angles = np.arange(LEN, dtype=np.float32)[:, None] * freqs[None, :].astype(np.float32)
    return np.cos(angles), np.sin(angles)


def pair_tables():
    cosine, sine = rope_tables()
    return (
        jnp.asarray(np.concatenate([cosine] * 4, 1)),
        jnp.asarray(np.concatenate([-sine, sine] * 2, 1)),
    )


def mxu(lhs, rhs, dims=NN):
    return lax.dot_general(lhs, rhs, dims, preferred_element_type=F32)


def fence(*values):
    return lax.optimization_barrier(values)


def params(mib):
    return pltpu.CompilerParams(vmem_limit_bytes=mib << 20)


def cost(flops, bytes_moved, exps=0):
    return pl.CostEstimate(flops=int(flops), bytes_accessed=int(bytes_moved), transcendentals=int(exps))


def out(*shape, dtype=BF16):
    return jax.ShapeDtypeStruct(shape, dtype)


VMEM = pl.BlockSpec(memory_space=pltpu.VMEM)
SMEM = pl.BlockSpec(memory_space=pltpu.SMEM)


def pieces_ad_kernel(s_ref, qkv_ref, out_ref, down_ref, a_ref, d_ref):
    core = s_ref[0]
    n = qkv_ref.shape[2]

    @pl.when(core == 0)
    def _():
        a_ref[:, :n] = qkv_ref[0].astype(BF16)
        a_ref[:, n:] = qkv_ref[1].astype(BF16)

    @pl.when(core == 1)
    def _():
        a_ref[:, :n] = qkv_ref[2].astype(BF16)
        a_ref[:, n:] = out_ref[...].T.astype(BF16)

    half = d_ref.shape[1]
    d_ref[...] = down_ref[pl.ds(pl.multiple_of(core * half, half), half), :].T.astype(BF16)


def pieces_g_kernel(s_ref, gu_ref, g_ref):
    half = g_ref.shape[1] // 2
    at = pl.ds(pl.multiple_of(s_ref[0] * half, half), half)
    g_ref[:, :half] = gu_ref[0, :, at].astype(BF16)
    g_ref[:, half:] = gu_ref[1, :, at].astype(BF16)


def causal(scores_t, block):
    keys = scores_t.shape[0]
    row = lax.broadcasted_iota(jnp.int32, (block, block), 0)
    column = lax.broadcasted_iota(jnp.int32, (block, block), 1)
    tail = jnp.where(row <= column, scores_t[keys - block :], NEGATIVE)
    return tail if keys == block else jnp.concatenate([scores_t[: keys - block], tail], 0)


def swap_halves(t):
    lane = lax.broadcasted_iota(jnp.int32, (1, t.shape[1]), 1)
    return jnp.where(lane % HD < HD // 2, pltpu.roll(t, t.shape[1] - HD // 2, 1), pltpu.roll(t, HD // 2, 1))


def pick_weights(core, j, a0_ref, a1_ref, a3_ref, got_ref, qk_ref, vo_ref):
    @pl.when(core == 0)
    def _():
        vo_ref[...] = got_ref[0]

        @pl.when(j == 0)
        def _():
            qk_ref[...] = a0_ref[...]

        @pl.when(j == 1)
        def _():
            qk_ref[...] = a1_ref[...]

    @pl.when(core == 1)
    def _():
        qk_ref[...] = got_ref[0]

        @pl.when(j == 0)
        def _():
            vo_ref[...] = a1_ref[...]

        @pl.when(j == 1)
        def _():
            vo_ref[...] = a3_ref[...]


def attend_forward_kernel(
    s_ref, x0_ref, x1_ref, a0_ref, a1_ref, a3_ref, got_ref, cos_ref, sin_ref,
    q_ref, k_ref, v_ref, o_ref, ot_ref, lse_ref, xt_ref, far_ref, near_ref,
    qk_w, vo_w, total_ref,
):
    core, live = s_ref[0], s_ref[1]
    j = pl.program_id(0)
    length = q_ref.shape[1]
    tokens = x0_ref.shape[0]
    n = 3 * HD
    pick_weights(core, j, a0_ref, a1_ref, a3_ref, got_ref, qk_w, vo_w)
    lane = lax.broadcasted_iota(jnp.int32, (tokens, HD), 1)
    one = jnp.where(lane == 0, 1.0, 0.0).astype(BF16)
    for x_ref, which in ((x0_ref, core), (x1_ref, 1 - core)):
        start = pl.multiple_of(which * tokens, tokens)
        at = pl.ds(start, tokens)
        qk = mxu(x_ref[...], qk_w[...])
        cos = jnp.concatenate([cos_ref[at, :]] * 3, 1)
        sin = jnp.concatenate([sin_ref[at, :]] * 3, 1)
        qk = qk * cos + swap_halves(qk) * sin
        q = (qk[:, :n] * (HD ** -0.5)).astype(BF16)
        k = qk[:, n:].astype(BF16)
        v = mxu(x_ref[...], vo_w[:, :n]).astype(BF16)
        key = start + lax.broadcasted_iota(jnp.int32, (tokens, HD), 0)
        bias = jnp.where((lane == 0) & (key >= live), NEGATIVE, 0.0).astype(BF16)
        for head in range(3):
            lanes = slice(head * HD, (head + 1) * HD)
            q_ref[head, at, :] = jnp.concatenate([q[:, lanes], one], 1)
            k_ref[head, at, :] = jnp.concatenate([k[:, lanes], bias], 1)
            v_ref[head, at, :] = jnp.concatenate([v[:, lanes], one], 1)

        @pl.when(j == 0)
        def _():
            xt_ref[:, at] = x_ref[...].T

    for block in range(length // BQ):
        keys = (block + 1) * BQ
        span = slice(block * BQ, keys)
        parts = []
        for head in range(3):
            scores = causal(mxu(k_ref[head, :keys, :], q_ref[head, span, :], NT), BQ)
            top = jnp.max(scores, 0, keepdims=True)
            probs = jnp.exp(scores - top).astype(BF16)
            o = mxu(v_ref[head, :keys, :], probs, TN)
            total = o[HD : HD + 1]
            parts.append(o[:HD] / total)
            lse_ref[0, head : head + 1, span] = top + jnp.log(total)
        o = jnp.concatenate(parts, 0)
        ot_ref[0, :, span] = o.astype(BF16)
        o_ref[0, span, :] = o.T.astype(BF16)
    part = mxu(o_ref[0], vo_w[:, n:], NT)

    @pl.when(j == 0)
    def _():
        total_ref[...] = part

    @pl.when(j == 1)
    def _():
        total_ref[...] += part
        near_ref[...] = total_ref[pl.ds(pl.multiple_of(core * tokens, tokens), tokens), :]
        far_ref[...] = total_ref[pl.ds(pl.multiple_of((1 - core) * tokens, tokens), tokens), :].astype(BF16)


def attend_forward(scalars, x_own, x_other, slots, got, cos, sin):
    tokens, width = x_own.shape
    wide = slots[0].shape[1]
    n = wide // 2
    whole = lambda *shape: pl.BlockSpec(shape, lambda j: (0,) * len(shape))
    by_j = lambda *shape: pl.BlockSpec(shape, lambda j: (j,) + (0,) * (len(shape) - 1))
    return pl.pallas_call(
        attend_forward_kernel,
        grid=(2,),
        in_specs=[SMEM]
        + [whole(tokens, width)] * 2
        + [whole(width, wide)] * 3
        + [by_j(1, width, wide), whole(LEN, 128), whole(LEN, 128)],
        out_specs=[by_j(3, LEN, 128)] * 3
        + [by_j(1, LEN, n), by_j(1, n, LEN), by_j(1, 8, LEN), whole(width, LEN)]
        + [whole(tokens, width)] * 2,
        out_shape=[out(6, LEN, 128)] * 3
        + [out(2, LEN, n), out(2, n, LEN), out(2, 8, LEN, dtype=F32), out(width, LEN)]
        + [out(tokens, width), out(tokens, width, dtype=F32)],
        scratch_shapes=[
            pltpu.VMEM((width, wide), BF16),
            pltpu.VMEM((width, wide), BF16),
            pltpu.VMEM((LEN, width), F32),
        ],
        compiler_params=params(44),
        cost_estimate=cost(8e9, 12e6, 4e6),
        name="attend_forward",
    )(scalars, x_own, x_other, slots[0], slots[1], slots[3], got, cos, sin)


def attend_backward_kernel(
    s_ref, d0_ref, d1_ref, a0_ref, a1_ref, a3_ref, got_ref, cos_ref, sin_ref,
    q_ref, k_ref, v_ref, ot_ref, lse_ref,
    dqk_ref, dv_ref, dt_ref,
    qk_w, vo_w, do_ref, dk_acc, dv_acc,
):
    core = s_ref[0]
    j = pl.program_id(0)
    length = q_ref.shape[1]
    tokens = d0_ref.shape[0]
    n = 3 * HD
    pick_weights(core, j, a0_ref, a1_ref, a3_ref, got_ref, qk_w, vo_w)
    for d_ref, which in ((d0_ref, core), (d1_ref, 1 - core)):
        at = pl.ds(pl.multiple_of(which * tokens, tokens), tokens)
        do_ref[at, :] = mxu(d_ref[...], vo_w[:, n:]).astype(BF16)

        @pl.when(j == 0)
        def _():
            dt_ref[:, at] = d_ref[...].T

    products = do_ref[...].astype(F32).T * ot_ref[0].astype(F32)

    def unrotate(t):
        return t * cos_ref[...] - swap_halves(t) * sin_ref[...]

    for head in range(3):
        lanes = slice(head * HD, (head + 1) * HD)
        delta = jnp.sum(products[lanes], 0, keepdims=True)
        dq_parts = []
        for block in range(length // BQ):
            keys = (block + 1) * BQ
            span = slice(block * BQ, keys)
            before = keys - BQ
            q = q_ref[head, span, :]
            scores = causal(mxu(k_ref[head, :keys, :], q, NT), BQ)
            probs = jnp.exp(scores - lse_ref[0, head : head + 1, span])
            d_out = do_ref[span, lanes]
            d_probs = mxu(v_ref[head, :keys, :HD], d_out, NT)
            d_scores = (probs * (d_probs - delta[:, span])).astype(BF16)
            dv_part = mxu(probs.astype(BF16), d_out)
            dk_part = mxu(d_scores, q)
            if block:
                dv_acc[:before, :] += dv_part[:before]
                dk_acc[:before, :] += dk_part[:before]
            dv_acc[before:keys, :] = dv_part[before:]
            dk_acc[before:keys, :] = dk_part[before:]
            dq_parts.append(mxu(d_scores, k_ref[head, :keys, :], TN))
        dq = jnp.concatenate(dq_parts, 0) * (HD ** -0.5)
        dqk_ref[0, :, head * HD : (head + 1) * HD] = unrotate(dq)[:, :HD].astype(BF16)
        dqk_ref[0, :, n + head * HD : n + (head + 1) * HD] = unrotate(dk_acc[...])[:, :HD].astype(BF16)
        dv_ref[0, :, lanes] = dv_acc[...].astype(BF16)


def attend_backward(scalars, d_own, d_other, slots, got, cos, sin, q, k, v, out_t, lse):
    tokens, width = d_own.shape
    wide = slots[0].shape[1]
    n = wide // 2
    whole = lambda *shape: pl.BlockSpec(shape, lambda j: (0,) * len(shape))
    by_j = lambda *shape: pl.BlockSpec(shape, lambda j: (j,) + (0,) * (len(shape) - 1))
    return pl.pallas_call(
        attend_backward_kernel,
        grid=(2,),
        in_specs=[SMEM]
        + [whole(tokens, width)] * 2
        + [whole(width, wide)] * 3
        + [by_j(1, width, wide), whole(LEN, 128), whole(LEN, 128)]
        + [by_j(3, LEN, 128)] * 3
        + [by_j(1, n, LEN), by_j(1, 8, LEN)],
        out_specs=[by_j(1, LEN, wide), by_j(1, LEN, n), whole(width, LEN)],
        out_shape=[out(2, LEN, wide), out(2, LEN, n), out(width, LEN)],
        scratch_shapes=[
            pltpu.VMEM((width, wide), BF16),
            pltpu.VMEM((width, wide), BF16),
            pltpu.VMEM((LEN, n), BF16),
            pltpu.VMEM((LEN, 128), F32),
            pltpu.VMEM((LEN, HD), F32),
        ],
        compiler_params=params(44),
        cost_estimate=cost(12e9, 14e6, 4e6),
        name="attend_backward",
    )(scalars, d_own, d_other, slots[0], slots[1], slots[3], got, cos, sin, q, k, v, out_t, lse)


def grads_a_kernel(s_ref, xt_ref, dt_ref, dqk_ref, dv_ref, o_ref, mine_ref, send_ref):
    n = dv_ref.shape[2]
    qk = mxu(xt_ref[...], dqk_ref[0]).astype(BF16)
    v = mxu(xt_ref[...], dv_ref[0]).astype(BF16)
    o = mxu(dt_ref[...], o_ref[0]).astype(BF16)

    @pl.when(s_ref[0] == 0)
    def _():
        mine_ref[0] = qk
        send_ref[0, :, :n] = v
        send_ref[0, :, n:] = o

    @pl.when(s_ref[0] == 1)
    def _():
        send_ref[0] = qk
        mine_ref[0, :, :n] = v
        mine_ref[0, :, n:] = o


def grads_a(scalars, x_t, d_t, d_qk, d_v, attended):
    width, length = x_t.shape
    wide, n = d_qk.shape[2], d_v.shape[2]
    whole = pl.BlockSpec((width, length), lambda j: (0, 0))
    by_j = lambda *shape: pl.BlockSpec(shape, lambda j: (j,) + (0,) * (len(shape) - 1))
    return pl.pallas_call(
        grads_a_kernel,
        grid=(2,),
        in_specs=[SMEM, whole, whole, by_j(1, length, wide), by_j(1, length, n), by_j(1, length, n)],
        out_specs=[by_j(1, width, wide)] * 2,
        out_shape=[out(2, width, wide)] * 2,
        compiler_params=params(32),
        cost_estimate=cost(2.4e9, 8e6),
        name="grads_a",
    )(scalars, x_t, d_t, d_qk, d_v, attended)


def input_grad_kernel(s_ref, dqk_ref, dv_ref, a0_ref, a1_ref, a3_ref, got_ref, far_ref, near_ref, qk_w, vo_w, total_ref):
    core = s_ref[0]
    j = pl.program_id(0)
    n = dv_ref.shape[2]
    tokens = far_ref.shape[0]
    pick_weights(core, j, a0_ref, a1_ref, a3_ref, got_ref, qk_w, vo_w)
    part = mxu(dqk_ref[0], qk_w[...], NT) + mxu(dv_ref[0], vo_w[:, :n], NT)

    @pl.when(j == 0)
    def _():
        total_ref[...] = part

    @pl.when(j == 1)
    def _():
        total_ref[...] += part
        near_ref[...] = total_ref[pl.ds(pl.multiple_of(core * tokens, tokens), tokens), :]
        far_ref[...] = total_ref[pl.ds(pl.multiple_of((1 - core) * tokens, tokens), tokens), :].astype(BF16)


def input_grad_parts(scalars, d_qk, d_v, slots, got, tokens):
    width, wide = slots[0].shape
    n = wide // 2
    whole = lambda *shape: pl.BlockSpec(shape, lambda j: (0,) * len(shape))
    by_j = lambda *shape: pl.BlockSpec(shape, lambda j: (j,) + (0,) * (len(shape) - 1))
    return pl.pallas_call(
        input_grad_kernel,
        grid=(2,),
        in_specs=[SMEM, by_j(1, LEN, wide), by_j(1, LEN, n)] + [whole(width, wide)] * 3 + [by_j(1, width, wide)],
        out_specs=[whole(tokens, width)] * 2,
        out_shape=[out(tokens, width), out(tokens, width, dtype=F32)],
        scratch_shapes=[
            pltpu.VMEM((width, wide), BF16),
            pltpu.VMEM((width, wide), BF16),
            pltpu.VMEM((LEN, width), F32),
        ],
        compiler_params=params(32),
        cost_estimate=cost(1.8e9, 8e6),
        name="input_grad",
    )(scalars, d_qk, d_v, slots[0], slots[1], slots[3], got)


def first_norm_kernel(x_ref, near_ref, far_ref, gain_ref, resid_ref, normed_ref):
    residual = x_ref[...].astype(F32) + (near_ref[...] + far_ref[...].astype(F32))
    scale = lax.rsqrt(jnp.mean(residual * residual, -1, keepdims=True) + EPSILON)
    resid_ref[...] = residual
    normed_ref[...] = (residual * scale * gain_ref[0:1, :]).astype(BF16)


def last_norm_kernel(s_ref, resid_ref, near_ref, far_ref, gain_ref, cot_ref, out_ref, dsum_ref, dffn_ref, dgain_ref):
    core, live = s_ref[0], s_ref[1]
    tokens, width = resid_ref.shape
    residual = resid_ref[...]
    scale = lax.rsqrt(jnp.mean(residual * residual, -1, keepdims=True) + EPSILON)
    summed = residual * scale * gain_ref[0:1, :] + (near_ref[...] + far_ref[...].astype(F32))
    scale = lax.rsqrt(jnp.mean(summed * summed, -1, keepdims=True) + EPSILON)
    unit = summed * scale
    out_ref[...] = (unit * gain_ref[1:2, :]).astype(BF16)
    position = core * tokens + lax.broadcasted_iota(jnp.int32, (tokens, 1), 0)
    cot = jnp.where(position < live, cot_ref[...].astype(F32), 0.0)
    dgain_ref[...] = jnp.sum(cot * unit, 0, keepdims=True)
    hat = cot * gain_ref[1:2, :]
    inner = jnp.mean(hat * unit, -1, keepdims=True)
    d_summed = scale * (hat - unit * inner)
    dsum_ref[...] = d_summed
    dffn_ref[...] = d_summed.astype(BF16)


def back_norm_kernel(resid_ref, near_ref, far_ref, dsum_ref, gain_ref, dres_ref, dbranch_ref, dgain_ref):
    residual = resid_ref[...]
    scale = lax.rsqrt(jnp.mean(residual * residual, -1, keepdims=True) + EPSILON)
    unit = residual * scale
    d_normed = dsum_ref[...] + (near_ref[...] + far_ref[...].astype(F32))
    dgain_ref[...] = jnp.sum(d_normed * unit, 0, keepdims=True)
    hat = d_normed * gain_ref[0:1, :]
    inner = jnp.mean(hat * unit, -1, keepdims=True)
    d_residual = scale * (hat - unit * inner)
    dres_ref[...] = d_residual
    dbranch_ref[...] = d_residual.astype(BF16)


def ffn_forward_kernel(y0_ref, y1_ref, g0_ref, g1_ref, g2_ref, g3_ref, dn_ref, hid_ref, silu_ref, slope_ref, far_ref, near_ref):
    tokens = y0_ref.shape[0]
    half = dn_ref.shape[2]
    for part, y_ref in ((1, y1_ref), (0, y0_ref)):
        at = slice(part * tokens, (part + 1) * tokens)
        total = None
        for slot, g_ref in enumerate((g0_ref, g1_ref, g2_ref, g3_ref)):
            both = mxu(y_ref[...], g_ref[...])
            gate, up = both[:, :half], both[:, half:]
            sig = jax.nn.sigmoid(gate)
            silu = gate * sig
            hidden = (silu * up).astype(BF16)
            hid_ref[slot, at, :] = hidden
            silu_ref[slot, at, :] = silu.astype(BF16)
            slope_ref[slot, at, :] = (up * (sig * (1.0 + gate * (1.0 - sig)))).astype(BF16)
            term = mxu(hidden, dn_ref[slot], NT)
            total = term if total is None else total + term
        if part:
            far_ref[...] = total.astype(BF16)
        else:
            near_ref[...] = total


def ffn_backward_kernel(d0_ref, d1_ref, silu_ref, slope_ref, dn_ref, g0_ref, g1_ref, g2_ref, g3_ref, dgu_ref, far_ref, near_ref):
    tokens = d0_ref.shape[0]
    half = dn_ref.shape[2]
    for part, d_ref in ((1, d1_ref), (0, d0_ref)):
        at = slice(part * tokens, (part + 1) * tokens)
        total = None
        for slot, g_ref in enumerate((g0_ref, g1_ref, g2_ref, g3_ref)):
            d_hidden = mxu(d_ref[...], dn_ref[slot])
            dgu_ref[slot, at, :half] = (d_hidden * slope_ref[slot, at, :].astype(F32)).astype(BF16)
            dgu_ref[slot, at, half:] = (d_hidden * silu_ref[slot, at, :].astype(F32)).astype(BF16)
            term = mxu(dgu_ref[slot, at, :], g_ref[...], NT)
            total = term if total is None else total + term
        if part:
            far_ref[...] = total.astype(BF16)
        else:
            near_ref[...] = total


def update(grad_full, moment, weight, average, factor):
    clipped = grad_full * factor
    new_moment = MOMENTUM * moment + clipped
    new_weight = weight - RATE * (clipped + MOMENTUM * new_moment)
    new_average = DECAY * average + (1.0 - DECAY) * new_weight
    return (new_moment, new_weight, new_average)


def update_kernel(s_ref, f_ref, a0_ref, a1_ref, g0_ref, g1_ref, d0_ref, d1_ref, *refs):
    old, new = refs[:12], refs[12:]
    factor = f_ref[0]
    n = old[0].shape[2]
    half = d0_ref.shape[1]

    def put(kind, at, grad):
        results = update(grad, old[4 + kind][at], old[kind][at], old[8 + kind][at], factor)
        for which, value in enumerate(results):
            new[4 * which + kind][at] = value

    def all_of(a_qk, a_vo, g_lo, g_hi, d_lo, d_hi):
        put(0, (0, slice(None), slice(None)), a_qk[:, :n].astype(F32))
        put(0, (1, slice(None), slice(None)), a_qk[:, n:].astype(F32))
        put(0, (2, slice(None), slice(None)), a_vo[:, :n].astype(F32))
        put(1, (slice(None), slice(None)), a_vo[:, n:].astype(F32).T)
        for which, (g_ref, d_ref) in enumerate(((g_lo, d_lo), (g_hi, d_hi))):
            lanes = slice(which * half, (which + 1) * half)
            put(2, (0, slice(None), lanes), g_ref[:, :half].astype(F32))
            put(2, (1, slice(None), lanes), g_ref[:, half:].astype(F32))
            put(3, (lanes, slice(None)), d_ref[...].astype(F32).T)

    @pl.when(s_ref[0] == 0)
    def _():
        all_of(a0_ref, a1_ref, g0_ref, g1_ref, d0_ref, d1_ref)

    @pl.when(s_ref[0] == 1)
    def _():
        all_of(a1_ref, a0_ref, g1_ref, g0_ref, d1_ref, d0_ref)


def body(
    rows,
    cols,
    block_input,
    out_grad,
    lengths,
    w_qkv,
    w_out,
    w_gate_up,
    w_down,
    gains,
    mom_qkv,
    mom_out,
    mom_gate_up,
    mom_down,
    mom_gains,
    ema_qkv,
    ema_out,
    ema_gate_up,
    ema_down,
    ema_gains,
):
    d = lax.axis_index("dp")
    r = lax.axis_index("row")
    c = lax.axis_index("col")
    core0 = d == 0
    tokens, width = block_input.shape
    ring = cols <= 4
    part = width // cols
    head_cols = w_qkv.shape[2]
    half = w_gate_up.shape[2] // 2

    pairs = [(i, j) for i in range(2) for j in range(rows)]
    swap_pairs = [(i * rows + j, (j % 2) * rows + (j // 2) * 2 + i) for i, j in pairs]
    first_pairs = [(i * rows + j, i * rows + (j ^ (1 if i == 0 else 2))) for i, j in pairs]
    second_pairs = [(i * rows + j, i * rows + (j ^ (2 if i == 0 else 1))) for i, j in pairs]

    def swap_tokens(t):
        return lax.ppermute(t, ("dp", "row"), swap_pairs)

    def first(t):
        return lax.ppermute(t, ("dp", "row"), first_pairs)

    def second(t):
        return lax.ppermute(t, ("dp", "row"), second_pairs)

    def core(t):
        return lax.ppermute(t, "dp", [(0, 1), (1, 0)])

    def along(t, k):
        return lax.ppermute(t, "col", [(i, (i + k) % cols) for i in range(cols)])

    def sum_over(t, axis, size):
        values = [t] + [lax.ppermute(t, axis, [(i, i ^ b) for i in range(size)]) for b in range(1, size)]
        while len(values) > 1:
            values = [values[i] + values[i + 1] for i in range(0, len(values), 2)]
        return values[0]

    def sum_chips(t):
        t = sum_over(t, "row", rows)
        if cols <= 4:
            return sum_over(t, "col", cols)
        return lax.psum(t, "col")

    def shift(k):
        return lax.rem(c + k + cols, cols) * part

    def spread_cols(t, axis):
        return [along(t, k) for k in range(1, cols)]

    def join_cols(t, got, axis):
        shape = list(t.shape)
        shape[axis] = width
        whole = jnp.zeros(shape, t.dtype)
        for k, block in enumerate([t] + got):
            whole = lax.dynamic_update_slice_in_dim(whole, block, shift(-k), axis)
        return whole

    def block_of(t, k, axis):
        return lax.dynamic_slice_in_dim(t, shift(k), part, axis)

    def scatter_cols(t):
        if not ring:
            return lax.psum_scatter(t, "col", scatter_dimension=0, tiled=True).astype(F32)
        got = [along(block_of(t, k, 0), k) for k in range(1, cols)]
        total = block_of(t, 0, 0).astype(F32)
        for block in got:
            total = total + block.astype(F32)
        return total

    core_id = jnp.full((1,), d, jnp.int32)
    piece_a, piece_d = pl.pallas_call(
        pieces_ad_kernel,
        in_specs=[SMEM, VMEM, VMEM, VMEM],
        out_specs=[VMEM] * 2,
        out_shape=[out(part, 2 * head_cols), out(part, half)],
        compiler_params=params(16),
        name="pieces_ad",
    )(core_id, w_qkv, w_out, w_down)

    x_own = swap_tokens(block_input)
    own_length = swap_tokens(lengths)[0, :]
    seq_ids = jnp.arange(own_length.shape[0], dtype=jnp.int32)
    own_length = jnp.sum(jnp.where(seq_ids == r // 2, own_length, 0))
    scalars = jnp.stack([d.astype(jnp.int32), own_length])
    (piece_g,) = pl.pallas_call(
        pieces_g_kernel,
        in_specs=[SMEM, VMEM],
        out_specs=[VMEM],
        out_shape=[out(part, 2 * half)],
        compiler_params=params(16),
        name="pieces_g",
    )(core_id, w_gate_up)

    got_a = spread_cols(piece_a, 0) if ring else lax.all_gather(piece_a, "col", axis=0, tiled=True)
    d1, d2 = first(piece_d), second(piece_d)
    got_a, d1, d2, piece_g, x_own = fence(got_a, d1, d2, piece_g, x_own)
    full_a = join_cols(piece_a, got_a, 0) if ring else got_a
    a1, a2 = first(full_a), second(full_a)
    got_g = spread_cols(piece_g, 0) if ring else lax.all_gather(piece_g, "col", axis=0, tiled=True)
    d3 = second(d1)
    x_other = core(x_own)
    full_a, a1, a2, got_g, d3, x_other = fence(full_a, a1, a2, got_g, d3, x_other)
    a3 = second(a1)
    slots_d = jnp.stack([piece_d, d1, d2, d3])
    if ring:
        ring_d = [along(slots_d, 1)]
    full_g = join_cols(piece_g, got_g, 0) if ring else got_g
    a3, ring_d, full_g = fence(a3, ring_d if ring else [], full_g)
    slots_a = [full_a, a1, a2, a3]
    send = jnp.where(core0, jnp.stack([a2, a3]), jnp.stack([full_a, a2]))
    got = core(send)
    g1, g2 = first(full_g), second(full_g)
    if ring and cols > 2:
        ring_d = ring_d + [along(ring_d[-1], 1)]

    cos, sin = pair_tables()
    q, k, v, attended, attended_t, lse, x_t, far, near = attend_forward(
        scalars, x_own, x_other, slots_a, got, cos, sin
    )
    far, g1, g2, ring_d = fence(far, g1, g2, ring_d)
    g3 = second(g1)
    if ring and cols > 3:
        ring_d = ring_d + [along(ring_d[-1], 1)]
    slots_g = [full_g, g1, g2, g3]
    if ring:
        w_dn = join_cols(slots_d, ring_d, 1)
    else:
        w_dn = lax.all_gather(slots_d, "col", axis=1, tiled=True)

    residual, normed = pl.pallas_call(
        first_norm_kernel,
        in_specs=[VMEM] * 4,
        out_specs=[VMEM] * 2,
        out_shape=[out(tokens, width, dtype=F32), out(tokens, width)],
        compiler_params=params(24),
        cost_estimate=cost(4e6, 6e6),
        name="first_norm",
    )(x_own, near, core(far), gains)
    normed_other = core(normed)

    hidden, silu, slope, far, near = pl.pallas_call(
        ffn_forward_kernel,
        in_specs=[VMEM] * 7,
        out_specs=[VMEM] * 5,
        out_shape=[out(4, 2 * tokens, half)] * 3 + [out(tokens, width), out(tokens, width, dtype=F32)],
        compiler_params=params(48),
        cost_estimate=cost(5e9, 15e6, 1e6),
        name="ffn_forward",
    )(normed, normed_other, *slots_g, w_dn)
    cot = swap_tokens(out_grad)
    output, d_summed, d_ffn, grad_gain_two = pl.pallas_call(
        last_norm_kernel,
        in_specs=[SMEM] + [VMEM] * 5,
        out_specs=[VMEM] * 4,
        out_shape=[out(tokens, width), out(tokens, width, dtype=F32), out(tokens, width), out(1, width, dtype=F32)],
        compiler_params=params(32),
        cost_estimate=cost(10e6, 8e6),
        name="last_norm",
    )(scalars, residual, near, core(far), gains, cot)
    d_ffn_other = core(d_ffn)
    d_ffn_full = jnp.concatenate([d_ffn, d_ffn_other], 0)
    normed_full = jnp.concatenate([normed, normed_other], 0)

    grad_dn = jnp.einsum("td,ste->sde", d_ffn_full, hidden, preferred_element_type=F32).astype(BF16)
    if ring:
        moving = along(block_of(grad_dn, cols - 1, 1), 1)
    d_gu, far, near = pl.pallas_call(
        ffn_backward_kernel,
        in_specs=[VMEM] * 9,
        out_specs=[VMEM] * 3,
        out_shape=[out(4, 2 * tokens, 2 * half), out(tokens, width), out(tokens, width, dtype=F32)],
        compiler_params=params(48),
        cost_estimate=cost(5e9, 15e6),
        name="ffn_backward",
    )(d_ffn, d_ffn_other, silu, slope, w_dn, *slots_g)
    if ring:
        far, moving, d_gu = fence(far, moving, d_gu)

    def grad_gu(s):
        return jnp.einsum("td,te->de", normed_full, d_gu[s], preferred_element_type=F32).astype(BF16)

    got_far = core(far)
    gu3 = grad_gu(3)
    gu1 = grad_gu(1)
    got_far, gu3, gu1 = fence(got_far, gu3, gu1)
    moved = second(gu3)
    if ring:
        for hop in range(cols - 2, 0, -1):
            block = (block_of(grad_dn, hop, 1).astype(F32) + moving.astype(F32)).astype(BF16)
            moving = along(block, 1)
        own_dn = (block_of(grad_dn, 0, 1).astype(F32) + moving.astype(F32)).astype(BF16)
    else:
        own_dn = lax.psum_scatter(grad_dn, "col", scatter_dimension=1, tiled=True)
    d_residual, d_branch, grad_gain_one = pl.pallas_call(
        back_norm_kernel,
        in_specs=[VMEM] * 5,
        out_specs=[VMEM] * 3,
        out_shape=[out(tokens, width, dtype=F32), out(tokens, width), out(1, width, dtype=F32)],
        compiler_params=params(32),
        cost_estimate=cost(10e6, 8e6),
        name="back_norm",
    )(residual, near, got_far, d_summed, gains)
    d_branch_other = core(d_branch)
    gu2, gu0 = grad_gu(2), grad_gu(0)
    moved, d_branch_other, gu2, gu0 = fence(moved, d_branch_other, gu2, gu0)
    gu1 = (gu1.astype(F32) + moved.astype(F32)).astype(BF16)
    moved_one, moved_two = first(gu1), second(gu2)
    d_qk, d_v, d_t = attend_backward(
        scalars, d_branch, d_branch_other, slots_a, got, cos, sin, q, k, v, attended_t, lse
    )
    moved_one, moved_two, d_qk, d_v, d_t = fence(moved_one, moved_two, d_qk, d_v, d_t)
    gu0 = (gu0.astype(F32) + moved_one.astype(F32) + moved_two.astype(F32)).astype(BF16)
    shard_g = scatter_cols(gu0).astype(BF16)
    mine, send = grads_a(scalars, x_t, d_t, d_qk, d_v, attended)
    theirs = core(send)
    s3 = jnp.where(core0, theirs[1], mine[1])
    s1 = jnp.where(core0, mine[1], mine[0])
    s2 = jnp.where(core0, theirs[0], theirs[1])
    s0 = jnp.where(core0, mine[0], theirs[0])
    moved = second(s3)
    far, near = input_grad_parts(scalars, d_qk, d_v, slots_a, got, tokens)
    moved, far, near = fence(moved, far, near)
    s1 = (s1.astype(F32) + moved.astype(F32)).astype(BF16)
    moved_one, moved_two = first(s1), second(s2)
    input_grad = (d_residual + (near + core(far).astype(F32))).astype(BF16)
    moved_dn = second(own_dn[3])
    moved_one, moved_two, input_grad, moved_dn = fence(moved_one, moved_two, input_grad, moved_dn)
    s0 = (s0.astype(F32) + moved_one.astype(F32) + moved_two.astype(F32)).astype(BF16)
    shard_a = scatter_cols(s0).astype(BF16)
    dn1 = (own_dn[1].astype(F32) + moved_dn.astype(F32)).astype(BF16)
    shard_d = (own_dn[0].astype(F32) + first(dn1).astype(F32) + second(own_dn[2]).astype(F32)).astype(BF16)
    input_grad = swap_tokens(input_grad).astype(F32)
    output = swap_tokens(output).astype(F32)

    far_a, far_g, far_d = core(shard_a), core(shard_g), core(shard_d)
    gain_total = jnp.concatenate([grad_gain_one, grad_gain_two], 0)
    gain_total = sum_chips(sum_over(gain_total, "dp", 2))
    local_squares = sum(jnp.sum(jnp.square(t.astype(F32))) for t in (shard_a, shard_g, shard_d))
    remote_squares = sum(jnp.sum(jnp.square(t.astype(F32))) for t in (far_a, far_g, far_d))
    local_squares = local_squares + remote_squares
    squares = sum_chips(jnp.full((8, 128), local_squares, F32))[0, 0] + jnp.sum(gain_total * gain_total)
    grad_norm = jnp.sqrt(squares)
    factor = jnp.minimum(1.0, CLIP / (grad_norm + 1e-06))
    weights = (w_qkv, w_out, w_gate_up, w_down)
    moments = (mom_qkv, mom_out, mom_gate_up, mom_down)
    averages = (ema_qkv, ema_out, ema_gate_up, ema_down)
    results = pl.pallas_call(
        update_kernel,
        in_specs=[SMEM, SMEM] + [VMEM] * 18,
        out_specs=[VMEM] * 12,
        out_shape=[out(*t.shape, dtype=F32) for t in weights * 3],
        compiler_params=params(40),
        cost_estimate=cost(5e6, 12e6),
        name="update",
    )(core_id, factor[None], shard_a, far_a, shard_g, far_g, shard_d, far_d, *weights, *moments, *averages)
    gain_new = update(gain_total, mom_gains, gains, ema_gains, factor)
    return (
        output,
        input_grad,
        grad_norm,
        *results[0:4],
        gain_new[0],
        *results[4:8],
        gain_new[1],
        *results[8:12],
        gain_new[2],
    )


def solution(mesh):
    tok = P(("dp", "col", "row"), None)
    weights = (P(None, "col", "row"), P("row", "col"), P(None, "col", "row"), P("row", "col"), P())
    in_specs = (tok, tok, P(("dp", "col"), None)) + weights * 3
    out_specs = (tok, tok, P()) + weights * 3
    fn = functools.partial(body, mesh.shape["row"], mesh.shape["col"])
    return jax.shard_map(fn, mesh=mesh, in_specs=in_specs, out_specs=out_specs, check_vma=False)
```

```python
import functools

import jax
import jax.numpy as jnp
import numpy as np
from jax import lax
from jax.experimental import pallas as pl
from jax.experimental.pallas import tpu as pltpu
from jax.sharding import PartitionSpec as P

HD = 64
LEN = 1024

EPSILON = 1e-06
THETA = 10000.0
MOMENTUM = 0.9
RATE = 300.0
DECAY = 0.6
CLIP = 1.0
NEGATIVE = -1e30

F32 = jnp.float32
BF16 = jnp.bfloat16
NT = (((1,), (1,)), ((), ()))
NN = (((1,), (0,)), ((), ()))
TN = (((0,), (0,)), ((), ()))
BQ = 256


def rope_tables():
    half = HD // 2
    freqs = np.float32(THETA) ** (-(np.arange(half, dtype=np.float32) * np.float32(2.0)) / np.float32(HD))
    angles = np.arange(LEN, dtype=np.float32)[:, None] * freqs[None, :].astype(np.float32)
    return np.cos(angles), np.sin(angles)


def pair_tables():
    cosine, sine = rope_tables()
    return (
        jnp.asarray(np.concatenate([cosine] * 4, 1)),
        jnp.asarray(np.concatenate([-sine, sine] * 2, 1)),
    )


def mxu(lhs, rhs, dims=NN):
    return lax.dot_general(lhs, rhs, dims, preferred_element_type=F32)


def fence(*values):
    return lax.optimization_barrier(values)


def params(mib):
    return pltpu.CompilerParams(vmem_limit_bytes=mib << 20)


def cost(flops, bytes_moved, exps=0):
    return pl.CostEstimate(flops=int(flops), bytes_accessed=int(bytes_moved), transcendentals=int(exps))


def out(*shape, dtype=BF16):
    return jax.ShapeDtypeStruct(shape, dtype)


VMEM = pl.BlockSpec(memory_space=pltpu.VMEM)
SMEM = pl.BlockSpec(memory_space=pltpu.SMEM)
ANY = pl.BlockSpec(memory_space=pl.ANY)
DMA = pltpu.SemaphoreType.DMA


def piece_a_kernel(s_ref, qkv_ref, out_ref, a_ref):
    n = qkv_ref.shape[2]

    @pl.when(s_ref[0] == 0)
    def _():
        a_ref[:, :n] = qkv_ref[0].astype(BF16)
        a_ref[:, n:] = qkv_ref[1].astype(BF16)

    @pl.when(s_ref[0] == 1)
    def _():
        a_ref[:, :n] = qkv_ref[2].astype(BF16)
        a_ref[:, n:] = out_ref[...].T.astype(BF16)


def piece_f_kernel(s_ref, gu_ref, down_ref, f_ref):
    half = f_ref.shape[1] // 3
    at = pl.ds(pl.multiple_of(s_ref[0] * half, half), half)
    f_ref[:, :half] = gu_ref[0, :, at].astype(BF16)
    f_ref[:, half : 2 * half] = gu_ref[1, :, at].astype(BF16)
    f_ref[:, 2 * half :] = down_ref[:, at].astype(BF16)


def causal(scores_t, block):
    keys = scores_t.shape[0]
    row = lax.broadcasted_iota(jnp.int32, (block, block), 0)
    column = lax.broadcasted_iota(jnp.int32, (block, block), 1)
    tail = jnp.where(row <= column, scores_t[keys - block :], NEGATIVE)
    return tail if keys == block else jnp.concatenate([scores_t[: keys - block], tail], 0)


def swap_halves(t):
    lane = lax.broadcasted_iota(jnp.int32, (1, t.shape[1]), 1)
    return jnp.where(lane % HD < HD // 2, pltpu.roll(t, t.shape[1] - HD // 2, 1), pltpu.roll(t, HD // 2, 1))


def pick_weights(core, j, a0_ref, a1_ref, a3_ref, got_ref, qk_ref, vo_ref):
    @pl.when(core == 0)
    def _():
        vo_ref[...] = got_ref[0]

        @pl.when(j == 0)
        def _():
            qk_ref[...] = a0_ref[...]

        @pl.when(j == 1)
        def _():
            qk_ref[...] = a1_ref[...]

    @pl.when(core == 1)
    def _():
        qk_ref[...] = got_ref[0]

        @pl.when(j == 0)
        def _():
            vo_ref[...] = a1_ref[...]

        @pl.when(j == 1)
        def _():
            vo_ref[...] = a3_ref[...]


def attend_forward_kernel(
    s_ref, x0_ref, x1_ref, a0_ref, a1_ref, a3_ref, got_ref, cos_ref, sin_ref,
    q_ref, k_ref, v_ref, ot_ref, lse_ref, xt_ref, far_ref, near_ref,
    qk_w, vo_w, o_ref, total_ref,
):
    core, live = s_ref[0], s_ref[1]
    j = pl.program_id(0)
    length = q_ref.shape[1]
    tokens = x0_ref.shape[0]
    n = 3 * HD
    pick_weights(core, j, a0_ref, a1_ref, a3_ref, got_ref, qk_w, vo_w)
    lane = lax.broadcasted_iota(jnp.int32, (tokens, HD), 1)
    one = jnp.where(lane == 0, 1.0, 0.0).astype(BF16)
    for x_ref, which in ((x0_ref, core), (x1_ref, 1 - core)):
        start = pl.multiple_of(which * tokens, tokens)
        at = pl.ds(start, tokens)
        qk = mxu(x_ref[...], qk_w[...])
        cos = jnp.concatenate([cos_ref[at, :]] * 3, 1)
        sin = jnp.concatenate([sin_ref[at, :]] * 3, 1)
        qk = qk * cos + swap_halves(qk) * sin
        q = (qk[:, :n] * (HD ** -0.5)).astype(BF16)
        k = qk[:, n:].astype(BF16)
        v = mxu(x_ref[...], vo_w[:, :n]).astype(BF16)
        key = start + lax.broadcasted_iota(jnp.int32, (tokens, HD), 0)
        bias = jnp.where((lane == 0) & (key >= live), NEGATIVE, 0.0).astype(BF16)
        for head in range(3):
            lanes = slice(head * HD, (head + 1) * HD)
            q_ref[head, at, :] = jnp.concatenate([q[:, lanes], one], 1)
            k_ref[head, at, :] = jnp.concatenate([k[:, lanes], bias], 1)
            v_ref[head, at, :] = jnp.concatenate([v[:, lanes], one], 1)

        @pl.when(j == 0)
        def _():
            xt_ref[:, at] = x_ref[...].T

    for block in range(length // BQ):
        keys = (block + 1) * BQ
        span = slice(block * BQ, keys)
        parts = []
        for head in range(3):
            scores = causal(mxu(k_ref[head, :keys, :], q_ref[head, span, :], NT), BQ)
            top = jnp.max(scores, 0, keepdims=True)
            probs = jnp.exp(scores - top).astype(BF16)
            o = mxu(v_ref[head, :keys, :], probs, TN)
            total = o[HD : HD + 1]
            parts.append(o[:HD] / total)
            lse_ref[0, head : head + 1, span] = top + jnp.log(total)
        o = jnp.concatenate(parts, 0)
        ot_ref[0, :, span] = o.astype(BF16)
        o_ref[span, :] = o.T.astype(BF16)
    part = mxu(o_ref[...], vo_w[:, n:], NT)

    @pl.when(j == 0)
    def _():
        total_ref[...] = part

    @pl.when(j == 1)
    def _():
        total_ref[...] += part
        near_ref[...] = total_ref[pl.ds(pl.multiple_of(core * tokens, tokens), tokens), :]
        far_ref[...] = total_ref[pl.ds(pl.multiple_of((1 - core) * tokens, tokens), tokens), :].astype(BF16)


def attend_forward(scalars, x_own, x_other, slots, got, cos, sin):
    tokens, width = x_own.shape
    wide = slots[0].shape[1]
    n = wide // 2
    whole = lambda *shape: pl.BlockSpec(shape, lambda j: (0,) * len(shape))
    by_j = lambda *shape: pl.BlockSpec(shape, lambda j: (j,) + (0,) * (len(shape) - 1))
    return pl.pallas_call(
        attend_forward_kernel,
        grid=(2,),
        in_specs=[SMEM]
        + [whole(tokens, width)] * 2
        + [whole(width, wide)] * 3
        + [by_j(1, width, wide), whole(LEN, 128), whole(LEN, 128)],
        out_specs=[by_j(3, LEN, 128)] * 3
        + [by_j(1, n, LEN), by_j(1, 8, LEN), whole(width, LEN)]
        + [whole(tokens, width)] * 2,
        out_shape=[out(6, LEN, 128)] * 3
        + [out(2, n, LEN), out(2, 8, LEN, dtype=F32), out(width, LEN)]
        + [out(tokens, width), out(tokens, width, dtype=F32)],
        scratch_shapes=[
            pltpu.VMEM((width, wide), BF16),
            pltpu.VMEM((width, wide), BF16),
            pltpu.VMEM((LEN, n), BF16),
            pltpu.VMEM((LEN, width), F32),
        ],
        compiler_params=params(44),
        cost_estimate=cost(8e9, 12e6, 4e6),
        name="attend_forward",
    )(scalars, x_own, x_other, slots[0], slots[1], slots[3], got, cos, sin)


def attend_backward_kernel(
    s_ref, d0_ref, d1_ref, lo_ref, hi_ref, got_ref, cos_ref, sin_ref, ot_ref, lse_ref,
    q_any, k_any, v_any, xt_any,
    dqk_ref, dv_ref, mine_ref, send_ref,
    q_ref, k_ref, v_ref, xt_ref, vo_w, do_ref, dk_acc, dv_acc, sems, *, j,
):
    core = s_ref[0]
    tokens = d0_ref.shape[0]
    n = 3 * HD
    heads = pl.ds(3 * j, 3)
    copies = [
        pltpu.make_async_copy(k_any.at[heads], k_ref, sems.at[0]),
        pltpu.make_async_copy(q_any.at[heads], q_ref, sems.at[1]),
        pltpu.make_async_copy(v_any.at[heads], v_ref, sems.at[2]),
        pltpu.make_async_copy(xt_any, xt_ref, sems.at[3]),
    ]
    for copy in copies:
        copy.start()

    @pl.when(core == 0)
    def _():
        vo_w[...] = got_ref[0, :, n:]

    @pl.when(core == 1)
    def _():
        vo_w[...] = hi_ref[:, n:]

    for d_ref, which in ((d0_ref, core), (d1_ref, 1 - core)):
        at = pl.ds(pl.multiple_of(which * tokens, tokens), tokens)
        do_ref[at, :] = mxu(d_ref[...], vo_w[...]).astype(BF16)

    length = do_ref.shape[0]
    products = do_ref[...].astype(F32).T * ot_ref[0].astype(F32)
    for copy in copies[:3]:
        copy.wait()

    def unrotate(t):
        return t * cos_ref[...] - swap_halves(t) * sin_ref[...]

    for head in range(3):
        lanes = slice(head * HD, (head + 1) * HD)
        delta = jnp.sum(products[lanes], 0, keepdims=True)
        dq_parts = []
        for block in range(length // BQ):
            keys = (block + 1) * BQ
            span = slice(block * BQ, keys)
            before = keys - BQ
            q = q_ref[head, span, :]
            scores = causal(mxu(k_ref[head, :keys, :], q, NT), BQ)
            probs = jnp.exp(scores - lse_ref[0, head : head + 1, span])
            d_out = do_ref[span, lanes]
            d_probs = mxu(v_ref[head, :keys, :HD], d_out, NT)
            d_scores = (probs * (d_probs - delta[:, span])).astype(BF16)
            dv_part = mxu(probs.astype(BF16), d_out)
            dk_part = mxu(d_scores, q)
            if block:
                dv_acc[:before, :] += dv_part[:before]
                dk_acc[:before, :] += dk_part[:before]
            dv_acc[before:keys, :] = dv_part[before:]
            dk_acc[before:keys, :] = dk_part[before:]
            dq_parts.append(mxu(d_scores, k_ref[head, :keys, :], TN))
        dq = jnp.concatenate(dq_parts, 0) * (HD ** -0.5)
        dqk_ref[:, head * HD : (head + 1) * HD] = unrotate(dq)[:, :HD].astype(BF16)
        dqk_ref[:, n + head * HD : n + (head + 1) * HD] = unrotate(dk_acc[...])[:, :HD].astype(BF16)
        dv_ref[:, lanes] = dv_acc[...].astype(BF16)

    copies[3].wait()
    own = jnp.where(core == 0, 0, tokens)
    grad_o = jnp.zeros((n, d0_ref.shape[1]), F32)
    for d_ref, which in ((d0_ref, core), (d1_ref, 1 - core)):
        at = pl.ds(pl.multiple_of(which * tokens, tokens), tokens)
        grad_o += mxu(ot_ref[0, :, at], d_ref[...])
    grad_o = grad_o.T.astype(BF16)
    grad_qk = mxu(xt_ref[...], dqk_ref[...]).astype(BF16)
    grad_v = mxu(xt_ref[...], dv_ref[...]).astype(BF16)

    @pl.when(core == 0)
    def _():
        mine_ref[...] = grad_qk
        send_ref[:, :n] = grad_v
        send_ref[:, n:] = grad_o

    @pl.when(core == 1)
    def _():
        send_ref[...] = grad_qk
        mine_ref[:, :n] = grad_v
        mine_ref[:, n:] = grad_o


def attend_backward(j, scalars, d_own, d_other, slots, got, cos, sin, q, k, v, out_t, lse, x_t):
    tokens, width = d_own.shape
    wide = slots[0].shape[1]
    n = wide // 2
    whole = lambda *shape: pl.BlockSpec(shape, lambda i: (0,) * len(shape))
    at_j = lambda *shape: pl.BlockSpec(shape, lambda i: (j,) + (0,) * (len(shape) - 1))
    lo, hi = (slots[0], slots[1]) if j == 0 else (slots[1], slots[3])
    return pl.pallas_call(
        functools.partial(attend_backward_kernel, j=j),
        grid=(1,),
        in_specs=[SMEM]
        + [whole(tokens, width)] * 2
        + [whole(width, wide)] * 2
        + [at_j(1, width, wide), whole(LEN, 128), whole(LEN, 128), at_j(1, n, LEN), at_j(1, 8, LEN)]
        + [ANY] * 4,
        out_specs=[whole(LEN, wide), whole(LEN, n), whole(width, wide), whole(width, wide)],
        out_shape=[out(LEN, wide), out(LEN, n), out(width, wide), out(width, wide)],
        scratch_shapes=[
            pltpu.VMEM((3, LEN, 128), BF16),
            pltpu.VMEM((3, LEN, 128), BF16),
            pltpu.VMEM((3, LEN, 128), BF16),
            pltpu.VMEM((width, LEN), BF16),
            pltpu.VMEM((width, n), BF16),
            pltpu.VMEM((LEN, n), BF16),
            pltpu.VMEM((LEN, 128), F32),
            pltpu.VMEM((LEN, HD), F32),
            DMA((4,)),
        ],
        compiler_params=params(40),
        cost_estimate=cost(6e9, 8e6, 2e6),
        name="attend_backward",
    )(scalars, d_own, d_other, lo, hi, got, cos, sin, out_t, lse, q, k, v, x_t)


def input_grad_kernel(s_ref, p0_ref, p1_ref, v0_ref, v1_ref, a0_ref, a1_ref, a3_ref, got_ref, far_ref, near_ref, qk_w, vo_w):
    core = s_ref[0]
    n = v0_ref.shape[1]
    tokens = far_ref.shape[0]
    for j, (lo, hi) in enumerate(((a0_ref, a1_ref), (a1_ref, a3_ref))):

        @pl.when(core == 0)
        def _():
            qk_w[j] = lo[...]
            vo_w[j] = got_ref[j, :, :n]

        @pl.when(core == 1)
        def _():
            qk_w[j] = got_ref[j]
            vo_w[j] = hi[:, :n]

    for which, dst in ((1 - core, far_ref), (core, near_ref)):
        at = pl.ds(pl.multiple_of(which * tokens, tokens), tokens)
        total = mxu(p0_ref[at, :], qk_w[0], NT) + mxu(v0_ref[at, :], vo_w[0], NT)
        total = total + (mxu(p1_ref[at, :], qk_w[1], NT) + mxu(v1_ref[at, :], vo_w[1], NT))
        dst[...] = total.astype(dst.dtype)


def input_grad_parts(scalars, d_qk, d_v, slots, got, tokens):
    width, wide = slots[0].shape
    return pl.pallas_call(
        input_grad_kernel,
        in_specs=[SMEM] + [VMEM] * 8,
        out_specs=[VMEM] * 2,
        out_shape=[out(tokens, width), out(tokens, width, dtype=F32)],
        scratch_shapes=[pltpu.VMEM((2, width, wide), BF16), pltpu.VMEM((2, width, wide // 2), BF16)],
        compiler_params=params(32),
        cost_estimate=cost(1.8e9, 8e6),
        name="input_grad",
    )(scalars, *d_qk, *d_v, slots[0], slots[1], slots[3], got)


def first_norm_kernel(x_ref, near_ref, far_ref, gain_ref, resid_ref, normed_ref):
    residual = x_ref[...].astype(F32) + (near_ref[...] + far_ref[...].astype(F32))
    scale = lax.rsqrt(jnp.mean(residual * residual, -1, keepdims=True) + EPSILON)
    resid_ref[...] = residual
    normed_ref[...] = (residual * scale * gain_ref[0:1, :]).astype(BF16)


def last_norm_kernel(s_ref, resid_ref, near_ref, far_ref, gain_ref, cot_ref, out_ref, dsum_ref, dffn_ref, dgain_ref):
    core, live = s_ref[0], s_ref[1]
    tokens, width = resid_ref.shape
    residual = resid_ref[...]
    scale = lax.rsqrt(jnp.mean(residual * residual, -1, keepdims=True) + EPSILON)
    summed = residual * scale * gain_ref[0:1, :] + (near_ref[...] + far_ref[...].astype(F32))
    scale = lax.rsqrt(jnp.mean(summed * summed, -1, keepdims=True) + EPSILON)
    unit = summed * scale
    out_ref[...] = (unit * gain_ref[1:2, :]).astype(BF16)
    position = core * tokens + lax.broadcasted_iota(jnp.int32, (tokens, 1), 0)
    cot = jnp.where(position < live, cot_ref[...].astype(F32), 0.0)
    dgain_ref[...] = jnp.sum(cot * unit, 0, keepdims=True)
    hat = cot * gain_ref[1:2, :]
    inner = jnp.mean(hat * unit, -1, keepdims=True)
    d_summed = scale * (hat - unit * inner)
    dsum_ref[...] = d_summed
    dffn_ref[...] = d_summed.astype(BF16)


def back_norm_kernel(resid_ref, near_ref, far_ref, dsum_ref, gain_ref, dres_ref, dbranch_ref, dgain_ref):
    residual = resid_ref[...]
    scale = lax.rsqrt(jnp.mean(residual * residual, -1, keepdims=True) + EPSILON)
    unit = residual * scale
    d_normed = dsum_ref[...] + (near_ref[...] + far_ref[...].astype(F32))
    dgain_ref[...] = jnp.sum(d_normed * unit, 0, keepdims=True)
    hat = d_normed * gain_ref[0:1, :]
    inner = jnp.mean(hat * unit, -1, keepdims=True)
    d_residual = scale * (hat - unit * inner)
    dres_ref[...] = d_residual
    dbranch_ref[...] = d_residual.astype(BF16)


def fetch_slots(step, sources, dst, sems):
    copies = [pltpu.make_async_copy(src, dst.at[i], sems.at[i]) for i, src in enumerate(sources)]

    @pl.when(step == 0)
    def _():
        for copy in copies:
            copy.start()

    for i, copy in enumerate(copies):

        @pl.when(step == i)
        def _():
            copy.wait()


def ffn_forward_kernel(
    y0_ref, y1_ref, f0_ref, f1_ref, f2_ref, f3_ref,
    hid_ref, silu_ref, slope_ref, far_ref, near_ref,
    w_ref, total_ref, sems,
):
    slot = pl.program_id(0)
    tokens = y0_ref.shape[0]
    half = hid_ref.shape[2]
    fetch_slots(slot, (f0_ref, f1_ref, f2_ref, f3_ref), w_ref, sems)
    for part, y_ref in ((0, y0_ref), (1, y1_ref)):
        at = slice(part * tokens, (part + 1) * tokens)
        both = mxu(y_ref[...], w_ref[slot, :, : 2 * half])
        gate, up = both[:, :half], both[:, half:]
        sig = jax.nn.sigmoid(gate)
        silu = gate * sig
        hidden = (silu * up).astype(BF16)
        hid_ref[0, at, :] = hidden
        silu_ref[0, at, :] = silu.astype(BF16)
        slope_ref[0, at, :] = (up * (sig * (1.0 + gate * (1.0 - sig)))).astype(BF16)
        term = mxu(hidden, w_ref[slot, :, 2 * half :], NT)

        @pl.when(slot == 0)
        def _():
            total_ref[at, :] = term

        @pl.when(slot > 0)
        def _():
            total_ref[at, :] += term

    @pl.when(slot == 3)
    def _():
        near_ref[...] = total_ref[:tokens, :]
        far_ref[...] = total_ref[tokens:, :].astype(BF16)


def ffn_backward_kernel(
    d0_ref, d1_ref, silu_ref, slope_ref, f0_ref, f1_ref, f2_ref, f3_ref,
    dgu_ref, far_ref, near_ref,
    w_ref, total_ref, sems,
):
    slot = pl.program_id(0)
    tokens = d0_ref.shape[0]
    half = silu_ref.shape[2]
    fetch_slots(slot, (f0_ref, f1_ref, f2_ref, f3_ref), w_ref, sems)
    for part, d_ref in ((0, d0_ref), (1, d1_ref)):
        at = slice(part * tokens, (part + 1) * tokens)
        d_hidden = mxu(d_ref[...], w_ref[slot, :, 2 * half :])
        dgu_ref[0, at, :half] = (d_hidden * slope_ref[0, at, :].astype(F32)).astype(BF16)
        dgu_ref[0, at, half:] = (d_hidden * silu_ref[0, at, :].astype(F32)).astype(BF16)
        term = mxu(dgu_ref[0, at, :], w_ref[slot, :, : 2 * half], NT)

        @pl.when(slot == 0)
        def _():
            total_ref[at, :] = term

        @pl.when(slot > 0)
        def _():
            total_ref[at, :] += term

    @pl.when(slot == 3)
    def _():
        near_ref[...] = total_ref[:tokens, :]
        far_ref[...] = total_ref[tokens:, :].astype(BF16)


def ffn_call(kernel, name, tokens_in, by_slot, slots, widths):
    tokens, width = tokens_in[0].shape
    lanes = slots[0].shape[1]
    whole = lambda *shape: pl.BlockSpec(shape, lambda s: (0,) * len(shape))
    per_slot = lambda n: pl.BlockSpec((1, 2 * tokens, n), lambda s: (s, 0, 0))
    return pl.pallas_call(
        kernel,
        grid=(4,),
        in_specs=[whole(tokens, width)] * 2 + [per_slot(t.shape[2]) for t in by_slot] + [ANY] * 4,
        out_specs=[per_slot(n) for n in widths] + [whole(tokens, width)] * 2,
        out_shape=[out(4, 2 * tokens, n) for n in widths]
        + [out(tokens, width), out(tokens, width, dtype=F32)],
        scratch_shapes=[
            pltpu.VMEM((4, width, lanes), BF16),
            pltpu.VMEM((2 * tokens, width), F32),
            DMA((4,)),
        ],
        compiler_params=params(40),
        cost_estimate=cost(5e9, 12e6, 1e6),
        name=name,
    )(*tokens_in, *by_slot, *slots)


def grads_d_kernel(s_ref, d0_ref, d1_ref, hid_ref, *refs):
    blocks, dt_ref = refs[:-1], refs[-1]
    tokens = d0_ref.shape[0]
    cols = len(blocks)
    part = blocks[0].shape[1]
    dt_ref[:, :tokens] = d0_ref[...].T
    dt_ref[:, tokens:] = d1_ref[...].T
    for hop, block_ref in enumerate(blocks):
        at = pl.ds(pl.multiple_of(lax.rem(s_ref[1] + hop, cols) * part, part), part)
        for slot in range(hid_ref.shape[0]):
            block_ref[slot] = mxu(dt_ref[at, :], hid_ref[slot]).astype(BF16)


def slots_kernel(s_ref, mine0_ref, mine1_ref, theirs0_ref, theirs1_ref, moved_ref, s1_ref, s2_ref):
    moved = moved_ref[...].astype(F32)

    @pl.when(s_ref[0] == 0)
    def _():
        s1_ref[...] = (mine1_ref[...].astype(F32) + moved).astype(BF16)
        s2_ref[...] = theirs0_ref[...]

    @pl.when(s_ref[0] == 1)
    def _():
        s1_ref[...] = (mine0_ref[...].astype(F32) + moved).astype(BF16)
        s2_ref[...] = theirs1_ref[...]


def merge_kernel(s_ref, base0_ref, base1_ref, one_ref, two_ref, *blocks):
    cols = len(blocks)
    part = blocks[0].shape[0]
    for hop, block_ref in enumerate(blocks):
        at = pl.ds(pl.multiple_of(lax.rem(s_ref[1] + hop, cols) * part, part), part)
        moved = one_ref[at, :].astype(F32) + two_ref[at, :].astype(F32)

        @pl.when(s_ref[0] == 0)
        def _():
            block_ref[...] = (base0_ref[at, :].astype(F32) + moved).astype(BF16)

        @pl.when(s_ref[0] == 1)
        def _():
            block_ref[...] = (base1_ref[at, :].astype(F32) + moved).astype(BF16)


def pack_kernel(*refs):
    shards, gain_ref, pack_ref = refs[:-2], refs[-2], refs[-1]
    total = jnp.zeros((1, 1), F32)
    for ref in shards:
        value = ref[...].astype(F32)
        total = total + jnp.sum(jnp.sum(value * value, 0, keepdims=True), 1, keepdims=True)
    row = lax.broadcasted_iota(jnp.int32, pack_ref.shape, 0)
    gain = jnp.where(row == 0, gain_ref[0:1, :], gain_ref[1:2, :])
    pack_ref[...] = jnp.where(row < 2, gain, jnp.broadcast_to(total, pack_ref.shape))


def update(grad_full, moment, weight, average, factor):
    clipped = grad_full * factor
    new_moment = MOMENTUM * moment + clipped
    new_weight = weight - RATE * (clipped + MOMENTUM * new_moment)
    new_average = DECAY * average + (1.0 - DECAY) * new_weight
    return (new_moment, new_weight, new_average)


def update_kernel(s_ref, pack_ref, a0_ref, a1_ref, g0_ref, g1_ref, d0_ref, d1_ref, gm_ref, gw_ref, ge_ref, *refs):
    old, refs = refs[:12], refs[12:]
    new, refs = refs[:12], refs[12:]
    gain_new, norm_ref, refs = refs[:3], refs[3], refs[4:]
    held, in_sems, out_sems = refs[:12], refs[12], refs[13]
    order = [3 * 0 + 0, 4, 8, 1, 5, 9, 3, 7, 11, 2, 6, 10]
    for i in order:
        pltpu.make_async_copy(old[i], held[i], in_sems.at[i]).start()
    gains = pack_ref[0:2, :]
    squares = pack_ref[2:3, 0:1] + jnp.sum(jnp.sum(gains * gains, 0, keepdims=True), 1, keepdims=True)
    norm = jnp.sqrt(squares)
    norm_ref[...] = norm
    factor = jnp.minimum(1.0, CLIP / (norm + 1e-06))
    for ref, value in zip(gain_new, update(gains, gm_ref[...], gw_ref[...], ge_ref[...], factor)):
        ref[...] = value
    n = held[0].shape[2]
    half = d0_ref.shape[1]

    def put(kind, at, grad):
        moment, weight, average = (held[kind + 4 * i] for i in range(3))
        results = update(grad, moment[at], weight[at], average[at], factor)
        for ref, value in zip((moment, weight, average), results):
            ref[at] = value

    every = slice(None)

    def parts(kind, mine, other):
        if kind == 0:
            qk, vo = mine[0], other[0]
            put(0, (0, every, every), qk[:, :n].astype(F32))
            put(0, (1, every, every), qk[:, n:].astype(F32))
            put(0, (2, every, every), vo[:, :n].astype(F32))
        elif kind == 1:
            put(1, (every, every), other[0][:, n:].astype(F32).T)
        else:
            for which, part in enumerate((mine, other)):
                lanes = slice(which * half, (which + 1) * half)
                if kind == 2:
                    put(2, (0, every, lanes), part[1][:, :half].astype(F32))
                    put(2, (1, every, lanes), part[1][:, half:].astype(F32))
                else:
                    put(3, (every, lanes), part[2][...].astype(F32))

    here, there = (a0_ref, g0_ref, d0_ref), (a1_ref, g1_ref, d1_ref)
    for kind in (0, 1, 3, 2):
        for i in (kind, kind + 4, kind + 8):
            pltpu.make_async_copy(old[i], held[i], in_sems.at[i]).wait()

        @pl.when(s_ref[0] == 0)
        def _():
            parts(kind, here, there)

        @pl.when(s_ref[0] == 1)
        def _():
            parts(kind, there, here)

        for i in (kind, kind + 4, kind + 8):
            pltpu.make_async_copy(held[i], new[i], out_sems.at[i]).start()
    for i in range(12):
        pltpu.make_async_copy(held[i], new[i], out_sems.at[i]).wait()


def body(
    rows,
    cols,
    block_input,
    out_grad,
    lengths,
    w_qkv,
    w_out,
    w_gate_up,
    w_down,
    gains,
    mom_qkv,
    mom_out,
    mom_gate_up,
    mom_down,
    mom_gains,
    ema_qkv,
    ema_out,
    ema_gate_up,
    ema_down,
    ema_gains,
):
    d = lax.axis_index("dp")
    r = lax.axis_index("row")
    c = lax.axis_index("col")
    core0 = d == 0
    stays = d == r % 2
    tokens, width = block_input.shape
    ring = cols <= 4
    part = width // cols
    head_cols = w_qkv.shape[2]
    half = w_gate_up.shape[2] // 2

    pairs = [(i, j) for i in range(2) for j in range(rows)]
    swap_pairs = [(i * rows + j, (j % 2) * rows + (j // 2) * 2 + i) for i, j in pairs]
    cross_pairs = [(i, j) for i, j in swap_pairs if i != j]
    first_pairs = [(i * rows + j, i * rows + (j ^ (1 if i == 0 else 2))) for i, j in pairs]
    second_pairs = [(i * rows + j, i * rows + (j ^ (2 if i == 0 else 1))) for i, j in pairs]

    def swap_tokens(t):
        return lax.ppermute(t, ("dp", "row"), swap_pairs)

    def cross_tokens(t):
        return lax.ppermute(t, ("dp", "row"), cross_pairs)

    def first(t):
        return lax.ppermute(t, ("dp", "row"), first_pairs)

    def second(t):
        return lax.ppermute(t, ("dp", "row"), second_pairs)

    def core(t):
        return lax.ppermute(t, "dp", [(0, 1), (1, 0)])

    def along(t, k):
        return lax.ppermute(t, "col", [(i, (i + k) % cols) for i in range(cols)])

    def sum_over(t, axis, size):
        values = [t] + [lax.ppermute(t, axis, [(i, i ^ b) for i in range(size)]) for b in range(1, size)]
        while len(values) > 1:
            values = [values[i] + values[i + 1] for i in range(0, len(values), 2)]
        return values[0]

    def shift(k):
        return lax.rem(c + k + cols, cols) * part

    def spread_cols(t):
        return [along(t, k) for k in range(1, cols)]

    def join_cols(t, got):
        whole = jnp.zeros((width, t.shape[1]), t.dtype)
        for k, block in enumerate([t] + got):
            whole = lax.dynamic_update_slice_in_dim(whole, block, shift(-k), 0)
        return whole

    def add(*values):
        total = values[0].astype(F32)
        for value in values[1:]:
            total = total + value.astype(F32)
        return total.astype(BF16)

    ids = jnp.stack([d, c]).astype(jnp.int32)
    (piece_a,) = pl.pallas_call(
        piece_a_kernel,
        in_specs=[SMEM, VMEM, VMEM],
        out_specs=[VMEM],
        out_shape=[out(part, 2 * head_cols)],
        compiler_params=params(16),
        name="piece_a",
    )(ids, w_qkv, w_out)
    (piece_f,) = pl.pallas_call(
        piece_f_kernel,
        in_specs=[SMEM, VMEM, VMEM],
        out_specs=[VMEM],
        out_shape=[out(part, 3 * half)],
        compiler_params=params(16),
        name="piece_f",
    )(ids, w_gate_up, w_down.T)

    got_a = spread_cols(piece_a) if ring else lax.all_gather(piece_a, "col", axis=0, tiled=True)
    x_own = swap_tokens(block_input)
    own_length = swap_tokens(lengths)[0, :]
    seq_ids = jnp.arange(own_length.shape[0], dtype=jnp.int32)
    own_length = jnp.sum(jnp.where(seq_ids == r // 2, own_length, 0))
    scalars = jnp.stack([d.astype(jnp.int32), own_length])
    got_a, piece_f, x_own, scalars = fence(got_a, piece_f, x_own, scalars)
    a0 = join_cols(piece_a, got_a) if ring else got_a
    a1, a2 = first(a0), second(a0)
    got_f = spread_cols(piece_f) if ring else lax.all_gather(piece_f, "col", axis=0, tiled=True)
    a0, a1, a2 = fence(a0, a1, a2)
    a3 = second(a1)
    x_other = core(x_own)
    a0, a1, a2, a3, got_f, x_other = fence(a0, a1, a2, a3, got_f, x_other)
    slots_a = [a0, a1, a2, a3]
    got = core(jnp.where(core0, jnp.stack([a2, a3]), jnp.stack([a0, a2])))
    f0 = join_cols(piece_f, got_f) if ring else got_f
    got, f0 = fence(got, f0)
    f1, f2 = first(f0), second(f0)
    cos, sin = pair_tables()
    q, k, v, attended_t, lse, x_t, far, near = attend_forward(scalars, x_own, x_other, slots_a, got, cos, sin)
    got_far = core(far)
    got_far, f1, f2 = fence(got_far, f1, f2)
    slots_f = [f0, f1, f2, second(f1)]
    cot = swap_tokens(out_grad)
    residual, normed = pl.pallas_call(
        first_norm_kernel,
        in_specs=[VMEM] * 4,
        out_specs=[VMEM] * 2,
        out_shape=[out(tokens, width, dtype=F32), out(tokens, width)],
        compiler_params=params(24),
        cost_estimate=cost(4e6, 6e6),
        name="first_norm",
    )(x_own, near, got_far, gains)
    normed_other = core(normed)

    hidden, silu, slope, far, near = ffn_call(
        ffn_forward_kernel, "ffn_forward", (normed, normed_other), (), slots_f, (half,) * 3
    )
    output, d_summed, d_ffn, grad_gain_two = pl.pallas_call(
        last_norm_kernel,
        in_specs=[SMEM] + [VMEM] * 5,
        out_specs=[VMEM] * 4,
        out_shape=[
            out(tokens, width),
            out(tokens, width, dtype=F32),
            out(tokens, width),
            out(1, width, dtype=F32),
        ],
        compiler_params=params(32),
        cost_estimate=cost(10e6, 8e6),
        name="last_norm",
    )(scalars, residual, near, core(far), gains, cot)
    d_ffn_other = core(d_ffn)
    normed_full = jnp.concatenate([normed, normed_other], 0)

    d_gu, far, near = ffn_call(
        ffn_backward_kernel, "ffn_backward", (d_ffn, d_ffn_other), (silu, slope), slots_f, (2 * half,)
    )

    def grad_gu(s):
        return jnp.einsum("td,te->de", normed_full, d_gu[s], preferred_element_type=F32).astype(BF16)

    got_far = core(far)
    gu3 = grad_gu(3)
    gu_moved = second(gu3)
    if ring:
        dn = pl.pallas_call(
            grads_d_kernel,
            in_specs=[SMEM] + [VMEM] * 3,
            out_specs=[VMEM] * cols,
            out_shape=[out(4, part, half)] * cols,
            scratch_shapes=[pltpu.VMEM((width, 2 * tokens), BF16)],
            compiler_params=params(32),
            cost_estimate=cost(1.6e9, 6e6),
            name="grads_d",
        )(ids, d_ffn, d_ffn_other, hidden)
        dn_moved = along(dn[cols - 1], 1)
    got_far, gu3, dn = fence(got_far, gu3, dn if ring else [])
    d_residual, d_branch, grad_gain_one = pl.pallas_call(
        back_norm_kernel,
        in_specs=[VMEM] * 5,
        out_specs=[VMEM] * 3,
        out_shape=[out(tokens, width, dtype=F32), out(tokens, width), out(1, width, dtype=F32)],
        compiler_params=params(32),
        cost_estimate=cost(10e6, 8e6),
        name="back_norm",
    )(residual, near, got_far, d_summed, gains)
    d_branch_other = core(d_branch)
    gu1, gu2 = grad_gu(1), grad_gu(2)
    d_branch_other, gu1, gu2 = fence(d_branch_other, gu1, gu2)
    back = (scalars, d_branch, d_branch_other, slots_a, got, cos, sin, q, k, v, attended_t, lse, x_t)
    dqk1, dv1, mine1, send1 = attend_backward(1, *back)
    dqk1, dv1, mine1, send1, gu_moved, d_branch = fence(dqk1, dv1, mine1, send1, gu_moved, d_branch)
    back = (scalars, d_branch) + back[2:]
    gu1 = add(gu1, gu_moved)
    gu_one, gu_two = first(gu1), second(gu2)
    theirs1 = core(send1)
    s3 = jnp.where(core0, theirs1, mine1)
    if ring:
        dn_moved, s3 = fence(dn_moved, s3)
        dn_moved = along(add(dn[2], dn_moved), 1) if cols > 2 else dn_moved
    a_moved = second(s3)
    gu0 = grad_gu(0)
    gu0, theirs1, d_branch = fence(gu0, theirs1, d_branch)
    back = (scalars, d_branch) + back[2:]
    dqk0, dv0, mine0, send0 = attend_backward(0, *back)
    theirs0 = core(send0)
    dqk0, dv0, mine0, theirs0, a_moved, gu_one, gu_two = fence(dqk0, dv0, mine0, theirs0, a_moved, gu_one, gu_two)
    s1, s2 = pl.pallas_call(
        slots_kernel,
        in_specs=[SMEM] + [VMEM] * 5,
        out_specs=[VMEM] * 2,
        out_shape=[out(width, 2 * head_cols)] * 2,
        compiler_params=params(16),
        name="slots",
    )(ids, mine0, mine1, theirs0, theirs1, a_moved)
    a_one, a_two = first(s1), second(s2)

    def merge(base0, base1, one, two):
        lanes = base0.shape[1]
        if not ring:
            return [add(jnp.where(core0, base0, base1), one, two)]
        return pl.pallas_call(
            merge_kernel,
            in_specs=[SMEM] + [VMEM] * 4,
            out_specs=[VMEM] * cols,
            out_shape=[out(part, lanes)] * cols,
            compiler_params=params(16),
            name="merge",
        )(ids, base0, base1, one, two)

    def to_owner(blocks):
        if not ring:
            return [lax.psum_scatter(blocks[0], "col", scatter_dimension=0, tiled=True)]
        return [blocks[0]] + [along(blocks[hop], hop) for hop in range(1, cols)]

    g_parts = to_owner(merge(gu0, gu0, gu_one, gu_two))
    if ring:
        if cols > 3:
            dn_moved = along(add(dn[1], dn_moved), 1)
        own_dn = add(dn[0], dn_moved)
    else:
        grad_dn = jnp.einsum(
            "td,ste->sde", jnp.concatenate([d_ffn, d_ffn_other], 0), hidden, preferred_element_type=F32
        ).astype(BF16)
        own_dn = lax.psum_scatter(grad_dn, "col", scatter_dimension=1, tiled=True)
    far, near = input_grad_parts(scalars, (dqk0, dqk1), (dv0, dv1), slots_a, got, tokens)
    got_far = core(far)
    a_one, a_two, own_dn, got_far = fence(a_one, a_two, own_dn, got_far)
    a_parts = to_owner(merge(mine0, theirs0, a_one, a_two))
    g_parts, own_dn = fence(g_parts, own_dn)
    shard_g = add(*g_parts)
    dn_moved = second(own_dn[3])
    input_grad = d_residual + (near + got_far.astype(F32))
    gain_pair = jnp.concatenate([grad_gain_one, grad_gain_two], 0)
    gain_pair = gain_pair + core(gain_pair)
    dn_one = first(add(own_dn[1], dn_moved))
    dn_two = second(own_dn[2])
    a_parts, dn_one, dn_two = fence(a_parts, dn_one, dn_two)
    shard_a = add(*a_parts)
    shard_d = add(own_dn[0], dn_one, dn_two)

    far_a, far_g, far_d = core(shard_a), core(shard_g), core(shard_d)
    (pack,) = pl.pallas_call(
        pack_kernel,
        in_specs=[VMEM] * 7,
        out_specs=[VMEM],
        out_shape=[out(8, width, dtype=F32)],
        compiler_params=params(16),
        name="pack",
    )(shard_a, far_a, shard_g, far_g, shard_d, far_d, gain_pair)
    pack = sum_over(pack, "row", rows)
    pack = sum_over(pack, "col", cols) if ring else lax.psum(pack, "col")
    moved_grad = cross_tokens(input_grad.astype(BF16))
    moved_out = cross_tokens(output)
    input_grad = jnp.where(stays, input_grad, moved_grad.astype(F32))
    output = jnp.where(stays, output.astype(F32), moved_out.astype(F32))

    old = (mom_qkv, mom_out, mom_gate_up, mom_down.T) + (w_qkv, w_out, w_gate_up, w_down.T)
    old = old + (ema_qkv, ema_out, ema_gate_up, ema_down.T)
    results = pl.pallas_call(
        update_kernel,
        in_specs=[SMEM] + [VMEM] * 10 + [ANY] * 12,
        out_specs=[ANY] * 12 + [VMEM] * 4,
        out_shape=[out(*t.shape, dtype=F32) for t in old]
        + [out(*gains.shape, dtype=F32)] * 3
        + [out(1, 1, dtype=F32)],
        scratch_shapes=[pltpu.VMEM(t.shape, F32) for t in old] + [DMA((12,)), DMA((12,))],
        compiler_params=params(24),
        cost_estimate=cost(5e6, 12e6),
        name="update",
    )(ids, pack, shard_a, far_a, shard_g, far_g, shard_d, far_d, mom_gains, gains, ema_gains, *old)
    new = results[:12]
    gain_new = results[12:15]
    grad_norm = results[15][0, 0]
    return (
        output,
        input_grad,
        grad_norm,
        *new[0:3],
        new[3].T,
        gain_new[0],
        *new[4:7],
        new[7].T,
        gain_new[1],
        *new[8:11],
        new[11].T,
        gain_new[2],
    )


def solution(mesh):
    tok = P(("dp", "col", "row"), None)
    weights = (P(None, "col", "row"), P("row", "col"), P(None, "col", "row"), P("row", "col"), P())
    in_specs = (tok, tok, P(("dp", "col"), None)) + weights * 3
    out_specs = (tok, tok, P()) + weights * 3
    fn = functools.partial(body, mesh.shape["row"], mesh.shape["col"])
    return jax.shard_map(fn, mesh=mesh, in_specs=in_specs, out_specs=out_specs, check_vma=False)
```

```python
import functools

import jax
import jax.numpy as jnp
import numpy as np
from jax import lax
from jax.experimental import pallas as pl
from jax.experimental.pallas import tpu as pltpu
from jax.sharding import PartitionSpec as P

HD = 64
LEN = 1024

EPSILON = 1e-06
THETA = 10000.0
MOMENTUM = 0.9
RATE = 300.0
DECAY = 0.6
CLIP = 1.0
NEGATIVE = -1e30

F32 = jnp.float32
BF16 = jnp.bfloat16
NT = (((1,), (1,)), ((), ()))
NN = (((1,), (0,)), ((), ()))
TN = (((0,), (0,)), ((), ()))
BQ = 256


def rope_tables():
    half = HD // 2
    freqs = np.float32(THETA) ** (-(np.arange(half, dtype=np.float32) * np.float32(2.0)) / np.float32(HD))
    angles = np.arange(LEN, dtype=np.float32)[:, None] * freqs[None, :].astype(np.float32)
    return np.cos(angles), np.sin(angles)


def pair_tables():
    cosine, sine = rope_tables()
    return (
        jnp.asarray(np.concatenate([cosine] * 4, 1)),
        jnp.asarray(np.concatenate([-sine, sine] * 2, 1)),
    )


def mxu(lhs, rhs, dims=NN):
    return lax.dot_general(lhs, rhs, dims, preferred_element_type=F32)


def fence(*values):
    return lax.optimization_barrier(values)


def params(mib):
    return pltpu.CompilerParams(vmem_limit_bytes=mib << 20)


def cost(microseconds):
    return pl.CostEstimate(flops=int(1e9 * microseconds), bytes_accessed=1 << 20, transcendentals=0)


def out(*shape, dtype=BF16):
    return jax.ShapeDtypeStruct(shape, dtype)


VMEM = pl.BlockSpec(memory_space=pltpu.VMEM)
SMEM = pl.BlockSpec(memory_space=pltpu.SMEM)
ANY = pl.BlockSpec(memory_space=pl.ANY)
DMA = pltpu.SemaphoreType.DMA


def piece_a_kernel(s_ref, qkv_ref, out_ref, a_ref):
    n = qkv_ref.shape[2]

    @pl.when(s_ref[0] == 0)
    def _():
        a_ref[:, :n] = qkv_ref[0].astype(BF16)
        a_ref[:, n:] = qkv_ref[1].astype(BF16)

    @pl.when(s_ref[0] == 1)
    def _():
        a_ref[:, :n] = qkv_ref[2].astype(BF16)
        a_ref[:, n:] = out_ref[...].T.astype(BF16)


def piece_f_kernel(s_ref, gu_ref, down_ref, f_ref):
    half = f_ref.shape[1] // 3
    at = pl.ds(pl.multiple_of(s_ref[0] * half, half), half)
    f_ref[:, :half] = gu_ref[0, :, at].astype(BF16)
    f_ref[:, half : 2 * half] = gu_ref[1, :, at].astype(BF16)
    f_ref[:, 2 * half :] = down_ref[:, at].astype(BF16)


def whole(*shape):
    return pl.BlockSpec(shape, lambda i: (0,) * len(shape))


def one_step(kernel, name, scalars, inputs, outputs, mib=24, scratch=(), us=1):
    return pl.pallas_call(
        kernel,
        grid=(1,),
        in_specs=[SMEM] + [whole(*t.shape) for t in inputs],
        out_specs=[whole(*t.shape) for t in outputs],
        out_shape=outputs,
        scratch_shapes=list(scratch),
        compiler_params=params(mib),
        cost_estimate=cost(us),
        name=name,
    )(scalars, *inputs)


def join_kernel(s_ref, *refs):
    blocks, whole_ref, sems = refs[:-2], refs[-2], refs[-1]
    cols, part = len(blocks), blocks[0].shape[0]
    copies = []
    for hop, block in enumerate(blocks):
        at = pl.multiple_of((s_ref[1] ^ hop) * part, part)
        copies.append(pltpu.make_async_copy(block, whole_ref.at[pl.ds(at, part)], sems.at[hop]))
    for copy in copies:
        copy.start()
    for copy in copies:
        copy.wait()


def pick_kernel(s_ref, a0_ref, a2_ref, a3_ref, send_ref, sems):
    def move(lo, hi):
        copies = [
            pltpu.make_async_copy(lo, send_ref.at[0], sems.at[0]),
            pltpu.make_async_copy(hi, send_ref.at[1], sems.at[1]),
        ]
        for copy in copies:
            copy.start()
        for copy in copies:
            copy.wait()

    @pl.when(s_ref[0] == 0)
    def _():
        move(a2_ref, a3_ref)

    @pl.when(s_ref[0] == 1)
    def _():
        move(a0_ref, a2_ref)


def causal(scores_t, block):
    keys = scores_t.shape[0]
    row = lax.broadcasted_iota(jnp.int32, (block, block), 0)
    column = lax.broadcasted_iota(jnp.int32, (block, block), 1)
    tail = jnp.where(row <= column, scores_t[keys - block :], NEGATIVE)
    return tail if keys == block else jnp.concatenate([scores_t[: keys - block], tail], 0)


def swap_halves(t):
    lane = lax.broadcasted_iota(jnp.int32, (1, t.shape[1]), 1)
    return jnp.where(lane % HD < HD // 2, pltpu.roll(t, t.shape[1] - HD // 2, 1), pltpu.roll(t, HD // 2, 1))


def pick_weights(core, j, a0_ref, a1_ref, a3_ref, got_ref, qk_ref, vo_ref):
    @pl.when(core == 0)
    def _():
        vo_ref[...] = got_ref[0]

        @pl.when(j == 0)
        def _():
            qk_ref[...] = a0_ref[...]

        @pl.when(j == 1)
        def _():
            qk_ref[...] = a1_ref[...]

    @pl.when(core == 1)
    def _():
        qk_ref[...] = got_ref[0]

        @pl.when(j == 0)
        def _():
            vo_ref[...] = a1_ref[...]

        @pl.when(j == 1)
        def _():
            vo_ref[...] = a3_ref[...]


def attend_forward_kernel(
    s_ref, x0_ref, x1_ref, a0_ref, a1_ref, a3_ref, got_ref, cos_ref, sin_ref,
    q_ref, k_ref, v_ref, ot_ref, lse_ref, xt_ref, far_ref, near_ref,
    qk_w, vo_w, o_ref, total_ref,
):
    core, live = s_ref[0], s_ref[1]
    j = pl.program_id(0)
    length = q_ref.shape[1]
    tokens = x0_ref.shape[0]
    n = 3 * HD
    pick_weights(core, j, a0_ref, a1_ref, a3_ref, got_ref, qk_w, vo_w)
    lane = lax.broadcasted_iota(jnp.int32, (tokens, HD), 1)
    one = jnp.where(lane == 0, 1.0, 0.0).astype(BF16)
    for x_ref, which in ((x0_ref, core), (x1_ref, 1 - core)):
        start = pl.multiple_of(which * tokens, tokens)
        at = pl.ds(start, tokens)
        qk = mxu(x_ref[...], qk_w[...])
        cos = jnp.concatenate([cos_ref[at, :]] * 3, 1)
        sin = jnp.concatenate([sin_ref[at, :]] * 3, 1)
        qk = qk * cos + swap_halves(qk) * sin
        q = (qk[:, :n] * (HD ** -0.5)).astype(BF16)
        k = qk[:, n:].astype(BF16)
        v = mxu(x_ref[...], vo_w[:, :n]).astype(BF16)
        key = start + lax.broadcasted_iota(jnp.int32, (tokens, HD), 0)
        bias = jnp.where((lane == 0) & (key >= live), NEGATIVE, 0.0).astype(BF16)
        for head in range(3):
            lanes = slice(head * HD, (head + 1) * HD)
            q_ref[head, at, :] = jnp.concatenate([q[:, lanes], one], 1)
            k_ref[head, at, :] = jnp.concatenate([k[:, lanes], bias], 1)
            v_ref[head, at, :] = jnp.concatenate([v[:, lanes], one], 1)

        @pl.when(j == 0)
        def _():
            xt_ref[:, at] = x_ref[...].T

    for block in range(length // BQ):
        keys = (block + 1) * BQ
        span = slice(block * BQ, keys)
        parts = []
        for head in range(3):
            scores = causal(mxu(k_ref[head, :keys, :], q_ref[head, span, :], NT), BQ)
            top = jnp.max(scores, 0, keepdims=True)
            probs = jnp.exp(scores - top).astype(BF16)
            o = mxu(v_ref[head, :keys, :], probs, TN)
            total = o[HD : HD + 1]
            parts.append(o[:HD] / total)
            lse_ref[0, head : head + 1, span] = top + jnp.log(total)
        o = jnp.concatenate(parts, 0)
        ot_ref[0, :, span] = o.astype(BF16)
        o_ref[span, :] = o.T.astype(BF16)
    part = mxu(o_ref[...], vo_w[:, n:], NT)

    @pl.when(j == 0)
    def _():
        total_ref[...] = part

    @pl.when(j == 1)
    def _():
        total_ref[...] += part
        near_ref[...] = total_ref[pl.ds(pl.multiple_of(core * tokens, tokens), tokens), :]
        far_ref[...] = total_ref[pl.ds(pl.multiple_of((1 - core) * tokens, tokens), tokens), :].astype(BF16)


def attend_forward(scalars, x_own, x_other, slots, got, cos, sin):
    tokens, width = x_own.shape
    wide = slots[0].shape[1]
    n = wide // 2
    by_j = lambda *shape: pl.BlockSpec(shape, lambda j: (j,) + (0,) * (len(shape) - 1))
    return pl.pallas_call(
        attend_forward_kernel,
        grid=(2,),
        in_specs=[SMEM]
        + [whole(tokens, width)] * 2
        + [whole(width, wide)] * 3
        + [by_j(1, width, wide), whole(LEN, 128), whole(LEN, 128)],
        out_specs=[by_j(3, LEN, 128)] * 3
        + [by_j(1, n, LEN), by_j(1, 8, LEN), whole(width, LEN)]
        + [whole(tokens, width)] * 2,
        out_shape=[out(6, LEN, 128)] * 3
        + [out(2, n, LEN), out(2, 8, LEN, dtype=F32), out(width, LEN)]
        + [out(tokens, width), out(tokens, width, dtype=F32)],
        scratch_shapes=[
            pltpu.VMEM((width, wide), BF16),
            pltpu.VMEM((width, wide), BF16),
            pltpu.VMEM((LEN, n), BF16),
            pltpu.VMEM((LEN, width), F32),
        ],
        compiler_params=params(44),
        cost_estimate=cost(2),
        name="attend_forward",
    )(scalars, x_own, x_other, slots[0], slots[1], slots[3], got, cos, sin)


def attend_backward_kernel(
    s_ref, d0_ref, d1_ref, lo_ref, hi_ref, got_ref, cos_ref, sin_ref, ot_ref, lse_ref,
    q_any, k_any, v_any, xt_any,
    dqk_ref, dv_ref, mine_ref, send_ref,
    q_ref, k_ref, v_ref, xt_ref, vo_w, do_ref, dk_acc, dv_acc, sems, *, j,
):
    core = s_ref[0]
    tokens = d0_ref.shape[0]
    n = 3 * HD
    heads = pl.ds(3 * j, 3)
    copies = [
        pltpu.make_async_copy(k_any.at[heads], k_ref, sems.at[0]),
        pltpu.make_async_copy(q_any.at[heads], q_ref, sems.at[1]),
        pltpu.make_async_copy(v_any.at[heads], v_ref, sems.at[2]),
        pltpu.make_async_copy(xt_any, xt_ref, sems.at[3]),
    ]
    for copy in copies:
        copy.start()

    @pl.when(core == 0)
    def _():
        vo_w[...] = got_ref[0, :, n:]

    @pl.when(core == 1)
    def _():
        vo_w[...] = hi_ref[:, n:]

    for d_ref, which in ((d0_ref, core), (d1_ref, 1 - core)):
        at = pl.ds(pl.multiple_of(which * tokens, tokens), tokens)
        do_ref[at, :] = mxu(d_ref[...], vo_w[...]).astype(BF16)

    length = do_ref.shape[0]
    products = do_ref[...].astype(F32).T * ot_ref[0].astype(F32)
    for copy in copies[:3]:
        copy.wait()

    def unrotate(t):
        return t * cos_ref[...] - swap_halves(t) * sin_ref[...]

    for head in range(3):
        lanes = slice(head * HD, (head + 1) * HD)
        delta = jnp.sum(products[lanes], 0, keepdims=True)
        dq_parts = []
        for block in range(length // BQ):
            keys = (block + 1) * BQ
            span = slice(block * BQ, keys)
            before = keys - BQ
            q = q_ref[head, span, :]
            scores = causal(mxu(k_ref[head, :keys, :], q, NT), BQ)
            probs = jnp.exp(scores - lse_ref[0, head : head + 1, span])
            d_out = do_ref[span, lanes]
            d_probs = mxu(v_ref[head, :keys, :HD], d_out, NT)
            d_scores = (probs * (d_probs - delta[:, span])).astype(BF16)
            dv_part = mxu(probs.astype(BF16), d_out)
            dk_part = mxu(d_scores, q)
            if block:
                dv_acc[:before, :] += dv_part[:before]
                dk_acc[:before, :] += dk_part[:before]
            dv_acc[before:keys, :] = dv_part[before:]
            dk_acc[before:keys, :] = dk_part[before:]
            dq_parts.append(mxu(d_scores, k_ref[head, :keys, :], TN))
        dq = jnp.concatenate(dq_parts, 0) * (HD ** -0.5)
        dqk_ref[:, head * HD : (head + 1) * HD] = unrotate(dq)[:, :HD].astype(BF16)
        dqk_ref[:, n + head * HD : n + (head + 1) * HD] = unrotate(dk_acc[...])[:, :HD].astype(BF16)
        dv_ref[:, lanes] = dv_acc[...].astype(BF16)

    copies[3].wait()
    own = jnp.where(core == 0, 0, tokens)
    grad_o = jnp.zeros((n, d0_ref.shape[1]), F32)
    for d_ref, which in ((d0_ref, core), (d1_ref, 1 - core)):
        at = pl.ds(pl.multiple_of(which * tokens, tokens), tokens)
        grad_o += mxu(ot_ref[0, :, at], d_ref[...])
    grad_o = grad_o.T.astype(BF16)
    grad_qk = mxu(xt_ref[...], dqk_ref[...]).astype(BF16)
    grad_v = mxu(xt_ref[...], dv_ref[...]).astype(BF16)

    @pl.when(core == 0)
    def _():
        mine_ref[...] = grad_qk
        send_ref[:, :n] = grad_v
        send_ref[:, n:] = grad_o

    @pl.when(core == 1)
    def _():
        send_ref[...] = grad_qk
        mine_ref[:, :n] = grad_v
        mine_ref[:, n:] = grad_o


def attend_backward(j, scalars, d_own, d_other, slots, got, cos, sin, q, k, v, out_t, lse, x_t):
    tokens, width = d_own.shape
    wide = slots[0].shape[1]
    n = wide // 2
    at_j = lambda *shape: pl.BlockSpec(shape, lambda i: (j,) + (0,) * (len(shape) - 1))
    lo, hi = (slots[0], slots[1]) if j == 0 else (slots[1], slots[3])
    return pl.pallas_call(
        functools.partial(attend_backward_kernel, j=j),
        grid=(1,),
        in_specs=[SMEM]
        + [whole(tokens, width)] * 2
        + [whole(width, wide)] * 2
        + [at_j(1, width, wide), whole(LEN, 128), whole(LEN, 128), at_j(1, n, LEN), at_j(1, 8, LEN)]
        + [ANY] * 4,
        out_specs=[whole(LEN, wide), whole(LEN, n), whole(width, wide), whole(width, wide)],
        out_shape=[out(LEN, wide), out(LEN, n), out(width, wide), out(width, wide)],
        scratch_shapes=[
            pltpu.VMEM((3, LEN, 128), BF16),
            pltpu.VMEM((3, LEN, 128), BF16),
            pltpu.VMEM((3, LEN, 128), BF16),
            pltpu.VMEM((width, LEN), BF16),
            pltpu.VMEM((width, n), BF16),
            pltpu.VMEM((LEN, n), BF16),
            pltpu.VMEM((LEN, 128), F32),
            pltpu.VMEM((LEN, HD), F32),
            DMA((4,)),
        ],
        compiler_params=params(44),
        cost_estimate=cost(2),
        name="attend_backward",
    )(scalars, d_own, d_other, lo, hi, got, cos, sin, out_t, lse, q, k, v, x_t)


def input_grad_kernel(s_ref, p0_ref, p1_ref, v0_ref, v1_ref, a0_ref, a1_ref, a3_ref, got_ref, far_ref, near_ref, qk_w, vo_w):
    core = s_ref[0]
    n = v0_ref.shape[1]
    tokens = far_ref.shape[0]
    for j, (lo, hi) in enumerate(((a0_ref, a1_ref), (a1_ref, a3_ref))):

        @pl.when(core == 0)
        def _():
            qk_w[j] = lo[...]
            vo_w[j] = got_ref[j, :, :n]

        @pl.when(core == 1)
        def _():
            qk_w[j] = got_ref[j]
            vo_w[j] = hi[:, :n]

    for which, dst in ((1 - core, far_ref), (core, near_ref)):
        at = pl.ds(pl.multiple_of(which * tokens, tokens), tokens)
        total = mxu(p0_ref[at, :], qk_w[0], NT) + mxu(v0_ref[at, :], vo_w[0], NT)
        total = total + (mxu(p1_ref[at, :], qk_w[1], NT) + mxu(v1_ref[at, :], vo_w[1], NT))
        dst[...] = total.astype(dst.dtype)


def input_grad_parts(scalars, d_qk, d_v, slots, got, tokens):
    width, wide = slots[0].shape
    return one_step(
        input_grad_kernel,
        "input_grad",
        scalars,
        (*d_qk, *d_v, slots[0], slots[1], slots[3], got),
        [out(tokens, width), out(tokens, width, dtype=F32)],
        40,
        [pltpu.VMEM((2, width, wide), BF16), pltpu.VMEM((2, width, wide // 2), BF16)],
        4,
    )


def first_norm_kernel(s_ref, x_ref, near_ref, far_ref, gain_ref, resid_ref, normed_ref):
    residual = x_ref[...].astype(F32) + (near_ref[...] + far_ref[...].astype(F32))
    scale = lax.rsqrt(jnp.mean(residual * residual, -1, keepdims=True) + EPSILON)
    resid_ref[...] = residual
    normed_ref[...] = (residual * scale * gain_ref[0:1, :]).astype(BF16)


def last_norm_kernel(s_ref, resid_ref, near_ref, far_ref, gain_ref, cot_ref, out_ref, dsum_ref, dffn_ref, dgain_ref):
    core, live = s_ref[0], s_ref[1]
    tokens, width = resid_ref.shape
    residual = resid_ref[...]
    scale = lax.rsqrt(jnp.mean(residual * residual, -1, keepdims=True) + EPSILON)
    summed = residual * scale * gain_ref[0:1, :] + (near_ref[...] + far_ref[...].astype(F32))
    scale = lax.rsqrt(jnp.mean(summed * summed, -1, keepdims=True) + EPSILON)
    unit = summed * scale
    out_ref[...] = (unit * gain_ref[1:2, :]).astype(BF16)
    position = core * tokens + lax.broadcasted_iota(jnp.int32, (tokens, 1), 0)
    cot = jnp.where(position < live, cot_ref[...].astype(F32), 0.0)
    dgain_ref[...] = jnp.sum(cot * unit, 0, keepdims=True)
    hat = cot * gain_ref[1:2, :]
    inner = jnp.mean(hat * unit, -1, keepdims=True)
    d_summed = scale * (hat - unit * inner)
    dsum_ref[...] = d_summed
    dffn_ref[...] = d_summed.astype(BF16)


def back_norm_kernel(s_ref, resid_ref, near_ref, far_ref, dsum_ref, gain_ref, dres_ref, dbranch_ref, dgain_ref):
    residual = resid_ref[...]
    scale = lax.rsqrt(jnp.mean(residual * residual, -1, keepdims=True) + EPSILON)
    unit = residual * scale
    d_normed = dsum_ref[...] + (near_ref[...] + far_ref[...].astype(F32))
    dgain_ref[...] = jnp.sum(d_normed * unit, 0, keepdims=True)
    hat = d_normed * gain_ref[0:1, :]
    inner = jnp.mean(hat * unit, -1, keepdims=True)
    d_residual = scale * (hat - unit * inner)
    dres_ref[...] = d_residual
    dbranch_ref[...] = d_residual.astype(BF16)


def fetch_slots(step, sources, dst, sems):
    copies = [pltpu.make_async_copy(src, dst.at[i], sems.at[i]) for i, src in enumerate(sources)]

    @pl.when(step == 0)
    def _():
        for copy in copies:
            copy.start()

    for i, copy in enumerate(copies):

        @pl.when(step == i)
        def _():
            copy.wait()


def ffn_forward_kernel(y0_ref, y1_ref, *refs, slots, start, finish):
    refs = list(refs)
    carry_ref = None if start else refs.pop(0)
    sources, refs = refs[:slots], refs[slots:]
    hid_ref, silu_ref, slope_ref = refs[:3]
    results = refs[3 : 5 if finish else 4]
    w_ref, total_ref, sems = refs[-3:]
    step = pl.program_id(0)
    tokens = y0_ref.shape[0]
    half = hid_ref.shape[2]
    fetch_slots(step, sources, w_ref, sems)

    @pl.when(step == 0)
    def _():
        total_ref[...] = jnp.zeros_like(total_ref) if start else carry_ref[...]

    for part, y_ref in ((0, y0_ref), (1, y1_ref)):
        at = slice(part * tokens, (part + 1) * tokens)
        both = mxu(y_ref[...], w_ref[step, :, : 2 * half])
        gate, up = both[:, :half], both[:, half:]
        sig = jax.nn.sigmoid(gate)
        silu = gate * sig
        hidden = (silu * up).astype(BF16)
        hid_ref[0, at, :] = hidden
        silu_ref[0, at, :] = silu.astype(BF16)
        slope_ref[0, at, :] = (up * (sig + silu * (1.0 - sig))).astype(BF16)
        total_ref[at, :] += mxu(hidden, w_ref[step, :, 2 * half :], NT)

    @pl.when(step == slots - 1)
    def _():
        if finish:
            far_ref, near_ref = results
            near_ref[...] = total_ref[:tokens, :]
            far_ref[...] = total_ref[tokens:, :].astype(BF16)
        else:
            results[0][...] = total_ref[...]


def ffn_forward(normed, normed_other, slots, carry, finish):
    tokens, width = normed.shape
    lanes = slots[0].shape[1]
    count = len(slots)
    half = lanes // 3
    per_slot = pl.BlockSpec((1, 2 * tokens, half), lambda s: (s, 0, 0))
    if finish:
        results = [out(tokens, width), out(tokens, width, dtype=F32)]
    else:
        results = [out(2 * tokens, width, dtype=F32)]
    inputs = (normed, normed_other) + (() if carry is None else (carry,))
    return pl.pallas_call(
        functools.partial(ffn_forward_kernel, slots=count, start=carry is None, finish=finish),
        grid=(count,),
        in_specs=[whole(*t.shape) for t in inputs] + [ANY] * count,
        out_specs=[per_slot] * 3 + [whole(*t.shape) for t in results],
        out_shape=[out(count, 2 * tokens, half)] * 3 + results,
        scratch_shapes=[
            pltpu.VMEM((count, width, lanes), BF16),
            pltpu.VMEM((2 * tokens, width), F32),
            DMA((count,)),
        ],
        compiler_params=params(36),
        cost_estimate=cost(2),
        name="ffn_forward",
    )(*inputs, *slots)


def ffn_backward_kernel(
    s_ref, d0_ref, d1_ref, y0_ref, y1_ref, hid_a, silu_a, slope_a, hid_b, silu_b, slope_b, *refs
):
    sources, refs = refs[:4], refs[4:]
    gu_outs, refs = refs[:4], refs[4:]
    far_ref, near_ref = refs[:2]
    blocks, (w_ref, total_ref, yt_ref, dt_ref, dgu_ref, gu_ref, sems, out_sems) = refs[2:-8], refs[-8:]
    step = pl.program_id(0)
    tokens = d0_ref.shape[0]
    half = hid_a.shape[2]
    fetch_slots(step, sources, w_ref, sems)
    leave = [pltpu.make_async_copy(gu_ref.at[i], gu_outs[i], out_sems.at[i]) for i in range(4)]

    @pl.when(step == 0)
    def _():
        total_ref[...] = jnp.zeros_like(total_ref)
        for part, (y_ref, d_ref) in enumerate(((y0_ref, d0_ref), (y1_ref, d1_ref))):
            at = slice(part * tokens, (part + 1) * tokens)
            yt_ref[:, at] = y_ref[...].T
            dt_ref[:, at] = d_ref[...].T

    def slot(index, hid_ref, silu_ref, slope_ref):
        for part, d_ref in ((0, d0_ref), (1, d1_ref)):
            at = slice(part * tokens, (part + 1) * tokens)
            d_hidden = mxu(d_ref[...], w_ref[index, :, 2 * half :])
            d_gate = (d_hidden * slope_ref[0, at, :].astype(F32)).astype(BF16)
            d_up = (d_hidden * silu_ref[0, at, :].astype(F32)).astype(BF16)
            dgu_ref[at, :half] = d_gate
            dgu_ref[at, half:] = d_up
            term = mxu(d_gate, w_ref[index, :, :half], NT) + mxu(d_up, w_ref[index, :, half : 2 * half], NT)
            total_ref[at, :] += term
        gu_ref[index] = mxu(yt_ref[...], dgu_ref[...]).astype(BF16)
        grad = mxu(dt_ref[...], hid_ref[0]).astype(BF16)
        part_rows = blocks[0].shape[1]
        for place in range(len(blocks)):
            rows = grad[place * part_rows : (place + 1) * part_rows]
            for hop, block_ref in enumerate(blocks):

                @pl.when((s_ref[1] ^ hop) == place if len(blocks) > 1 else step >= 0)
                def _():
                    block_ref[index] = rows

    @pl.when(step < 3)
    def _():
        slot(step, hid_a, silu_a, slope_a)

    @pl.when(step == 3)
    def _():
        slot(3, hid_b, silu_b, slope_b)

    for i, copy in enumerate(leave):

        @pl.when(step == i)
        def _():
            copy.start()

    @pl.when(step == 3)
    def _():
        near_ref[...] = total_ref[:tokens, :]
        far_ref[...] = total_ref[tokens:, :].astype(BF16)
        for copy in leave:
            copy.wait()


def ffn_backward(ids, d_ffn, d_other, normed, normed_other, low, high, slots, cols, part):
    tokens, width = d_ffn.shape
    lanes = slots[0].shape[1]
    half = lanes // 3
    first_three = pl.BlockSpec((1, 2 * tokens, half), lambda s: (jnp.minimum(s, 2), 0, 0))
    return pl.pallas_call(
        ffn_backward_kernel,
        grid=(4,),
        in_specs=[SMEM]
        + [whole(tokens, width)] * 4
        + [first_three] * 3
        + [whole(1, 2 * tokens, half)] * 3
        + [ANY] * 4,
        out_specs=[ANY] * 4 + [whole(tokens, width)] * 2 + [whole(4, part, half)] * cols,
        out_shape=[out(width, 2 * half)] * 4
        + [out(tokens, width), out(tokens, width, dtype=F32)]
        + [out(4, part, half)] * cols,
        scratch_shapes=[
            pltpu.VMEM((4, width, lanes), BF16),
            pltpu.VMEM((2 * tokens, width), F32),
            pltpu.VMEM((width, 2 * tokens), BF16),
            pltpu.VMEM((width, 2 * tokens), BF16),
            pltpu.VMEM((2 * tokens, 2 * half), BF16),
            pltpu.VMEM((4, width, 2 * half), BF16),
            DMA((4,)),
            DMA((4,)),
        ],
        compiler_params=params(48),
        cost_estimate=cost(2),
        name="ffn_backward",
    )(ids, d_ffn, d_other, normed, normed_other, *low, *high, *slots)


def slots_kernel(s_ref, mine0_ref, mine1_ref, theirs0_ref, theirs1_ref, moved_ref, s1_ref, s2_ref):
    moved = moved_ref[...].astype(F32)

    @pl.when(s_ref[0] == 0)
    def _():
        s1_ref[...] = (mine1_ref[...].astype(F32) + moved).astype(BF16)
        s2_ref[...] = theirs0_ref[...]

    @pl.when(s_ref[0] == 1)
    def _():
        s1_ref[...] = (mine0_ref[...].astype(F32) + moved).astype(BF16)
        s2_ref[...] = theirs1_ref[...]


def merge_kernel(s_ref, base0_ref, base1_ref, one_ref, two_ref, *blocks):
    cols = len(blocks)
    part = blocks[0].shape[0]
    for hop, block_ref in enumerate(blocks):
        at = pl.ds(pl.multiple_of((s_ref[1] ^ hop) * part, part), part)
        moved = one_ref[at, :].astype(F32) + two_ref[at, :].astype(F32)

        @pl.when(s_ref[0] == 0)
        def _():
            block_ref[...] = (base0_ref[at, :].astype(F32) + moved).astype(BF16)

        @pl.when(s_ref[0] == 1)
        def _():
            block_ref[...] = (base1_ref[at, :].astype(F32) + moved).astype(BF16)


def pack_kernel(s_ref, *refs):
    shards, gain_ref, pack_ref = refs[:-2], refs[-2], refs[-1]
    total = jnp.zeros((1, 1), F32)
    for ref in shards:
        value = ref[...].astype(F32)
        total = total + jnp.sum(jnp.sum(value * value, 0, keepdims=True), 1, keepdims=True)
    row = lax.broadcasted_iota(jnp.int32, pack_ref.shape, 0)
    gain = jnp.where(row == 0, gain_ref[0:1, :], gain_ref[1:2, :])
    pack_ref[...] = jnp.where(row < 2, gain, jnp.broadcast_to(total, pack_ref.shape))


def update(grad_full, moment, weight, average, factor):
    clipped = grad_full * factor
    new_moment = MOMENTUM * moment + clipped
    new_weight = weight - RATE * (clipped + MOMENTUM * new_moment)
    new_average = DECAY * average + (1.0 - DECAY) * new_weight
    return (new_moment, new_weight, new_average)


def update_kernel(s_ref, pack_ref, a0_ref, a1_ref, g0_ref, g1_ref, d0_ref, d1_ref, gm_ref, gw_ref, ge_ref, *refs):
    old, refs = refs[:12], refs[12:]
    new, refs = refs[:12], refs[12:]
    gain_new, norm_ref, refs = refs[:3], refs[3], refs[4:]
    held, in_sems, out_sems = refs[:12], refs[12], refs[13]
    order = [3 * 0 + 0, 4, 8, 1, 5, 9, 3, 7, 11, 2, 6, 10]
    for i in order:
        pltpu.make_async_copy(old[i], held[i], in_sems.at[i]).start()
    gains = pack_ref[0:2, :]
    squares = pack_ref[2:3, 0:1] + jnp.sum(jnp.sum(gains * gains, 0, keepdims=True), 1, keepdims=True)
    norm = jnp.sqrt(squares)
    norm_ref[...] = norm
    factor = jnp.minimum(1.0, CLIP / (norm + 1e-06))
    for ref, value in zip(gain_new, update(gains, gm_ref[...], gw_ref[...], ge_ref[...], factor)):
        ref[...] = value
    n = held[0].shape[2]
    half = d0_ref.shape[1]

    def put(kind, at, grad):
        moment, weight, average = (held[kind + 4 * i] for i in range(3))
        results = update(grad, moment[at], weight[at], average[at], factor)
        for ref, value in zip((moment, weight, average), results):
            ref[at] = value

    every = slice(None)

    def parts(kind, mine, other):
        if kind == 0:
            qk, vo = mine[0], other[0]
            put(0, (0, every, every), qk[:, :n].astype(F32))
            put(0, (1, every, every), qk[:, n:].astype(F32))
            put(0, (2, every, every), vo[:, :n].astype(F32))
        elif kind == 1:
            put(1, (every, every), other[0][:, n:].astype(F32).T)
        else:
            for which, part in enumerate((mine, other)):
                lanes = slice(which * half, (which + 1) * half)
                if kind == 2:
                    put(2, (0, every, lanes), part[1][:, :half].astype(F32))
                    put(2, (1, every, lanes), part[1][:, half:].astype(F32))
                else:
                    put(3, (every, lanes), part[2][...].astype(F32))

    here, there = (a0_ref, g0_ref, d0_ref), (a1_ref, g1_ref, d1_ref)
    for kind in (0, 1, 3, 2):
        for i in (kind, kind + 4, kind + 8):
            pltpu.make_async_copy(old[i], held[i], in_sems.at[i]).wait()

        @pl.when(s_ref[0] == 0)
        def _():
            parts(kind, here, there)

        @pl.when(s_ref[0] == 1)
        def _():
            parts(kind, there, here)

        for i in (kind, kind + 4, kind + 8):
            pltpu.make_async_copy(held[i], new[i], out_sems.at[i]).start()
    for i in range(12):
        pltpu.make_async_copy(held[i], new[i], out_sems.at[i]).wait()


def body(
    rows,
    cols,
    block_input,
    out_grad,
    lengths,
    w_qkv,
    w_out,
    w_gate_up,
    w_down,
    gains,
    mom_qkv,
    mom_out,
    mom_gate_up,
    mom_down,
    mom_gains,
    ema_qkv,
    ema_out,
    ema_gate_up,
    ema_down,
    ema_gains,
):
    d = lax.axis_index("dp")
    r = lax.axis_index("row")
    c = lax.axis_index("col")
    core0 = d == 0
    stays = d == r % 2
    tokens, width = block_input.shape
    ring = cols == 4
    mesh_sizes = {"row": rows, "col": cols}
    part = width // cols
    head_cols = w_qkv.shape[2]
    half = w_gate_up.shape[2] // 2

    pairs = [(i, j) for i in range(2) for j in range(rows)]
    swap_pairs = [(i * rows + j, (j % 2) * rows + (j // 2) * 2 + i) for i, j in pairs]
    cross_pairs = [(i, j) for i, j in swap_pairs if i != j]
    first_pairs = [(i * rows + j, i * rows + (j ^ (1 if i == 0 else 2))) for i, j in pairs]
    second_pairs = [(i * rows + j, i * rows + (j ^ (2 if i == 0 else 1))) for i, j in pairs]

    def swap_tokens(t):
        return lax.ppermute(t, ("dp", "row"), swap_pairs)

    def cross_tokens(t):
        return lax.ppermute(t, ("dp", "row"), cross_pairs)

    def first(t):
        return lax.ppermute(t, ("dp", "row"), first_pairs)

    def second(t):
        return lax.ppermute(t, ("dp", "row"), second_pairs)

    def core(t):
        return lax.ppermute(t, "dp", [(0, 1), (1, 0)])

    def along(t, k):
        return lax.ppermute(t, "col", [(i, i ^ k) for i in range(cols)])

    def join_cols(*blocks):
        return pl.pallas_call(
            join_kernel,
            in_specs=[SMEM] + [ANY] * cols,
            out_specs=ANY,
            out_shape=out(width, blocks[0].shape[1]),
            scratch_shapes=[DMA((cols,))],
            compiler_params=params(16),
            cost_estimate=cost(1),
            name="join",
        )(ids, *blocks)

    def gather_cols(t):
        return lax.all_gather(t, "col", axis=t.ndim - 2, tiled=True)

    def add(*values):
        total = values[0].astype(F32)
        for value in values[1:]:
            total = total + value.astype(F32)
        return total.astype(BF16)

    ids = jnp.stack([d, c]).astype(jnp.int32)
    (piece_a,) = one_step(piece_a_kernel, "piece_a", ids, (w_qkv, w_out), [out(part, 2 * head_cols)], 60)
    piece_a, block_input = fence(piece_a, block_input)
    a_cols = [along(piece_a, 1), along(piece_a, 2)] if ring else [gather_cols(piece_a)]
    x_own = swap_tokens(block_input)
    (piece_f,) = one_step(piece_f_kernel, "piece_f", ids, (w_gate_up, w_down.T), [out(part, 3 * half)], 60)
    a_cols, piece_f = fence(a_cols, piece_f)
    if ring:
        a_cols = a_cols + [along(a_cols[1], 1)]
        f_cols = [along(piece_f, 1), along(piece_f, 2)]
    else:
        f_cols = [gather_cols(piece_f)]
    a_cols, piece_a, lengths = fence(a_cols, piece_a, lengths)
    a0 = join_cols(piece_a, *a_cols) if ring else a_cols[0]
    a1, a2 = first(a0), second(a0)
    a0, a1, a2, f_cols, x_own = fence(a0, a1, a2, f_cols, x_own)
    a3 = second(a1)
    if ring:
        f_cols = f_cols + [along(f_cols[1], 1)]
    x_other = core(x_own)
    own_length = swap_tokens(lengths)[0, :]
    seq_ids = jnp.arange(own_length.shape[0], dtype=jnp.int32)
    own_length = jnp.sum(jnp.where(seq_ids == r // 2, own_length, 0))
    scalars = jnp.stack([d.astype(jnp.int32), own_length])
    a0, a1, a2, a3, f_cols, x_own, x_other, scalars = fence(a0, a1, a2, a3, f_cols, x_own, x_other, scalars)
    slots_a = [a0, a1, a2, a3]
    send = pl.pallas_call(
        pick_kernel,
        in_specs=[SMEM] + [ANY] * 3,
        out_specs=ANY,
        out_shape=out(2, width, 2 * head_cols),
        scratch_shapes=[DMA((2,))],
        compiler_params=params(16),
        cost_estimate=cost(1),
        name="pick",
    )(ids, a0, a2, a3)
    got = core(send)
    f0 = join_cols(piece_f, *f_cols) if ring else f_cols[0]
    got, f0 = fence(got, f0)
    f1, f2 = first(f0), second(f0)
    cos, sin = pair_tables()
    q, k, v, attended_t, lse, x_t, far, near = attend_forward(scalars, x_own, x_other, slots_a, got, cos, sin)
    far, near, f1, f2 = fence(far, near, f1, f2)
    f3 = second(f1)
    residual, normed = one_step(
        first_norm_kernel,
        "first_norm",
        ids,
        (x_own, near, core(far), gains),
        [out(tokens, width, dtype=F32), out(tokens, width)],
    )
    normed_other = core(normed)

    *low, carry = ffn_forward(normed, normed_other, [f0, f1, f2], None, False)
    carry, f3, out_grad = fence(carry, f3, out_grad)
    slots_f = [f0, f1, f2, f3]
    cot = swap_tokens(out_grad)
    *high, far, near = ffn_forward(normed, normed_other, [f3], carry, True)
    output, d_summed, d_ffn, grad_gain_two = one_step(
        last_norm_kernel,
        "last_norm",
        scalars,
        (residual, near, core(far), gains, cot),
        [out(tokens, width), out(tokens, width, dtype=F32), out(tokens, width), out(1, width, dtype=F32)],
        32,
    )
    d_ffn_other = core(d_ffn)
    moved_out = cross_tokens(output)

    gu0, gu1, gu2, gu3, far, near, *dn = ffn_backward(
        ids, d_ffn, d_ffn_other, normed, normed_other, low, high, slots_f, cols if ring else 1, part if ring else width
    )
    far, near, moved_out, gu3, dn = fence(far, near, moved_out, gu3, dn)
    got_far = core(far)
    gu_moved = second(gu3)
    d_residual, d_branch, grad_gain_one = one_step(
        back_norm_kernel,
        "back_norm",
        ids,
        (residual, near, got_far, d_summed, gains),
        [out(tokens, width, dtype=F32), out(tokens, width), out(1, width, dtype=F32)],
    )
    d_branch_other = core(d_branch)
    dn_near = [along(dn[1], 1), along(dn[3], 3)] if ring else []
    back = (scalars, d_branch, d_branch_other, slots_a, got, cos, sin, q, k, v, attended_t, lse, x_t)
    dqk1, dv1, mine1, send1 = attend_backward(1, *back)
    dqk1, dv1, mine1, send1, gu_moved, dn_near, dn, d_branch = fence(
        dqk1, dv1, mine1, send1, gu_moved, dn_near, dn, d_branch
    )
    theirs1 = core(send1)
    gu1 = add(gu1, gu_moved)
    s3 = jnp.where(core0, theirs1, mine1)
    s3, gu1, d_branch = fence(s3, gu1, d_branch)
    a_moved = second(s3)
    gu_one, gu_two = first(gu1), second(gu2)
    dn_far = [along(dn[2], 2)] if ring else []
    back = (scalars, d_branch) + back[2:]
    dqk0, dv0, mine0, send0 = attend_backward(0, *back)
    dqk0, dv0, mine0, send0, a_moved, gu_one, gu_two, dn_far = fence(
        dqk0, dv0, mine0, send0, a_moved, gu_one, gu_two, dn_far
    )
    theirs0 = core(send0)
    if ring:
        own_dn = add(dn[0], *dn_near, *dn_far)
    else:
        own_dn = lax.psum_scatter(dn[0], "col", scatter_dimension=1, tiled=True)

    def merge(base0, base1, one, two):
        if not ring:
            return [add(jnp.where(core0, base0, base1), one, two)]
        return one_step(merge_kernel, "merge", ids, (base0, base1, one, two), [out(part, base0.shape[1])] * cols)

    def to_owner(blocks):
        if not ring:
            return [lax.psum_scatter(blocks[0], "col", scatter_dimension=0, tiled=True)]
        return [blocks[0]] + [along(blocks[hop], hop) for hop in range(1, cols)]

    g_parts = merge(gu0, gu0, gu_one, gu_two)
    theirs0, own_dn, g_parts = fence(theirs0, own_dn, g_parts)
    dn_moved = second(own_dn[3])
    s1, s2 = one_step(
        slots_kernel, "slots", ids, (mine0, mine1, theirs0, theirs1, a_moved), [out(width, 2 * head_cols)] * 2
    )
    s1, s2, dn_moved, dqk0 = fence(s1, s2, dn_moved, dqk0)
    a_one, a_two = first(s1), second(s2)
    g_parts = to_owner(g_parts)
    far, near = input_grad_parts(scalars, (dqk0, dqk1), (dv0, dv1), slots_a, got, tokens)
    gain_pair = jnp.concatenate([grad_gain_one, grad_gain_two], 0)
    gain_pair = gain_pair + core(gain_pair)
    output = jnp.where(stays, output.astype(F32), moved_out.astype(F32))
    a_one, a_two, g_parts, far, near, gain_pair, output = fence(
        a_one, a_two, g_parts, far, near, gain_pair, output
    )
    a_parts = to_owner(merge(mine0, theirs0, a_one, a_two))
    got_far = core(far)
    dn_one, dn_two = first(add(own_dn[1], dn_moved)), second(own_dn[2])
    shard_g = add(*g_parts)
    input_grad = d_residual + (near + got_far.astype(F32))
    far_g = core(shard_g)
    a_parts, dn_one, dn_two, shard_g, far_g, input_grad = fence(a_parts, dn_one, dn_two, shard_g, far_g, input_grad)
    shard_a = add(*a_parts)
    shard_d = add(own_dn[0], dn_one, dn_two)

    far_a, far_d = core(shard_a), core(shard_d)
    moved_grad = cross_tokens(input_grad.astype(BF16))
    pack = one_step(
        pack_kernel,
        "pack",
        ids,
        (shard_a, far_a, shard_g, far_g, shard_d, far_d, gain_pair),
        [out(8, width, dtype=F32)],
    )[0]
    for axis, bits in (("col", (2, 1) if ring else ()), ("row", (2, 1))):
        size = mesh_sizes[axis]
        for bit in bits:
            pack = pack + lax.ppermute(pack, axis, [(i, i ^ bit) for i in range(size)])
    if not ring:
        pack = lax.psum(pack, "col")
    input_grad = jnp.where(stays, input_grad, moved_grad.astype(F32))

    old = (mom_qkv, mom_out, mom_gate_up, mom_down.T) + (w_qkv, w_out, w_gate_up, w_down.T)
    old = old + (ema_qkv, ema_out, ema_gate_up, ema_down.T)
    results = pl.pallas_call(
        update_kernel,
        in_specs=[SMEM] + [VMEM] * 10 + [ANY] * 12,
        out_specs=[ANY] * 12 + [VMEM] * 4,
        out_shape=[out(*t.shape, dtype=F32) for t in old]
        + [out(*gains.shape, dtype=F32)] * 3
        + [out(1, 1, dtype=F32)],
        scratch_shapes=[pltpu.VMEM(t.shape, F32) for t in old] + [DMA((12,)), DMA((12,))],
        compiler_params=params(60),
        cost_estimate=cost(1),
        name="update",
    )(ids, pack, shard_a, far_a, shard_g, far_g, shard_d, far_d, mom_gains, gains, ema_gains, *old)
    new = results[:12]
    gain_new = results[12:15]
    grad_norm = results[15][0, 0]
    return (
        output,
        input_grad,
        grad_norm,
        *new[0:3],
        new[3].T,
        gain_new[0],
        *new[4:7],
        new[7].T,
        gain_new[1],
        *new[8:11],
        new[11].T,
        gain_new[2],
    )


def solution(mesh):
    tok = P(("dp", "col", "row"), None)
    weights = (P(None, "col", "row"), P("row", "col"), P(None, "col", "row"), P("row", "col"), P())
    in_specs = (tok, tok, P(("dp", "col"), None)) + weights * 3
    out_specs = (tok, tok, P()) + weights * 3
    fn = functools.partial(body, mesh.shape["row"], mesh.shape["col"])
    return jax.shard_map(fn, mesh=mesh, in_specs=in_specs, out_specs=out_specs, check_vma=False)
```

```python
import functools

import jax
import jax.numpy as jnp
import numpy as np
from jax import lax
from jax.experimental import pallas as pl
from jax.experimental.pallas import tpu as pltpu
from jax.sharding import PartitionSpec as P

HD = 64
LEN = 1024

EPSILON = 1e-06
THETA = 10000.0
MOMENTUM = 0.9
RATE = 300.0
DECAY = 0.6
CLIP = 1.0
NEGATIVE = -1e30

F32 = jnp.float32
BF16 = jnp.bfloat16
NT = (((1,), (1,)), ((), ()))
NN = (((1,), (0,)), ((), ()))
TN = (((0,), (0,)), ((), ()))
BQ = 256


def rope_tables():
    half = HD // 2
    freqs = np.float32(THETA) ** (-(np.arange(half, dtype=np.float32) * np.float32(2.0)) / np.float32(HD))
    angles = np.arange(LEN, dtype=np.float32)[:, None] * freqs[None, :].astype(np.float32)
    return np.cos(angles), np.sin(angles)


def pair_tables():
    cosine, sine = rope_tables()
    return (
        jnp.asarray(np.concatenate([cosine] * 4, 1)),
        jnp.asarray(np.concatenate([-sine, sine] * 2, 1)),
    )


def mxu(lhs, rhs, dims=NN):
    return lax.dot_general(lhs, rhs, dims, preferred_element_type=F32)


def fence(*values):
    return lax.optimization_barrier(values)


def params(mib):
    return pltpu.CompilerParams(vmem_limit_bytes=mib << 20)


def cost(microseconds):
    return pl.CostEstimate(flops=int(1e9 * microseconds), bytes_accessed=1 << 20, transcendentals=0)


def out(*shape, dtype=BF16):
    return jax.ShapeDtypeStruct(shape, dtype)


def hbm(*shape, dtype=BF16):
    return pltpu.HBM(shape, dtype)


def stay(t):
    return jax.tree.map(lambda v: pltpu.with_memory_space_constraint(v, pltpu.HBM), t)


VMEM = pl.BlockSpec(memory_space=pltpu.VMEM)
SMEM = pl.BlockSpec(memory_space=pltpu.SMEM)
ANY = pl.BlockSpec(memory_space=pl.ANY)
DMA = pltpu.SemaphoreType.DMA


def piece_a_kernel(s_ref, qkv_ref, out_ref, a_ref):
    n = qkv_ref.shape[2]

    @pl.when(s_ref[0] == 0)
    def _():
        a_ref[:, :n] = qkv_ref[0].astype(BF16)
        a_ref[:, n:] = qkv_ref[1].astype(BF16)

    @pl.when(s_ref[0] == 1)
    def _():
        a_ref[:, :n] = qkv_ref[2].astype(BF16)
        a_ref[:, n:] = out_ref[...].T.astype(BF16)


def piece_f_kernel(s_ref, gu_ref, down_ref, f_ref):
    half = f_ref.shape[1] // 3
    at = pl.ds(pl.multiple_of(s_ref[0] * half, half), half)
    f_ref[:, :half] = gu_ref[0, :, at].astype(BF16)
    f_ref[:, half : 2 * half] = gu_ref[1, :, at].astype(BF16)
    f_ref[:, 2 * half :] = down_ref[:, at].astype(BF16)


def whole(*shape):
    return pl.BlockSpec(shape, lambda i: (0,) * len(shape))


def one_step(kernel, name, scalars, inputs, outputs, mib=24, scratch=(), us=1):
    return pl.pallas_call(
        kernel,
        grid=(1,),
        in_specs=[SMEM] + [whole(*t.shape) for t in inputs],
        out_specs=[whole(*t.shape) for t in outputs],
        out_shape=outputs,
        scratch_shapes=list(scratch),
        compiler_params=params(mib),
        cost_estimate=cost(us),
        name=name,
    )(scalars, *inputs)


def join_kernel(s_ref, *refs):
    blocks, whole_ref, sems = refs[:-2], refs[-2], refs[-1]
    cols, part = len(blocks), blocks[0].shape[0]
    copies = []
    for hop, block in enumerate(blocks):
        at = pl.multiple_of((s_ref[1] ^ hop) * part, part)
        copies.append(pltpu.make_async_copy(block, whole_ref.at[pl.ds(at, part)], sems.at[hop]))
    for copy in copies:
        copy.start()
    for copy in copies:
        copy.wait()


def pick_kernel(s_ref, a0_ref, a2_ref, a3_ref, send_ref, sems):
    def move(lo, hi):
        copies = [
            pltpu.make_async_copy(lo, send_ref.at[0], sems.at[0]),
            pltpu.make_async_copy(hi, send_ref.at[1], sems.at[1]),
        ]
        for copy in copies:
            copy.start()
        for copy in copies:
            copy.wait()

    @pl.when(s_ref[0] == 0)
    def _():
        move(a2_ref, a3_ref)

    @pl.when(s_ref[0] == 1)
    def _():
        move(a0_ref, a2_ref)


def causal(scores_t, block):
    keys = scores_t.shape[0]
    row = lax.broadcasted_iota(jnp.int32, (block, block), 0)
    column = lax.broadcasted_iota(jnp.int32, (block, block), 1)
    tail = jnp.where(row <= column, scores_t[keys - block :], NEGATIVE)
    return tail if keys == block else jnp.concatenate([scores_t[: keys - block], tail], 0)


def swap_halves(t):
    lane = lax.broadcasted_iota(jnp.int32, (1, t.shape[1]), 1)
    return jnp.where(lane % HD < HD // 2, pltpu.roll(t, t.shape[1] - HD // 2, 1), pltpu.roll(t, HD // 2, 1))


def pick_weights(core, j, a0_ref, a1_ref, a3_ref, got_ref, qk_ref, vo_ref):
    @pl.when(core == 0)
    def _():
        vo_ref[...] = got_ref[0]

        @pl.when(j == 0)
        def _():
            qk_ref[...] = a0_ref[...]

        @pl.when(j == 1)
        def _():
            qk_ref[...] = a1_ref[...]

    @pl.when(core == 1)
    def _():
        qk_ref[...] = got_ref[0]

        @pl.when(j == 0)
        def _():
            vo_ref[...] = a1_ref[...]

        @pl.when(j == 1)
        def _():
            vo_ref[...] = a3_ref[...]


def attend_forward_kernel(
    s_ref, x0_ref, x1_ref, a0_ref, a1_ref, a3_ref, got_ref, cos_ref, sin_ref,
    q_ref, k_ref, v_ref, ot_ref, lse_ref, xt_ref, far_ref, near_ref,
    qk_w, vo_w, o_ref, total_ref,
):
    core, live = s_ref[0], s_ref[1]
    j = pl.program_id(0)
    length = q_ref.shape[1]
    tokens = x0_ref.shape[0]
    n = 3 * HD
    pick_weights(core, j, a0_ref, a1_ref, a3_ref, got_ref, qk_w, vo_w)
    lane = lax.broadcasted_iota(jnp.int32, (tokens, HD), 1)
    one = jnp.where(lane == 0, 1.0, 0.0).astype(BF16)
    for x_ref, which in ((x0_ref, core), (x1_ref, 1 - core)):
        start = pl.multiple_of(which * tokens, tokens)
        at = pl.ds(start, tokens)
        qk = mxu(x_ref[...], qk_w[...])
        cos = jnp.concatenate([cos_ref[at, :]] * 3, 1)
        sin = jnp.concatenate([sin_ref[at, :]] * 3, 1)
        qk = qk * cos + swap_halves(qk) * sin
        q = (qk[:, :n] * (HD ** -0.5)).astype(BF16)
        k = qk[:, n:].astype(BF16)
        v = mxu(x_ref[...], vo_w[:, :n]).astype(BF16)
        key = start + lax.broadcasted_iota(jnp.int32, (tokens, HD), 0)
        bias = jnp.where((lane == 0) & (key >= live), NEGATIVE, 0.0).astype(BF16)
        for head in range(3):
            lanes = slice(head * HD, (head + 1) * HD)
            q_ref[head, at, :] = jnp.concatenate([q[:, lanes], one], 1)
            k_ref[head, at, :] = jnp.concatenate([k[:, lanes], bias], 1)
            v_ref[head, at, :] = jnp.concatenate([v[:, lanes], one], 1)

        @pl.when(j == 0)
        def _():
            xt_ref[:, at] = x_ref[...].T

    for block in range(length // BQ):
        keys = (block + 1) * BQ
        span = slice(block * BQ, keys)
        parts = []
        for head in range(3):
            scores = causal(mxu(k_ref[head, :keys, :], q_ref[head, span, :], NT), BQ)
            top = jnp.max(scores, 0, keepdims=True)
            probs = jnp.exp(scores - top).astype(BF16)
            o = mxu(probs, v_ref[head, :keys, :], TN).T
            total = o[HD : HD + 1]
            parts.append(o[:HD] / total)
            lse_ref[0, head : head + 1, span] = top + jnp.log(total)
        o = jnp.concatenate(parts, 0)
        ot_ref[0, :, span] = o.astype(BF16)
        o_ref[span, :] = o.T.astype(BF16)
    part = mxu(o_ref[...], vo_w[:, n:], NT)

    @pl.when(j == 0)
    def _():
        total_ref[...] = part

    @pl.when(j == 1)
    def _():
        total_ref[...] += part
        near_ref[...] = total_ref[pl.ds(pl.multiple_of(core * tokens, tokens), tokens), :]
        far_ref[...] = total_ref[pl.ds(pl.multiple_of((1 - core) * tokens, tokens), tokens), :].astype(BF16)


def attend_forward(scalars, x_own, x_other, slots, got, cos, sin):
    tokens, width = x_own.shape
    wide = slots[0].shape[1]
    n = wide // 2
    by_j = lambda *shape: pl.BlockSpec(shape, lambda j: (j,) + (0,) * (len(shape) - 1))
    return pl.pallas_call(
        attend_forward_kernel,
        grid=(2,),
        in_specs=[SMEM]
        + [whole(tokens, width)] * 2
        + [whole(width, wide)] * 3
        + [by_j(1, width, wide), whole(LEN, 128), whole(LEN, 128)],
        out_specs=[by_j(3, LEN, 128)] * 3
        + [by_j(1, n, LEN), by_j(1, 8, LEN), whole(width, LEN)]
        + [whole(tokens, width)] * 2,
        out_shape=[hbm(6, LEN, 128)] * 3
        + [hbm(2, n, LEN), hbm(2, 8, LEN, dtype=F32), hbm(width, LEN)]
        + [out(tokens, width), out(tokens, width, dtype=F32)],
        scratch_shapes=[
            pltpu.VMEM((width, wide), BF16),
            pltpu.VMEM((width, wide), BF16),
            pltpu.VMEM((LEN, n), BF16),
            pltpu.VMEM((LEN, width), F32),
        ],
        compiler_params=params(44),
        cost_estimate=cost(2),
        name="attend_forward",
    )(scalars, x_own, x_other, *stay((slots[0], slots[1], slots[3])), got, *stay((cos, sin)))


def attend_backward_kernel(
    s_ref, d0_ref, d1_ref, lo_ref, hi_ref, got_ref, cos_ref, sin_ref, ot_ref, lse_ref,
    q_any, k_any, v_any, xt_any,
    dqk_ref, dv_ref, mine_ref, send_ref,
    q_ref, k_ref, v_ref, xt_ref, vo_w, do_ref, dk_acc, dv_acc, sems, *, j,
):
    core = s_ref[0]
    tokens = d0_ref.shape[0]
    n = 3 * HD
    heads = pl.ds(3 * j, 3)
    copies = [
        pltpu.make_async_copy(k_any.at[heads], k_ref, sems.at[0]),
        pltpu.make_async_copy(q_any.at[heads], q_ref, sems.at[1]),
        pltpu.make_async_copy(v_any.at[heads], v_ref, sems.at[2]),
        pltpu.make_async_copy(xt_any, xt_ref, sems.at[3]),
    ]
    for copy in copies:
        copy.start()

    @pl.when(core == 0)
    def _():
        vo_w[...] = got_ref[0, :, n:]

    @pl.when(core == 1)
    def _():
        vo_w[...] = hi_ref[:, n:]

    for d_ref, which in ((d0_ref, core), (d1_ref, 1 - core)):
        at = pl.ds(pl.multiple_of(which * tokens, tokens), tokens)
        do_ref[at, :] = mxu(d_ref[...], vo_w[...]).astype(BF16)

    length = do_ref.shape[0]
    products = do_ref[...].astype(F32).T * ot_ref[0].astype(F32)
    for copy in copies[:3]:
        copy.wait()

    def unrotate(t):
        return t * cos_ref[...] - swap_halves(t) * sin_ref[...]

    for head in range(3):
        lanes = slice(head * HD, (head + 1) * HD)
        delta = jnp.sum(products[lanes], 0, keepdims=True)
        dq_parts = []
        for block in range(length // BQ):
            keys = (block + 1) * BQ
            span = slice(block * BQ, keys)
            before = keys - BQ
            q = q_ref[head, span, :]
            scores = causal(mxu(k_ref[head, :keys, :], q, NT), BQ)
            probs = jnp.exp(scores - lse_ref[0, head : head + 1, span])
            d_out = do_ref[span, lanes]
            d_probs = mxu(v_ref[head, :keys, :HD], d_out, NT)
            d_scores = (probs * (d_probs - delta[:, span])).astype(BF16)
            dv_part = mxu(probs.astype(BF16), d_out)
            dk_part = mxu(d_scores, q)
            if block:
                dv_acc[:before, :] += dv_part[:before]
                dk_acc[:before, :] += dk_part[:before]
            dv_acc[before:keys, :] = dv_part[before:]
            dk_acc[before:keys, :] = dk_part[before:]
            dq_parts.append(mxu(d_scores, k_ref[head, :keys, :], TN))
        dq = jnp.concatenate(dq_parts, 0) * (HD ** -0.5)
        dqk_ref[:, head * HD : (head + 1) * HD] = unrotate(dq)[:, :HD].astype(BF16)
        dqk_ref[:, n + head * HD : n + (head + 1) * HD] = unrotate(dk_acc[...])[:, :HD].astype(BF16)
        dv_ref[:, lanes] = dv_acc[...].astype(BF16)

    copies[3].wait()
    own = jnp.where(core == 0, 0, tokens)
    grad_o = jnp.zeros((n, d0_ref.shape[1]), F32)
    for d_ref, which in ((d0_ref, core), (d1_ref, 1 - core)):
        at = pl.ds(pl.multiple_of(which * tokens, tokens), tokens)
        grad_o += mxu(ot_ref[0, :, at], d_ref[...])
    grad_o = grad_o.T.astype(BF16)
    grad_qk = mxu(xt_ref[...], dqk_ref[...]).astype(BF16)
    grad_v = mxu(xt_ref[...], dv_ref[...]).astype(BF16)

    @pl.when(core == 0)
    def _():
        mine_ref[...] = grad_qk
        send_ref[:, :n] = grad_v
        send_ref[:, n:] = grad_o

    @pl.when(core == 1)
    def _():
        send_ref[...] = grad_qk
        mine_ref[:, :n] = grad_v
        mine_ref[:, n:] = grad_o


def attend_backward(j, scalars, d_own, d_other, slots, got, cos, sin, q, k, v, out_t, lse, x_t):
    tokens, width = d_own.shape
    wide = slots[0].shape[1]
    n = wide // 2
    at_j = lambda *shape: pl.BlockSpec(shape, lambda i: (j,) + (0,) * (len(shape) - 1))
    lo, hi = (slots[0], slots[1]) if j == 0 else (slots[1], slots[3])
    return pl.pallas_call(
        functools.partial(attend_backward_kernel, j=j),
        grid=(1,),
        in_specs=[SMEM]
        + [whole(tokens, width)] * 2
        + [whole(width, wide)] * 2
        + [at_j(1, width, wide), whole(LEN, 128), whole(LEN, 128), at_j(1, n, LEN), at_j(1, 8, LEN)]
        + [ANY] * 4,
        out_specs=[whole(LEN, wide), whole(LEN, n), whole(width, wide), whole(width, wide)],
        out_shape=[hbm(LEN, wide), hbm(LEN, n), hbm(width, wide), hbm(width, wide)],
        scratch_shapes=[
            pltpu.VMEM((3, LEN, 128), BF16),
            pltpu.VMEM((3, LEN, 128), BF16),
            pltpu.VMEM((3, LEN, 128), BF16),
            pltpu.VMEM((width, LEN), BF16),
            pltpu.VMEM((width, n), BF16),
            pltpu.VMEM((LEN, n), BF16),
            pltpu.VMEM((LEN, 128), F32),
            pltpu.VMEM((LEN, HD), F32),
            DMA((4,)),
        ],
        compiler_params=params(44),
        cost_estimate=cost(2),
        name="attend_backward",
    )(scalars, d_own, d_other, *stay((lo, hi, got, cos, sin, out_t, lse, q, k, v, x_t)))


def input_grad_kernel(s_ref, p0_ref, p1_ref, v0_ref, v1_ref, a0_ref, a1_ref, a3_ref, got_ref, far_ref, near_ref, qk_w, vo_w):
    core = s_ref[0]
    n = v0_ref.shape[1]
    tokens = far_ref.shape[0]
    for j, (lo, hi) in enumerate(((a0_ref, a1_ref), (a1_ref, a3_ref))):

        @pl.when(core == 0)
        def _():
            qk_w[j] = lo[...]
            vo_w[j] = got_ref[j, :, :n]

        @pl.when(core == 1)
        def _():
            qk_w[j] = got_ref[j]
            vo_w[j] = hi[:, :n]

    for which, dst in ((1 - core, far_ref), (core, near_ref)):
        at = pl.ds(pl.multiple_of(which * tokens, tokens), tokens)
        total = mxu(p0_ref[at, :], qk_w[0], NT) + mxu(v0_ref[at, :], vo_w[0], NT)
        total = total + (mxu(p1_ref[at, :], qk_w[1], NT) + mxu(v1_ref[at, :], vo_w[1], NT))
        dst[...] = total.astype(dst.dtype)


def input_grad_parts(scalars, d_qk, d_v, slots, got, tokens):
    width, wide = slots[0].shape
    return one_step(
        input_grad_kernel,
        "input_grad",
        scalars,
        stay((*d_qk, *d_v, slots[0], slots[1], slots[3], got)),
        [out(tokens, width), out(tokens, width, dtype=F32)],
        40,
        [pltpu.VMEM((2, width, wide), BF16), pltpu.VMEM((2, width, wide // 2), BF16)],
        4,
    )


def first_norm_kernel(s_ref, x_ref, near_ref, far_ref, gain_ref, resid_ref, normed_ref):
    residual = x_ref[...].astype(F32) + (near_ref[...] + far_ref[...].astype(F32))
    scale = lax.rsqrt(jnp.mean(residual * residual, -1, keepdims=True) + EPSILON)
    resid_ref[...] = residual
    normed_ref[...] = (residual * scale * gain_ref[0:1, :]).astype(BF16)


def last_norm_kernel(s_ref, resid_ref, near_ref, far_ref, gain_ref, cot_ref, out_ref, dsum_ref, dffn_ref, dgain_ref):
    core, live = s_ref[0], s_ref[1]
    tokens, width = resid_ref.shape
    residual = resid_ref[...]
    scale = lax.rsqrt(jnp.mean(residual * residual, -1, keepdims=True) + EPSILON)
    summed = residual * scale * gain_ref[0:1, :] + (near_ref[...] + far_ref[...].astype(F32))
    scale = lax.rsqrt(jnp.mean(summed * summed, -1, keepdims=True) + EPSILON)
    unit = summed * scale
    out_ref[...] = (unit * gain_ref[1:2, :]).astype(BF16)
    position = core * tokens + lax.broadcasted_iota(jnp.int32, (tokens, 1), 0)
    cot = jnp.where(position < live, cot_ref[...].astype(F32), 0.0)
    dgain_ref[...] = jnp.sum(cot * unit, 0, keepdims=True)
    hat = cot * gain_ref[1:2, :]
    inner = jnp.mean(hat * unit, -1, keepdims=True)
    d_summed = scale * (hat - unit * inner)
    dsum_ref[...] = d_summed
    dffn_ref[...] = d_summed.astype(BF16)


def back_norm_kernel(s_ref, resid_ref, near_ref, far_ref, dsum_ref, gain_ref, dres_ref, dbranch_ref, dgain_ref):
    residual = resid_ref[...]
    scale = lax.rsqrt(jnp.mean(residual * residual, -1, keepdims=True) + EPSILON)
    unit = residual * scale
    d_normed = dsum_ref[...] + (near_ref[...] + far_ref[...].astype(F32))
    dgain_ref[...] = jnp.sum(d_normed * unit, 0, keepdims=True)
    hat = d_normed * gain_ref[0:1, :]
    inner = jnp.mean(hat * unit, -1, keepdims=True)
    d_residual = scale * (hat - unit * inner)
    dres_ref[...] = d_residual
    dbranch_ref[...] = d_residual.astype(BF16)


def fetch_slots(step, sources, dst, sems):
    copies = [pltpu.make_async_copy(src, dst.at[i], sems.at[i]) for i, src in enumerate(sources)]

    @pl.when(step == 0)
    def _():
        for copy in copies:
            copy.start()

    for i, copy in enumerate(copies):

        @pl.when(step == i)
        def _():
            copy.wait()


def ffn_forward_kernel(y0_ref, y1_ref, *refs, slots, start, finish):
    refs = list(refs)
    carry_ref = None if start else refs.pop(0)
    sources, refs = refs[:slots], refs[slots:]
    hid_ref, silu_ref, slope_ref = refs[:3]
    results = refs[3 : 5 if finish else 4]
    w_ref, total_ref, sems = refs[-3:]
    step = pl.program_id(0)
    tokens = y0_ref.shape[0]
    half = hid_ref.shape[2]
    fetch_slots(step, sources, w_ref, sems)

    @pl.when(step == 0)
    def _():
        total_ref[...] = jnp.zeros_like(total_ref) if start else carry_ref[...]

    for part, y_ref in ((0, y0_ref), (1, y1_ref)):
        at = slice(part * tokens, (part + 1) * tokens)
        both = mxu(y_ref[...], w_ref[step, :, : 2 * half])
        gate, up = both[:, :half], both[:, half:]
        sig = jax.nn.sigmoid(gate)
        silu = gate * sig
        hidden = (silu * up).astype(BF16)
        hid_ref[0, at, :] = hidden
        silu_ref[0, at, :] = silu.astype(BF16)
        slope_ref[0, at, :] = (up * (sig + silu * (1.0 - sig))).astype(BF16)
        total_ref[at, :] += mxu(hidden, w_ref[step, :, 2 * half :], NT)

    @pl.when(step == slots - 1)
    def _():
        if finish:
            far_ref, near_ref = results
            near_ref[...] = total_ref[:tokens, :]
            far_ref[...] = total_ref[tokens:, :].astype(BF16)
        else:
            results[0][...] = total_ref[...]


def ffn_forward(normed, normed_other, slots, carry, finish):
    tokens, width = normed.shape
    lanes = slots[0].shape[1]
    count = len(slots)
    half = lanes // 3
    per_slot = pl.BlockSpec((1, 2 * tokens, half), lambda s: (s, 0, 0))
    if finish:
        results = [out(tokens, width), out(tokens, width, dtype=F32)]
    else:
        results = [out(2 * tokens, width, dtype=F32)]
    inputs = (normed, normed_other) + (() if carry is None else (carry,))
    return pl.pallas_call(
        functools.partial(ffn_forward_kernel, slots=count, start=carry is None, finish=finish),
        grid=(count,),
        in_specs=[whole(*t.shape) for t in inputs] + [ANY] * count,
        out_specs=[per_slot] * 3 + [whole(*t.shape) for t in results],
        out_shape=[hbm(count, 2 * tokens, half)] * 3 + results,
        scratch_shapes=[
            pltpu.VMEM((count, width, lanes), BF16),
            pltpu.VMEM((2 * tokens, width), F32),
            DMA((count,)),
        ],
        compiler_params=params(36),
        cost_estimate=cost(2),
        name="ffn_forward",
    )(*inputs, *slots)


def ffn_backward_kernel(
    s_ref, d0_ref, d1_ref, y0_ref, y1_ref, hid_a, silu_a, slope_a, hid_b, silu_b, slope_b, *refs
):
    sources, refs = refs[:4], refs[4:]
    gu_outs, refs = refs[:4], refs[4:]
    far_ref, near_ref = refs[:2]
    blocks, (w_ref, total_ref, yt_ref, dt_ref, dgu_ref, gu_ref, sems, out_sems) = refs[2:-8], refs[-8:]
    step = pl.program_id(0)
    tokens = d0_ref.shape[0]
    half = hid_a.shape[2]
    fetch_slots(step, sources, w_ref, sems)
    leave = [pltpu.make_async_copy(gu_ref.at[i], gu_outs[i], out_sems.at[i]) for i in range(4)]

    @pl.when(step == 0)
    def _():
        total_ref[...] = jnp.zeros_like(total_ref)
        for part, (y_ref, d_ref) in enumerate(((y0_ref, d0_ref), (y1_ref, d1_ref))):
            at = slice(part * tokens, (part + 1) * tokens)
            yt_ref[:, at] = y_ref[...].T
            dt_ref[:, at] = d_ref[...].T

    def slot(index, hid_ref, silu_ref, slope_ref):
        for part, d_ref in ((0, d0_ref), (1, d1_ref)):
            at = slice(part * tokens, (part + 1) * tokens)
            d_hidden = mxu(d_ref[...], w_ref[index, :, 2 * half :])
            d_gate = (d_hidden * slope_ref[0, at, :].astype(F32)).astype(BF16)
            d_up = (d_hidden * silu_ref[0, at, :].astype(F32)).astype(BF16)
            dgu_ref[at, :half] = d_gate
            dgu_ref[at, half:] = d_up
            term = mxu(d_gate, w_ref[index, :, :half], NT) + mxu(d_up, w_ref[index, :, half : 2 * half], NT)
            total_ref[at, :] += term
        gu_ref[index] = mxu(yt_ref[...], dgu_ref[...]).astype(BF16)
        for hop, block_ref in enumerate(blocks):
            rows = block_ref.shape[1]
            place = (s_ref[1] ^ hop) if len(blocks) > 1 else 0
            at = pl.ds(pl.multiple_of(place * rows, rows), rows)
            block_ref[index] = mxu(dt_ref[at, :], hid_ref[0]).astype(BF16)

    @pl.when(step < 3)
    def _():
        slot(step, hid_a, silu_a, slope_a)

    @pl.when(step == 3)
    def _():
        slot(3, hid_b, silu_b, slope_b)

    for i, copy in enumerate(leave):

        @pl.when(step == i)
        def _():
            copy.start()

    @pl.when(step == 3)
    def _():
        near_ref[...] = total_ref[:tokens, :]
        far_ref[...] = total_ref[tokens:, :].astype(BF16)
        for copy in leave:
            copy.wait()


def ffn_backward(ids, d_ffn, d_other, normed, normed_other, low, high, slots, cols, part):
    tokens, width = d_ffn.shape
    lanes = slots[0].shape[1]
    half = lanes // 3
    first_three = pl.BlockSpec((1, 2 * tokens, half), lambda s: (jnp.minimum(s, 2), 0, 0))
    return pl.pallas_call(
        ffn_backward_kernel,
        grid=(4,),
        in_specs=[SMEM]
        + [whole(tokens, width)] * 4
        + [first_three] * 3
        + [whole(1, 2 * tokens, half)] * 3
        + [ANY] * 4,
        out_specs=[ANY] * 4 + [whole(tokens, width)] * 2 + [whole(4, part, half)] * cols,
        out_shape=[hbm(width, 2 * half)] * 4
        + [out(tokens, width), out(tokens, width, dtype=F32)]
        + [out(4, part, half)] * cols,
        scratch_shapes=[
            pltpu.VMEM((4, width, lanes), BF16),
            pltpu.VMEM((2 * tokens, width), F32),
            pltpu.VMEM((width, 2 * tokens), BF16),
            pltpu.VMEM((width, 2 * tokens), BF16),
            pltpu.VMEM((2 * tokens, 2 * half), BF16),
            pltpu.VMEM((4, width, 2 * half), BF16),
            DMA((4,)),
            DMA((4,)),
        ],
        compiler_params=params(48),
        cost_estimate=cost(2),
        name="ffn_backward",
    )(ids, d_ffn, d_other, *stay((normed, normed_other, *low, *high, *slots)))


def first_slots_kernel(s_ref, gu1_ref, moved_ref, mine1_ref, theirs1_ref, g_ref, s3_ref):
    g_ref[...] = (gu1_ref[...].astype(F32) + moved_ref[...].astype(F32)).astype(BF16)

    @pl.when(s_ref[0] == 0)
    def _():
        s3_ref[...] = theirs1_ref[...]

    @pl.when(s_ref[0] == 1)
    def _():
        s3_ref[...] = mine1_ref[...]


def slots_kernel(s_ref, mine0_ref, mine1_ref, theirs0_ref, theirs1_ref, moved_ref, s1_ref, s2_ref):
    moved = moved_ref[...].astype(F32)

    @pl.when(s_ref[0] == 0)
    def _():
        s1_ref[...] = (mine1_ref[...].astype(F32) + moved).astype(BF16)
        s2_ref[...] = theirs0_ref[...]

    @pl.when(s_ref[0] == 1)
    def _():
        s1_ref[...] = (mine0_ref[...].astype(F32) + moved).astype(BF16)
        s2_ref[...] = theirs1_ref[...]


def merge_kernel(s_ref, base0_ref, base1_ref, one_ref, two_ref, *blocks):
    cols = len(blocks)
    part = blocks[0].shape[0]
    for hop, block_ref in enumerate(blocks):
        at = pl.ds(pl.multiple_of((s_ref[1] ^ hop) * part, part), part)
        moved = one_ref[at, :].astype(F32) + two_ref[at, :].astype(F32)

        @pl.when(s_ref[0] == 0)
        def _():
            block_ref[...] = (base0_ref[at, :].astype(F32) + moved).astype(BF16)

        @pl.when(s_ref[0] == 1)
        def _():
            block_ref[...] = (base1_ref[at, :].astype(F32) + moved).astype(BF16)


def pack_kernel(s_ref, *refs):
    shards, gain_ref, pack_ref = refs[:-2], refs[-2], refs[-1]
    total = jnp.zeros((1, 1), F32)
    for ref in shards:
        value = ref[...].astype(F32)
        total = total + jnp.sum(jnp.sum(value * value, 0, keepdims=True), 1, keepdims=True)
    row = lax.broadcasted_iota(jnp.int32, pack_ref.shape, 0)
    gain = jnp.where(row == 0, gain_ref[0:1, :], gain_ref[1:2, :])
    pack_ref[...] = jnp.where(row < 2, gain, jnp.broadcast_to(total, pack_ref.shape))


def update(grad_full, moment, weight, average, factor):
    clipped = grad_full * factor
    new_moment = MOMENTUM * moment + clipped
    new_weight = weight - RATE * (clipped + MOMENTUM * new_moment)
    new_average = DECAY * average + (1.0 - DECAY) * new_weight
    return (new_moment, new_weight, new_average)


def update_kernel(s_ref, pack_ref, a0_ref, a1_ref, g0_ref, g1_ref, d0_ref, d1_ref, gm_ref, gw_ref, ge_ref, *refs):
    old, refs = refs[:12], refs[12:]
    new, refs = refs[:12], refs[12:]
    gain_new, norm_ref, refs = refs[:3], refs[3], refs[4:]
    held, in_sems, out_sems = refs[:12], refs[12], refs[13]
    order = [3 * 0 + 0, 4, 8, 1, 5, 9, 3, 7, 11, 2, 6, 10]
    for i in order:
        pltpu.make_async_copy(old[i], held[i], in_sems.at[i]).start()
    gains = pack_ref[0:2, :]
    squares = pack_ref[2:3, 0:1] + jnp.sum(jnp.sum(gains * gains, 0, keepdims=True), 1, keepdims=True)
    norm = jnp.sqrt(squares)
    norm_ref[...] = norm
    factor = jnp.minimum(1.0, CLIP / (norm + 1e-06))
    for ref, value in zip(gain_new, update(gains, gm_ref[...], gw_ref[...], ge_ref[...], factor)):
        ref[...] = value
    n = held[0].shape[2]
    half = d0_ref.shape[1]

    def put(kind, at, grad):
        moment, weight, average = (held[kind + 4 * i] for i in range(3))
        results = update(grad, moment[at], weight[at], average[at], factor)
        for ref, value in zip((moment, weight, average), results):
            ref[at] = value

    every = slice(None)

    def parts(kind, mine, other):
        if kind == 0:
            qk, vo = mine[0], other[0]
            put(0, (0, every, every), qk[:, :n].astype(F32))
            put(0, (1, every, every), qk[:, n:].astype(F32))
            put(0, (2, every, every), vo[:, :n].astype(F32))
        elif kind == 1:
            put(1, (every, every), other[0][:, n:].astype(F32).T)
        else:
            for which, part in enumerate((mine, other)):
                lanes = slice(which * half, (which + 1) * half)
                if kind == 2:
                    put(2, (0, every, lanes), part[1][:, :half].astype(F32))
                    put(2, (1, every, lanes), part[1][:, half:].astype(F32))
                else:
                    put(3, (every, lanes), part[2][...].astype(F32))

    here, there = (a0_ref, g0_ref, d0_ref), (a1_ref, g1_ref, d1_ref)
    for kind in (0, 1, 3, 2):
        for i in (kind, kind + 4, kind + 8):
            pltpu.make_async_copy(old[i], held[i], in_sems.at[i]).wait()

        @pl.when(s_ref[0] == 0)
        def _():
            parts(kind, here, there)

        @pl.when(s_ref[0] == 1)
        def _():
            parts(kind, there, here)

        for i in (kind, kind + 4, kind + 8):
            pltpu.make_async_copy(held[i], new[i], out_sems.at[i]).start()
    for i in range(12):
        pltpu.make_async_copy(held[i], new[i], out_sems.at[i]).wait()


def body(
    rows,
    cols,
    block_input,
    out_grad,
    lengths,
    w_qkv,
    w_out,
    w_gate_up,
    w_down,
    gains,
    mom_qkv,
    mom_out,
    mom_gate_up,
    mom_down,
    mom_gains,
    ema_qkv,
    ema_out,
    ema_gate_up,
    ema_down,
    ema_gains,
):
    d = lax.axis_index("dp")
    r = lax.axis_index("row")
    c = lax.axis_index("col")
    core0 = d == 0
    stays = d == r % 2
    tokens, width = block_input.shape
    ring = cols == 4
    mesh_sizes = {"row": rows, "col": cols}
    part = width // cols
    head_cols = w_qkv.shape[2]
    half = w_gate_up.shape[2] // 2

    pairs = [(i, j) for i in range(2) for j in range(rows)]
    swap_pairs = [(i * rows + j, (j % 2) * rows + (j // 2) * 2 + i) for i, j in pairs]
    cross_pairs = [(i, j) for i, j in swap_pairs if i != j]
    first_pairs = [(i * rows + j, i * rows + (j ^ (1 if i == 0 else 2))) for i, j in pairs]
    second_pairs = [(i * rows + j, i * rows + (j ^ (2 if i == 0 else 1))) for i, j in pairs]

    def swap_tokens(t):
        return lax.ppermute(t, ("dp", "row"), swap_pairs)

    def cross_tokens(t):
        return lax.ppermute(t, ("dp", "row"), cross_pairs)

    def first(t):
        return lax.ppermute(t, ("dp", "row"), first_pairs)

    def second(t):
        return lax.ppermute(t, ("dp", "row"), second_pairs)

    def core(t):
        return lax.ppermute(t, "dp", [(0, 1), (1, 0)])

    def along(t, k):
        return lax.ppermute(t, "col", [(i, i ^ k) for i in range(cols)])

    def join_cols(*blocks):
        return pl.pallas_call(
            join_kernel,
            in_specs=[SMEM] + [ANY] * cols,
            out_specs=ANY,
            out_shape=out(width, blocks[0].shape[1]),
            scratch_shapes=[DMA((cols,))],
            compiler_params=params(16),
            cost_estimate=cost(1),
            name="join",
        )(ids, *blocks)

    def gather_cols(t):
        return lax.all_gather(t, "col", axis=t.ndim - 2, tiled=True)

    def add(*values):
        total = values[0].astype(F32)
        for value in values[1:]:
            total = total + value.astype(F32)
        return total.astype(BF16)

    ids = jnp.stack([d, c]).astype(jnp.int32)
    (piece_a,) = one_step(piece_a_kernel, "piece_a", ids, stay((w_qkv, w_out)), [out(part, 2 * head_cols)], 60)
    piece_a, block_input = fence(piece_a, block_input)
    a_cols = [along(piece_a, 1), along(piece_a, 2)] if ring else [gather_cols(piece_a)]
    x_own = swap_tokens(block_input)
    (piece_f,) = one_step(piece_f_kernel, "piece_f", ids, stay((w_gate_up, w_down.T)), [out(part, 3 * half)], 60)
    a_cols, piece_f, x_own, out_grad = fence(a_cols, piece_f, x_own, out_grad)
    cot = swap_tokens(out_grad)
    if ring:
        a_cols = a_cols + [along(a_cols[1], 1)]
        f_cols = [along(piece_f, 1), along(piece_f, 2)]
    else:
        f_cols = [gather_cols(piece_f)]
    a_cols, piece_a, lengths = fence(a_cols, piece_a, lengths)
    a0 = join_cols(piece_a, *a_cols) if ring else a_cols[0]
    a1, a2 = first(a0), second(a0)
    a0, a1, a2, f_cols, x_own, cot = fence(a0, a1, a2, f_cols, x_own, cot)
    a3 = second(a1)
    if ring:
        f_cols = f_cols + [along(f_cols[1], 1)]
    x_other = core(x_own)
    own_length = swap_tokens(lengths)[0, :]
    seq_ids = jnp.arange(own_length.shape[0], dtype=jnp.int32)
    own_length = jnp.sum(jnp.where(seq_ids == r // 2, own_length, 0))
    scalars = jnp.stack([d.astype(jnp.int32), own_length])
    a0, a1, a2, a3, f_cols, x_own, x_other, scalars = fence(a0, a1, a2, a3, f_cols, x_own, x_other, scalars)
    slots_a = [a0, a1, a2, a3]
    send = pl.pallas_call(
        pick_kernel,
        in_specs=[SMEM] + [ANY] * 3,
        out_specs=ANY,
        out_shape=out(2, width, 2 * head_cols),
        scratch_shapes=[DMA((2,))],
        compiler_params=params(16),
        cost_estimate=cost(1),
        name="pick",
    )(ids, a0, a2, a3)
    got = core(send)
    f0 = join_cols(piece_f, *f_cols) if ring else f_cols[0]
    got, f0 = fence(got, f0)
    f1, f2 = first(f0), second(f0)
    cos, sin = pair_tables()
    q, k, v, attended_t, lse, x_t, far, near = attend_forward(scalars, x_own, x_other, slots_a, got, cos, sin)
    far, near, f1, f2 = fence(far, near, f1, f2)
    f3 = second(f1)
    residual, normed = one_step(
        first_norm_kernel,
        "first_norm",
        ids,
        (x_own, near, core(far), gains),
        [out(tokens, width, dtype=F32), out(tokens, width)],
    )
    normed_other = core(normed)

    *low, carry = ffn_forward(normed, normed_other, [f0, f1, f2], None, False)
    carry, f3 = fence(carry, f3)
    slots_f = [f0, f1, f2, f3]
    *high, far, near = ffn_forward(normed, normed_other, [f3], carry, True)
    output, d_summed, d_ffn, grad_gain_two = one_step(
        last_norm_kernel,
        "last_norm",
        scalars,
        (residual, near, core(far), gains, cot),
        [out(tokens, width), out(tokens, width, dtype=F32), out(tokens, width), out(1, width, dtype=F32)],
        32,
    )
    d_ffn_other = core(d_ffn)
    moved_out = cross_tokens(output)

    gu0, gu1, gu2, gu3, far, near, *dn = ffn_backward(
        ids, d_ffn, d_ffn_other, normed, normed_other, low, high, slots_f, cols if ring else 1, part if ring else width
    )
    far, near, moved_out, gu3, dn = fence(far, near, moved_out, gu3, dn)
    got_far = core(far)
    gu_moved = second(gu3)
    d_residual, d_branch, grad_gain_one = one_step(
        back_norm_kernel,
        "back_norm",
        ids,
        (residual, near, got_far, d_summed, gains),
        [out(tokens, width, dtype=F32), out(tokens, width), out(1, width, dtype=F32)],
    )
    d_branch_other = core(d_branch)
    dn_near = [along(dn[1], 1), along(dn[3], 3)] if ring else []
    back = (scalars, d_branch, d_branch_other, slots_a, got, cos, sin, q, k, v, attended_t, lse, x_t)
    dqk1, dv1, mine1, send1 = attend_backward(1, *back)
    dqk1, dv1, mine1, send1, gu_moved, dn_near, dn, d_branch = fence(
        dqk1, dv1, mine1, send1, gu_moved, dn_near, dn, d_branch
    )
    theirs1 = core(send1)
    gu1, s3 = one_step(
        first_slots_kernel,
        "first_slots",
        ids,
        (gu1, gu_moved, mine1, theirs1),
        [out(width, 2 * half), out(width, 2 * head_cols)],
    )
    s3, gu1, d_branch = fence(s3, gu1, d_branch)
    a_moved = second(s3)
    gu_one, gu_two = first(gu1), second(gu2)
    dn_far = [along(dn[2], 2)] if ring else []
    back = (scalars, d_branch) + back[2:]
    dqk0, dv0, mine0, send0 = attend_backward(0, *back)
    dqk0, dv0, mine0, send0, a_moved, gu_one, gu_two, dn_far = fence(
        dqk0, dv0, mine0, send0, a_moved, gu_one, gu_two, dn_far
    )
    theirs0 = core(send0)
    if ring:
        own_dn = add(dn[0], *dn_near, *dn_far)
    else:
        own_dn = lax.psum_scatter(dn[0], "col", scatter_dimension=1, tiled=True)

    def merge(base0, base1, one, two):
        if not ring:
            return [add(jnp.where(core0, base0, base1), one, two)]
        return one_step(merge_kernel, "merge", ids, (base0, base1, one, two), [out(part, base0.shape[1])] * cols)

    def to_owner(blocks):
        if not ring:
            return [lax.psum_scatter(blocks[0], "col", scatter_dimension=0, tiled=True)]
        return [blocks[0]] + [along(blocks[hop], hop) for hop in range(1, cols)]

    g_parts = merge(gu0, gu0, gu_one, gu_two)
    theirs0, own_dn, g_parts = fence(theirs0, own_dn, g_parts)
    dn_moved = second(own_dn[3])
    s1, s2 = one_step(
        slots_kernel, "slots", ids, (mine0, mine1, theirs0, theirs1, a_moved), [out(width, 2 * head_cols)] * 2
    )
    s1, s2, dn_moved, dqk0 = fence(s1, s2, dn_moved, dqk0)
    a_one, a_two = first(s1), second(s2)
    g_parts = to_owner(g_parts)
    far, near = input_grad_parts(scalars, (dqk0, dqk1), (dv0, dv1), slots_a, got, tokens)
    gain_pair = jnp.concatenate([grad_gain_one, grad_gain_two], 0)
    gain_pair = gain_pair + core(gain_pair)
    output = jnp.where(stays, output.astype(F32), moved_out.astype(F32))
    a_one, a_two, g_parts, far, near, gain_pair, output = fence(
        a_one, a_two, g_parts, far, near, gain_pair, output
    )
    a_parts = to_owner(merge(mine0, theirs0, a_one, a_two))
    got_far = core(far)
    dn_one, dn_two = first(add(own_dn[1], dn_moved)), second(own_dn[2])
    shard_g = add(*g_parts)
    input_grad = d_residual + (near + got_far.astype(F32))
    far_g = core(shard_g)
    a_parts, dn_one, dn_two, shard_g, far_g, input_grad = fence(a_parts, dn_one, dn_two, shard_g, far_g, input_grad)
    shard_a = add(*a_parts)
    shard_d = add(own_dn[0], dn_one, dn_two)

    far_a, far_d = core(shard_a), core(shard_d)
    moved_grad = cross_tokens(input_grad.astype(BF16))
    pack = one_step(
        pack_kernel,
        "pack",
        ids,
        (shard_a, far_a, shard_g, far_g, shard_d, far_d, gain_pair),
        [out(8, width, dtype=F32)],
    )[0]
    for axis, bits in (("col", (2, 1) if ring else ()), ("row", (2, 1))):
        size = mesh_sizes[axis]
        for bit in bits:
            pack = pack + lax.ppermute(pack, axis, [(i, i ^ bit) for i in range(size)])
    if not ring:
        pack = lax.psum(pack, "col")
    input_grad = jnp.where(stays, input_grad, moved_grad.astype(F32))

    old = (mom_qkv, mom_out, mom_gate_up, mom_down.T) + (w_qkv, w_out, w_gate_up, w_down.T)
    old = old + (ema_qkv, ema_out, ema_gate_up, ema_down.T)
    results = pl.pallas_call(
        update_kernel,
        in_specs=[SMEM] + [VMEM] * 10 + [ANY] * 12,
        out_specs=[ANY] * 12 + [VMEM] * 4,
        out_shape=[out(*t.shape, dtype=F32) for t in old]
        + [out(*gains.shape, dtype=F32)] * 3
        + [out(1, 1, dtype=F32)],
        scratch_shapes=[pltpu.VMEM(t.shape, F32) for t in old] + [DMA((12,)), DMA((12,))],
        compiler_params=params(60),
        cost_estimate=cost(1),
        name="update",
    )(ids, pack, shard_a, far_a, shard_g, far_g, shard_d, far_d, mom_gains, gains, ema_gains, *stay(old))
    new = results[:12]
    gain_new = results[12:15]
    grad_norm = results[15][0, 0]
    return (
        output,
        input_grad,
        grad_norm,
        *new[0:3],
        new[3].T,
        gain_new[0],
        *new[4:7],
        new[7].T,
        gain_new[1],
        *new[8:11],
        new[11].T,
        gain_new[2],
    )


def solution(mesh):
    tok = P(("dp", "col", "row"), None)
    weights = (P(None, "col", "row"), P("row", "col"), P(None, "col", "row"), P("row", "col"), P())
    in_specs = (tok, tok, P(("dp", "col"), None)) + weights * 3
    out_specs = (tok, tok, P()) + weights * 3
    fn = functools.partial(body, mesh.shape["row"], mesh.shape["col"])
    return jax.shard_map(fn, mesh=mesh, in_specs=in_specs, out_specs=out_specs, check_vma=False)
```

```python
import functools

import jax
import jax.numpy as jnp
import numpy as np
from jax import lax
from jax.experimental import pallas as pl
from jax.experimental.pallas import tpu as pltpu
from jax.sharding import PartitionSpec as P

HD = 64
LEN = 1024

EPSILON = 1e-06
THETA = 10000.0
MOMENTUM = 0.9
RATE = 300.0
DECAY = 0.6
CLIP = 1.0
NEGATIVE = -1e30

F32 = jnp.float32
BF16 = jnp.bfloat16
NT = (((1,), (1,)), ((), ()))
NN = (((1,), (0,)), ((), ()))
TN = (((0,), (0,)), ((), ()))
BQ = 256


def rope_tables():
    half = HD // 2
    freqs = np.float32(THETA) ** (-(np.arange(half, dtype=np.float32) * np.float32(2.0)) / np.float32(HD))
    angles = np.arange(LEN, dtype=np.float32)[:, None] * freqs[None, :].astype(np.float32)
    return np.cos(angles), np.sin(angles)


def pair_tables():
    cosine, sine = rope_tables()
    return (
        jnp.asarray(np.concatenate([cosine] * 4, 1)),
        jnp.asarray(np.concatenate([-sine, sine] * 2, 1)),
    )


def mxu(lhs, rhs, dims=NN):
    return lax.dot_general(lhs, rhs, dims, preferred_element_type=F32)


def fence(*values):
    return lax.optimization_barrier(values)


def params(mib):
    return pltpu.CompilerParams(vmem_limit_bytes=mib << 20)


def cost(microseconds):
    return pl.CostEstimate(flops=int(1e9 * microseconds), bytes_accessed=1 << 10, transcendentals=0)


def out(*shape, dtype=BF16):
    return jax.ShapeDtypeStruct(shape, dtype)


def hbm(*shape, dtype=BF16):
    return pltpu.HBM(shape, dtype)


def stay(t):
    return jax.tree.map(lambda v: pltpu.with_memory_space_constraint(v, pltpu.HBM), t)


VMEM = pl.BlockSpec(memory_space=pltpu.VMEM)
SMEM = pl.BlockSpec(memory_space=pltpu.SMEM)
ANY = pl.BlockSpec(memory_space=pl.ANY)
DMA = pltpu.SemaphoreType.DMA


def piece_a_kernel(s_ref, qkv_ref, out_ref, a_ref):
    n = qkv_ref.shape[2]

    @pl.when(s_ref[0] == 0)
    def _():
        a_ref[:, :n] = qkv_ref[0].astype(BF16)
        a_ref[:, n:] = qkv_ref[1].astype(BF16)

    @pl.when(s_ref[0] == 1)
    def _():
        a_ref[:, :n] = qkv_ref[2].astype(BF16)
        a_ref[:, n:] = out_ref[...].T.astype(BF16)


def piece_f_kernel(s_ref, gu_ref, down_ref, f_ref):
    half = f_ref.shape[1] // 3
    at = pl.ds(pl.multiple_of(s_ref[0] * half, half), half)
    f_ref[:, :half] = gu_ref[0, :, at].astype(BF16)
    f_ref[:, half : 2 * half] = gu_ref[1, :, at].astype(BF16)
    f_ref[:, 2 * half :] = down_ref[:, at].astype(BF16)


def whole(*shape):
    return pl.BlockSpec(shape, lambda i: (0,) * len(shape))


def one_step(kernel, name, scalars, inputs, outputs, mib=24, scratch=(), us=0.1):
    return pl.pallas_call(
        kernel,
        grid=(1,),
        in_specs=[SMEM] + [whole(*t.shape) for t in inputs],
        out_specs=[whole(*t.shape) for t in outputs],
        out_shape=outputs,
        scratch_shapes=list(scratch),
        compiler_params=params(mib),
        cost_estimate=cost(us),
        name=name,
    )(scalars, *inputs)


def join_kernel(s_ref, *refs):
    blocks, whole_ref, sems = refs[:-2], refs[-2], refs[-1]
    cols, part = len(blocks), blocks[0].shape[0]
    copies = []
    for hop, block in enumerate(blocks):
        at = pl.multiple_of((s_ref[1] ^ hop) * part, part)
        copies.append(pltpu.make_async_copy(block, whole_ref.at[pl.ds(at, part)], sems.at[hop]))
    for copy in copies:
        copy.start()
    for copy in copies:
        copy.wait()


def pick_kernel(s_ref, a0_ref, a2_ref, a3_ref, send_ref, sems):
    def move(lo, hi):
        copies = [
            pltpu.make_async_copy(lo, send_ref.at[0], sems.at[0]),
            pltpu.make_async_copy(hi, send_ref.at[1], sems.at[1]),
        ]
        for copy in copies:
            copy.start()
        for copy in copies:
            copy.wait()

    @pl.when(s_ref[0] == 0)
    def _():
        move(a2_ref, a3_ref)

    @pl.when(s_ref[0] == 1)
    def _():
        move(a0_ref, a2_ref)


def causal(scores_t, block):
    keys = scores_t.shape[0]
    row = lax.broadcasted_iota(jnp.int32, (block, block), 0)
    column = lax.broadcasted_iota(jnp.int32, (block, block), 1)
    tail = jnp.where(row <= column, scores_t[keys - block :], NEGATIVE)
    return tail if keys == block else jnp.concatenate([scores_t[: keys - block], tail], 0)


def swap_halves(t):
    lane = lax.broadcasted_iota(jnp.int32, (1, t.shape[1]), 1)
    return jnp.where(lane % HD < HD // 2, pltpu.roll(t, t.shape[1] - HD // 2, 1), pltpu.roll(t, HD // 2, 1))


def pick_weights(core, j, a0_ref, a1_ref, a3_ref, got_ref, qk_ref, vo_ref):
    @pl.when(core == 0)
    def _():
        vo_ref[...] = got_ref[0]

        @pl.when(j == 0)
        def _():
            qk_ref[...] = a0_ref[...]

        @pl.when(j == 1)
        def _():
            qk_ref[...] = a1_ref[...]

    @pl.when(core == 1)
    def _():
        qk_ref[...] = got_ref[0]

        @pl.when(j == 0)
        def _():
            vo_ref[...] = a1_ref[...]

        @pl.when(j == 1)
        def _():
            vo_ref[...] = a3_ref[...]


def attend_forward_kernel(
    s_ref, x0_ref, x1_ref, a0_ref, a1_ref, a3_ref, got_ref, cos_ref, sin_ref,
    q_ref, k_ref, v_ref, ot_ref, lse_ref, xt_ref, far_ref, near_ref,
    qk_w, vo_w, o_ref, total_ref,
):
    core, live = s_ref[0], s_ref[1]
    j = pl.program_id(0)
    length = q_ref.shape[1]
    tokens = x0_ref.shape[0]
    n = 3 * HD
    pick_weights(core, j, a0_ref, a1_ref, a3_ref, got_ref, qk_w, vo_w)
    lane = lax.broadcasted_iota(jnp.int32, (tokens, HD), 1)
    one = jnp.where(lane == 0, 1.0, 0.0).astype(BF16)
    for x_ref, which in ((x0_ref, core), (x1_ref, 1 - core)):
        start = pl.multiple_of(which * tokens, tokens)
        at = pl.ds(start, tokens)
        qk = mxu(x_ref[...], qk_w[...])
        cos = jnp.concatenate([cos_ref[at, :]] * 3, 1)
        sin = jnp.concatenate([sin_ref[at, :]] * 3, 1)
        qk = qk * cos + swap_halves(qk) * sin
        q = (qk[:, :n] * (HD ** -0.5)).astype(BF16)
        k = qk[:, n:].astype(BF16)
        v = mxu(x_ref[...], vo_w[:, :n]).astype(BF16)
        key = start + lax.broadcasted_iota(jnp.int32, (tokens, HD), 0)
        bias = jnp.where((lane == 0) & (key >= live), NEGATIVE, 0.0).astype(BF16)
        for head in range(3):
            lanes = slice(head * HD, (head + 1) * HD)
            q_ref[head, at, :] = jnp.concatenate([q[:, lanes], one], 1)
            k_ref[head, at, :] = jnp.concatenate([k[:, lanes], bias], 1)
            v_ref[head, at, :] = jnp.concatenate([v[:, lanes], one], 1)

        @pl.when(j == 0)
        def _():
            xt_ref[:, at] = x_ref[...].T

    for block in range(length // BQ):
        keys = (block + 1) * BQ
        span = slice(block * BQ, keys)
        parts = []
        for head in range(3):
            scores = causal(mxu(k_ref[head, :keys, :], q_ref[head, span, :], NT), BQ)
            top = jnp.max(scores, 0, keepdims=True)
            probs = jnp.exp(scores - top).astype(BF16)
            o = mxu(probs, v_ref[head, :keys, :], TN).T
            total = o[HD : HD + 1]
            parts.append(o[:HD] / total)
            lse_ref[0, head : head + 1, span] = top + jnp.log(total)
        o = jnp.concatenate(parts, 0)
        ot_ref[0, :, span] = o.astype(BF16)
        o_ref[span, :] = o.T.astype(BF16)
    part = mxu(o_ref[...], vo_w[:, n:], NT)

    @pl.when(j == 0)
    def _():
        total_ref[...] = part

    @pl.when(j == 1)
    def _():
        total_ref[...] += part
        near_ref[...] = total_ref[pl.ds(pl.multiple_of(core * tokens, tokens), tokens), :]
        far_ref[...] = total_ref[pl.ds(pl.multiple_of((1 - core) * tokens, tokens), tokens), :].astype(BF16)


def attend_forward(scalars, x_own, x_other, slots, got, cos, sin):
    tokens, width = x_own.shape
    wide = slots[0].shape[1]
    n = wide // 2
    by_j = lambda *shape: pl.BlockSpec(shape, lambda j: (j,) + (0,) * (len(shape) - 1))
    return pl.pallas_call(
        attend_forward_kernel,
        grid=(2,),
        in_specs=[SMEM]
        + [whole(tokens, width)] * 2
        + [whole(width, wide)] * 3
        + [by_j(1, width, wide), whole(LEN, 128), whole(LEN, 128)],
        out_specs=[by_j(3, LEN, 128)] * 3
        + [by_j(1, n, LEN), by_j(1, 8, LEN), whole(width, LEN)]
        + [whole(tokens, width)] * 2,
        out_shape=[hbm(6, LEN, 128)] * 3
        + [hbm(2, n, LEN), hbm(2, 8, LEN, dtype=F32), hbm(width, LEN)]
        + [out(tokens, width), out(tokens, width, dtype=F32)],
        scratch_shapes=[
            pltpu.VMEM((width, wide), BF16),
            pltpu.VMEM((width, wide), BF16),
            pltpu.VMEM((LEN, n), BF16),
            pltpu.VMEM((LEN, width), F32),
        ],
        compiler_params=params(44),
        cost_estimate=cost(2),
        name="attend_forward",
    )(scalars, x_own, x_other, *stay((slots[0], slots[1], slots[3])), got, *stay((cos, sin)))


def attend_backward_kernel(
    s_ref, d0_ref, d1_ref, lo_ref, hi_ref, got_ref, cos_ref, sin_ref, ot_ref, lse_ref,
    q_any, k_any, v_any, xt_any,
    dqk_ref, dv_ref, mine_ref, send_ref,
    q_ref, k_ref, v_ref, xt_ref, vo_w, do_ref, dk_acc, dv_acc, sems, *, j,
):
    core = s_ref[0]
    tokens = d0_ref.shape[0]
    n = 3 * HD
    heads = pl.ds(3 * j, 3)
    copies = [
        pltpu.make_async_copy(k_any.at[heads], k_ref, sems.at[0]),
        pltpu.make_async_copy(q_any.at[heads], q_ref, sems.at[1]),
        pltpu.make_async_copy(v_any.at[heads], v_ref, sems.at[2]),
        pltpu.make_async_copy(xt_any, xt_ref, sems.at[3]),
    ]
    for copy in copies:
        copy.start()

    @pl.when(core == 0)
    def _():
        vo_w[...] = got_ref[0, :, n:]

    @pl.when(core == 1)
    def _():
        vo_w[...] = hi_ref[:, n:]

    for d_ref, which in ((d0_ref, core), (d1_ref, 1 - core)):
        at = pl.ds(pl.multiple_of(which * tokens, tokens), tokens)
        do_ref[at, :] = mxu(d_ref[...], vo_w[...]).astype(BF16)

    length = do_ref.shape[0]
    products = do_ref[...].astype(F32).T * ot_ref[0].astype(F32)
    for copy in copies[:3]:
        copy.wait()

    def unrotate(t):
        return t * cos_ref[...] - swap_halves(t) * sin_ref[...]

    for head in range(3):
        lanes = slice(head * HD, (head + 1) * HD)
        delta = jnp.sum(products[lanes], 0, keepdims=True)
        dq_parts = []
        for block in range(length // BQ):
            keys = (block + 1) * BQ
            span = slice(block * BQ, keys)
            before = keys - BQ
            q = q_ref[head, span, :]
            scores = causal(mxu(k_ref[head, :keys, :], q, NT), BQ)
            probs = jnp.exp(scores - lse_ref[0, head : head + 1, span])
            d_out = do_ref[span, lanes]
            d_probs = mxu(v_ref[head, :keys, :HD], d_out, NT)
            d_scores = (probs * (d_probs - delta[:, span])).astype(BF16)
            dv_part = mxu(probs.astype(BF16), d_out)
            dk_part = mxu(d_scores, q)
            if block:
                dv_acc[:before, :] += dv_part[:before]
                dk_acc[:before, :] += dk_part[:before]
            dv_acc[before:keys, :] = dv_part[before:]
            dk_acc[before:keys, :] = dk_part[before:]
            dq_parts.append(mxu(d_scores, k_ref[head, :keys, :], TN))
        dq = jnp.concatenate(dq_parts, 0) * (HD ** -0.5)
        dqk_ref[:, head * HD : (head + 1) * HD] = unrotate(dq)[:, :HD].astype(BF16)
        dqk_ref[:, n + head * HD : n + (head + 1) * HD] = unrotate(dk_acc[...])[:, :HD].astype(BF16)
        dv_ref[:, lanes] = dv_acc[...].astype(BF16)

    copies[3].wait()
    own = jnp.where(core == 0, 0, tokens)
    grad_o = jnp.zeros((n, d0_ref.shape[1]), F32)
    for d_ref, which in ((d0_ref, core), (d1_ref, 1 - core)):
        at = pl.ds(pl.multiple_of(which * tokens, tokens), tokens)
        grad_o += mxu(ot_ref[0, :, at], d_ref[...])
    grad_o = grad_o.T.astype(BF16)
    grad_qk = mxu(xt_ref[...], dqk_ref[...]).astype(BF16)
    grad_v = mxu(xt_ref[...], dv_ref[...]).astype(BF16)

    @pl.when(core == 0)
    def _():
        mine_ref[...] = grad_qk
        send_ref[:, :n] = grad_v
        send_ref[:, n:] = grad_o

    @pl.when(core == 1)
    def _():
        send_ref[...] = grad_qk
        mine_ref[:, :n] = grad_v
        mine_ref[:, n:] = grad_o


def attend_backward(j, scalars, d_own, d_other, slots, got, cos, sin, q, k, v, out_t, lse, x_t):
    tokens, width = d_own.shape
    wide = slots[0].shape[1]
    n = wide // 2
    at_j = lambda *shape: pl.BlockSpec(shape, lambda i: (j,) + (0,) * (len(shape) - 1))
    lo, hi = (slots[0], slots[1]) if j == 0 else (slots[1], slots[3])
    return pl.pallas_call(
        functools.partial(attend_backward_kernel, j=j),
        grid=(1,),
        in_specs=[SMEM]
        + [whole(tokens, width)] * 2
        + [whole(width, wide)] * 2
        + [at_j(1, width, wide), whole(LEN, 128), whole(LEN, 128), at_j(1, n, LEN), at_j(1, 8, LEN)]
        + [ANY] * 4,
        out_specs=[whole(LEN, wide), whole(LEN, n), whole(width, wide), whole(width, wide)],
        out_shape=[hbm(LEN, wide), hbm(LEN, n), hbm(width, wide), hbm(width, wide)],
        scratch_shapes=[
            pltpu.VMEM((3, LEN, 128), BF16),
            pltpu.VMEM((3, LEN, 128), BF16),
            pltpu.VMEM((3, LEN, 128), BF16),
            pltpu.VMEM((width, LEN), BF16),
            pltpu.VMEM((width, n), BF16),
            pltpu.VMEM((LEN, n), BF16),
            pltpu.VMEM((LEN, 128), F32),
            pltpu.VMEM((LEN, HD), F32),
            DMA((4,)),
        ],
        compiler_params=params(44),
        cost_estimate=cost(2),
        name="attend_backward",
    )(scalars, d_own, d_other, *stay((lo, hi, got, cos, sin, out_t, lse, q, k, v, x_t)))


def input_grad_kernel(s_ref, p0_ref, p1_ref, v0_ref, v1_ref, a0_ref, a1_ref, a3_ref, got_ref, far_ref, near_ref, qk_w, vo_w):
    core = s_ref[0]
    n = v0_ref.shape[1]
    tokens = far_ref.shape[0]
    for j, (lo, hi) in enumerate(((a0_ref, a1_ref), (a1_ref, a3_ref))):

        @pl.when(core == 0)
        def _():
            qk_w[j] = lo[...]
            vo_w[j] = got_ref[j, :, :n]

        @pl.when(core == 1)
        def _():
            qk_w[j] = got_ref[j]
            vo_w[j] = hi[:, :n]

    for which, dst in ((1 - core, far_ref), (core, near_ref)):
        at = pl.ds(pl.multiple_of(which * tokens, tokens), tokens)
        total = mxu(p0_ref[at, :], qk_w[0], NT) + mxu(v0_ref[at, :], vo_w[0], NT)
        total = total + (mxu(p1_ref[at, :], qk_w[1], NT) + mxu(v1_ref[at, :], vo_w[1], NT))
        dst[...] = total.astype(dst.dtype)


def input_grad_parts(scalars, d_qk, d_v, slots, got, tokens):
    width, wide = slots[0].shape
    return one_step(
        input_grad_kernel,
        "input_grad",
        scalars,
        stay((*d_qk, *d_v, slots[0], slots[1], slots[3], got)),
        [out(tokens, width), out(tokens, width, dtype=F32)],
        40,
        [pltpu.VMEM((2, width, wide), BF16), pltpu.VMEM((2, width, wide // 2), BF16)],
    )


def first_norm_kernel(s_ref, x_ref, near_ref, far_ref, gain_ref, resid_ref, normed_ref):
    residual = x_ref[...].astype(F32) + (near_ref[...] + far_ref[...].astype(F32))
    scale = lax.rsqrt(jnp.mean(residual * residual, -1, keepdims=True) + EPSILON)
    resid_ref[...] = residual
    normed_ref[...] = (residual * scale * gain_ref[0:1, :]).astype(BF16)


def last_norm_kernel(s_ref, resid_ref, near_ref, far_ref, gain_ref, cot_ref, out_ref, dsum_ref, dffn_ref, dgain_ref):
    core, live = s_ref[0], s_ref[1]
    tokens, width = resid_ref.shape
    residual = resid_ref[...]
    scale = lax.rsqrt(jnp.mean(residual * residual, -1, keepdims=True) + EPSILON)
    summed = residual * scale * gain_ref[0:1, :] + (near_ref[...] + far_ref[...].astype(F32))
    scale = lax.rsqrt(jnp.mean(summed * summed, -1, keepdims=True) + EPSILON)
    unit = summed * scale
    out_ref[...] = (unit * gain_ref[1:2, :]).astype(BF16)
    position = core * tokens + lax.broadcasted_iota(jnp.int32, (tokens, 1), 0)
    cot = jnp.where(position < live, cot_ref[...].astype(F32), 0.0)
    dgain_ref[...] = jnp.sum(cot * unit, 0, keepdims=True)
    hat = cot * gain_ref[1:2, :]
    inner = jnp.mean(hat * unit, -1, keepdims=True)
    d_summed = scale * (hat - unit * inner)
    dsum_ref[...] = d_summed
    dffn_ref[...] = d_summed.astype(BF16)


def back_norm_kernel(s_ref, resid_ref, near_ref, far_ref, dsum_ref, gain_ref, dres_ref, dbranch_ref, dgain_ref):
    residual = resid_ref[...]
    scale = lax.rsqrt(jnp.mean(residual * residual, -1, keepdims=True) + EPSILON)
    unit = residual * scale
    d_normed = dsum_ref[...] + (near_ref[...] + far_ref[...].astype(F32))
    dgain_ref[...] = jnp.sum(d_normed * unit, 0, keepdims=True)
    hat = d_normed * gain_ref[0:1, :]
    inner = jnp.mean(hat * unit, -1, keepdims=True)
    d_residual = scale * (hat - unit * inner)
    dres_ref[...] = d_residual
    dbranch_ref[...] = d_residual.astype(BF16)


def fetch_slots(step, sources, dst, sems):
    copies = [pltpu.make_async_copy(src, dst.at[i], sems.at[i]) for i, src in enumerate(sources)]

    @pl.when(step == 0)
    def _():
        for copy in copies:
            copy.start()

    for i, copy in enumerate(copies):

        @pl.when(step == i)
        def _():
            copy.wait()


def ffn_forward_kernel(y0_ref, y1_ref, *refs, slots, start, finish):
    refs = list(refs)
    carry_ref = None if start else refs.pop(0)
    sources, refs = refs[:slots], refs[slots:]
    hid_ref, silu_ref, slope_ref = refs[:3]
    results = refs[3 : 5 if finish else 4]
    w_ref, total_ref, sems = refs[-3:]
    step = pl.program_id(0)
    tokens = y0_ref.shape[0]
    half = hid_ref.shape[2]
    fetch_slots(step, sources, w_ref, sems)

    @pl.when(step == 0)
    def _():
        total_ref[...] = jnp.zeros_like(total_ref) if start else carry_ref[...]

    for part, y_ref in ((0, y0_ref), (1, y1_ref)):
        at = slice(part * tokens, (part + 1) * tokens)
        both = mxu(y_ref[...], w_ref[step, :, : 2 * half])
        gate, up = both[:, :half], both[:, half:]
        sig = jax.nn.sigmoid(gate)
        silu = gate * sig
        hidden = (silu * up).astype(BF16)
        hid_ref[0, at, :] = hidden
        silu_ref[0, at, :] = silu.astype(BF16)
        slope_ref[0, at, :] = (up * (sig + silu * (1.0 - sig))).astype(BF16)
        total_ref[at, :] += mxu(hidden, w_ref[step, :, 2 * half :], NT)

    @pl.when(step == slots - 1)
    def _():
        if finish:
            far_ref, near_ref = results
            near_ref[...] = total_ref[:tokens, :]
            far_ref[...] = total_ref[tokens:, :].astype(BF16)
        else:
            results[0][...] = total_ref[...]


def ffn_forward(normed, normed_other, slots, carry, finish):
    tokens, width = normed.shape
    lanes = slots[0].shape[1]
    count = len(slots)
    half = lanes // 3
    per_slot = pl.BlockSpec((1, 2 * tokens, half), lambda s: (s, 0, 0))
    if finish:
        results = [out(tokens, width), out(tokens, width, dtype=F32)]
    else:
        results = [out(2 * tokens, width, dtype=F32)]
    inputs = (normed, normed_other) + (() if carry is None else (carry,))
    return pl.pallas_call(
        functools.partial(ffn_forward_kernel, slots=count, start=carry is None, finish=finish),
        grid=(count,),
        in_specs=[whole(*t.shape) for t in inputs] + [ANY] * count,
        out_specs=[per_slot] * 3 + [whole(*t.shape) for t in results],
        out_shape=[hbm(count, 2 * tokens, half)] * 3 + results,
        scratch_shapes=[
            pltpu.VMEM((count, width, lanes), BF16),
            pltpu.VMEM((2 * tokens, width), F32),
            DMA((count,)),
        ],
        compiler_params=params(36),
        cost_estimate=cost(2),
        name="ffn_forward",
    )(*inputs, *slots)


def ffn_backward_kernel(d0_ref, d1_ref, silu_a, slope_a, silu_b, slope_b, *refs):
    sources, (dgu_ref, far_ref, near_ref, w_ref, total_ref, sems) = refs[:4], refs[4:]
    step = pl.program_id(0)
    tokens = d0_ref.shape[0]
    half = silu_a.shape[2]
    fetch_slots(step, sources, w_ref, sems)

    @pl.when(step == 0)
    def _():
        total_ref[...] = jnp.zeros_like(total_ref)

    def slot(silu_ref, slope_ref):
        for part, d_ref in ((0, d0_ref), (1, d1_ref)):
            at = slice(part * tokens, (part + 1) * tokens)
            d_hidden = mxu(d_ref[...], w_ref[step, :, 2 * half :])
            d_gate = (d_hidden * slope_ref[0, at, :].astype(F32)).astype(BF16)
            d_up = (d_hidden * silu_ref[0, at, :].astype(F32)).astype(BF16)
            dgu_ref[0, at, :half] = d_gate
            dgu_ref[0, at, half:] = d_up
            term = mxu(d_gate, w_ref[step, :, :half], NT) + mxu(d_up, w_ref[step, :, half : 2 * half], NT)
            total_ref[at, :] += term

    @pl.when(step < 3)
    def _():
        slot(silu_a, slope_a)

    @pl.when(step == 3)
    def _():
        slot(silu_b, slope_b)
        near_ref[...] = total_ref[:tokens, :]
        far_ref[...] = total_ref[tokens:, :].astype(BF16)


def ffn_backward(d_ffn, d_other, low, high, slots):
    tokens, width = d_ffn.shape
    lanes = slots[0].shape[1]
    half = lanes // 3
    first_three = pl.BlockSpec((1, 2 * tokens, half), lambda s: (jnp.minimum(s, 2), 0, 0))
    return pl.pallas_call(
        ffn_backward_kernel,
        grid=(4,),
        in_specs=[whole(tokens, width)] * 2
        + [first_three] * 2
        + [whole(1, 2 * tokens, half)] * 2
        + [ANY] * 4,
        out_specs=[pl.BlockSpec((1, 2 * tokens, 2 * half), lambda s: (s, 0, 0))] + [whole(tokens, width)] * 2,
        out_shape=[hbm(4, 2 * tokens, 2 * half), out(tokens, width), out(tokens, width, dtype=F32)],
        scratch_shapes=[
            pltpu.VMEM((4, width, lanes), BF16),
            pltpu.VMEM((2 * tokens, width), F32),
            DMA((4,)),
        ],
        compiler_params=params(40),
        cost_estimate=cost(2),
        name="ffn_backward",
    )(d_ffn, d_other, *stay((*low[1:], *high[1:], *slots)))


def grads_g_kernel(*refs, count, moved):
    yt_ref, refs = refs[0], refs[1:]
    dgu, refs = refs[:count], refs[count:]
    moved_ref, results = (refs[0], refs[1:]) if moved else (None, refs)
    for i, (dgu_ref, result_ref) in enumerate(zip(dgu, results)):
        grad = mxu(yt_ref[...], dgu_ref[0])
        if moved and i == 0:
            grad = grad + moved_ref[...].astype(F32)
        result_ref[...] = grad.astype(BF16)


def grads_g(y_t, d_gu, slots, moved=None):
    width, length = y_t.shape
    wide = d_gu.shape[2]
    at_slot = [pl.BlockSpec((1, length, wide), functools.partial(lambda n, i: (n, 0, 0), n)) for n in slots]
    extra = [] if moved is None else [moved]
    return pl.pallas_call(
        functools.partial(grads_g_kernel, count=len(slots), moved=moved is not None),
        grid=(1,),
        in_specs=[whole(width, length)] + at_slot + [whole(*t.shape) for t in extra],
        out_specs=[whole(width, wide)] * len(slots),
        out_shape=[out(width, wide)] * len(slots),
        compiler_params=params(32),
        cost_estimate=cost(0.1),
        name="grads_g",
    )(stay(y_t), *[stay(d_gu)] * len(slots), *extra)


def grads_g3_kernel(s_ref, y0_ref, y1_ref, dgu_ref, g_ref, yt_ref):
    tokens = y0_ref.shape[0]
    yt_ref[:, :tokens] = y0_ref[...].T
    yt_ref[:, tokens:] = y1_ref[...].T
    g_ref[...] = mxu(yt_ref[...], dgu_ref[0]).astype(BF16)


def grads_d_kernel(s_ref, d0_ref, d1_ref, hid_a, hid_b, *refs):
    blocks, dt_ref = refs[:-1], refs[-1]
    tokens = d0_ref.shape[0]
    dt_ref[:, :tokens] = d0_ref[...].T
    dt_ref[:, tokens:] = d1_ref[...].T
    for hop, block_ref in enumerate(blocks):
        rows = block_ref.shape[1]
        place = (s_ref[1] ^ hop) if len(blocks) > 1 else 0
        at = pl.ds(pl.multiple_of(place * rows, rows), rows)
        for slot in range(3):
            block_ref[slot] = mxu(dt_ref[at, :], hid_a[slot]).astype(BF16)
        block_ref[3] = mxu(dt_ref[at, :], hid_b[0]).astype(BF16)


def first_slots_kernel(s_ref, mine1_ref, theirs1_ref, dn_ref, dn_moved_ref, s3_ref, sum_ref):
    sum_ref[...] = (dn_ref[...].astype(F32) + dn_moved_ref[...].astype(F32)).astype(BF16)

    @pl.when(s_ref[0] == 0)
    def _():
        s3_ref[...] = theirs1_ref[...]

    @pl.when(s_ref[0] == 1)
    def _():
        s3_ref[...] = mine1_ref[...]


def slots_kernel(s_ref, mine0_ref, mine1_ref, theirs0_ref, theirs1_ref, moved_ref, s1_ref, s2_ref):
    moved = moved_ref[...].astype(F32)

    @pl.when(s_ref[0] == 0)
    def _():
        s1_ref[...] = (mine1_ref[...].astype(F32) + moved).astype(BF16)
        s2_ref[...] = theirs0_ref[...]

    @pl.when(s_ref[0] == 1)
    def _():
        s1_ref[...] = (mine0_ref[...].astype(F32) + moved).astype(BF16)
        s2_ref[...] = theirs1_ref[...]


def merge_kernel(s_ref, base0_ref, base1_ref, one_ref, two_ref, *blocks):
    cols = len(blocks)
    part = blocks[0].shape[0]
    for hop, block_ref in enumerate(blocks):
        at = pl.ds(pl.multiple_of((s_ref[1] ^ hop) * part, part), part)
        moved = one_ref[at, :].astype(F32) + two_ref[at, :].astype(F32)

        @pl.when(s_ref[0] == 0)
        def _():
            block_ref[...] = (base0_ref[at, :].astype(F32) + moved).astype(BF16)

        @pl.when(s_ref[0] == 1)
        def _():
            block_ref[...] = (base1_ref[at, :].astype(F32) + moved).astype(BF16)


def pack_kernel(s_ref, *refs):
    shards, gain_ref, pack_ref = refs[:-2], refs[-2], refs[-1]
    total = jnp.zeros((1, 1), F32)
    for ref in shards:
        value = ref[...].astype(F32)
        total = total + jnp.sum(jnp.sum(value * value, 0, keepdims=True), 1, keepdims=True)
    row = lax.broadcasted_iota(jnp.int32, pack_ref.shape, 0)
    gain = jnp.where(row == 0, gain_ref[0:1, :], gain_ref[1:2, :])
    pack_ref[...] = jnp.where(row < 2, gain, jnp.broadcast_to(total, pack_ref.shape))


def update(grad_full, moment, weight, average, factor):
    clipped = grad_full * factor
    new_moment = MOMENTUM * moment + clipped
    new_weight = weight - RATE * (clipped + MOMENTUM * new_moment)
    new_average = DECAY * average + (1.0 - DECAY) * new_weight
    return (new_moment, new_weight, new_average)


def fetch_kernel(*refs):
    count = (len(refs) - 1) // 2
    sems = refs[-1]
    copies = [pltpu.make_async_copy(refs[i], refs[count + i], sems.at[i]) for i in range(count)]
    for copy in copies:
        copy.start()
    for copy in copies:
        copy.wait()


def update_kernel(s_ref, pack_ref, a0_ref, a1_ref, g0_ref, g1_ref, d0_ref, d1_ref, gm_ref, gw_ref, ge_ref, *refs):
    old, refs = refs[:12], refs[12:]
    new, refs = refs[:12], refs[12:]
    gain_new, norm_ref, refs = refs[:3], refs[3], refs[4:]
    held, out_sems = refs[:12], refs[12]
    gains = pack_ref[0:2, :]
    squares = pack_ref[2:3, 0:1] + jnp.sum(jnp.sum(gains * gains, 0, keepdims=True), 1, keepdims=True)
    norm = jnp.sqrt(squares)
    norm_ref[...] = norm
    factor = jnp.minimum(1.0, CLIP / (norm + 1e-06))
    for ref, value in zip(gain_new, update(gains, gm_ref[...], gw_ref[...], ge_ref[...], factor)):
        ref[...] = value
    n = held[0].shape[2]
    half = d0_ref.shape[1]

    def put(kind, at, grad):
        moment, weight, average = (old[kind + 4 * i] for i in range(3))
        results = update(grad, moment[at], weight[at], average[at], factor)
        for i, value in enumerate(results):
            held[kind + 4 * i][at] = value

    every = slice(None)

    def parts(kind, mine, other):
        if kind == 0:
            qk, vo = mine[0], other[0]
            put(0, (0, every, every), qk[:, :n].astype(F32))
            put(0, (1, every, every), qk[:, n:].astype(F32))
            put(0, (2, every, every), vo[:, :n].astype(F32))
        elif kind == 1:
            put(1, (every, every), other[0][:, n:].astype(F32).T)
        else:
            for which, part in enumerate((mine, other)):
                lanes = slice(which * half, (which + 1) * half)
                if kind == 2:
                    put(2, (0, every, lanes), part[1][:, :half].astype(F32))
                    put(2, (1, every, lanes), part[1][:, half:].astype(F32))
                else:
                    put(3, (every, lanes), part[2][...].astype(F32))

    here, there = (a0_ref, g0_ref, d0_ref), (a1_ref, g1_ref, d1_ref)
    for kind in (0, 1, 3, 2):
        @pl.when(s_ref[0] == 0)
        def _():
            parts(kind, here, there)

        @pl.when(s_ref[0] == 1)
        def _():
            parts(kind, there, here)

        for i in (kind, kind + 4, kind + 8):
            pltpu.make_async_copy(held[i], new[i], out_sems.at[i]).start()
    for i in range(12):
        pltpu.make_async_copy(held[i], new[i], out_sems.at[i]).wait()


def body(
    rows,
    cols,
    block_input,
    out_grad,
    lengths,
    w_qkv,
    w_out,
    w_gate_up,
    w_down,
    gains,
    mom_qkv,
    mom_out,
    mom_gate_up,
    mom_down,
    mom_gains,
    ema_qkv,
    ema_out,
    ema_gate_up,
    ema_down,
    ema_gains,
):
    d = lax.axis_index("dp")
    r = lax.axis_index("row")
    c = lax.axis_index("col")
    core0 = d == 0
    stays = d == r % 2
    tokens, width = block_input.shape
    ring = cols == 4
    mesh_sizes = {"row": rows, "col": cols}
    part = width // cols
    head_cols = w_qkv.shape[2]
    half = w_gate_up.shape[2] // 2

    pairs = [(i, j) for i in range(2) for j in range(rows)]
    swap_pairs = [(i * rows + j, (j % 2) * rows + (j // 2) * 2 + i) for i, j in pairs]
    cross_pairs = [(i, j) for i, j in swap_pairs if i != j]
    first_pairs = [(i * rows + j, i * rows + (j ^ (1 if i == 0 else 2))) for i, j in pairs]
    second_pairs = [(i * rows + j, i * rows + (j ^ (2 if i == 0 else 1))) for i, j in pairs]

    def swap_tokens(t):
        return lax.ppermute(t, ("dp", "row"), swap_pairs)

    def cross_tokens(t):
        return lax.ppermute(t, ("dp", "row"), cross_pairs)

    def first(t):
        return lax.ppermute(t, ("dp", "row"), first_pairs)

    def second(t):
        return lax.ppermute(t, ("dp", "row"), second_pairs)

    def core(t):
        return lax.ppermute(t, "dp", [(0, 1), (1, 0)])

    def along(t, k):
        return lax.ppermute(t, "col", [(i, i ^ k) for i in range(cols)])

    def join_cols(*blocks):
        return pl.pallas_call(
            join_kernel,
            in_specs=[SMEM] + [ANY] * cols,
            out_specs=ANY,
            out_shape=out(width, blocks[0].shape[1]),
            scratch_shapes=[DMA((cols,))],
            compiler_params=params(16),
            cost_estimate=cost(0.1),
            name="join",
        )(ids, *blocks)

    def gather_cols(t):
        return lax.all_gather(t, "col", axis=t.ndim - 2, tiled=True)

    def add(*values):
        total = values[0].astype(F32)
        for value in values[1:]:
            total = total + value.astype(F32)
        return total.astype(BF16)

    ids = jnp.stack([d, c]).astype(jnp.int32)
    (piece_a,) = one_step(piece_a_kernel, "piece_a", ids, stay((w_qkv, w_out)), [out(part, 2 * head_cols)], 60)
    piece_a, block_input = fence(piece_a, block_input)
    a_cols = [along(piece_a, 1), along(piece_a, 2)] if ring else [gather_cols(piece_a)]
    x_own = swap_tokens(block_input)
    (piece_f,) = one_step(piece_f_kernel, "piece_f", ids, stay((w_gate_up, w_down.T)), [out(part, 3 * half)], 60)
    a_cols, piece_f, x_own, out_grad = fence(a_cols, piece_f, x_own, out_grad)
    cot = swap_tokens(out_grad)
    if ring:
        a_cols = a_cols + [along(a_cols[1], 1)]
        f_cols = [along(piece_f, 1), along(piece_f, 2)]
    else:
        f_cols = [gather_cols(piece_f)]
    a_cols, piece_a, lengths = fence(a_cols, piece_a, lengths)
    a0 = join_cols(piece_a, *a_cols) if ring else a_cols[0]
    a1, a2 = first(a0), second(a0)
    a0, a1, a2, f_cols, x_own, cot = fence(a0, a1, a2, f_cols, x_own, cot)
    a3 = second(a1)
    if ring:
        f_cols = f_cols + [along(f_cols[1], 1)]
    x_other = core(x_own)
    own_length = swap_tokens(lengths)[0, :]
    seq_ids = jnp.arange(own_length.shape[0], dtype=jnp.int32)
    own_length = jnp.sum(jnp.where(seq_ids == r // 2, own_length, 0))
    scalars = jnp.stack([d.astype(jnp.int32), own_length])
    a0, a1, a2, a3, f_cols, x_own, x_other, scalars = fence(a0, a1, a2, a3, f_cols, x_own, x_other, scalars)
    f0 = join_cols(piece_f, *f_cols) if ring else f_cols[0]
    f0, a0, a2, a3 = fence(f0, a0, a2, a3)
    slots_a = [a0, a1, a2, a3]
    send = pl.pallas_call(
        pick_kernel,
        in_specs=[SMEM] + [ANY] * 3,
        out_specs=ANY,
        out_shape=out(2, width, 2 * head_cols),
        scratch_shapes=[DMA((2,))],
        compiler_params=params(16),
        cost_estimate=cost(0.1),
        name="pick",
    )(ids, a0, a2, a3)
    got = core(send)
    f1, f2 = first(f0), second(f0)
    cos, sin = pair_tables()
    q, k, v, attended_t, lse, x_t, far, near = attend_forward(scalars, x_own, x_other, slots_a, got, cos, sin)
    far, near, f1, f2 = fence(far, near, f1, f2)
    f3 = second(f1)
    residual, normed = one_step(
        first_norm_kernel,
        "first_norm",
        ids,
        (x_own, near, core(far), gains),
        [out(tokens, width, dtype=F32), out(tokens, width)],
    )
    normed_other = core(normed)

    *low, carry = ffn_forward(normed, normed_other, [f0, f1, f2], None, False)
    carry, f3 = fence(carry, f3)
    slots_f = [f0, f1, f2, f3]
    *high, far, near = ffn_forward(normed, normed_other, [f3], carry, True)
    output, d_summed, d_ffn, grad_gain_two = one_step(
        last_norm_kernel,
        "last_norm",
        scalars,
        (residual, near, core(far), gains, cot),
        [out(tokens, width), out(tokens, width, dtype=F32), out(tokens, width), out(1, width, dtype=F32)],
        32,
    )
    d_ffn_other = core(d_ffn)
    moved_out = cross_tokens(output)

    d_gu, far, near = ffn_backward(d_ffn, d_ffn_other, low, high, slots_f)
    far, near, moved_out, d_gu = fence(far, near, moved_out, d_gu)
    got_far = core(far)
    gu3, y_t = pl.pallas_call(
        grads_g3_kernel,
        grid=(1,),
        in_specs=[SMEM]
        + [whole(tokens, width)] * 2
        + [pl.BlockSpec((1, 2 * tokens, 2 * half), lambda i: (3, 0, 0))],
        out_specs=[whole(width, 2 * half), whole(width, 2 * tokens)],
        out_shape=[out(width, 2 * half), hbm(width, 2 * tokens)],
        compiler_params=params(24),
        cost_estimate=cost(0.1),
        name="grads_g3",
    )(ids, *stay((normed, normed_other, d_gu)))
    got_far, gu3 = fence(got_far, gu3)
    gu_moved = second(gu3)
    d_residual, d_branch, grad_gain_one = one_step(
        back_norm_kernel,
        "back_norm",
        ids,
        (residual, near, got_far, d_summed, gains),
        [out(tokens, width, dtype=F32), out(tokens, width), out(1, width, dtype=F32)],
    )
    d_branch_other = core(d_branch)
    dn = one_step(
        grads_d_kernel,
        "grads_d",
        ids,
        stay((d_ffn, d_ffn_other, low[0], high[0])),
        [hbm(4, part if ring else width, half)] * (cols if ring else 1),
        32,
        [pltpu.VMEM((width, 2 * tokens), BF16)],
    )
    d_branch_other, dn = fence(d_branch_other, dn)
    gain_pair = jnp.concatenate([grad_gain_one, grad_gain_two], 0)
    gain_pair = gain_pair + core(gain_pair)
    dn_one = along(dn[3], 1) if ring else dn[0]
    back = (scalars, d_branch, d_branch_other, slots_a, got, cos, sin, q, k, v, attended_t, lse, x_t)
    dqk1, dv1, mine1, send1 = attend_backward(1, *back)
    dqk1, dv1, mine1, send1, gu_moved, dn_one, d_branch, gain_pair = fence(
        dqk1, dv1, mine1, send1, gu_moved, dn_one, d_branch, gain_pair
    )
    theirs1 = core(send1)
    gu1, gu2 = grads_g(y_t, d_gu, (1, 2), gu_moved)
    theirs1, gu1, gu2 = fence(theirs1, gu1, gu2)
    s3, dn_two = one_step(
        first_slots_kernel,
        "first_slots",
        ids,
        (mine1, theirs1, dn[2] if ring else dn[0], dn_one),
        [out(width, 2 * head_cols), out(*dn[0].shape)],
    )
    s3, dn_two, gu1, gu2, d_branch = fence(s3, dn_two, gu1, gu2, d_branch)
    a_moved = second(s3)
    gu_one, gu_two = first(gu1), second(gu2)
    dn_last = [along(dn_two, 2), along(dn[1], 1)] if ring else []
    back = (scalars, d_branch) + back[2:]
    dqk0, dv0, mine0, send0 = attend_backward(0, *back)
    dqk0, dv0, mine0, send0, a_moved, gu_one, gu_two, dn_last = fence(
        dqk0, dv0, mine0, send0, a_moved, gu_one, gu_two, dn_last
    )
    theirs0 = core(send0)
    if ring:
        own_dn = add(dn[0], *dn_last)
    else:
        own_dn = lax.psum_scatter(dn[0], "col", scatter_dimension=1, tiled=True)
    dn_moved = second(own_dn[3])
    (gu0,) = grads_g(y_t, d_gu, (0,))
    theirs0, gu0, dn_moved = fence(theirs0, gu0, dn_moved)

    def merge(base0, base1, one, two):
        if not ring:
            return [add(jnp.where(core0, base0, base1), one, two)]
        return one_step(merge_kernel, "merge", ids, (base0, base1, one, two), [out(part, base0.shape[1])] * cols)

    def to_owner(blocks):
        if not ring:
            return [lax.psum_scatter(blocks[0], "col", scatter_dimension=0, tiled=True)]
        return [blocks[0]] + [along(blocks[hop], hop) for hop in range(1, cols)]

    s1, s2 = one_step(
        slots_kernel, "slots", ids, (mine0, mine1, theirs0, theirs1, a_moved), [out(width, 2 * head_cols)] * 2
    )
    s1, s2, gu0, dqk0, output = fence(s1, s2, gu0, dqk0, output)
    a_one, a_two = first(s1), second(s2)
    g_parts = to_owner(merge(gu0, gu0, gu_one, gu_two))
    far, near = input_grad_parts(scalars, (dqk0, dqk1), (dv0, dv1), slots_a, got, tokens)
    output = jnp.where(stays, output.astype(F32), moved_out.astype(F32))
    a_one, a_two, g_parts, far, near, output, mom_gains = fence(
        a_one, a_two, g_parts, far, near, output, mom_gains
    )
    old = (mom_qkv, mom_out, mom_gate_up, mom_down.T) + (w_qkv, w_out, w_gate_up, w_down.T)
    old = old + (ema_qkv, ema_out, ema_gate_up, ema_down.T)
    old, a_one = fence(old, a_one)
    a_parts = to_owner(merge(mine0, theirs0, a_one, a_two))
    dn_one, dn_two = first(add(own_dn[1], dn_moved)), second(own_dn[2])
    shard_g = add(*g_parts)
    held = pl.pallas_call(
        fetch_kernel,
        in_specs=[ANY] * 12,
        out_specs=[VMEM] * 12,
        out_shape=[pltpu.VMEM(t.shape, F32) for t in old],
        scratch_shapes=[DMA((12,))],
        compiler_params=params(16),
        cost_estimate=cost(0.1),
        name="fetch",
    )(*stay(old))
    a_parts, dn_one, dn_two, shard_g, held, far = fence(a_parts, dn_one, dn_two, shard_g, held, far)
    shard_a = add(*a_parts)
    shard_d = add(own_dn[0], dn_one, dn_two)

    far_a, far_d, far_g = core(shard_a), core(shard_d), core(shard_g)
    got_far = core(far)
    far_a, far_d, far_g, got_far = fence(far_a, far_d, far_g, got_far)
    input_grad = d_residual + (near + got_far.astype(F32))
    moved_grad = cross_tokens(input_grad.astype(BF16))
    pack = one_step(
        pack_kernel,
        "pack",
        ids,
        (shard_a, far_a, shard_g, far_g, shard_d, far_d, gain_pair),
        [out(8, width, dtype=F32)],
    )[0]
    for axis, bits in (("col", (2, 1) if ring else ()), ("row", (2, 1))):
        size = mesh_sizes[axis]
        for bit in bits:
            pack = pack + lax.ppermute(pack, axis, [(i, i ^ bit) for i in range(size)])
    if not ring:
        pack = lax.psum(pack, "col")
    input_grad = jnp.where(stays, input_grad, moved_grad.astype(F32))
    pack, input_grad = fence(pack, input_grad)

    results = pl.pallas_call(
        update_kernel,
        in_specs=[SMEM] + [VMEM] * 22,
        out_specs=[ANY] * 12 + [VMEM] * 4,
        out_shape=[out(*t.shape, dtype=F32) for t in old]
        + [out(*gains.shape, dtype=F32)] * 3
        + [out(1, 1, dtype=F32)],
        scratch_shapes=[pltpu.VMEM(t.shape, F32) for t in old] + [DMA((12,))],
        compiler_params=params(24),
        cost_estimate=cost(0.1),
        name="update",
    )(ids, pack, shard_a, far_a, shard_g, far_g, shard_d, far_d, mom_gains, gains, ema_gains, *held)
    new = results[:12]
    gain_new = results[12:15]
    grad_norm = results[15][0, 0]
    return (
        output,
        input_grad,
        grad_norm,
        *new[0:3],
        new[3].T,
        gain_new[0],
        *new[4:7],
        new[7].T,
        gain_new[1],
        *new[8:11],
        new[11].T,
        gain_new[2],
    )


def solution(mesh):
    tok = P(("dp", "col", "row"), None)
    weights = (P(None, "col", "row"), P("row", "col"), P(None, "col", "row"), P("row", "col"), P())
    in_specs = (tok, tok, P(("dp", "col"), None)) + weights * 3
    out_specs = (tok, tok, P()) + weights * 3
    fn = functools.partial(body, mesh.shape["row"], mesh.shape["col"])
    return jax.shard_map(fn, mesh=mesh, in_specs=in_specs, out_specs=out_specs, check_vma=False)
```

```python
import functools

import jax
import jax.numpy as jnp
import numpy as np
from jax import lax
from jax.experimental import pallas as pl
from jax.experimental.pallas import tpu as pltpu
from jax.sharding import PartitionSpec as P

HD = 64
LEN = 1024

EPSILON = 1e-06
THETA = 10000.0
MOMENTUM = 0.9
RATE = 300.0
DECAY = 0.6
CLIP = 1.0
NEGATIVE = -1e30

F32 = jnp.float32
BF16 = jnp.bfloat16
NT = (((1,), (1,)), ((), ()))
NN = (((1,), (0,)), ((), ()))
TN = (((0,), (0,)), ((), ()))
BQ = 256


def rope_tables():
    half = HD // 2
    freqs = np.float32(THETA) ** (-(np.arange(half, dtype=np.float32) * np.float32(2.0)) / np.float32(HD))
    angles = np.arange(LEN, dtype=np.float32)[:, None] * freqs[None, :].astype(np.float32)
    return np.cos(angles), np.sin(angles)


def pair_tables():
    cosine, sine = rope_tables()
    return (
        jnp.asarray(np.concatenate([cosine] * 4, 1)),
        jnp.asarray(np.concatenate([-sine, sine] * 2, 1)),
    )


def mxu(lhs, rhs, dims=NN):
    return lax.dot_general(lhs, rhs, dims, preferred_element_type=F32)


def fence(*values):
    return lax.optimization_barrier(values)


def params(mib):
    return pltpu.CompilerParams(vmem_limit_bytes=mib << 20)


def cost(microseconds):
    return pl.CostEstimate(flops=int(1e9 * microseconds), bytes_accessed=1 << 10, transcendentals=0)


def out(*shape, dtype=BF16):
    return jax.ShapeDtypeStruct(shape, dtype)


def hbm(*shape, dtype=BF16):
    return pltpu.HBM(shape, dtype)


def stay(t):
    return jax.tree.map(lambda v: pltpu.with_memory_space_constraint(v, pltpu.HBM), t)


VMEM = pl.BlockSpec(memory_space=pltpu.VMEM)
SMEM = pl.BlockSpec(memory_space=pltpu.SMEM)
ANY = pl.BlockSpec(memory_space=pl.ANY)
DMA = pltpu.SemaphoreType.DMA


def piece_a_kernel(s_ref, qkv_ref, out_ref, a_ref):
    n = qkv_ref.shape[2]

    @pl.when(s_ref[0] == 0)
    def _():
        a_ref[:, :n] = qkv_ref[0].astype(BF16)
        a_ref[:, n:] = qkv_ref[1].astype(BF16)

    @pl.when(s_ref[0] == 1)
    def _():
        a_ref[:, :n] = qkv_ref[2].astype(BF16)
        a_ref[:, n:] = out_ref[...].T.astype(BF16)


def piece_f_kernel(s_ref, gu_ref, down_ref, f_ref):
    half = f_ref.shape[1] // 3
    at = pl.ds(pl.multiple_of(s_ref[0] * half, half), half)
    f_ref[:, :half] = gu_ref[0, :, at].astype(BF16)
    f_ref[:, half : 2 * half] = gu_ref[1, :, at].astype(BF16)
    f_ref[:, 2 * half :] = down_ref[:, at].astype(BF16)


def whole(*shape):
    return pl.BlockSpec(shape, lambda i: (0,) * len(shape))


def one_step(kernel, name, scalars, inputs, outputs, mib=24, scratch=(), us=0.1):
    return pl.pallas_call(
        kernel,
        grid=(1,),
        in_specs=[SMEM] + [whole(*t.shape) for t in inputs],
        out_specs=[whole(*t.shape) for t in outputs],
        out_shape=outputs,
        scratch_shapes=list(scratch),
        compiler_params=params(mib),
        cost_estimate=cost(us),
        name=name,
    )(scalars, *inputs)


def join_kernel(s_ref, *refs):
    blocks, whole_ref, sems = refs[:-2], refs[-2], refs[-1]
    cols, part = len(blocks), blocks[0].shape[0]
    copies = []
    for hop, block in enumerate(blocks):
        at = pl.multiple_of((s_ref[1] ^ hop) * part, part)
        copies.append(pltpu.make_async_copy(block, whole_ref.at[pl.ds(at, part)], sems.at[hop]))
    for copy in copies:
        copy.start()
    for copy in copies:
        copy.wait()


def pick_kernel(s_ref, a0_ref, a2_ref, a3_ref, send_ref, sems):
    def move(lo, hi):
        copies = [
            pltpu.make_async_copy(lo, send_ref.at[0], sems.at[0]),
            pltpu.make_async_copy(hi, send_ref.at[1], sems.at[1]),
        ]
        for copy in copies:
            copy.start()
        for copy in copies:
            copy.wait()

    @pl.when(s_ref[0] == 0)
    def _():
        move(a2_ref, a3_ref)

    @pl.when(s_ref[0] == 1)
    def _():
        move(a0_ref, a2_ref)


def causal(scores_t, block):
    keys = scores_t.shape[0]
    row = lax.broadcasted_iota(jnp.int32, (block, block), 0)
    column = lax.broadcasted_iota(jnp.int32, (block, block), 1)
    tail = jnp.where(row <= column, scores_t[keys - block :], NEGATIVE)
    return tail if keys == block else jnp.concatenate([scores_t[: keys - block], tail], 0)


def swap_halves(t):
    lane = lax.broadcasted_iota(jnp.int32, (1, t.shape[1]), 1)
    return jnp.where(lane % HD < HD // 2, pltpu.roll(t, t.shape[1] - HD // 2, 1), pltpu.roll(t, HD // 2, 1))


def pick_weights(core, j, a0_ref, a1_ref, a3_ref, got_ref, qk_ref, vo_ref):
    @pl.when(core == 0)
    def _():
        vo_ref[...] = got_ref[0]

        @pl.when(j == 0)
        def _():
            qk_ref[...] = a0_ref[...]

        @pl.when(j == 1)
        def _():
            qk_ref[...] = a1_ref[...]

    @pl.when(core == 1)
    def _():
        qk_ref[...] = got_ref[0]

        @pl.when(j == 0)
        def _():
            vo_ref[...] = a1_ref[...]

        @pl.when(j == 1)
        def _():
            vo_ref[...] = a3_ref[...]


def attend_forward_kernel(
    s_ref, x0_ref, x1_ref, a0_ref, a1_ref, a3_ref, got_ref, cos_ref, sin_ref,
    q_ref, k_ref, v_ref, ot_ref, lse_ref, xt_ref, far_ref, near_ref,
    qk_w, vo_w, o_ref, total_ref,
):
    core, live = s_ref[0], s_ref[1]
    j = pl.program_id(0)
    length = q_ref.shape[1]
    tokens = x0_ref.shape[0]
    n = 3 * HD
    pick_weights(core, j, a0_ref, a1_ref, a3_ref, got_ref, qk_w, vo_w)
    lane = lax.broadcasted_iota(jnp.int32, (tokens, HD), 1)
    one = jnp.where(lane == 0, 1.0, 0.0).astype(BF16)
    for x_ref, which in ((x0_ref, core), (x1_ref, 1 - core)):
        start = pl.multiple_of(which * tokens, tokens)
        at = pl.ds(start, tokens)
        qk = mxu(x_ref[...], qk_w[...])
        cos = jnp.concatenate([cos_ref[at, :]] * 3, 1)
        sin = jnp.concatenate([sin_ref[at, :]] * 3, 1)
        qk = qk * cos + swap_halves(qk) * sin
        q = (qk[:, :n] * (HD ** -0.5)).astype(BF16)
        k = qk[:, n:].astype(BF16)
        v = mxu(x_ref[...], vo_w[:, :n]).astype(BF16)
        key = start + lax.broadcasted_iota(jnp.int32, (tokens, HD), 0)
        bias = jnp.where((lane == 0) & (key >= live), NEGATIVE, 0.0).astype(BF16)
        for head in range(3):
            lanes = slice(head * HD, (head + 1) * HD)
            q_ref[head, at, :] = jnp.concatenate([q[:, lanes], one], 1)
            k_ref[head, at, :] = jnp.concatenate([k[:, lanes], bias], 1)
            v_ref[head, at, :] = jnp.concatenate([v[:, lanes], one], 1)

        @pl.when(j == 0)
        def _():
            xt_ref[:, at] = x_ref[...].T

    for block in range(length // BQ):
        keys = (block + 1) * BQ
        span = slice(block * BQ, keys)
        parts = []
        for head in range(3):
            scores = causal(mxu(k_ref[head, :keys, :], q_ref[head, span, :], NT), BQ)
            top = jnp.max(scores, 0, keepdims=True)
            probs = jnp.exp(scores - top).astype(BF16)
            o = mxu(probs, v_ref[head, :keys, :], TN).T
            total = o[HD : HD + 1]
            parts.append(o[:HD] / total)
            lse_ref[0, head : head + 1, span] = top + jnp.log(total)
        o = jnp.concatenate(parts, 0)
        ot_ref[0, :, span] = o.astype(BF16)
        o_ref[span, :] = o.T.astype(BF16)
    part = mxu(o_ref[...], vo_w[:, n:], NT)

    @pl.when(j == 0)
    def _():
        total_ref[...] = part

    @pl.when(j == 1)
    def _():
        total_ref[...] += part
        near_ref[...] = total_ref[pl.ds(pl.multiple_of(core * tokens, tokens), tokens), :]
        far_ref[...] = total_ref[pl.ds(pl.multiple_of((1 - core) * tokens, tokens), tokens), :].astype(BF16)


def attend_forward(scalars, x_own, x_other, slots, got, cos, sin):
    tokens, width = x_own.shape
    wide = slots[0].shape[1]
    n = wide // 2
    by_j = lambda *shape: pl.BlockSpec(shape, lambda j: (j,) + (0,) * (len(shape) - 1))
    return pl.pallas_call(
        attend_forward_kernel,
        grid=(2,),
        in_specs=[SMEM]
        + [whole(tokens, width)] * 2
        + [whole(width, wide)] * 3
        + [by_j(1, width, wide), whole(LEN, 128), whole(LEN, 128)],
        out_specs=[by_j(3, LEN, 128)] * 3
        + [by_j(1, n, LEN), by_j(1, 8, LEN), whole(width, LEN)]
        + [whole(tokens, width)] * 2,
        out_shape=[hbm(6, LEN, 128)] * 3
        + [hbm(2, n, LEN), hbm(2, 8, LEN, dtype=F32), hbm(width, LEN)]
        + [out(tokens, width), out(tokens, width, dtype=F32)],
        scratch_shapes=[
            pltpu.VMEM((width, wide), BF16),
            pltpu.VMEM((width, wide), BF16),
            pltpu.VMEM((LEN, n), BF16),
            pltpu.VMEM((LEN, width), F32),
        ],
        compiler_params=params(44),
        cost_estimate=cost(2),
        name="attend_forward",
    )(scalars, x_own, x_other, *stay((slots[0], slots[1], slots[3])), got, *stay((cos, sin)))


def attend_backward_kernel(
    s_ref, d0_ref, d1_ref, lo_ref, hi_ref, got_ref, cos_ref, sin_ref, ot_ref, lse_ref,
    q_any, k_any, v_any, xt_any,
    dqk_ref, dv_ref, mine_ref, send_ref,
    q_ref, k_ref, v_ref, xt_ref, vo_w, do_ref, dk_acc, dv_acc, sems, *, j,
):
    core = s_ref[0]
    tokens = d0_ref.shape[0]
    n = 3 * HD
    heads = pl.ds(3 * j, 3)
    copies = [
        pltpu.make_async_copy(k_any.at[heads], k_ref, sems.at[0]),
        pltpu.make_async_copy(q_any.at[heads], q_ref, sems.at[1]),
        pltpu.make_async_copy(v_any.at[heads], v_ref, sems.at[2]),
        pltpu.make_async_copy(xt_any, xt_ref, sems.at[3]),
    ]
    for copy in copies:
        copy.start()

    @pl.when(core == 0)
    def _():
        vo_w[...] = got_ref[0, :, n:]

    @pl.when(core == 1)
    def _():
        vo_w[...] = hi_ref[:, n:]

    for d_ref, which in ((d0_ref, core), (d1_ref, 1 - core)):
        at = pl.ds(pl.multiple_of(which * tokens, tokens), tokens)
        do_ref[at, :] = mxu(d_ref[...], vo_w[...]).astype(BF16)

    length = do_ref.shape[0]
    products = do_ref[...].astype(F32).T * ot_ref[0].astype(F32)
    for copy in copies[:3]:
        copy.wait()

    def unrotate(t):
        return t * cos_ref[...] - swap_halves(t) * sin_ref[...]

    for head in range(3):
        lanes = slice(head * HD, (head + 1) * HD)
        delta = jnp.sum(products[lanes], 0, keepdims=True)
        dq_parts = []
        for block in range(length // BQ):
            keys = (block + 1) * BQ
            span = slice(block * BQ, keys)
            before = keys - BQ
            q = q_ref[head, span, :]
            scores = causal(mxu(k_ref[head, :keys, :], q, NT), BQ)
            probs = jnp.exp(scores - lse_ref[0, head : head + 1, span])
            d_out = do_ref[span, lanes]
            d_probs = mxu(v_ref[head, :keys, :HD], d_out, NT)
            d_scores = (probs * (d_probs - delta[:, span])).astype(BF16)
            dv_part = mxu(probs.astype(BF16), d_out)
            dk_part = mxu(d_scores, q)
            if block:
                dv_acc[:before, :] += dv_part[:before]
                dk_acc[:before, :] += dk_part[:before]
            dv_acc[before:keys, :] = dv_part[before:]
            dk_acc[before:keys, :] = dk_part[before:]
            dq_parts.append(mxu(d_scores, k_ref[head, :keys, :], TN))
        dq = jnp.concatenate(dq_parts, 0) * (HD ** -0.5)
        dqk_ref[:, head * HD : (head + 1) * HD] = unrotate(dq)[:, :HD].astype(BF16)
        dqk_ref[:, n + head * HD : n + (head + 1) * HD] = unrotate(dk_acc[...])[:, :HD].astype(BF16)
        dv_ref[:, lanes] = dv_acc[...].astype(BF16)

    copies[3].wait()
    own = jnp.where(core == 0, 0, tokens)
    grad_o = jnp.zeros((n, d0_ref.shape[1]), F32)
    for d_ref, which in ((d0_ref, core), (d1_ref, 1 - core)):
        at = pl.ds(pl.multiple_of(which * tokens, tokens), tokens)
        grad_o += mxu(ot_ref[0, :, at], d_ref[...])
    grad_o = grad_o.T.astype(BF16)
    grad_qk = mxu(xt_ref[...], dqk_ref[...]).astype(BF16)
    grad_v = mxu(xt_ref[...], dv_ref[...]).astype(BF16)

    @pl.when(core == 0)
    def _():
        mine_ref[...] = grad_qk
        send_ref[:, :n] = grad_v
        send_ref[:, n:] = grad_o

    @pl.when(core == 1)
    def _():
        send_ref[...] = grad_qk
        mine_ref[:, :n] = grad_v
        mine_ref[:, n:] = grad_o


def attend_backward(j, scalars, d_own, d_other, slots, got, cos, sin, q, k, v, out_t, lse, x_t):
    tokens, width = d_own.shape
    wide = slots[0].shape[1]
    n = wide // 2
    at_j = lambda *shape: pl.BlockSpec(shape, lambda i: (j,) + (0,) * (len(shape) - 1))
    lo, hi = (slots[0], slots[1]) if j == 0 else (slots[1], slots[3])
    return pl.pallas_call(
        functools.partial(attend_backward_kernel, j=j),
        grid=(1,),
        in_specs=[SMEM]
        + [whole(tokens, width)] * 2
        + [whole(width, wide)] * 2
        + [at_j(1, width, wide), whole(LEN, 128), whole(LEN, 128), at_j(1, n, LEN), at_j(1, 8, LEN)]
        + [ANY] * 4,
        out_specs=[whole(LEN, wide), whole(LEN, n), whole(width, wide), whole(width, wide)],
        out_shape=[hbm(LEN, wide), hbm(LEN, n), hbm(width, wide), hbm(width, wide)],
        scratch_shapes=[
            pltpu.VMEM((3, LEN, 128), BF16),
            pltpu.VMEM((3, LEN, 128), BF16),
            pltpu.VMEM((3, LEN, 128), BF16),
            pltpu.VMEM((width, LEN), BF16),
            pltpu.VMEM((width, n), BF16),
            pltpu.VMEM((LEN, n), BF16),
            pltpu.VMEM((LEN, 128), F32),
            pltpu.VMEM((LEN, HD), F32),
            DMA((4,)),
        ],
        compiler_params=params(44),
        cost_estimate=cost(2),
        name="attend_backward",
    )(scalars, d_own, d_other, *stay((lo, hi, got, cos, sin, out_t, lse, q, k, v, x_t)))


def input_grad_kernel(s_ref, p0_ref, p1_ref, v0_ref, v1_ref, a0_ref, a1_ref, a3_ref, got_ref, far_ref, near_ref, qk_w, vo_w):
    core = s_ref[0]
    n = v0_ref.shape[1]
    tokens = far_ref.shape[0]
    for j, (lo, hi) in enumerate(((a0_ref, a1_ref), (a1_ref, a3_ref))):

        @pl.when(core == 0)
        def _():
            qk_w[j] = lo[...]
            vo_w[j] = got_ref[j, :, :n]

        @pl.when(core == 1)
        def _():
            qk_w[j] = got_ref[j]
            vo_w[j] = hi[:, :n]

    for which, dst in ((1 - core, far_ref), (core, near_ref)):
        at = pl.ds(pl.multiple_of(which * tokens, tokens), tokens)
        total = mxu(p0_ref[at, :], qk_w[0], NT) + mxu(v0_ref[at, :], vo_w[0], NT)
        total = total + (mxu(p1_ref[at, :], qk_w[1], NT) + mxu(v1_ref[at, :], vo_w[1], NT))
        dst[...] = total.astype(dst.dtype)


def input_grad_parts(scalars, d_qk, d_v, slots, got, tokens):
    width, wide = slots[0].shape
    return one_step(
        input_grad_kernel,
        "input_grad",
        scalars,
        stay((*d_qk, *d_v, slots[0], slots[1], slots[3], got)),
        [out(tokens, width), out(tokens, width, dtype=F32)],
        40,
        [pltpu.VMEM((2, width, wide), BF16), pltpu.VMEM((2, width, wide // 2), BF16)],
    )


def first_norm_kernel(s_ref, x_ref, near_ref, far_ref, gain_ref, resid_ref, normed_ref):
    residual = x_ref[...].astype(F32) + (near_ref[...] + far_ref[...].astype(F32))
    scale = lax.rsqrt(jnp.mean(residual * residual, -1, keepdims=True) + EPSILON)
    resid_ref[...] = residual
    normed_ref[...] = (residual * scale * gain_ref[0:1, :]).astype(BF16)


def last_norm_kernel(s_ref, resid_ref, near_ref, far_ref, gain_ref, cot_ref, out_ref, dsum_ref, dffn_ref, dgain_ref):
    core, live = s_ref[0], s_ref[1]
    tokens, width = resid_ref.shape
    residual = resid_ref[...]
    scale = lax.rsqrt(jnp.mean(residual * residual, -1, keepdims=True) + EPSILON)
    summed = residual * scale * gain_ref[0:1, :] + (near_ref[...] + far_ref[...].astype(F32))
    scale = lax.rsqrt(jnp.mean(summed * summed, -1, keepdims=True) + EPSILON)
    unit = summed * scale
    out_ref[...] = (unit * gain_ref[1:2, :]).astype(BF16)
    position = core * tokens + lax.broadcasted_iota(jnp.int32, (tokens, 1), 0)
    cot = jnp.where(position < live, cot_ref[...].astype(F32), 0.0)
    dgain_ref[...] = jnp.sum(cot * unit, 0, keepdims=True)
    hat = cot * gain_ref[1:2, :]
    inner = jnp.mean(hat * unit, -1, keepdims=True)
    d_summed = scale * (hat - unit * inner)
    dsum_ref[...] = d_summed
    dffn_ref[...] = d_summed.astype(BF16)


def back_norm_kernel(s_ref, resid_ref, near_ref, far_ref, dsum_ref, gain_ref, dres_ref, dbranch_ref, dgain_ref):
    residual = resid_ref[...]
    scale = lax.rsqrt(jnp.mean(residual * residual, -1, keepdims=True) + EPSILON)
    unit = residual * scale
    d_normed = dsum_ref[...] + (near_ref[...] + far_ref[...].astype(F32))
    dgain_ref[...] = jnp.sum(d_normed * unit, 0, keepdims=True)
    hat = d_normed * gain_ref[0:1, :]
    inner = jnp.mean(hat * unit, -1, keepdims=True)
    d_residual = scale * (hat - unit * inner)
    dres_ref[...] = d_residual
    dbranch_ref[...] = d_residual.astype(BF16)


def fetch_slots(step, sources, dst, sems):
    copies = [pltpu.make_async_copy(src, dst.at[i], sems.at[i]) for i, src in enumerate(sources)]

    @pl.when(step == 0)
    def _():
        for copy in copies:
            copy.start()

    for i, copy in enumerate(copies):

        @pl.when(step == i)
        def _():
            copy.wait()


def ffn_forward_kernel(y0_ref, y1_ref, *refs, slots, start, finish):
    refs = list(refs)
    carry_ref = None if start else refs.pop(0)
    sources, refs = refs[:slots], refs[slots:]
    hid_ref, silu_ref, slope_ref = refs[:3]
    results = refs[3 : 5 if finish else 4]
    w_ref, total_ref, sems = refs[-3:]
    step = pl.program_id(0)
    tokens = y0_ref.shape[0]
    half = hid_ref.shape[2]
    fetch_slots(step, sources, w_ref, sems)

    @pl.when(step == 0)
    def _():
        total_ref[...] = jnp.zeros_like(total_ref) if start else carry_ref[...]

    for part, y_ref in ((0, y0_ref), (1, y1_ref)):
        at = slice(part * tokens, (part + 1) * tokens)
        both = mxu(y_ref[...], w_ref[step, :, : 2 * half])
        gate, up = both[:, :half], both[:, half:]
        sig = jax.nn.sigmoid(gate)
        silu = gate * sig
        hidden = (silu * up).astype(BF16)
        hid_ref[0, at, :] = hidden
        silu_ref[0, at, :] = silu.astype(BF16)
        slope_ref[0, at, :] = (up * (sig + silu * (1.0 - sig))).astype(BF16)
        total_ref[at, :] += mxu(hidden, w_ref[step, :, 2 * half :], NT)

    @pl.when(step == slots - 1)
    def _():
        if finish:
            far_ref, near_ref = results
            near_ref[...] = total_ref[:tokens, :]
            far_ref[...] = total_ref[tokens:, :].astype(BF16)
        else:
            results[0][...] = total_ref[...]


def ffn_forward(normed, normed_other, slots, carry, finish):
    tokens, width = normed.shape
    lanes = slots[0].shape[1]
    count = len(slots)
    half = lanes // 3
    per_slot = pl.BlockSpec((1, 2 * tokens, half), lambda s: (s, 0, 0))
    if finish:
        results = [out(tokens, width), out(tokens, width, dtype=F32)]
    else:
        results = [out(2 * tokens, width, dtype=F32)]
    inputs = (normed, normed_other) + (() if carry is None else (carry,))
    return pl.pallas_call(
        functools.partial(ffn_forward_kernel, slots=count, start=carry is None, finish=finish),
        grid=(count,),
        in_specs=[whole(*t.shape) for t in inputs] + [ANY] * count,
        out_specs=[per_slot] * 3 + [whole(*t.shape) for t in results],
        out_shape=[hbm(count, 2 * tokens, half)] * 3 + results,
        scratch_shapes=[
            pltpu.VMEM((count, width, lanes), BF16),
            pltpu.VMEM((2 * tokens, width), F32),
            DMA((count,)),
        ],
        compiler_params=params(36),
        cost_estimate=cost(2),
        name="ffn_forward",
    )(*inputs, *slots)


def ffn_backward_kernel(d0_ref, d1_ref, silu_a, slope_a, silu_b, slope_b, *refs):
    sources, (dgu_ref, far_ref, near_ref, w_ref, total_ref, sems) = refs[:4], refs[4:]
    step = pl.program_id(0)
    tokens = d0_ref.shape[0]
    half = silu_a.shape[2]
    fetch_slots(step, sources, w_ref, sems)

    @pl.when(step == 0)
    def _():
        total_ref[...] = jnp.zeros_like(total_ref)

    def slot(silu_ref, slope_ref):
        for part, d_ref in ((0, d0_ref), (1, d1_ref)):
            at = slice(part * tokens, (part + 1) * tokens)
            d_hidden = mxu(d_ref[...], w_ref[step, :, 2 * half :])
            d_gate = (d_hidden * slope_ref[0, at, :].astype(F32)).astype(BF16)
            d_up = (d_hidden * silu_ref[0, at, :].astype(F32)).astype(BF16)
            dgu_ref[0, at, :half] = d_gate
            dgu_ref[0, at, half:] = d_up
            term = mxu(d_gate, w_ref[step, :, :half], NT) + mxu(d_up, w_ref[step, :, half : 2 * half], NT)
            total_ref[at, :] += term

    @pl.when(step < 3)
    def _():
        slot(silu_a, slope_a)

    @pl.when(step == 3)
    def _():
        slot(silu_b, slope_b)
        near_ref[...] = total_ref[:tokens, :]
        far_ref[...] = total_ref[tokens:, :].astype(BF16)


def ffn_backward(d_ffn, d_other, low, high, slots):
    tokens, width = d_ffn.shape
    lanes = slots[0].shape[1]
    half = lanes // 3
    first_three = pl.BlockSpec((1, 2 * tokens, half), lambda s: (jnp.minimum(s, 2), 0, 0))
    return pl.pallas_call(
        ffn_backward_kernel,
        grid=(4,),
        in_specs=[whole(tokens, width)] * 2
        + [first_three] * 2
        + [whole(1, 2 * tokens, half)] * 2
        + [ANY] * 4,
        out_specs=[pl.BlockSpec((1, 2 * tokens, 2 * half), lambda s: (s, 0, 0))] + [whole(tokens, width)] * 2,
        out_shape=[hbm(4, 2 * tokens, 2 * half), out(tokens, width), out(tokens, width, dtype=F32)],
        scratch_shapes=[
            pltpu.VMEM((4, width, lanes), BF16),
            pltpu.VMEM((2 * tokens, width), F32),
            DMA((4,)),
        ],
        compiler_params=params(40),
        cost_estimate=cost(2),
        name="ffn_backward",
    )(d_ffn, d_other, *stay((*low[1:], *high[1:], *slots)))


def grads_g_kernel(*refs, count, moved):
    yt_ref, refs = refs[0], refs[1:]
    dgu, refs = refs[:count], refs[count:]
    moved_ref, results = (refs[0], refs[1:]) if moved else (None, refs)
    for i, (dgu_ref, result_ref) in enumerate(zip(dgu, results)):
        grad = mxu(yt_ref[...], dgu_ref[0])
        if moved and i == 0:
            grad = grad + moved_ref[...].astype(F32)
        result_ref[...] = grad.astype(BF16)


def grads_g(y_t, d_gu, slots, moved=None):
    width, length = y_t.shape
    wide = d_gu.shape[2]
    at_slot = [pl.BlockSpec((1, length, wide), functools.partial(lambda n, i: (n, 0, 0), n)) for n in slots]
    extra = [] if moved is None else [moved]
    return pl.pallas_call(
        functools.partial(grads_g_kernel, count=len(slots), moved=moved is not None),
        grid=(1,),
        in_specs=[whole(width, length)] + at_slot + [whole(*t.shape) for t in extra],
        out_specs=[whole(width, wide)] * len(slots),
        out_shape=[out(width, wide)] * len(slots),
        compiler_params=params(32),
        cost_estimate=cost(0.1),
        name="grads_g",
    )(stay(y_t), *[stay(d_gu)] * len(slots), *extra)


def grads_g3_kernel(s_ref, y0_ref, y1_ref, dgu_ref, g_ref, yt_ref):
    tokens = y0_ref.shape[0]
    yt_ref[:, :tokens] = y0_ref[...].T
    yt_ref[:, tokens:] = y1_ref[...].T
    g_ref[...] = mxu(yt_ref[...], dgu_ref[0]).astype(BF16)


def grads_d_kernel(s_ref, d0_ref, d1_ref, hid_a, hid_b, *refs):
    blocks, dt_ref, grad_ref = refs[:-2], refs[-2], refs[-1]
    tokens = d0_ref.shape[0]
    dt_ref[:, :tokens] = d0_ref[...].T
    dt_ref[:, tokens:] = d1_ref[...].T
    for slot in range(4):
        hidden = hid_a[slot] if slot < 3 else hid_b[0]
        grad_ref[slot] = mxu(dt_ref[...], hidden).astype(BF16)
    for hop, block_ref in enumerate(blocks):
        rows = block_ref.shape[1]
        place = (s_ref[1] ^ hop) if len(blocks) > 1 else 0
        at = pl.ds(pl.multiple_of(place * rows, rows), rows)
        for slot in range(4):
            block_ref[slot] = grad_ref[slot, at, :]


def first_slots_kernel(s_ref, mine1_ref, theirs1_ref, dn_ref, dn_moved_ref, s3_ref, sum_ref):
    sum_ref[...] = (dn_ref[...].astype(F32) + dn_moved_ref[...].astype(F32)).astype(BF16)

    @pl.when(s_ref[0] == 0)
    def _():
        s3_ref[...] = theirs1_ref[...]

    @pl.when(s_ref[0] == 1)
    def _():
        s3_ref[...] = mine1_ref[...]


def slots_kernel(s_ref, mine0_ref, mine1_ref, theirs0_ref, theirs1_ref, moved_ref, s1_ref, s2_ref):
    moved = moved_ref[...].astype(F32)

    @pl.when(s_ref[0] == 0)
    def _():
        s1_ref[...] = (mine1_ref[...].astype(F32) + moved).astype(BF16)
        s2_ref[...] = theirs0_ref[...]

    @pl.when(s_ref[0] == 1)
    def _():
        s1_ref[...] = (mine0_ref[...].astype(F32) + moved).astype(BF16)
        s2_ref[...] = theirs1_ref[...]


def merge_kernel(s_ref, base0_ref, base1_ref, one_ref, two_ref, *blocks):
    cols = len(blocks)
    part = blocks[0].shape[0]
    for hop, block_ref in enumerate(blocks):
        at = pl.ds(pl.multiple_of((s_ref[1] ^ hop) * part, part), part)
        moved = one_ref[at, :].astype(F32) + two_ref[at, :].astype(F32)

        @pl.when(s_ref[0] == 0)
        def _():
            block_ref[...] = (base0_ref[at, :].astype(F32) + moved).astype(BF16)

        @pl.when(s_ref[0] == 1)
        def _():
            block_ref[...] = (base1_ref[at, :].astype(F32) + moved).astype(BF16)


def pack_kernel(s_ref, *refs):
    shards, gain_ref, pack_ref = refs[:-2], refs[-2], refs[-1]
    total = jnp.zeros((1, 1), F32)
    for ref in shards:
        value = ref[...].astype(F32)
        total = total + jnp.sum(jnp.sum(value * value, 0, keepdims=True), 1, keepdims=True)
    row = lax.broadcasted_iota(jnp.int32, pack_ref.shape, 0)
    gain = jnp.where(row == 0, gain_ref[0:1, :], gain_ref[1:2, :])
    pack_ref[...] = jnp.where(row < 2, gain, jnp.broadcast_to(total, pack_ref.shape))


def update(grad_full, moment, weight, average, factor):
    clipped = grad_full * factor
    new_moment = MOMENTUM * moment + clipped
    new_weight = weight - RATE * (clipped + MOMENTUM * new_moment)
    new_average = DECAY * average + (1.0 - DECAY) * new_weight
    return (new_moment, new_weight, new_average)


def fetch_kernel(*refs):
    count = (len(refs) - 1) // 2
    sems = refs[-1]
    copies = [pltpu.make_async_copy(refs[i], refs[count + i], sems.at[i]) for i in range(count)]
    for copy in copies:
        copy.start()
    for copy in copies:
        copy.wait()


def update_kernel(s_ref, pack_ref, a0_ref, a1_ref, g0_ref, g1_ref, d0_ref, d1_ref, gm_ref, gw_ref, ge_ref, *refs):
    old, refs = refs[:12], refs[12:]
    new, refs = refs[:12], refs[12:]
    gain_new, norm_ref, refs = refs[:3], refs[3], refs[4:]
    held, out_sems = refs[:12], refs[12]
    gains = pack_ref[0:2, :]
    squares = pack_ref[2:3, 0:1] + jnp.sum(jnp.sum(gains * gains, 0, keepdims=True), 1, keepdims=True)
    norm = jnp.sqrt(squares)
    norm_ref[...] = norm
    factor = jnp.minimum(1.0, CLIP / (norm + 1e-06))
    for ref, value in zip(gain_new, update(gains, gm_ref[...], gw_ref[...], ge_ref[...], factor)):
        ref[...] = value
    n = held[0].shape[2]
    half = d0_ref.shape[1]

    def put(kind, at, grad):
        moment, weight, average = (old[kind + 4 * i] for i in range(3))
        results = update(grad, moment[at], weight[at], average[at], factor)
        for i, value in enumerate(results):
            held[kind + 4 * i][at] = value

    every = slice(None)

    def parts(kind, mine, other):
        if kind == 0:
            qk, vo = mine[0], other[0]
            put(0, (0, every, every), qk[:, :n].astype(F32))
            put(0, (1, every, every), qk[:, n:].astype(F32))
            put(0, (2, every, every), vo[:, :n].astype(F32))
        elif kind == 1:
            put(1, (every, every), other[0][:, n:].astype(F32).T)
        else:
            for which, part in enumerate((mine, other)):
                lanes = slice(which * half, (which + 1) * half)
                if kind == 2:
                    put(2, (0, every, lanes), part[1][:, :half].astype(F32))
                    put(2, (1, every, lanes), part[1][:, half:].astype(F32))
                else:
                    put(3, (every, lanes), part[2][...].astype(F32))

    here, there = (a0_ref, g0_ref, d0_ref), (a1_ref, g1_ref, d1_ref)
    for kind in (2, 3, 0, 1):
        @pl.when(s_ref[0] == 0)
        def _():
            parts(kind, here, there)

        @pl.when(s_ref[0] == 1)
        def _():
            parts(kind, there, here)

        for i in (kind, kind + 4, kind + 8):
            pltpu.make_async_copy(held[i], new[i], out_sems.at[i]).start()
    for i in range(12):
        pltpu.make_async_copy(held[i], new[i], out_sems.at[i]).wait()


def body(
    rows,
    cols,
    block_input,
    out_grad,
    lengths,
    w_qkv,
    w_out,
    w_gate_up,
    w_down,
    gains,
    mom_qkv,
    mom_out,
    mom_gate_up,
    mom_down,
    mom_gains,
    ema_qkv,
    ema_out,
    ema_gate_up,
    ema_down,
    ema_gains,
):
    d = lax.axis_index("dp")
    r = lax.axis_index("row")
    c = lax.axis_index("col")
    core0 = d == 0
    stays = d == r % 2
    tokens, width = block_input.shape
    ring = cols == 4
    mesh_sizes = {"row": rows, "col": cols}
    part = width // cols
    head_cols = w_qkv.shape[2]
    half = w_gate_up.shape[2] // 2

    pairs = [(i, j) for i in range(2) for j in range(rows)]
    swap_pairs = [(i * rows + j, (j % 2) * rows + (j // 2) * 2 + i) for i, j in pairs]
    cross_pairs = [(i, j) for i, j in swap_pairs if i != j]
    first_pairs = [(i * rows + j, i * rows + (j ^ (1 if i == 0 else 2))) for i, j in pairs]
    second_pairs = [(i * rows + j, i * rows + (j ^ (2 if i == 0 else 1))) for i, j in pairs]

    def swap_tokens(t):
        return lax.ppermute(t, ("dp", "row"), swap_pairs)

    def cross_tokens(t):
        return lax.ppermute(t, ("dp", "row"), cross_pairs)

    def first(t):
        return lax.ppermute(t, ("dp", "row"), first_pairs)

    def second(t):
        return lax.ppermute(t, ("dp", "row"), second_pairs)

    def core(t):
        return lax.ppermute(t, "dp", [(0, 1), (1, 0)])

    def along(t, k):
        return lax.ppermute(t, "col", [(i, i ^ k) for i in range(cols)])

    def join_cols(*blocks):
        return pl.pallas_call(
            join_kernel,
            in_specs=[SMEM] + [ANY] * cols,
            out_specs=ANY,
            out_shape=out(width, blocks[0].shape[1]),
            scratch_shapes=[DMA((cols,))],
            compiler_params=params(16),
            cost_estimate=cost(0.1),
            name="join",
        )(ids, *blocks)

    def gather_cols(t):
        return lax.all_gather(t, "col", axis=t.ndim - 2, tiled=True)

    def add(*values):
        total = values[0].astype(F32)
        for value in values[1:]:
            total = total + value.astype(F32)
        return total.astype(BF16)

    ids = jnp.stack([d, c]).astype(jnp.int32)
    (piece_a,) = one_step(piece_a_kernel, "piece_a", ids, stay((w_qkv, w_out)), [out(part, 2 * head_cols)], 60)
    piece_a, block_input = fence(piece_a, block_input)
    a_cols = [along(piece_a, 1), along(piece_a, 2)] if ring else [gather_cols(piece_a)]
    x_own = swap_tokens(block_input)
    (piece_f,) = one_step(piece_f_kernel, "piece_f", ids, stay((w_gate_up, w_down.T)), [out(part, 3 * half)], 60)
    a_cols, piece_f, x_own, out_grad = fence(a_cols, piece_f, x_own, out_grad)
    cot = swap_tokens(out_grad)
    if ring:
        a_cols = a_cols + [along(a_cols[1], 1)]
        f_cols = [along(piece_f, 1), along(piece_f, 2)]
    else:
        f_cols = [gather_cols(piece_f)]
    a_cols, piece_a, lengths = fence(a_cols, piece_a, lengths)
    a0 = join_cols(piece_a, *a_cols) if ring else a_cols[0]
    a1, a2 = first(a0), second(a0)
    a0, a1, a2, f_cols, x_own, cot = fence(a0, a1, a2, f_cols, x_own, cot)
    a3 = second(a1)
    if ring:
        f_cols = f_cols + [along(f_cols[1], 1)]
    x_other = core(x_own)
    own_length = swap_tokens(lengths)[0, :]
    seq_ids = jnp.arange(own_length.shape[0], dtype=jnp.int32)
    own_length = jnp.sum(jnp.where(seq_ids == r // 2, own_length, 0))
    scalars = jnp.stack([d.astype(jnp.int32), own_length])
    a0, a1, a2, a3, f_cols, x_own, x_other, scalars = fence(a0, a1, a2, a3, f_cols, x_own, x_other, scalars)
    f0 = join_cols(piece_f, *f_cols) if ring else f_cols[0]
    f0, a0, a2, a3 = fence(f0, a0, a2, a3)
    slots_a = [a0, a1, a2, a3]
    send = pl.pallas_call(
        pick_kernel,
        in_specs=[SMEM] + [ANY] * 3,
        out_specs=ANY,
        out_shape=out(2, width, 2 * head_cols),
        scratch_shapes=[DMA((2,))],
        compiler_params=params(16),
        cost_estimate=cost(0.1),
        name="pick",
    )(ids, a0, a2, a3)
    got = core(send)
    f1, f2 = first(f0), second(f0)
    cos, sin = pair_tables()
    q, k, v, attended_t, lse, x_t, far, near = attend_forward(scalars, x_own, x_other, slots_a, got, cos, sin)
    far, near, f1, f2 = fence(far, near, f1, f2)
    f3 = second(f1)
    residual, normed = one_step(
        first_norm_kernel,
        "first_norm",
        ids,
        (x_own, near, core(far), gains),
        [out(tokens, width, dtype=F32), out(tokens, width)],
    )
    normed_other = core(normed)

    *low, carry = ffn_forward(normed, normed_other, [f0, f1, f2], None, False)
    carry, f3 = fence(carry, f3)
    slots_f = [f0, f1, f2, f3]
    *high, far, near = ffn_forward(normed, normed_other, [f3], carry, True)
    output, d_summed, d_ffn, grad_gain_two = one_step(
        last_norm_kernel,
        "last_norm",
        scalars,
        (residual, near, core(far), gains, cot),
        [out(tokens, width), out(tokens, width, dtype=F32), out(tokens, width), out(1, width, dtype=F32)],
        32,
    )
    d_ffn_other = core(d_ffn)
    moved_out = cross_tokens(output)

    d_gu, far, near = ffn_backward(d_ffn, d_ffn_other, low, high, slots_f)
    far, near, moved_out, d_gu = fence(far, near, moved_out, d_gu)
    got_far = core(far)
    gu3, y_t = pl.pallas_call(
        grads_g3_kernel,
        grid=(1,),
        in_specs=[SMEM]
        + [whole(tokens, width)] * 2
        + [pl.BlockSpec((1, 2 * tokens, 2 * half), lambda i: (3, 0, 0))],
        out_specs=[whole(width, 2 * half), whole(width, 2 * tokens)],
        out_shape=[out(width, 2 * half), hbm(width, 2 * tokens)],
        compiler_params=params(24),
        cost_estimate=cost(0.1),
        name="grads_g3",
    )(ids, *stay((normed, normed_other, d_gu)))
    got_far, gu3 = fence(got_far, gu3)
    gu_moved = second(gu3)
    d_residual, d_branch, grad_gain_one = one_step(
        back_norm_kernel,
        "back_norm",
        ids,
        (residual, near, got_far, d_summed, gains),
        [out(tokens, width, dtype=F32), out(tokens, width), out(1, width, dtype=F32)],
    )
    d_branch_other = core(d_branch)
    dn = one_step(
        grads_d_kernel,
        "grads_d",
        ids,
        stay((d_ffn, d_ffn_other, low[0], high[0])),
        [hbm(4, part if ring else width, half)] * (cols if ring else 1),
        32,
        [pltpu.VMEM((width, 2 * tokens), BF16), pltpu.VMEM((4, width, half), BF16)],
    )
    d_branch_other, dn = fence(d_branch_other, dn)
    gain_pair = jnp.concatenate([grad_gain_one, grad_gain_two], 0)
    gain_pair = gain_pair + core(gain_pair)
    dn_one = along(dn[3], 1) if ring else dn[0]
    back = (scalars, d_branch, d_branch_other, slots_a, got, cos, sin, q, k, v, attended_t, lse, x_t)
    dqk1, dv1, mine1, send1 = attend_backward(1, *back)
    dqk1, dv1, mine1, send1, gu_moved, dn_one, d_branch, gain_pair = fence(
        dqk1, dv1, mine1, send1, gu_moved, dn_one, d_branch, gain_pair
    )
    theirs1 = core(send1)
    gu1, gu2, gu0 = grads_g(y_t, d_gu, (1, 2, 0), gu_moved)
    theirs1, gu1, gu2 = fence(theirs1, gu1, gu2)
    s3, dn_two = one_step(
        first_slots_kernel,
        "first_slots",
        ids,
        (mine1, theirs1, dn[2] if ring else dn[0], dn_one),
        [out(width, 2 * head_cols), out(*dn[0].shape)],
    )
    s3, dn_two, gu1, gu2, d_branch = fence(s3, dn_two, gu1, gu2, d_branch)
    a_moved = second(s3)
    gu_one, gu_two = first(gu1), second(gu2)
    dn_last = [along(dn_two, 2), along(dn[1], 1)] if ring else []
    back = (scalars, d_branch) + back[2:]
    dqk0, dv0, mine0, send0 = attend_backward(0, *back)
    dqk0, dv0, mine0, send0, a_moved, gu_one, gu_two, dn_last = fence(
        dqk0, dv0, mine0, send0, a_moved, gu_one, gu_two, dn_last
    )
    theirs0 = core(send0)
    if ring:
        own_dn = add(dn[0], *dn_last)
    else:
        own_dn = lax.psum_scatter(dn[0], "col", scatter_dimension=1, tiled=True)
    dn_moved = second(own_dn[3])

    def merge(base0, base1, one, two):
        if not ring:
            return [add(jnp.where(core0, base0, base1), one, two)]
        return one_step(merge_kernel, "merge", ids, (base0, base1, one, two), [out(part, base0.shape[1])] * cols)

    def to_owner(blocks):
        if not ring:
            return [lax.psum_scatter(blocks[0], "col", scatter_dimension=0, tiled=True)]
        return [blocks[0]] + [along(blocks[hop], hop) for hop in range(1, cols)]

    g_parts = merge(gu0, gu0, gu_one, gu_two)
    theirs0, g_parts = fence(theirs0, g_parts)
    s1, s2 = one_step(
        slots_kernel, "slots", ids, (mine0, mine1, theirs0, theirs1, a_moved), [out(width, 2 * head_cols)] * 2
    )
    s1, s2, g_parts, dqk0, output, dn_moved = fence(s1, s2, g_parts, dqk0, output, dn_moved)
    a_one, a_two = first(s1), second(s2)
    g_parts = to_owner(g_parts)
    far, near = input_grad_parts(scalars, (dqk0, dqk1), (dv0, dv1), slots_a, got, tokens)
    output = jnp.where(stays, output.astype(F32), moved_out.astype(F32))
    a_one, a_two, g_parts, far, near, output, mom_gains = fence(
        a_one, a_two, g_parts, far, near, output, mom_gains
    )
    old = (mom_qkv, mom_out, mom_gate_up, mom_down.T) + (w_qkv, w_out, w_gate_up, w_down.T)
    old = old + (ema_qkv, ema_out, ema_gate_up, ema_down.T)
    old, a_one = fence(old, a_one)
    a_parts = to_owner(merge(mine0, theirs0, a_one, a_two))
    dn_one, dn_two = first(add(own_dn[1], dn_moved)), second(own_dn[2])
    shard_g = add(*g_parts)
    held = pl.pallas_call(
        fetch_kernel,
        in_specs=[ANY] * 12,
        out_specs=[VMEM] * 12,
        out_shape=[pltpu.VMEM(t.shape, F32) for t in old],
        scratch_shapes=[DMA((12,))],
        compiler_params=params(16),
        cost_estimate=cost(0.1),
        name="fetch",
    )(*stay(old))
    a_parts, dn_one, dn_two, shard_g, held, far = fence(a_parts, dn_one, dn_two, shard_g, held, far)
    shard_a = add(*a_parts)
    shard_d = add(own_dn[0], dn_one, dn_two)

    far_a, far_d, far_g = core(shard_a), core(shard_d), core(shard_g)
    got_far = core(far)
    far_a, far_d, far_g, got_far = fence(far_a, far_d, far_g, got_far)
    input_grad = d_residual + (near + got_far.astype(F32))
    moved_grad = cross_tokens(input_grad.astype(BF16))
    pack = one_step(
        pack_kernel,
        "pack",
        ids,
        (shard_a, far_a, shard_g, far_g, shard_d, far_d, gain_pair),
        [out(8, width, dtype=F32)],
    )[0]
    for axis, bits in (("col", (2, 1) if ring else ()), ("row", (2, 1))):
        size = mesh_sizes[axis]
        for bit in bits:
            pack = pack + lax.ppermute(pack, axis, [(i, i ^ bit) for i in range(size)])
    if not ring:
        pack = lax.psum(pack, "col")
    input_grad = jnp.where(stays, input_grad, moved_grad.astype(F32))
    pack, input_grad = fence(pack, input_grad)

    results = pl.pallas_call(
        update_kernel,
        in_specs=[SMEM] + [VMEM] * 22,
        out_specs=[ANY] * 12 + [VMEM] * 4,
        out_shape=[out(*t.shape, dtype=F32) for t in old]
        + [out(*gains.shape, dtype=F32)] * 3
        + [out(1, 1, dtype=F32)],
        scratch_shapes=[pltpu.VMEM(t.shape, F32) for t in old] + [DMA((12,))],
        compiler_params=params(24),
        cost_estimate=cost(0.1),
        name="update",
    )(ids, pack, shard_a, far_a, shard_g, far_g, shard_d, far_d, mom_gains, gains, ema_gains, *held)
    new = results[:12]
    gain_new = results[12:15]
    grad_norm = results[15][0, 0]
    return (
        output,
        input_grad,
        grad_norm,
        *new[0:3],
        new[3].T,
        gain_new[0],
        *new[4:7],
        new[7].T,
        gain_new[1],
        *new[8:11],
        new[11].T,
        gain_new[2],
    )


def solution(mesh):
    tok = P(("dp", "col", "row"), None)
    weights = (P(None, "col", "row"), P("row", "col"), P(None, "col", "row"), P("row", "col"), P())
    in_specs = (tok, tok, P(("dp", "col"), None)) + weights * 3
    out_specs = (tok, tok, P()) + weights * 3
    fn = functools.partial(body, mesh.shape["row"], mesh.shape["col"])
    return jax.shard_map(fn, mesh=mesh, in_specs=in_specs, out_specs=out_specs, check_vma=False)
```

```python
import functools

import jax
import jax.numpy as jnp
import numpy as np
from jax import lax
from jax.experimental import pallas as pl
from jax.experimental.pallas import tpu as pltpu
from jax.sharding import PartitionSpec as P

HD = 64
LEN = 1024

EPSILON = 1e-06
THETA = 10000.0
MOMENTUM = 0.9
RATE = 300.0
DECAY = 0.6
CLIP = 1.0
NEGATIVE = -1e30

F32 = jnp.float32
BF16 = jnp.bfloat16
NT = (((1,), (1,)), ((), ()))
NN = (((1,), (0,)), ((), ()))
TN = (((0,), (0,)), ((), ()))
BQ = 256


def rope_tables():
    half = HD // 2
    freqs = np.float32(THETA) ** (-(np.arange(half, dtype=np.float32) * np.float32(2.0)) / np.float32(HD))
    angles = np.arange(LEN, dtype=np.float32)[:, None] * freqs[None, :].astype(np.float32)
    return np.cos(angles), np.sin(angles)


def pair_tables():
    cosine, sine = rope_tables()
    return (
        jnp.asarray(np.concatenate([cosine] * 4, 1)),
        jnp.asarray(np.concatenate([-sine, sine] * 2, 1)),
    )


def mxu(lhs, rhs, dims=NN):
    return lax.dot_general(lhs, rhs, dims, preferred_element_type=F32)


def fence(*values):
    return lax.optimization_barrier(values)


def params(mib):
    return pltpu.CompilerParams(vmem_limit_bytes=mib << 20)


def cost(microseconds):
    return pl.CostEstimate(flops=int(1e9 * microseconds), bytes_accessed=1 << 10, transcendentals=0)


def out(*shape, dtype=BF16):
    return jax.ShapeDtypeStruct(shape, dtype)


def hbm(*shape, dtype=BF16):
    return pltpu.HBM(shape, dtype)


def stay(t):
    return jax.tree.map(lambda v: pltpu.with_memory_space_constraint(v, pltpu.HBM), t)


VMEM = pl.BlockSpec(memory_space=pltpu.VMEM)
SMEM = pl.BlockSpec(memory_space=pltpu.SMEM)
ANY = pl.BlockSpec(memory_space=pl.ANY)
DMA = pltpu.SemaphoreType.DMA


def piece_a_kernel(s_ref, qkv_ref, out_ref, a_ref):
    n = qkv_ref.shape[2]

    @pl.when(s_ref[0] == 0)
    def _():
        a_ref[:, :n] = qkv_ref[0].astype(BF16)
        a_ref[:, n:] = qkv_ref[1].astype(BF16)

    @pl.when(s_ref[0] == 1)
    def _():
        a_ref[:, :n] = qkv_ref[2].astype(BF16)
        a_ref[:, n:] = out_ref[...].T.astype(BF16)


def piece_f_kernel(s_ref, gu_ref, down_ref, f_ref):
    half = f_ref.shape[1] // 3
    at = pl.ds(pl.multiple_of(s_ref[0] * half, half), half)
    f_ref[:, :half] = gu_ref[0, :, at].astype(BF16)
    f_ref[:, half : 2 * half] = gu_ref[1, :, at].astype(BF16)
    f_ref[:, 2 * half :] = down_ref[:, at].astype(BF16)


def whole(*shape):
    return pl.BlockSpec(shape, lambda i: (0,) * len(shape))


def one_step(kernel, name, scalars, inputs, outputs, mib=24, scratch=(), us=0.1):
    return pl.pallas_call(
        kernel,
        grid=(1,),
        in_specs=[SMEM] + [whole(*t.shape) for t in inputs],
        out_specs=[whole(*t.shape) for t in outputs],
        out_shape=outputs,
        scratch_shapes=list(scratch),
        compiler_params=params(mib),
        cost_estimate=cost(us),
        name=name,
    )(scalars, *inputs)


def join_kernel(s_ref, *refs):
    blocks, whole_ref, sems = refs[:-2], refs[-2], refs[-1]
    cols, part = len(blocks), blocks[0].shape[0]
    copies = []
    for hop, block in enumerate(blocks):
        at = pl.multiple_of((s_ref[1] ^ hop) * part, part)
        copies.append(pltpu.make_async_copy(block, whole_ref.at[pl.ds(at, part)], sems.at[hop]))
    for copy in copies:
        copy.start()
    for copy in copies:
        copy.wait()


def pick_kernel(s_ref, a0_ref, a2_ref, a3_ref, send_ref, sems):
    def move(lo, hi):
        copies = [
            pltpu.make_async_copy(lo, send_ref.at[0], sems.at[0]),
            pltpu.make_async_copy(hi, send_ref.at[1], sems.at[1]),
        ]
        for copy in copies:
            copy.start()
        for copy in copies:
            copy.wait()

    @pl.when(s_ref[0] == 0)
    def _():
        move(a2_ref, a3_ref)

    @pl.when(s_ref[0] == 1)
    def _():
        move(a0_ref, a2_ref)


def causal(scores_t, block):
    keys = scores_t.shape[0]
    row = lax.broadcasted_iota(jnp.int32, (block, block), 0)
    column = lax.broadcasted_iota(jnp.int32, (block, block), 1)
    tail = jnp.where(row <= column, scores_t[keys - block :], NEGATIVE)
    return tail if keys == block else jnp.concatenate([scores_t[: keys - block], tail], 0)


def swap_halves(t):
    lane = lax.broadcasted_iota(jnp.int32, (1, t.shape[1]), 1)
    return jnp.where(lane % HD < HD // 2, pltpu.roll(t, t.shape[1] - HD // 2, 1), pltpu.roll(t, HD // 2, 1))


def pick_weights(core, j, a0_ref, a1_ref, a3_ref, got_ref, qk_ref, vo_ref):
    @pl.when(core == 0)
    def _():
        vo_ref[...] = got_ref[0]

        @pl.when(j == 0)
        def _():
            qk_ref[...] = a0_ref[...]

        @pl.when(j == 1)
        def _():
            qk_ref[...] = a1_ref[...]

    @pl.when(core == 1)
    def _():
        qk_ref[...] = got_ref[0]

        @pl.when(j == 0)
        def _():
            vo_ref[...] = a1_ref[...]

        @pl.when(j == 1)
        def _():
            vo_ref[...] = a3_ref[...]


def attend_forward_kernel(
    s_ref, x0_ref, x1_ref, a0_ref, a1_ref, a3_ref, got_ref, cos_ref, sin_ref,
    q_ref, k_ref, v_ref, ot_ref, lse_ref, xt_ref, far_ref, near_ref,
    qk_w, vo_w, o_ref, total_ref,
):
    core, live = s_ref[0], s_ref[1]
    j = pl.program_id(0)
    length = q_ref.shape[1]
    tokens = x0_ref.shape[0]
    n = 3 * HD
    pick_weights(core, j, a0_ref, a1_ref, a3_ref, got_ref, qk_w, vo_w)
    lane = lax.broadcasted_iota(jnp.int32, (tokens, HD), 1)
    one = jnp.where(lane == 0, 1.0, 0.0).astype(BF16)
    for x_ref, which in ((x0_ref, core), (x1_ref, 1 - core)):
        start = pl.multiple_of(which * tokens, tokens)
        at = pl.ds(start, tokens)
        qk = mxu(x_ref[...], qk_w[...])
        cos = jnp.concatenate([cos_ref[at, :]] * 3, 1)
        sin = jnp.concatenate([sin_ref[at, :]] * 3, 1)
        qk = qk * cos + swap_halves(qk) * sin
        q = (qk[:, :n] * (HD ** -0.5)).astype(BF16)
        k = qk[:, n:].astype(BF16)
        v = mxu(x_ref[...], vo_w[:, :n]).astype(BF16)
        key = start + lax.broadcasted_iota(jnp.int32, (tokens, HD), 0)
        bias = jnp.where((lane == 0) & (key >= live), NEGATIVE, 0.0).astype(BF16)
        for head in range(3):
            lanes = slice(head * HD, (head + 1) * HD)
            q_ref[head, at, :] = jnp.concatenate([q[:, lanes], one], 1)
            k_ref[head, at, :] = jnp.concatenate([k[:, lanes], bias], 1)
            v_ref[head, at, :] = jnp.concatenate([v[:, lanes], one], 1)

        @pl.when(j == 0)
        def _():
            xt_ref[:, at] = x_ref[...].T

    for block in range(length // BQ):
        keys = (block + 1) * BQ
        span = slice(block * BQ, keys)
        parts = []
        for head in range(3):
            scores = causal(mxu(k_ref[head, :keys, :], q_ref[head, span, :], NT), BQ)
            top = jnp.max(scores, 0, keepdims=True)
            probs = jnp.exp(scores - top).astype(BF16)
            o = mxu(probs, v_ref[head, :keys, :], TN).T
            total = o[HD : HD + 1]
            parts.append(o[:HD] / total)
            lse_ref[0, head : head + 1, span] = top + jnp.log(total)
        o = jnp.concatenate(parts, 0)
        ot_ref[0, :, span] = o.astype(BF16)
        o_ref[span, :] = o.T.astype(BF16)
    part = mxu(o_ref[...], vo_w[:, n:], NT)

    @pl.when(j == 0)
    def _():
        total_ref[...] = part

    @pl.when(j == 1)
    def _():
        total_ref[...] += part
        near_ref[...] = total_ref[pl.ds(pl.multiple_of(core * tokens, tokens), tokens), :]
        far_ref[...] = total_ref[pl.ds(pl.multiple_of((1 - core) * tokens, tokens), tokens), :].astype(BF16)


def attend_forward(scalars, x_own, x_other, slots, got, cos, sin):
    tokens, width = x_own.shape
    wide = slots[0].shape[1]
    n = wide // 2
    by_j = lambda *shape: pl.BlockSpec(shape, lambda j: (j,) + (0,) * (len(shape) - 1))
    return pl.pallas_call(
        attend_forward_kernel,
        grid=(2,),
        in_specs=[SMEM]
        + [whole(tokens, width)] * 2
        + [whole(width, wide)] * 3
        + [by_j(1, width, wide), whole(LEN, 128), whole(LEN, 128)],
        out_specs=[by_j(3, LEN, 128)] * 3
        + [by_j(1, n, LEN), by_j(1, 8, LEN), whole(width, LEN)]
        + [whole(tokens, width)] * 2,
        out_shape=[hbm(6, LEN, 128)] * 3
        + [hbm(2, n, LEN), hbm(2, 8, LEN, dtype=F32), hbm(width, LEN)]
        + [out(tokens, width), out(tokens, width, dtype=F32)],
        scratch_shapes=[
            pltpu.VMEM((width, wide), BF16),
            pltpu.VMEM((width, wide), BF16),
            pltpu.VMEM((LEN, n), BF16),
            pltpu.VMEM((LEN, width), F32),
        ],
        compiler_params=params(44),
        cost_estimate=cost(2),
        name="attend_forward",
    )(scalars, x_own, x_other, *stay((slots[0], slots[1], slots[3])), got, *stay((cos, sin)))


def attend_backward_kernel(
    s_ref, d0_ref, d1_ref, lo_ref, hi_ref, got_ref, cos_ref, sin_ref, ot_ref, lse_ref,
    q_any, k_any, v_any, xt_any,
    dqk_ref, dv_ref, mine_ref, send_ref,
    q_ref, k_ref, v_ref, xt_ref, vo_w, do_ref, dk_acc, dv_acc, sems, *, j,
):
    core = s_ref[0]
    tokens = d0_ref.shape[0]
    n = 3 * HD
    heads = pl.ds(3 * j, 3)
    copies = [
        pltpu.make_async_copy(k_any.at[heads], k_ref, sems.at[0]),
        pltpu.make_async_copy(q_any.at[heads], q_ref, sems.at[1]),
        pltpu.make_async_copy(v_any.at[heads], v_ref, sems.at[2]),
        pltpu.make_async_copy(xt_any, xt_ref, sems.at[3]),
    ]
    for copy in copies:
        copy.start()

    @pl.when(core == 0)
    def _():
        vo_w[...] = got_ref[0, :, n:]

    @pl.when(core == 1)
    def _():
        vo_w[...] = hi_ref[:, n:]

    for d_ref, which in ((d0_ref, core), (d1_ref, 1 - core)):
        at = pl.ds(pl.multiple_of(which * tokens, tokens), tokens)
        do_ref[at, :] = mxu(d_ref[...], vo_w[...]).astype(BF16)

    length = do_ref.shape[0]
    products = do_ref[...].astype(F32).T * ot_ref[0].astype(F32)
    for copy in copies[:3]:
        copy.wait()

    def unrotate(t):
        return t * cos_ref[...] - swap_halves(t) * sin_ref[...]

    for head in range(3):
        lanes = slice(head * HD, (head + 1) * HD)
        delta = jnp.sum(products[lanes], 0, keepdims=True)
        dq_parts = []
        for block in range(length // BQ):
            keys = (block + 1) * BQ
            span = slice(block * BQ, keys)
            before = keys - BQ
            q = q_ref[head, span, :]
            scores = causal(mxu(k_ref[head, :keys, :], q, NT), BQ)
            probs = jnp.exp(scores - lse_ref[0, head : head + 1, span])
            d_out = do_ref[span, lanes]
            d_probs = mxu(v_ref[head, :keys, :HD], d_out, NT)
            d_scores = (probs * (d_probs - delta[:, span])).astype(BF16)
            dv_part = mxu(probs.astype(BF16), d_out)
            dk_part = mxu(d_scores, q)
            if block:
                dv_acc[:before, :] += dv_part[:before]
                dk_acc[:before, :] += dk_part[:before]
            dv_acc[before:keys, :] = dv_part[before:]
            dk_acc[before:keys, :] = dk_part[before:]
            dq_parts.append(mxu(d_scores, k_ref[head, :keys, :], TN))
        dq = jnp.concatenate(dq_parts, 0) * (HD ** -0.5)
        dqk_ref[:, head * HD : (head + 1) * HD] = unrotate(dq)[:, :HD].astype(BF16)
        dqk_ref[:, n + head * HD : n + (head + 1) * HD] = unrotate(dk_acc[...])[:, :HD].astype(BF16)
        dv_ref[:, lanes] = dv_acc[...].astype(BF16)

    copies[3].wait()
    own = jnp.where(core == 0, 0, tokens)
    grad_o = jnp.zeros((n, d0_ref.shape[1]), F32)
    for d_ref, which in ((d0_ref, core), (d1_ref, 1 - core)):
        at = pl.ds(pl.multiple_of(which * tokens, tokens), tokens)
        grad_o += mxu(ot_ref[0, :, at], d_ref[...])
    grad_o = grad_o.T.astype(BF16)
    grad_qk = mxu(xt_ref[...], dqk_ref[...]).astype(BF16)
    grad_v = mxu(xt_ref[...], dv_ref[...]).astype(BF16)

    @pl.when(core == 0)
    def _():
        mine_ref[...] = grad_qk
        send_ref[:, :n] = grad_v
        send_ref[:, n:] = grad_o

    @pl.when(core == 1)
    def _():
        send_ref[...] = grad_qk
        mine_ref[:, :n] = grad_v
        mine_ref[:, n:] = grad_o


def attend_backward(j, scalars, d_own, d_other, slots, got, cos, sin, q, k, v, out_t, lse, x_t):
    tokens, width = d_own.shape
    wide = slots[0].shape[1]
    n = wide // 2
    at_j = lambda *shape: pl.BlockSpec(shape, lambda i: (j,) + (0,) * (len(shape) - 1))
    lo, hi = (slots[0], slots[1]) if j == 0 else (slots[1], slots[3])
    return pl.pallas_call(
        functools.partial(attend_backward_kernel, j=j),
        grid=(1,),
        in_specs=[SMEM]
        + [whole(tokens, width)] * 2
        + [whole(width, wide)] * 2
        + [at_j(1, width, wide), whole(LEN, 128), whole(LEN, 128), at_j(1, n, LEN), at_j(1, 8, LEN)]
        + [ANY] * 4,
        out_specs=[whole(LEN, wide), whole(LEN, n), whole(width, wide), whole(width, wide)],
        out_shape=[hbm(LEN, wide), hbm(LEN, n), hbm(width, wide), hbm(width, wide)],
        scratch_shapes=[
            pltpu.VMEM((3, LEN, 128), BF16),
            pltpu.VMEM((3, LEN, 128), BF16),
            pltpu.VMEM((3, LEN, 128), BF16),
            pltpu.VMEM((width, LEN), BF16),
            pltpu.VMEM((width, n), BF16),
            pltpu.VMEM((LEN, n), BF16),
            pltpu.VMEM((LEN, 128), F32),
            pltpu.VMEM((LEN, HD), F32),
            DMA((4,)),
        ],
        compiler_params=params(44),
        cost_estimate=cost(2),
        name="attend_backward",
    )(scalars, d_own, d_other, *stay((lo, hi, got, cos, sin, out_t, lse, q, k, v, x_t)))


def input_grad_kernel(s_ref, p0_ref, p1_ref, v0_ref, v1_ref, a0_ref, a1_ref, a3_ref, got_ref, far_ref, near_ref, qk_w, vo_w):
    core = s_ref[0]
    n = v0_ref.shape[1]
    tokens = far_ref.shape[0]
    for j, (lo, hi) in enumerate(((a0_ref, a1_ref), (a1_ref, a3_ref))):

        @pl.when(core == 0)
        def _():
            qk_w[j] = lo[...]
            vo_w[j] = got_ref[j, :, :n]

        @pl.when(core == 1)
        def _():
            qk_w[j] = got_ref[j]
            vo_w[j] = hi[:, :n]

    for which, dst in ((1 - core, far_ref), (core, near_ref)):
        at = pl.ds(pl.multiple_of(which * tokens, tokens), tokens)
        total = mxu(p0_ref[at, :], qk_w[0], NT) + mxu(v0_ref[at, :], vo_w[0], NT)
        total = total + (mxu(p1_ref[at, :], qk_w[1], NT) + mxu(v1_ref[at, :], vo_w[1], NT))
        dst[...] = total.astype(dst.dtype)


def input_grad_parts(scalars, d_qk, d_v, slots, got, tokens):
    width, wide = slots[0].shape
    return one_step(
        input_grad_kernel,
        "input_grad",
        scalars,
        stay((*d_qk, *d_v, slots[0], slots[1], slots[3], got)),
        [out(tokens, width), out(tokens, width, dtype=F32)],
        40,
        [pltpu.VMEM((2, width, wide), BF16), pltpu.VMEM((2, width, wide // 2), BF16)],
    )


def first_norm_kernel(s_ref, x_ref, near_ref, far_ref, gain_ref, resid_ref, normed_ref):
    residual = x_ref[...].astype(F32) + (near_ref[...] + far_ref[...].astype(F32))
    scale = lax.rsqrt(jnp.mean(residual * residual, -1, keepdims=True) + EPSILON)
    resid_ref[...] = residual
    normed_ref[...] = (residual * scale * gain_ref[0:1, :]).astype(BF16)


def last_norm_kernel(s_ref, resid_ref, near_ref, far_ref, gain_ref, own_cot_ref, moved_cot_ref, out_ref, dsum_ref, dffn_ref, dgain_ref):
    core, live = s_ref[0], s_ref[1]
    tokens, width = resid_ref.shape
    residual = resid_ref[...]
    scale = lax.rsqrt(jnp.mean(residual * residual, -1, keepdims=True) + EPSILON)
    summed = residual * scale * gain_ref[0:1, :] + (near_ref[...] + far_ref[...].astype(F32))
    scale = lax.rsqrt(jnp.mean(summed * summed, -1, keepdims=True) + EPSILON)
    unit = summed * scale
    out_ref[...] = (unit * gain_ref[1:2, :]).astype(BF16)
    position = core * tokens + lax.broadcasted_iota(jnp.int32, (tokens, 1), 0)
    cot = jnp.where(s_ref[2] == 1, own_cot_ref[...].astype(F32), moved_cot_ref[...].astype(F32))
    cot = jnp.where(position < live, cot, 0.0)
    dgain_ref[...] = jnp.sum(cot * unit, 0, keepdims=True)
    hat = cot * gain_ref[1:2, :]
    inner = jnp.mean(hat * unit, -1, keepdims=True)
    d_summed = scale * (hat - unit * inner)
    dsum_ref[...] = d_summed
    dffn_ref[...] = d_summed.astype(BF16)


def back_norm_kernel(s_ref, resid_ref, near_ref, far_ref, dsum_ref, gain_ref, dres_ref, dbranch_ref, dgain_ref):
    residual = resid_ref[...]
    scale = lax.rsqrt(jnp.mean(residual * residual, -1, keepdims=True) + EPSILON)
    unit = residual * scale
    d_normed = dsum_ref[...] + (near_ref[...] + far_ref[...].astype(F32))
    dgain_ref[...] = jnp.sum(d_normed * unit, 0, keepdims=True)
    hat = d_normed * gain_ref[0:1, :]
    inner = jnp.mean(hat * unit, -1, keepdims=True)
    d_residual = scale * (hat - unit * inner)
    dres_ref[...] = d_residual
    dbranch_ref[...] = d_residual.astype(BF16)


def fetch_slots(step, sources, dst, sems):
    copies = [pltpu.make_async_copy(src, dst.at[i], sems.at[i]) for i, src in enumerate(sources)]

    @pl.when(step == 0)
    def _():
        for copy in copies:
            copy.start()

    for i, copy in enumerate(copies):

        @pl.when(step == i)
        def _():
            copy.wait()


def ffn_forward_kernel(y0_ref, y1_ref, *refs, slots, start, finish):
    refs = list(refs)
    carry_ref = None if start else refs.pop(0)
    sources, refs = refs[:slots], refs[slots:]
    hid_ref, silu_ref, slope_ref = refs[:3]
    results = refs[3:5]
    w_ref, total_ref, sems = refs[-3:]
    step = pl.program_id(0)
    tokens = y0_ref.shape[0]
    half = hid_ref.shape[2]
    fetch_slots(step, sources, w_ref, sems)

    @pl.when(step == 0)
    def _():
        total_ref[...] = jnp.zeros_like(total_ref) if start else carry_ref[...]
        if start:
            results[1][:, :tokens] = y0_ref[...].T
            results[1][:, tokens:] = y1_ref[...].T

    for part, y_ref in ((0, y0_ref), (1, y1_ref)):
        at = slice(part * tokens, (part + 1) * tokens)
        both = mxu(y_ref[...], w_ref[step, :, : 2 * half])
        gate, up = both[:, :half], both[:, half:]
        sig = jax.nn.sigmoid(gate)
        silu = gate * sig
        hidden = (silu * up).astype(BF16)
        hid_ref[0, at, :] = hidden
        silu_ref[0, at, :] = silu.astype(BF16)
        slope_ref[0, at, :] = (up * (sig + silu * (1.0 - sig))).astype(BF16)
        total_ref[at, :] += mxu(hidden, w_ref[step, :, 2 * half :], NT)

    @pl.when(step == slots - 1)
    def _():
        if finish:
            far_ref, near_ref = results
            near_ref[...] = total_ref[:tokens, :]
            far_ref[...] = total_ref[tokens:, :].astype(BF16)
        else:
            results[0][...] = total_ref[...]


def ffn_forward(normed, normed_other, slots, carry, finish):
    tokens, width = normed.shape
    lanes = slots[0].shape[1]
    count = len(slots)
    half = lanes // 3
    per_slot = pl.BlockSpec((1, 2 * tokens, half), lambda s: (s, 0, 0))
    if finish:
        results = [out(tokens, width), out(tokens, width, dtype=F32)]
    else:
        results = [out(2 * tokens, width, dtype=F32), hbm(width, 2 * tokens)]
    inputs = (normed, normed_other) + (() if carry is None else (carry,))
    return pl.pallas_call(
        functools.partial(ffn_forward_kernel, slots=count, start=carry is None, finish=finish),
        grid=(count,),
        in_specs=[whole(*t.shape) for t in inputs] + [ANY] * count,
        out_specs=[per_slot] * 3 + [whole(*t.shape) for t in results],
        out_shape=[hbm(count, 2 * tokens, half)] * 3 + results,
        scratch_shapes=[
            pltpu.VMEM((count, width, lanes), BF16),
            pltpu.VMEM((2 * tokens, width), F32),
            DMA((count,)),
        ],
        compiler_params=params(36),
        cost_estimate=cost(2),
        name="ffn_forward",
    )(*inputs, *slots)


def ffn_backward_kernel(d0_ref, d1_ref, silu_a, slope_a, silu_b, slope_b, *refs):
    sources, (dgu_ref, far_ref, near_ref, w_ref, total_ref, sems) = refs[:4], refs[4:]
    step = pl.program_id(0)
    tokens = d0_ref.shape[0]
    half = silu_a.shape[2]
    fetch_slots(step, sources, w_ref, sems)

    @pl.when(step == 0)
    def _():
        total_ref[...] = jnp.zeros_like(total_ref)

    def slot(silu_ref, slope_ref):
        for part, d_ref in ((0, d0_ref), (1, d1_ref)):
            at = slice(part * tokens, (part + 1) * tokens)
            d_hidden = mxu(d_ref[...], w_ref[step, :, 2 * half :])
            d_gate = (d_hidden * slope_ref[0, at, :].astype(F32)).astype(BF16)
            d_up = (d_hidden * silu_ref[0, at, :].astype(F32)).astype(BF16)
            dgu_ref[0, at, :half] = d_gate
            dgu_ref[0, at, half:] = d_up
            term = mxu(d_gate, w_ref[step, :, :half], NT) + mxu(d_up, w_ref[step, :, half : 2 * half], NT)
            total_ref[at, :] += term

    @pl.when(step < 3)
    def _():
        slot(silu_a, slope_a)

    @pl.when(step == 3)
    def _():
        slot(silu_b, slope_b)
        near_ref[...] = total_ref[:tokens, :]
        far_ref[...] = total_ref[tokens:, :].astype(BF16)


def ffn_backward(d_ffn, d_other, low, high, slots):
    tokens, width = d_ffn.shape
    lanes = slots[0].shape[1]
    half = lanes // 3
    first_three = pl.BlockSpec((1, 2 * tokens, half), lambda s: (jnp.minimum(s, 2), 0, 0))
    return pl.pallas_call(
        ffn_backward_kernel,
        grid=(4,),
        in_specs=[whole(tokens, width)] * 2
        + [first_three] * 2
        + [whole(1, 2 * tokens, half)] * 2
        + [ANY] * 4,
        out_specs=[pl.BlockSpec((1, 2 * tokens, 2 * half), lambda s: (s, 0, 0))] + [whole(tokens, width)] * 2,
        out_shape=[hbm(4, 2 * tokens, 2 * half), out(tokens, width), out(tokens, width, dtype=F32)],
        scratch_shapes=[
            pltpu.VMEM((4, width, lanes), BF16),
            pltpu.VMEM((2 * tokens, width), F32),
            DMA((4,)),
        ],
        compiler_params=params(40),
        cost_estimate=cost(2),
        name="ffn_backward",
    )(d_ffn, d_other, *stay((*low[1:], *high[1:], *slots)))


def grads_g_kernel(*refs, count, moved):
    yt_ref, refs = refs[0], refs[1:]
    dgu, refs = refs[:count], refs[count:]
    moved_ref, results = (refs[0], refs[1:]) if moved else (None, refs)
    for i, (dgu_ref, result_ref) in enumerate(zip(dgu, results)):
        grad = mxu(yt_ref[...], dgu_ref[0])
        if moved and i == 0:
            grad = grad + moved_ref[...].astype(F32)
        result_ref[...] = grad.astype(BF16)


def grads_g(y_t, d_gu, slots, moved=None):
    width, length = y_t.shape
    wide = d_gu.shape[2]
    at_slot = [pl.BlockSpec((1, length, wide), functools.partial(lambda n, i: (n, 0, 0), n)) for n in slots]
    extra = [] if moved is None else [moved]
    return pl.pallas_call(
        functools.partial(grads_g_kernel, count=len(slots), moved=moved is not None),
        grid=(1,),
        in_specs=[whole(width, length)] + at_slot + [whole(*t.shape) for t in extra],
        out_specs=[whole(width, wide)] * len(slots),
        out_shape=[out(width, wide)] * len(slots),
        compiler_params=params(32),
        cost_estimate=cost(0.1),
        name="grads_g",
    )(stay(y_t), *[stay(d_gu)] * len(slots), *extra)


def grads_d_kernel(s_ref, d0_ref, d1_ref, hid_a, hid_b, *refs):
    blocks, dt_ref, grad_ref = refs[:-2], refs[-2], refs[-1]
    tokens = d0_ref.shape[0]
    dt_ref[:, :tokens] = d0_ref[...].T
    dt_ref[:, tokens:] = d1_ref[...].T
    for slot in range(4):
        hidden = hid_a[slot] if slot < 3 else hid_b[0]
        grad_ref[slot] = mxu(dt_ref[...], hidden).astype(BF16)
    for hop, block_ref in enumerate(blocks):
        rows = block_ref.shape[1]
        place = (s_ref[1] ^ hop) if len(blocks) > 1 else 0
        at = pl.ds(pl.multiple_of(place * rows, rows), rows)
        for slot in range(4):
            block_ref[slot] = grad_ref[slot, at, :]


def first_slots_kernel(s_ref, mine1_ref, theirs1_ref, dn_ref, dn_moved_ref, s3_ref, sum_ref):
    sum_ref[...] = (dn_ref[...].astype(F32) + dn_moved_ref[...].astype(F32)).astype(BF16)

    @pl.when(s_ref[0] == 0)
    def _():
        s3_ref[...] = theirs1_ref[...]

    @pl.when(s_ref[0] == 1)
    def _():
        s3_ref[...] = mine1_ref[...]


def slots_kernel(s_ref, mine0_ref, mine1_ref, theirs0_ref, theirs1_ref, moved_ref, s1_ref, s2_ref):
    moved = moved_ref[...].astype(F32)

    @pl.when(s_ref[0] == 0)
    def _():
        s1_ref[...] = (mine1_ref[...].astype(F32) + moved).astype(BF16)
        s2_ref[...] = theirs0_ref[...]

    @pl.when(s_ref[0] == 1)
    def _():
        s1_ref[...] = (mine0_ref[...].astype(F32) + moved).astype(BF16)
        s2_ref[...] = theirs1_ref[...]


def merge_kernel(s_ref, base0_ref, base1_ref, one_ref, two_ref, *blocks):
    cols = len(blocks)
    part = blocks[0].shape[0]
    for hop, block_ref in enumerate(blocks):
        at = pl.ds(pl.multiple_of((s_ref[1] ^ hop) * part, part), part)
        moved = one_ref[at, :].astype(F32) + two_ref[at, :].astype(F32)

        @pl.when(s_ref[0] == 0)
        def _():
            block_ref[...] = (base0_ref[at, :].astype(F32) + moved).astype(BF16)

        @pl.when(s_ref[0] == 1)
        def _():
            block_ref[...] = (base1_ref[at, :].astype(F32) + moved).astype(BF16)


def pack_kernel(s_ref, *refs):
    shards, gain_ref, pack_ref = refs[:-2], refs[-2], refs[-1]
    total = jnp.zeros((1, 1), F32)
    for ref in shards:
        value = ref[...].astype(F32)
        total = total + jnp.sum(jnp.sum(value * value, 0, keepdims=True), 1, keepdims=True)
    row = lax.broadcasted_iota(jnp.int32, pack_ref.shape, 0)
    gain = jnp.where(row == 0, gain_ref[0:1, :], gain_ref[1:2, :])
    pack_ref[...] = jnp.where(row < 2, gain, jnp.broadcast_to(total, pack_ref.shape))


def update(grad_full, moment, weight, average, factor):
    clipped = grad_full * factor
    new_moment = MOMENTUM * moment + clipped
    new_weight = weight - RATE * (clipped + MOMENTUM * new_moment)
    new_average = DECAY * average + (1.0 - DECAY) * new_weight
    return (new_moment, new_weight, new_average)


def fetch_kernel(*refs):
    count = (len(refs) - 1) // 2
    sems = refs[-1]
    copies = [pltpu.make_async_copy(refs[i], refs[count + i], sems.at[i]) for i in range(count)]
    for copy in copies:
        copy.start()
    for copy in copies:
        copy.wait()


def update_kernel(s_ref, pack_ref, a0_ref, a1_ref, g0_ref, g1_ref, d0_ref, d1_ref, gm_ref, gw_ref, ge_ref, *refs):
    old, refs = refs[:12], refs[12:]
    new, refs = refs[:12], refs[12:]
    gain_new, norm_ref, refs = refs[:3], refs[3], refs[4:]
    held, out_sems = refs[:12], refs[12]
    gains = pack_ref[0:2, :]
    squares = pack_ref[2:3, 0:1] + jnp.sum(jnp.sum(gains * gains, 0, keepdims=True), 1, keepdims=True)
    norm = jnp.sqrt(squares)
    norm_ref[...] = norm
    factor = jnp.minimum(1.0, CLIP / (norm + 1e-06))
    for ref, value in zip(gain_new, update(gains, gm_ref[...], gw_ref[...], ge_ref[...], factor)):
        ref[...] = value
    n = held[0].shape[2]
    half = d0_ref.shape[1]

    def put(kind, at, grad):
        moment, weight, average = (old[kind + 4 * i] for i in range(3))
        results = update(grad, moment[at], weight[at], average[at], factor)
        for i, value in enumerate(results):
            held[kind + 4 * i][at] = value

    every = slice(None)

    def parts(kind, mine, other):
        if kind == 0:
            qk, vo = mine[0], other[0]
            put(0, (0, every, every), qk[:, :n].astype(F32))
            put(0, (1, every, every), qk[:, n:].astype(F32))
            put(0, (2, every, every), vo[:, :n].astype(F32))
        elif kind == 1:
            put(1, (every, every), other[0][:, n:].astype(F32).T)
        else:
            for which, part in enumerate((mine, other)):
                lanes = slice(which * half, (which + 1) * half)
                if kind == 2:
                    put(2, (0, every, lanes), part[1][:, :half].astype(F32))
                    put(2, (1, every, lanes), part[1][:, half:].astype(F32))
                else:
                    put(3, (every, lanes), part[2][...].astype(F32))

    here, there = (a0_ref, g0_ref, d0_ref), (a1_ref, g1_ref, d1_ref)
    for kind in (2, 3, 0, 1):
        @pl.when(s_ref[0] == 0)
        def _():
            parts(kind, here, there)

        @pl.when(s_ref[0] == 1)
        def _():
            parts(kind, there, here)

        for i in (kind, kind + 4, kind + 8):
            pltpu.make_async_copy(held[i], new[i], out_sems.at[i]).start()
    for i in range(12):
        pltpu.make_async_copy(held[i], new[i], out_sems.at[i]).wait()


def body(
    rows,
    cols,
    block_input,
    out_grad,
    lengths,
    w_qkv,
    w_out,
    w_gate_up,
    w_down,
    gains,
    mom_qkv,
    mom_out,
    mom_gate_up,
    mom_down,
    mom_gains,
    ema_qkv,
    ema_out,
    ema_gate_up,
    ema_down,
    ema_gains,
):
    d = lax.axis_index("dp")
    r = lax.axis_index("row")
    c = lax.axis_index("col")
    core0 = d == 0
    stays = d == r % 2
    tokens, width = block_input.shape
    ring = cols == 4
    mesh_sizes = {"row": rows, "col": cols}
    part = width // cols
    head_cols = w_qkv.shape[2]
    half = w_gate_up.shape[2] // 2

    pairs = [(i, j) for i in range(2) for j in range(rows)]
    swap_pairs = [(i * rows + j, (j % 2) * rows + (j // 2) * 2 + i) for i, j in pairs]
    cross_pairs = [(i, j) for i, j in swap_pairs if i != j]
    first_pairs = [(i * rows + j, i * rows + (j ^ (1 if i == 0 else 2))) for i, j in pairs]
    second_pairs = [(i * rows + j, i * rows + (j ^ (2 if i == 0 else 1))) for i, j in pairs]

    def swap_tokens(t):
        return lax.ppermute(t, ("dp", "row"), swap_pairs)

    def cross_tokens(t):
        return lax.ppermute(t, ("dp", "row"), cross_pairs)

    def first(t):
        return lax.ppermute(t, ("dp", "row"), first_pairs)

    def second(t):
        return lax.ppermute(t, ("dp", "row"), second_pairs)

    def core(t):
        return lax.ppermute(t, "dp", [(0, 1), (1, 0)])

    def along(t, k):
        return lax.ppermute(t, "col", [(i, i ^ k) for i in range(cols)])

    def join_cols(*blocks):
        return pl.pallas_call(
            join_kernel,
            in_specs=[SMEM] + [ANY] * cols,
            out_specs=ANY,
            out_shape=out(width, blocks[0].shape[1]),
            scratch_shapes=[DMA((cols,))],
            compiler_params=params(16),
            cost_estimate=cost(0.1),
            name="join",
        )(ids, *blocks)

    def gather_cols(t):
        return lax.all_gather(t, "col", axis=t.ndim - 2, tiled=True)

    def add(*values):
        total = values[0].astype(F32)
        for value in values[1:]:
            total = total + value.astype(F32)
        return total.astype(BF16)

    ids = jnp.stack([d, c]).astype(jnp.int32)
    (piece_a,) = one_step(piece_a_kernel, "piece_a", ids, stay((w_qkv, w_out)), [out(part, 2 * head_cols)], 60)
    piece_a, block_input = fence(piece_a, block_input)
    a_cols = [along(piece_a, 1), along(piece_a, 2)] if ring else [gather_cols(piece_a)]
    moved_x = cross_tokens(block_input)
    (piece_f,) = one_step(piece_f_kernel, "piece_f", ids, stay((w_gate_up, w_down.T)), [out(part, 3 * half)], 60)
    a_cols, piece_f, moved_x, out_grad = fence(a_cols, piece_f, moved_x, out_grad)
    moved_cot = cross_tokens(out_grad)
    if ring:
        a_cols = a_cols + [along(a_cols[1], 1)]
        f_cols = [along(piece_f, 1), along(piece_f, 2)]
    else:
        f_cols = [gather_cols(piece_f)]
    a_cols, piece_a, lengths = fence(a_cols, piece_a, lengths)
    a0 = join_cols(piece_a, *a_cols) if ring else a_cols[0]
    a1, a2 = first(a0), second(a0)
    x_own = jnp.where(stays, block_input, moved_x)
    a0, a1, a2, f_cols, x_own, moved_cot = fence(a0, a1, a2, f_cols, x_own, moved_cot)
    a3 = second(a1)
    if ring:
        f_cols = f_cols + [along(f_cols[1], 1)]
    x_other = core(x_own)
    own_length = swap_tokens(lengths)[0, :]
    seq_ids = jnp.arange(own_length.shape[0], dtype=jnp.int32)
    own_length = jnp.sum(jnp.where(seq_ids == r // 2, own_length, 0))
    scalars = jnp.stack([d.astype(jnp.int32), own_length, stays.astype(jnp.int32)])
    a0, a1, a2, a3, f_cols, x_own, x_other, scalars = fence(a0, a1, a2, a3, f_cols, x_own, x_other, scalars)
    f0 = join_cols(piece_f, *f_cols) if ring else f_cols[0]
    f0, a0, a2, a3 = fence(f0, a0, a2, a3)
    slots_a = [a0, a1, a2, a3]
    send = pl.pallas_call(
        pick_kernel,
        in_specs=[SMEM] + [ANY] * 3,
        out_specs=ANY,
        out_shape=out(2, width, 2 * head_cols),
        scratch_shapes=[DMA((2,))],
        compiler_params=params(16),
        cost_estimate=cost(0.1),
        name="pick",
    )(ids, a0, a2, a3)
    got = core(send)
    f1, f2 = first(f0), second(f0)
    cos, sin = pair_tables()
    q, k, v, attended_t, lse, x_t, far, near = attend_forward(scalars, x_own, x_other, slots_a, got, cos, sin)
    far, near, f1, f2 = fence(far, near, f1, f2)
    f3 = second(f1)
    residual, normed = one_step(
        first_norm_kernel,
        "first_norm",
        ids,
        (x_own, near, core(far), gains),
        [out(tokens, width, dtype=F32), out(tokens, width)],
    )
    normed_other = core(normed)

    *low, carry, y_t = ffn_forward(normed, normed_other, [f0, f1, f2], None, False)
    carry, f3 = fence(carry, f3)
    slots_f = [f0, f1, f2, f3]
    *high, far, near = ffn_forward(normed, normed_other, [f3], carry, True)
    output, d_summed, d_ffn, grad_gain_two = one_step(
        last_norm_kernel,
        "last_norm",
        scalars,
        (residual, near, core(far), gains, out_grad, moved_cot),
        [out(tokens, width), out(tokens, width, dtype=F32), out(tokens, width), out(1, width, dtype=F32)],
        32,
    )
    d_ffn_other = core(d_ffn)
    moved_out = cross_tokens(output)

    d_gu, far, near = ffn_backward(d_ffn, d_ffn_other, low, high, slots_f)
    far, near, moved_out, d_gu = fence(far, near, moved_out, d_gu)
    got_far = core(far)
    (gu3,) = grads_g(y_t, d_gu, (3,))
    got_far, gu3 = fence(got_far, gu3)
    gu_moved = second(gu3)
    d_residual, d_branch, grad_gain_one = one_step(
        back_norm_kernel,
        "back_norm",
        ids,
        (residual, near, got_far, d_summed, gains),
        [out(tokens, width, dtype=F32), out(tokens, width), out(1, width, dtype=F32)],
    )
    d_branch_other = core(d_branch)
    dn = one_step(
        grads_d_kernel,
        "grads_d",
        ids,
        stay((d_ffn, d_ffn_other, low[0], high[0])),
        [hbm(4, part if ring else width, half)] * (cols if ring else 1),
        32,
        [pltpu.VMEM((width, 2 * tokens), BF16), pltpu.VMEM((4, width, half), BF16)],
    )
    d_branch_other, dn = fence(d_branch_other, dn)
    gain_pair = jnp.concatenate([grad_gain_one, grad_gain_two], 0)
    gain_pair = gain_pair + core(gain_pair)
    dn_one = along(dn[3], 1) if ring else dn[0]
    back = (scalars, d_branch, d_branch_other, slots_a, got, cos, sin, q, k, v, attended_t, lse, x_t)
    dqk1, dv1, mine1, send1 = attend_backward(1, *back)
    dqk1, dv1, mine1, send1, gu_moved, dn_one, d_branch, gain_pair = fence(
        dqk1, dv1, mine1, send1, gu_moved, dn_one, d_branch, gain_pair
    )
    theirs1 = core(send1)
    gu1, gu2, gu0 = grads_g(y_t, d_gu, (1, 2, 0), gu_moved)
    theirs1, gu1, gu2 = fence(theirs1, gu1, gu2)
    s3, dn_two = one_step(
        first_slots_kernel,
        "first_slots",
        ids,
        (mine1, theirs1, dn[2] if ring else dn[0], dn_one),
        [out(width, 2 * head_cols), out(*dn[0].shape)],
    )
    s3, dn_two, gu1, gu2, d_branch = fence(s3, dn_two, gu1, gu2, d_branch)
    a_moved = second(s3)
    gu_one, gu_two = first(gu1), second(gu2)
    dn_last = [along(dn_two, 2), along(dn[1], 1)] if ring else []
    back = (scalars, d_branch) + back[2:]
    dqk0, dv0, mine0, send0 = attend_backward(0, *back)
    dqk0, dv0, mine0, send0, a_moved, gu_one, gu_two, dn_last = fence(
        dqk0, dv0, mine0, send0, a_moved, gu_one, gu_two, dn_last
    )
    theirs0 = core(send0)
    if ring:
        own_dn = add(dn[0], *dn_last)
    else:
        own_dn = lax.psum_scatter(dn[0], "col", scatter_dimension=1, tiled=True)
    dn_moved = second(own_dn[3])

    def merge(base0, base1, one, two):
        if not ring:
            return [add(jnp.where(core0, base0, base1), one, two)]
        return one_step(merge_kernel, "merge", ids, (base0, base1, one, two), [out(part, base0.shape[1])] * cols)

    def to_owner(blocks):
        if not ring:
            return [lax.psum_scatter(blocks[0], "col", scatter_dimension=0, tiled=True)]
        return [blocks[0]] + [along(blocks[hop], hop) for hop in range(1, cols)]

    g_parts = merge(gu0, gu0, gu_one, gu_two)
    theirs0, g_parts = fence(theirs0, g_parts)
    s1, s2 = one_step(
        slots_kernel, "slots", ids, (mine0, mine1, theirs0, theirs1, a_moved), [out(width, 2 * head_cols)] * 2
    )
    s1, s2, g_parts, dqk0, output, dn_moved = fence(s1, s2, g_parts, dqk0, output, dn_moved)
    a_one, a_two = first(s1), second(s2)
    g_parts = to_owner(g_parts)
    far, near = input_grad_parts(scalars, (dqk0, dqk1), (dv0, dv1), slots_a, got, tokens)
    output = jnp.where(stays, output.astype(F32), moved_out.astype(F32))
    a_one, a_two, g_parts, far, near, output, mom_gains = fence(
        a_one, a_two, g_parts, far, near, output, mom_gains
    )
    old = (mom_qkv, mom_out, mom_gate_up, mom_down.T) + (w_qkv, w_out, w_gate_up, w_down.T)
    old = old + (ema_qkv, ema_out, ema_gate_up, ema_down.T)
    old, a_one = fence(old, a_one)
    a_parts = to_owner(merge(mine0, theirs0, a_one, a_two))
    dn_one, dn_two = first(add(own_dn[1], dn_moved)), second(own_dn[2])
    shard_g = add(*g_parts)
    held = pl.pallas_call(
        fetch_kernel,
        in_specs=[ANY] * 12,
        out_specs=[VMEM] * 12,
        out_shape=[pltpu.VMEM(t.shape, F32) for t in old],
        scratch_shapes=[DMA((12,))],
        compiler_params=params(16),
        cost_estimate=cost(0.1),
        name="fetch",
    )(*stay(old))
    a_parts, dn_one, dn_two, shard_g, held, far = fence(a_parts, dn_one, dn_two, shard_g, held, far)
    shard_a = add(*a_parts)
    shard_d = add(own_dn[0], dn_one, dn_two)

    far_a, far_d, far_g = core(shard_a), core(shard_d), core(shard_g)
    got_far = core(far)
    far_a, far_d, far_g, got_far = fence(far_a, far_d, far_g, got_far)
    input_grad = d_residual + (near + got_far.astype(F32))
    moved_grad = cross_tokens(input_grad.astype(BF16))
    pack = one_step(
        pack_kernel,
        "pack",
        ids,
        (shard_a, far_a, shard_g, far_g, shard_d, far_d, gain_pair),
        [out(8, width, dtype=F32)],
    )[0]
    for axis, bits in (("col", (2, 1) if ring else ()), ("row", (2, 1))):
        size = mesh_sizes[axis]
        for bit in bits:
            moved = lax.ppermute(pack, axis, [(i, i ^ bit) for i in range(size)])
            if (axis, bit) == ("row", 1):
                input_grad = jnp.where(stays, input_grad, moved_grad.astype(F32))
                moved, input_grad = fence(moved, input_grad)
            pack = pack + moved
    if not ring:
        pack = lax.psum(pack, "col")

    results = pl.pallas_call(
        update_kernel,
        in_specs=[SMEM] + [VMEM] * 22,
        out_specs=[ANY] * 12 + [VMEM] * 4,
        out_shape=[out(*t.shape, dtype=F32) for t in old]
        + [out(*gains.shape, dtype=F32)] * 3
        + [out(1, 1, dtype=F32)],
        scratch_shapes=[pltpu.VMEM(t.shape, F32) for t in old] + [DMA((12,))],
        compiler_params=params(24),
        cost_estimate=cost(0.1),
        name="update",
    )(ids, pack, shard_a, far_a, shard_g, far_g, shard_d, far_d, mom_gains, gains, ema_gains, *held)
    new = results[:12]
    gain_new = results[12:15]
    grad_norm = results[15][0, 0]
    return (
        output,
        input_grad,
        grad_norm,
        *new[0:3],
        new[3].T,
        gain_new[0],
        *new[4:7],
        new[7].T,
        gain_new[1],
        *new[8:11],
        new[11].T,
        gain_new[2],
    )


def solution(mesh):
    tok = P(("dp", "col", "row"), None)
    weights = (P(None, "col", "row"), P("row", "col"), P(None, "col", "row"), P("row", "col"), P())
    in_specs = (tok, tok, P(("dp", "col"), None)) + weights * 3
    out_specs = (tok, tok, P()) + weights * 3
    fn = functools.partial(body, mesh.shape["row"], mesh.shape["col"])
    return jax.shard_map(fn, mesh=mesh, in_specs=in_specs, out_specs=out_specs, check_vma=False)
```

```python
import functools

import jax
import jax.numpy as jnp
import numpy as np
from jax import lax
from jax.experimental import pallas as pl
from jax.experimental.pallas import tpu as pltpu
from jax.sharding import PartitionSpec as P

HD = 64
LEN = 1024

EPSILON = 1e-06
THETA = 10000.0
MOMENTUM = 0.9
RATE = 300.0
DECAY = 0.6
CLIP = 1.0
NEGATIVE = -1e30

F32 = jnp.float32
BF16 = jnp.bfloat16
NT = (((1,), (1,)), ((), ()))
NN = (((1,), (0,)), ((), ()))
TN = (((0,), (0,)), ((), ()))
BQ = 256


def rope_tables():
    half = HD // 2
    freqs = np.float32(THETA) ** (-(np.arange(half, dtype=np.float32) * np.float32(2.0)) / np.float32(HD))
    angles = np.arange(LEN, dtype=np.float32)[:, None] * freqs[None, :].astype(np.float32)
    return np.cos(angles), np.sin(angles)


def pair_tables():
    cosine, sine = rope_tables()
    return (
        jnp.asarray(np.concatenate([cosine] * 4, 1)),
        jnp.asarray(np.concatenate([-sine, sine] * 2, 1)),
    )


def mxu(lhs, rhs, dims=NN):
    return lax.dot_general(lhs, rhs, dims, preferred_element_type=F32)


def fence(*values):
    return lax.optimization_barrier(values)


def params(mib):
    return pltpu.CompilerParams(vmem_limit_bytes=mib << 20)


def cost(microseconds):
    return pl.CostEstimate(flops=int(1e9 * microseconds), bytes_accessed=1 << 10, transcendentals=0)


def out(*shape, dtype=BF16):
    return jax.ShapeDtypeStruct(shape, dtype)


def hbm(*shape, dtype=BF16):
    return pltpu.HBM(shape, dtype)


def stay(t):
    return jax.tree.map(lambda v: pltpu.with_memory_space_constraint(v, pltpu.HBM), t)


VMEM = pl.BlockSpec(memory_space=pltpu.VMEM)
SMEM = pl.BlockSpec(memory_space=pltpu.SMEM)
ANY = pl.BlockSpec(memory_space=pl.ANY)
DMA = pltpu.SemaphoreType.DMA


def piece_a_kernel(s_ref, qkv_ref, out_ref, a_ref):
    n = qkv_ref.shape[2]

    @pl.when(s_ref[0] == 0)
    def _():
        a_ref[:, :n] = qkv_ref[0].astype(BF16)
        a_ref[:, n:] = qkv_ref[1].astype(BF16)

    @pl.when(s_ref[0] == 1)
    def _():
        a_ref[:, :n] = qkv_ref[2].astype(BF16)
        a_ref[:, n:] = out_ref[...].T.astype(BF16)


def piece_f_kernel(s_ref, gu_ref, down_ref, f_ref):
    half = f_ref.shape[1] // 3
    at = pl.ds(pl.multiple_of(s_ref[0] * half, half), half)
    f_ref[:, :half] = gu_ref[0, :, at].astype(BF16)
    f_ref[:, half : 2 * half] = gu_ref[1, :, at].astype(BF16)
    f_ref[:, 2 * half :] = down_ref[:, at].astype(BF16)


def whole(*shape):
    return pl.BlockSpec(shape, lambda i: (0,) * len(shape))


def one_step(kernel, name, scalars, inputs, outputs, mib=24, scratch=(), us=0.1):
    return pl.pallas_call(
        kernel,
        grid=(1,),
        in_specs=[SMEM] + [whole(*t.shape) for t in inputs],
        out_specs=[whole(*t.shape) for t in outputs],
        out_shape=outputs,
        scratch_shapes=list(scratch),
        compiler_params=params(mib),
        cost_estimate=cost(us),
        name=name,
    )(scalars, *inputs)


def join_kernel(s_ref, *refs):
    blocks, whole_ref, sems = refs[:-2], refs[-2], refs[-1]
    cols, part = len(blocks), blocks[0].shape[0]
    copies = []
    for hop, block in enumerate(blocks):
        at = pl.multiple_of((s_ref[1] ^ hop) * part, part)
        copies.append(pltpu.make_async_copy(block, whole_ref.at[pl.ds(at, part)], sems.at[hop]))
    for copy in copies:
        copy.start()
    for copy in copies:
        copy.wait()


def pick_kernel(s_ref, a0_ref, a2_ref, a3_ref, send_ref, sems):
    def move(lo, hi):
        copies = [
            pltpu.make_async_copy(lo, send_ref.at[0], sems.at[0]),
            pltpu.make_async_copy(hi, send_ref.at[1], sems.at[1]),
        ]
        for copy in copies:
            copy.start()
        for copy in copies:
            copy.wait()

    @pl.when(s_ref[0] == 0)
    def _():
        move(a2_ref, a3_ref)

    @pl.when(s_ref[0] == 1)
    def _():
        move(a0_ref, a2_ref)


def causal(scores_t, block):
    keys = scores_t.shape[0]
    row = lax.broadcasted_iota(jnp.int32, (block, block), 0)
    column = lax.broadcasted_iota(jnp.int32, (block, block), 1)
    tail = jnp.where(row <= column, scores_t[keys - block :], NEGATIVE)
    return tail if keys == block else jnp.concatenate([scores_t[: keys - block], tail], 0)


def swap_halves(t):
    lane = lax.broadcasted_iota(jnp.int32, (1, t.shape[1]), 1)
    return jnp.where(lane % HD < HD // 2, pltpu.roll(t, t.shape[1] - HD // 2, 1), pltpu.roll(t, HD // 2, 1))


def pick_weights(core, j, a0_ref, a1_ref, a3_ref, got_ref, qk_ref, vo_ref):
    @pl.when(core == 0)
    def _():
        vo_ref[...] = got_ref[0]

        @pl.when(j == 0)
        def _():
            qk_ref[...] = a0_ref[...]

        @pl.when(j == 1)
        def _():
            qk_ref[...] = a1_ref[...]

    @pl.when(core == 1)
    def _():
        qk_ref[...] = got_ref[0]

        @pl.when(j == 0)
        def _():
            vo_ref[...] = a1_ref[...]

        @pl.when(j == 1)
        def _():
            vo_ref[...] = a3_ref[...]


def attend_forward_kernel(
    s_ref, x0_ref, x1_ref, a0_ref, a1_ref, a3_ref, got_ref, cos_ref, sin_ref,
    q_ref, k_ref, v_ref, ot_ref, lse_ref, xt_ref, far_ref, near_ref,
    qk_w, vo_w, o_ref, total_ref,
):
    core, live = s_ref[0], s_ref[1]
    j = pl.program_id(0)
    length = q_ref.shape[1]
    tokens = x0_ref.shape[0]
    n = 3 * HD
    pick_weights(core, j, a0_ref, a1_ref, a3_ref, got_ref, qk_w, vo_w)
    lane = lax.broadcasted_iota(jnp.int32, (tokens, HD), 1)
    one = jnp.where(lane == 0, 1.0, 0.0).astype(BF16)
    for x_ref, which in ((x0_ref, core), (x1_ref, 1 - core)):
        start = pl.multiple_of(which * tokens, tokens)
        at = pl.ds(start, tokens)
        qk = mxu(x_ref[...], qk_w[...])
        cos = jnp.concatenate([cos_ref[at, :]] * 3, 1)
        sin = jnp.concatenate([sin_ref[at, :]] * 3, 1)
        qk = qk * cos + swap_halves(qk) * sin
        q = (qk[:, :n] * (HD ** -0.5)).astype(BF16)
        k = qk[:, n:].astype(BF16)
        v = mxu(x_ref[...], vo_w[:, :n]).astype(BF16)
        key = start + lax.broadcasted_iota(jnp.int32, (tokens, HD), 0)
        bias = jnp.where((lane == 0) & (key >= live), NEGATIVE, 0.0).astype(BF16)
        for head in range(3):
            lanes = slice(head * HD, (head + 1) * HD)
            q_ref[head, at, :] = jnp.concatenate([q[:, lanes], one], 1)
            k_ref[head, at, :] = jnp.concatenate([k[:, lanes], bias], 1)
            v_ref[head, at, :] = jnp.concatenate([v[:, lanes], one], 1)

        @pl.when(j == 0)
        def _():
            xt_ref[:, at] = x_ref[...].T

    for block in range(length // BQ):
        keys = (block + 1) * BQ
        span = slice(block * BQ, keys)
        parts = []
        for head in range(3):
            scores = causal(mxu(k_ref[head, :keys, :], q_ref[head, span, :], NT), BQ)
            top = jnp.max(scores, 0, keepdims=True)
            probs = jnp.exp(scores - top).astype(BF16)
            o = mxu(probs, v_ref[head, :keys, :], TN).T
            total = o[HD : HD + 1]
            parts.append(o[:HD] / total)
            lse_ref[0, head : head + 1, span] = top + jnp.log(total)
        o = jnp.concatenate(parts, 0)
        ot_ref[0, :, span] = o.astype(BF16)
        o_ref[span, :] = o.T.astype(BF16)
    part = mxu(o_ref[...], vo_w[:, n:], NT)

    @pl.when(j == 0)
    def _():
        total_ref[...] = part

    @pl.when(j == 1)
    def _():
        total_ref[...] += part
        near_ref[...] = total_ref[pl.ds(pl.multiple_of(core * tokens, tokens), tokens), :]
        far_ref[...] = total_ref[pl.ds(pl.multiple_of((1 - core) * tokens, tokens), tokens), :].astype(BF16)


def attend_forward(scalars, x_own, x_other, slots, got, cos, sin):
    tokens, width = x_own.shape
    wide = slots[0].shape[1]
    n = wide // 2
    by_j = lambda *shape: pl.BlockSpec(shape, lambda j: (j,) + (0,) * (len(shape) - 1))
    return pl.pallas_call(
        attend_forward_kernel,
        grid=(2,),
        in_specs=[SMEM]
        + [whole(tokens, width)] * 2
        + [whole(width, wide)] * 3
        + [by_j(1, width, wide), whole(LEN, 128), whole(LEN, 128)],
        out_specs=[by_j(3, LEN, 128)] * 3
        + [by_j(1, n, LEN), by_j(1, 8, LEN), whole(width, LEN)]
        + [whole(tokens, width)] * 2,
        out_shape=[hbm(6, LEN, 128)] * 3
        + [hbm(2, n, LEN), hbm(2, 8, LEN, dtype=F32), hbm(width, LEN)]
        + [out(tokens, width), out(tokens, width, dtype=F32)],
        scratch_shapes=[
            pltpu.VMEM((width, wide), BF16),
            pltpu.VMEM((width, wide), BF16),
            pltpu.VMEM((LEN, n), BF16),
            pltpu.VMEM((LEN, width), F32),
        ],
        compiler_params=params(44),
        cost_estimate=cost(2),
        name="attend_forward",
    )(scalars, x_own, x_other, *stay((slots[0], slots[1], slots[3])), got, *stay((cos, sin)))


def attend_backward_kernel(
    s_ref, d0_ref, d1_ref, lo_ref, hi_ref, got_ref, cos_ref, sin_ref, ot_ref, lse_ref,
    q_any, k_any, v_any, xt_any,
    dqk_ref, dv_ref, mine_ref, send_ref,
    q_ref, k_ref, v_ref, xt_ref, vo_w, do_ref, dk_acc, dv_acc, sems, *, j,
):
    core = s_ref[0]
    tokens = d0_ref.shape[0]
    n = 3 * HD
    heads = pl.ds(3 * j, 3)
    copies = [
        pltpu.make_async_copy(k_any.at[heads], k_ref, sems.at[0]),
        pltpu.make_async_copy(q_any.at[heads], q_ref, sems.at[1]),
        pltpu.make_async_copy(v_any.at[heads], v_ref, sems.at[2]),
        pltpu.make_async_copy(xt_any, xt_ref, sems.at[3]),
    ]
    for copy in copies:
        copy.start()

    @pl.when(core == 0)
    def _():
        vo_w[...] = got_ref[0, :, n:]

    @pl.when(core == 1)
    def _():
        vo_w[...] = hi_ref[:, n:]

    for d_ref, which in ((d0_ref, core), (d1_ref, 1 - core)):
        at = pl.ds(pl.multiple_of(which * tokens, tokens), tokens)
        do_ref[at, :] = mxu(d_ref[...], vo_w[...]).astype(BF16)

    length = do_ref.shape[0]
    products = do_ref[...].astype(F32).T * ot_ref[0].astype(F32)
    for copy in copies[:3]:
        copy.wait()

    def unrotate(t):
        return t * cos_ref[...] - swap_halves(t) * sin_ref[...]

    for head in range(3):
        lanes = slice(head * HD, (head + 1) * HD)
        delta = jnp.sum(products[lanes], 0, keepdims=True)
        dq_parts = []
        for block in range(length // BQ):
            keys = (block + 1) * BQ
            span = slice(block * BQ, keys)
            before = keys - BQ
            q = q_ref[head, span, :]
            scores = causal(mxu(k_ref[head, :keys, :], q, NT), BQ)
            probs = jnp.exp(scores - lse_ref[0, head : head + 1, span])
            d_out = do_ref[span, lanes]
            d_probs = mxu(v_ref[head, :keys, :HD], d_out, NT)
            d_scores = (probs * (d_probs - delta[:, span])).astype(BF16)
            dv_part = mxu(probs.astype(BF16), d_out)
            dk_part = mxu(d_scores, q)
            if block:
                dv_acc[:before, :] += dv_part[:before]
                dk_acc[:before, :] += dk_part[:before]
            dv_acc[before:keys, :] = dv_part[before:]
            dk_acc[before:keys, :] = dk_part[before:]
            dq_parts.append(mxu(d_scores, k_ref[head, :keys, :], TN))
        dq = jnp.concatenate(dq_parts, 0) * (HD ** -0.5)
        dqk_ref[:, head * HD : (head + 1) * HD] = unrotate(dq)[:, :HD].astype(BF16)
        dqk_ref[:, n + head * HD : n + (head + 1) * HD] = unrotate(dk_acc[...])[:, :HD].astype(BF16)
        dv_ref[:, lanes] = dv_acc[...].astype(BF16)

    copies[3].wait()
    own = jnp.where(core == 0, 0, tokens)
    grad_o = jnp.zeros((n, d0_ref.shape[1]), F32)
    for d_ref, which in ((d0_ref, core), (d1_ref, 1 - core)):
        at = pl.ds(pl.multiple_of(which * tokens, tokens), tokens)
        grad_o += mxu(ot_ref[0, :, at], d_ref[...])
    grad_o = grad_o.T.astype(BF16)
    grad_qk = mxu(xt_ref[...], dqk_ref[...]).astype(BF16)
    grad_v = mxu(xt_ref[...], dv_ref[...]).astype(BF16)

    @pl.when(core == 0)
    def _():
        mine_ref[...] = grad_qk
        send_ref[:, :n] = grad_v
        send_ref[:, n:] = grad_o

    @pl.when(core == 1)
    def _():
        send_ref[...] = grad_qk
        mine_ref[:, :n] = grad_v
        mine_ref[:, n:] = grad_o


def attend_backward(j, scalars, d_own, d_other, slots, got, cos, sin, q, k, v, out_t, lse, x_t):
    tokens, width = d_own.shape
    wide = slots[0].shape[1]
    n = wide // 2
    at_j = lambda *shape: pl.BlockSpec(shape, lambda i: (j,) + (0,) * (len(shape) - 1))
    lo, hi = (slots[0], slots[1]) if j == 0 else (slots[1], slots[3])
    return pl.pallas_call(
        functools.partial(attend_backward_kernel, j=j),
        grid=(1,),
        in_specs=[SMEM]
        + [whole(tokens, width)] * 2
        + [whole(width, wide)] * 2
        + [at_j(1, width, wide), whole(LEN, 128), whole(LEN, 128), at_j(1, n, LEN), at_j(1, 8, LEN)]
        + [ANY] * 4,
        out_specs=[whole(LEN, wide), whole(LEN, n), whole(width, wide), whole(width, wide)],
        out_shape=[hbm(LEN, wide), hbm(LEN, n), hbm(width, wide), hbm(width, wide)],
        scratch_shapes=[
            pltpu.VMEM((3, LEN, 128), BF16),
            pltpu.VMEM((3, LEN, 128), BF16),
            pltpu.VMEM((3, LEN, 128), BF16),
            pltpu.VMEM((width, LEN), BF16),
            pltpu.VMEM((width, n), BF16),
            pltpu.VMEM((LEN, n), BF16),
            pltpu.VMEM((LEN, 128), F32),
            pltpu.VMEM((LEN, HD), F32),
            DMA((4,)),
        ],
        compiler_params=params(44),
        cost_estimate=cost(2),
        name="attend_backward",
    )(scalars, d_own, d_other, *stay((lo, hi, got, cos, sin, out_t, lse, q, k, v, x_t)))


def input_grad_kernel(s_ref, p0_ref, p1_ref, v0_ref, v1_ref, a0_ref, a1_ref, a3_ref, got_ref, far_ref, near_ref, qk_w, vo_w):
    core = s_ref[0]
    n = v0_ref.shape[1]
    tokens = far_ref.shape[0]
    for j, (lo, hi) in enumerate(((a0_ref, a1_ref), (a1_ref, a3_ref))):

        @pl.when(core == 0)
        def _():
            qk_w[j] = lo[...]
            vo_w[j] = got_ref[j, :, :n]

        @pl.when(core == 1)
        def _():
            qk_w[j] = got_ref[j]
            vo_w[j] = hi[:, :n]

    for which, dst in ((1 - core, far_ref), (core, near_ref)):
        at = pl.ds(pl.multiple_of(which * tokens, tokens), tokens)
        total = mxu(p0_ref[at, :], qk_w[0], NT) + mxu(v0_ref[at, :], vo_w[0], NT)
        total = total + (mxu(p1_ref[at, :], qk_w[1], NT) + mxu(v1_ref[at, :], vo_w[1], NT))
        dst[...] = total.astype(dst.dtype)


def input_grad_parts(scalars, d_qk, d_v, slots, got, tokens):
    width, wide = slots[0].shape
    return one_step(
        input_grad_kernel,
        "input_grad",
        scalars,
        stay((*d_qk, *d_v, slots[0], slots[1], slots[3], got)),
        [out(tokens, width), out(tokens, width, dtype=F32)],
        40,
        [pltpu.VMEM((2, width, wide), BF16), pltpu.VMEM((2, width, wide // 2), BF16)],
    )


def first_norm_kernel(s_ref, x_ref, near_ref, far_ref, gain_ref, resid_ref, normed_ref):
    residual = x_ref[...].astype(F32) + (near_ref[...] + far_ref[...].astype(F32))
    scale = lax.rsqrt(jnp.mean(residual * residual, -1, keepdims=True) + EPSILON)
    resid_ref[...] = residual
    normed_ref[...] = (residual * scale * gain_ref[0:1, :]).astype(BF16)


def last_norm_kernel(s_ref, resid_ref, near_ref, far_ref, gain_ref, own_cot_ref, moved_cot_ref, out_ref, dsum_ref, dffn_ref, dgain_ref):
    core, live = s_ref[0], s_ref[1]
    tokens, width = resid_ref.shape
    residual = resid_ref[...]
    scale = lax.rsqrt(jnp.mean(residual * residual, -1, keepdims=True) + EPSILON)
    summed = residual * scale * gain_ref[0:1, :] + (near_ref[...] + far_ref[...].astype(F32))
    scale = lax.rsqrt(jnp.mean(summed * summed, -1, keepdims=True) + EPSILON)
    unit = summed * scale
    out_ref[...] = (unit * gain_ref[1:2, :]).astype(BF16)
    position = core * tokens + lax.broadcasted_iota(jnp.int32, (tokens, 1), 0)
    cot = jnp.where(s_ref[2] == 1, own_cot_ref[...].astype(F32), moved_cot_ref[...].astype(F32))
    cot = jnp.where(position < live, cot, 0.0)
    dgain_ref[...] = jnp.sum(cot * unit, 0, keepdims=True)
    hat = cot * gain_ref[1:2, :]
    inner = jnp.mean(hat * unit, -1, keepdims=True)
    d_summed = scale * (hat - unit * inner)
    dsum_ref[...] = d_summed
    dffn_ref[...] = d_summed.astype(BF16)


def back_norm_kernel(s_ref, resid_ref, near_ref, far_ref, dsum_ref, gain_ref, dres_ref, dbranch_ref, dgain_ref):
    residual = resid_ref[...]
    scale = lax.rsqrt(jnp.mean(residual * residual, -1, keepdims=True) + EPSILON)
    unit = residual * scale
    d_normed = dsum_ref[...] + (near_ref[...] + far_ref[...].astype(F32))
    dgain_ref[...] = jnp.sum(d_normed * unit, 0, keepdims=True)
    hat = d_normed * gain_ref[0:1, :]
    inner = jnp.mean(hat * unit, -1, keepdims=True)
    d_residual = scale * (hat - unit * inner)
    dres_ref[...] = d_residual
    dbranch_ref[...] = d_residual.astype(BF16)


def fetch_slots(step, sources, dst, sems):
    copies = [pltpu.make_async_copy(src, dst.at[i], sems.at[i]) for i, src in enumerate(sources)]

    @pl.when(step == 0)
    def _():
        for copy in copies:
            copy.start()

    for i, copy in enumerate(copies):

        @pl.when(step == i)
        def _():
            copy.wait()


def ffn_forward_kernel(y0_ref, y1_ref, *refs, slots, start, finish):
    refs = list(refs)
    carry_ref = None if start else refs.pop(0)
    sources, refs = refs[:slots], refs[slots:]
    hid_ref, silu_ref, slope_ref = refs[:3]
    results = refs[3:5]
    w_ref, total_ref, sems = refs[-3:]
    step = pl.program_id(0)
    tokens = y0_ref.shape[0]
    half = hid_ref.shape[2]
    fetch_slots(step, sources, w_ref, sems)

    @pl.when(step == 0)
    def _():
        total_ref[...] = jnp.zeros_like(total_ref) if start else carry_ref[...]
        if start:
            results[1][:, :tokens] = y0_ref[...].T
            results[1][:, tokens:] = y1_ref[...].T

    for part, y_ref in ((0, y0_ref), (1, y1_ref)):
        at = slice(part * tokens, (part + 1) * tokens)
        both = mxu(y_ref[...], w_ref[step, :, : 2 * half])
        gate, up = both[:, :half], both[:, half:]
        sig = jax.nn.sigmoid(gate)
        silu = gate * sig
        hidden = (silu * up).astype(BF16)
        hid_ref[0, at, :] = hidden
        silu_ref[0, at, :] = silu.astype(BF16)
        slope_ref[0, at, :] = (up * (sig + silu * (1.0 - sig))).astype(BF16)
        total_ref[at, :] += mxu(hidden, w_ref[step, :, 2 * half :], NT)

    @pl.when(step == slots - 1)
    def _():
        if finish:
            far_ref, near_ref = results
            near_ref[...] = total_ref[:tokens, :]
            far_ref[...] = total_ref[tokens:, :].astype(BF16)
        else:
            results[0][...] = total_ref[...]


def ffn_forward(normed, normed_other, slots, carry, finish):
    tokens, width = normed.shape
    lanes = slots[0].shape[1]
    count = len(slots)
    half = lanes // 3
    per_slot = pl.BlockSpec((1, 2 * tokens, half), lambda s: (s, 0, 0))
    if finish:
        results = [out(tokens, width), out(tokens, width, dtype=F32)]
    else:
        results = [out(2 * tokens, width, dtype=F32), hbm(width, 2 * tokens)]
    inputs = (normed, normed_other) + (() if carry is None else (carry,))
    return pl.pallas_call(
        functools.partial(ffn_forward_kernel, slots=count, start=carry is None, finish=finish),
        grid=(count,),
        in_specs=[whole(*t.shape) for t in inputs] + [ANY] * count,
        out_specs=[per_slot] * 3 + [whole(*t.shape) for t in results],
        out_shape=[hbm(count, 2 * tokens, half)] * 3 + results,
        scratch_shapes=[
            pltpu.VMEM((count, width, lanes), BF16),
            pltpu.VMEM((2 * tokens, width), F32),
            DMA((count,)),
        ],
        compiler_params=params(36),
        cost_estimate=cost(2),
        name="ffn_forward",
    )(*inputs, *slots)


def ffn_backward_kernel(d0_ref, d1_ref, silu_a, slope_a, silu_b, slope_b, *refs):
    sources, (dgu_ref, far_ref, near_ref, w_ref, total_ref, sems) = refs[:4], refs[4:]
    step = pl.program_id(0)
    tokens = d0_ref.shape[0]
    half = silu_a.shape[2]
    fetch_slots(step, sources, w_ref, sems)

    @pl.when(step == 0)
    def _():
        total_ref[...] = jnp.zeros_like(total_ref)

    def slot(silu_ref, slope_ref):
        for part, d_ref in ((0, d0_ref), (1, d1_ref)):
            at = slice(part * tokens, (part + 1) * tokens)
            d_hidden = mxu(d_ref[...], w_ref[step, :, 2 * half :])
            d_gate = (d_hidden * slope_ref[0, at, :].astype(F32)).astype(BF16)
            d_up = (d_hidden * silu_ref[0, at, :].astype(F32)).astype(BF16)
            dgu_ref[0, at, :half] = d_gate
            dgu_ref[0, at, half:] = d_up
            term = mxu(d_gate, w_ref[step, :, :half], NT) + mxu(d_up, w_ref[step, :, half : 2 * half], NT)
            total_ref[at, :] += term

    @pl.when(step < 3)
    def _():
        slot(silu_a, slope_a)

    @pl.when(step == 3)
    def _():
        slot(silu_b, slope_b)
        near_ref[...] = total_ref[:tokens, :]
        far_ref[...] = total_ref[tokens:, :].astype(BF16)


def ffn_backward(d_ffn, d_other, low, high, slots):
    tokens, width = d_ffn.shape
    lanes = slots[0].shape[1]
    half = lanes // 3
    first_three = pl.BlockSpec((1, 2 * tokens, half), lambda s: (jnp.minimum(s, 2), 0, 0))
    return pl.pallas_call(
        ffn_backward_kernel,
        grid=(4,),
        in_specs=[whole(tokens, width)] * 2
        + [first_three] * 2
        + [whole(1, 2 * tokens, half)] * 2
        + [ANY] * 4,
        out_specs=[pl.BlockSpec((1, 2 * tokens, 2 * half), lambda s: (s, 0, 0))] + [whole(tokens, width)] * 2,
        out_shape=[hbm(4, 2 * tokens, 2 * half), out(tokens, width), out(tokens, width, dtype=F32)],
        scratch_shapes=[
            pltpu.VMEM((4, width, lanes), BF16),
            pltpu.VMEM((2 * tokens, width), F32),
            DMA((4,)),
        ],
        compiler_params=params(40),
        cost_estimate=cost(2),
        name="ffn_backward",
    )(d_ffn, d_other, *stay((*low[1:], *high[1:], *slots)))


def grads_g_kernel(*refs, count, moved):
    yt_ref, refs = refs[0], refs[1:]
    dgu, refs = refs[:count], refs[count:]
    moved_ref, results = (refs[0], refs[1:]) if moved else (None, refs)
    for i, (dgu_ref, result_ref) in enumerate(zip(dgu, results)):
        grad = mxu(yt_ref[...], dgu_ref[0])
        if moved and i == 0:
            grad = grad + moved_ref[...].astype(F32)
        result_ref[...] = grad.astype(BF16)


def grads_g(y_t, d_gu, slots, moved=None):
    width, length = y_t.shape
    wide = d_gu.shape[2]
    at_slot = [pl.BlockSpec((1, length, wide), functools.partial(lambda n, i: (n, 0, 0), n)) for n in slots]
    extra = [] if moved is None else [moved]
    return pl.pallas_call(
        functools.partial(grads_g_kernel, count=len(slots), moved=moved is not None),
        grid=(1,),
        in_specs=[whole(width, length)] + at_slot + [whole(*t.shape) for t in extra],
        out_specs=[whole(width, wide)] * len(slots),
        out_shape=[out(width, wide)] * len(slots),
        compiler_params=params(32),
        cost_estimate=cost(0.1),
        name="grads_g",
    )(stay(y_t), *[stay(d_gu)] * len(slots), *extra)


def grads_d_kernel(s_ref, d0_ref, d1_ref, hid_a, hid_b, *refs):
    blocks, dt_ref, grad_ref = refs[:-2], refs[-2], refs[-1]
    tokens = d0_ref.shape[0]
    dt_ref[:, :tokens] = d0_ref[...].T
    dt_ref[:, tokens:] = d1_ref[...].T
    for slot in range(4):
        hidden = hid_a[slot] if slot < 3 else hid_b[0]
        grad_ref[slot] = mxu(dt_ref[...], hidden).astype(BF16)
    for hop, block_ref in enumerate(blocks):
        rows = block_ref.shape[1]
        place = (s_ref[1] ^ hop) if len(blocks) > 1 else 0
        at = pl.ds(pl.multiple_of(place * rows, rows), rows)
        for slot in range(4):
            block_ref[slot] = grad_ref[slot, at, :]


def first_slots_kernel(s_ref, mine1_ref, theirs1_ref, dn_ref, dn_moved_ref, s3_ref, sum_ref):
    sum_ref[...] = (dn_ref[...].astype(F32) + dn_moved_ref[...].astype(F32)).astype(BF16)

    @pl.when(s_ref[0] == 0)
    def _():
        s3_ref[...] = theirs1_ref[...]

    @pl.when(s_ref[0] == 1)
    def _():
        s3_ref[...] = mine1_ref[...]


def slots_kernel(s_ref, mine0_ref, mine1_ref, theirs0_ref, theirs1_ref, moved_ref, s1_ref, s2_ref):
    moved = moved_ref[...].astype(F32)

    @pl.when(s_ref[0] == 0)
    def _():
        s1_ref[...] = (mine1_ref[...].astype(F32) + moved).astype(BF16)
        s2_ref[...] = theirs0_ref[...]

    @pl.when(s_ref[0] == 1)
    def _():
        s1_ref[...] = (mine0_ref[...].astype(F32) + moved).astype(BF16)
        s2_ref[...] = theirs1_ref[...]


def merge_kernel(s_ref, base0_ref, base1_ref, one_ref, two_ref, *blocks):
    cols = len(blocks)
    part = blocks[0].shape[0]
    for hop, block_ref in enumerate(blocks):
        at = pl.ds(pl.multiple_of((s_ref[1] ^ hop) * part, part), part)
        moved = one_ref[at, :].astype(F32) + two_ref[at, :].astype(F32)

        @pl.when(s_ref[0] == 0)
        def _():
            block_ref[...] = (base0_ref[at, :].astype(F32) + moved).astype(BF16)

        @pl.when(s_ref[0] == 1)
        def _():
            block_ref[...] = (base1_ref[at, :].astype(F32) + moved).astype(BF16)


def pack_kernel(s_ref, *refs):
    shards, gain_ref, pack_ref = refs[:-2], refs[-2], refs[-1]
    total = jnp.zeros((1, 1), F32)
    for ref in shards:
        value = ref[...].astype(F32)
        total = total + jnp.sum(jnp.sum(value * value, 0, keepdims=True), 1, keepdims=True)
    row = lax.broadcasted_iota(jnp.int32, pack_ref.shape, 0)
    gain = jnp.where(row == 0, gain_ref[0:1, :], gain_ref[1:2, :])
    pack_ref[...] = jnp.where(row < 2, gain, jnp.broadcast_to(total, pack_ref.shape))


def update(grad_full, moment, weight, average, factor):
    clipped = grad_full * factor
    new_moment = MOMENTUM * moment + clipped
    new_weight = weight - RATE * (clipped + MOMENTUM * new_moment)
    new_average = DECAY * average + (1.0 - DECAY) * new_weight
    return (new_moment, new_weight, new_average)


def fetch_kernel(*refs):
    count = (len(refs) - 1) // 2
    sems = refs[-1]
    copies = [pltpu.make_async_copy(refs[i], refs[count + i], sems.at[i]) for i in range(count)]
    for copy in copies:
        copy.start()
    for copy in copies:
        copy.wait()


def update_kernel(s_ref, pack_ref, a0_ref, a1_ref, g0_ref, g1_ref, d0_ref, d1_ref, gm_ref, gw_ref, ge_ref, *refs):
    old, refs = refs[:12], refs[12:]
    new, refs = refs[:12], refs[12:]
    gain_new, norm_ref, refs = refs[:3], refs[3], refs[4:]
    held, out_sems = refs[:12], refs[12]
    gains = pack_ref[0:2, :]
    squares = pack_ref[2:3, 0:1] + jnp.sum(jnp.sum(gains * gains, 0, keepdims=True), 1, keepdims=True)
    norm = jnp.sqrt(squares)
    norm_ref[...] = norm
    factor = jnp.minimum(1.0, CLIP / (norm + 1e-06))
    for ref, value in zip(gain_new, update(gains, gm_ref[...], gw_ref[...], ge_ref[...], factor)):
        ref[...] = value
    n = held[0].shape[2]
    half = d0_ref.shape[1]

    def put(kind, at, grad):
        moment, weight, average = (old[kind + 4 * i] for i in range(3))
        results = update(grad, moment[at], weight[at], average[at], factor)
        for i, value in enumerate(results):
            held[kind + 4 * i][at] = value

    every = slice(None)

    def parts(kind, mine, other):
        if kind == 0:
            qk, vo = mine[0], other[0]
            put(0, (0, every, every), qk[:, :n].astype(F32))
            put(0, (1, every, every), qk[:, n:].astype(F32))
            put(0, (2, every, every), vo[:, :n].astype(F32))
        elif kind == 1:
            put(1, (every, every), other[0][:, n:].astype(F32).T)
        else:
            for which, part in enumerate((mine, other)):
                lanes = slice(which * half, (which + 1) * half)
                if kind == 2:
                    put(2, (0, every, lanes), part[1][:, :half].astype(F32))
                    put(2, (1, every, lanes), part[1][:, half:].astype(F32))
                else:
                    put(3, (every, lanes), part[2][...].astype(F32))

    here, there = (a0_ref, g0_ref, d0_ref), (a1_ref, g1_ref, d1_ref)
    for kind in (2, 3, 0, 1):
        @pl.when(s_ref[0] == 0)
        def _():
            parts(kind, here, there)

        @pl.when(s_ref[0] == 1)
        def _():
            parts(kind, there, here)

        for i in (kind, kind + 4, kind + 8):
            pltpu.make_async_copy(held[i], new[i], out_sems.at[i]).start()
    for i in range(12):
        pltpu.make_async_copy(held[i], new[i], out_sems.at[i]).wait()


def body(
    rows,
    cols,
    block_input,
    out_grad,
    lengths,
    w_qkv,
    w_out,
    w_gate_up,
    w_down,
    gains,
    mom_qkv,
    mom_out,
    mom_gate_up,
    mom_down,
    mom_gains,
    ema_qkv,
    ema_out,
    ema_gate_up,
    ema_down,
    ema_gains,
):
    d = lax.axis_index("dp")
    r = lax.axis_index("row")
    c = lax.axis_index("col")
    core0 = d == 0
    stays = d == r % 2
    tokens, width = block_input.shape
    ring = cols == 4
    mesh_sizes = {"row": rows, "col": cols}
    part = width // cols
    head_cols = w_qkv.shape[2]
    half = w_gate_up.shape[2] // 2

    pairs = [(i, j) for i in range(2) for j in range(rows)]
    swap_pairs = [(i * rows + j, (j % 2) * rows + (j // 2) * 2 + i) for i, j in pairs]
    cross_pairs = [(i, j) for i, j in swap_pairs if i != j]
    first_pairs = [(i * rows + j, i * rows + (j ^ (1 if i == 0 else 2))) for i, j in pairs]
    second_pairs = [(i * rows + j, i * rows + (j ^ (2 if i == 0 else 1))) for i, j in pairs]

    def swap_tokens(t):
        return lax.ppermute(t, ("dp", "row"), swap_pairs)

    def cross_tokens(t):
        return lax.ppermute(t, ("dp", "row"), cross_pairs)

    def first(t):
        return lax.ppermute(t, ("dp", "row"), first_pairs)

    def second(t):
        return lax.ppermute(t, ("dp", "row"), second_pairs)

    def core(t):
        return lax.ppermute(t, "dp", [(0, 1), (1, 0)])

    def along(t, k):
        return lax.ppermute(t, "col", [(i, i ^ k) for i in range(cols)])

    def join_cols(*blocks):
        return pl.pallas_call(
            join_kernel,
            in_specs=[SMEM] + [ANY] * cols,
            out_specs=ANY,
            out_shape=out(width, blocks[0].shape[1]),
            scratch_shapes=[DMA((cols,))],
            compiler_params=params(16),
            cost_estimate=cost(0.1),
            name="join",
        )(ids, *blocks)

    def gather_cols(t):
        return lax.all_gather(t, "col", axis=t.ndim - 2, tiled=True)

    def add(*values):
        total = values[0].astype(F32)
        for value in values[1:]:
            total = total + value.astype(F32)
        return total.astype(BF16)

    ids = jnp.stack([d, c]).astype(jnp.int32)
    (piece_a,) = one_step(piece_a_kernel, "piece_a", ids, stay((w_qkv, w_out)), [out(part, 2 * head_cols)], 60)
    piece_a, block_input = fence(piece_a, block_input)
    a_cols = [along(piece_a, 1), along(piece_a, 2)] if ring else [gather_cols(piece_a)]
    moved_x = cross_tokens(block_input)
    (piece_f,) = one_step(piece_f_kernel, "piece_f", ids, stay((w_gate_up, w_down.T)), [out(part, 3 * half)], 60)
    a_cols, piece_f, out_grad = fence(a_cols, piece_f, out_grad)
    moved_cot = cross_tokens(out_grad)
    if ring:
        a_cols = a_cols + [along(a_cols[1], 1)]
        f_cols = [along(piece_f, 1), along(piece_f, 2)]
    else:
        f_cols = [gather_cols(piece_f)]
    a_cols, piece_a, lengths, moved_x = fence(a_cols, piece_a, lengths, moved_x)
    a0 = join_cols(piece_a, *a_cols) if ring else a_cols[0]
    a1, a2 = first(a0), second(a0)
    x_own = jnp.where(stays, block_input, moved_x)
    a0, a1, a2, f_cols, x_own, moved_cot = fence(a0, a1, a2, f_cols, x_own, moved_cot)
    a3 = second(a1)
    if ring:
        f_cols = f_cols + [along(f_cols[1], 1)]
    x_other = core(x_own)
    own_length = swap_tokens(lengths)[0, :]
    seq_ids = jnp.arange(own_length.shape[0], dtype=jnp.int32)
    own_length = jnp.sum(jnp.where(seq_ids == r // 2, own_length, 0))
    scalars = jnp.stack([d.astype(jnp.int32), own_length, stays.astype(jnp.int32)])
    a0, a1, a2, a3, f_cols, x_own, x_other, scalars = fence(a0, a1, a2, a3, f_cols, x_own, x_other, scalars)
    f0 = join_cols(piece_f, *f_cols) if ring else f_cols[0]
    f0, a0, a2, a3 = fence(f0, a0, a2, a3)
    slots_a = [a0, a1, a2, a3]
    send = pl.pallas_call(
        pick_kernel,
        in_specs=[SMEM] + [ANY] * 3,
        out_specs=ANY,
        out_shape=out(2, width, 2 * head_cols),
        scratch_shapes=[DMA((2,))],
        compiler_params=params(16),
        cost_estimate=cost(0.1),
        name="pick",
    )(ids, a0, a2, a3)
    got = core(send)
    f1, f2 = first(f0), second(f0)
    cos, sin = pair_tables()
    q, k, v, attended_t, lse, x_t, far, near = attend_forward(scalars, x_own, x_other, slots_a, got, cos, sin)
    far, near, f1, f2 = fence(far, near, f1, f2)
    f3 = second(f1)
    residual, normed = one_step(
        first_norm_kernel,
        "first_norm",
        ids,
        (x_own, near, core(far), gains),
        [out(tokens, width, dtype=F32), out(tokens, width)],
    )
    normed_other = core(normed)

    *low, carry, y_t = ffn_forward(normed, normed_other, [f0, f1, f2], None, False)
    carry, f3 = fence(carry, f3)
    slots_f = [f0, f1, f2, f3]
    *high, far, near = ffn_forward(normed, normed_other, [f3], carry, True)
    output, d_summed, d_ffn, grad_gain_two = one_step(
        last_norm_kernel,
        "last_norm",
        scalars,
        (residual, near, core(far), gains, out_grad, moved_cot),
        [out(tokens, width), out(tokens, width, dtype=F32), out(tokens, width), out(1, width, dtype=F32)],
        32,
    )
    d_ffn_other = core(d_ffn)
    moved_out = cross_tokens(output)

    d_gu, far, near = ffn_backward(d_ffn, d_ffn_other, low, high, slots_f)
    far, near, moved_out, d_gu = fence(far, near, moved_out, d_gu)
    got_far = core(far)
    (gu3,) = grads_g(y_t, d_gu, (3,))
    got_far, gu3 = fence(got_far, gu3)
    gu_moved = second(gu3)
    d_residual, d_branch, grad_gain_one = one_step(
        back_norm_kernel,
        "back_norm",
        ids,
        (residual, near, got_far, d_summed, gains),
        [out(tokens, width, dtype=F32), out(tokens, width), out(1, width, dtype=F32)],
    )
    d_branch_other = core(d_branch)
    dn = one_step(
        grads_d_kernel,
        "grads_d",
        ids,
        stay((d_ffn, d_ffn_other, low[0], high[0])),
        [hbm(4, part if ring else width, half)] * (cols if ring else 1),
        32,
        [pltpu.VMEM((width, 2 * tokens), BF16), pltpu.VMEM((4, width, half), BF16)],
    )
    d_branch_other, dn = fence(d_branch_other, dn)
    gain_pair = jnp.concatenate([grad_gain_one, grad_gain_two], 0)
    gain_pair = gain_pair + core(gain_pair)
    dn_one = along(dn[3], 1) if ring else dn[0]
    back = (scalars, d_branch, d_branch_other, slots_a, got, cos, sin, q, k, v, attended_t, lse, x_t)
    dqk1, dv1, mine1, send1 = attend_backward(1, *back)
    dqk1, dv1, mine1, send1, gu_moved, dn_one, d_branch, gain_pair = fence(
        dqk1, dv1, mine1, send1, gu_moved, dn_one, d_branch, gain_pair
    )
    theirs1 = core(send1)
    gu1, gu2, gu0 = grads_g(y_t, d_gu, (1, 2, 0), gu_moved)
    theirs1, gu1, gu2 = fence(theirs1, gu1, gu2)
    s3, dn_two = one_step(
        first_slots_kernel,
        "first_slots",
        ids,
        (mine1, theirs1, dn[2] if ring else dn[0], dn_one),
        [out(width, 2 * head_cols), out(*dn[0].shape)],
    )
    s3, dn_two, gu1, gu2, d_branch = fence(s3, dn_two, gu1, gu2, d_branch)
    a_moved = second(s3)
    gu_one, gu_two = first(gu1), second(gu2)
    dn_last = [along(dn_two, 2), along(dn[1], 1)] if ring else []
    back = (scalars, d_branch) + back[2:]
    dqk0, dv0, mine0, send0 = attend_backward(0, *back)
    dqk0, dv0, mine0, send0, a_moved, gu_one, gu_two, dn_last = fence(
        dqk0, dv0, mine0, send0, a_moved, gu_one, gu_two, dn_last
    )
    theirs0 = core(send0)
    if ring:
        own_dn = add(dn[0], *dn_last)
    else:
        own_dn = lax.psum_scatter(dn[0], "col", scatter_dimension=1, tiled=True)
    dn_moved = second(own_dn[3])

    def merge(base0, base1, one, two):
        if not ring:
            return [add(jnp.where(core0, base0, base1), one, two)]
        return one_step(merge_kernel, "merge", ids, (base0, base1, one, two), [out(part, base0.shape[1])] * cols)

    def to_owner(blocks):
        if not ring:
            return [lax.psum_scatter(blocks[0], "col", scatter_dimension=0, tiled=True)]
        return [blocks[0]] + [along(blocks[hop], hop) for hop in range(1, cols)]

    g_parts = merge(gu0, gu0, gu_one, gu_two)
    theirs0, g_parts = fence(theirs0, g_parts)
    s1, s2 = one_step(
        slots_kernel, "slots", ids, (mine0, mine1, theirs0, theirs1, a_moved), [out(width, 2 * head_cols)] * 2
    )
    s1, s2, g_parts, dqk0, output, dn_moved = fence(s1, s2, g_parts, dqk0, output, dn_moved)
    a_one, a_two = first(s1), second(s2)
    g_parts = to_owner(g_parts)
    far, near = input_grad_parts(scalars, (dqk0, dqk1), (dv0, dv1), slots_a, got, tokens)
    output = jnp.where(stays, output.astype(F32), moved_out.astype(F32))
    a_one, a_two, g_parts, far, near, output, mom_gains = fence(
        a_one, a_two, g_parts, far, near, output, mom_gains
    )
    old = (mom_qkv, mom_out, mom_gate_up, mom_down.T) + (w_qkv, w_out, w_gate_up, w_down.T)
    old = old + (ema_qkv, ema_out, ema_gate_up, ema_down.T)
    old, a_one = fence(old, a_one)
    a_parts = to_owner(merge(mine0, theirs0, a_one, a_two))
    dn_one, dn_two = first(add(own_dn[1], dn_moved)), second(own_dn[2])
    shard_g = add(*g_parts)
    held = pl.pallas_call(
        fetch_kernel,
        in_specs=[ANY] * 12,
        out_specs=[VMEM] * 12,
        out_shape=[pltpu.VMEM(t.shape, F32) for t in old],
        scratch_shapes=[DMA((12,))],
        compiler_params=params(16),
        cost_estimate=cost(0.1),
        name="fetch",
    )(*stay(old))
    a_parts, dn_one, dn_two, shard_g, held, far = fence(a_parts, dn_one, dn_two, shard_g, held, far)
    shard_a = add(*a_parts)
    shard_d = add(own_dn[0], dn_one, dn_two)

    far_a, far_d, far_g = core(shard_a), core(shard_d), core(shard_g)
    got_far = core(far)
    far_a, far_d, far_g, got_far = fence(far_a, far_d, far_g, got_far)
    input_grad = d_residual + (near + got_far.astype(F32))
    moved_grad = cross_tokens(input_grad.astype(BF16))
    pack = one_step(
        pack_kernel,
        "pack",
        ids,
        (shard_a, far_a, shard_g, far_g, shard_d, far_d, gain_pair),
        [out(8, width, dtype=F32)],
    )[0]
    for axis, bits in (("col", (2, 1) if ring else ()), ("row", (2, 1))):
        size = mesh_sizes[axis]
        for bit in bits:
            moved = lax.ppermute(pack, axis, [(i, i ^ bit) for i in range(size)])
            if (axis, bit) == ("row", 1):
                input_grad = jnp.where(stays, input_grad, moved_grad.astype(F32))
                moved, input_grad = fence(moved, input_grad)
            pack = pack + moved
    if not ring:
        pack = lax.psum(pack, "col")

    results = pl.pallas_call(
        update_kernel,
        in_specs=[SMEM] + [VMEM] * 22,
        out_specs=[ANY] * 12 + [VMEM] * 4,
        out_shape=[out(*t.shape, dtype=F32) for t in old]
        + [out(*gains.shape, dtype=F32)] * 3
        + [out(1, 1, dtype=F32)],
        scratch_shapes=[pltpu.VMEM(t.shape, F32) for t in old] + [DMA((12,))],
        compiler_params=params(24),
        cost_estimate=cost(0.1),
        name="update",
    )(ids, pack, shard_a, far_a, shard_g, far_g, shard_d, far_d, mom_gains, gains, ema_gains, *held)
    new = results[:12]
    gain_new = results[12:15]
    grad_norm = results[15][0, 0]
    return (
        output,
        input_grad,
        grad_norm,
        *new[0:3],
        new[3].T,
        gain_new[0],
        *new[4:7],
        new[7].T,
        gain_new[1],
        *new[8:11],
        new[11].T,
        gain_new[2],
    )


def solution(mesh):
    tok = P(("dp", "col", "row"), None)
    weights = (P(None, "col", "row"), P("row", "col"), P(None, "col", "row"), P("row", "col"), P())
    in_specs = (tok, tok, P(("dp", "col"), None)) + weights * 3
    out_specs = (tok, tok, P()) + weights * 3
    fn = functools.partial(body, mesh.shape["row"], mesh.shape["col"])
    return jax.shard_map(fn, mesh=mesh, in_specs=in_specs, out_specs=out_specs, check_vma=False)
```

```python
import functools

import jax
import jax.numpy as jnp
import numpy as np
from jax import lax
from jax.experimental import pallas as pl
from jax.experimental.pallas import tpu as pltpu
from jax.sharding import PartitionSpec as P

HD = 64
LEN = 1024

EPSILON = 1e-06
THETA = 10000.0
MOMENTUM = 0.9
RATE = 300.0
DECAY = 0.6
CLIP = 1.0
NEGATIVE = -1e30

F32 = jnp.float32
BF16 = jnp.bfloat16
NT = (((1,), (1,)), ((), ()))
NN = (((1,), (0,)), ((), ()))
TN = (((0,), (0,)), ((), ()))
BQ = 256


def rope_tables():
    half = HD // 2
    freqs = np.float32(THETA) ** (-(np.arange(half, dtype=np.float32) * np.float32(2.0)) / np.float32(HD))
    angles = np.arange(LEN, dtype=np.float32)[:, None] * freqs[None, :].astype(np.float32)
    return np.cos(angles), np.sin(angles)


def pair_tables():
    cosine, sine = rope_tables()
    return (
        jnp.asarray(np.concatenate([cosine] * 4, 1)),
        jnp.asarray(np.concatenate([-sine, sine] * 2, 1)),
    )


def mxu(lhs, rhs, dims=NN):
    return lax.dot_general(lhs, rhs, dims, preferred_element_type=F32)


def fence(*values):
    return lax.optimization_barrier(values)


def params(mib):
    return pltpu.CompilerParams(vmem_limit_bytes=mib << 20)


def cost(microseconds):
    return pl.CostEstimate(flops=int(1e9 * microseconds), bytes_accessed=1 << 10, transcendentals=0)


def out(*shape, dtype=BF16):
    return jax.ShapeDtypeStruct(shape, dtype)


def hbm(*shape, dtype=BF16):
    return pltpu.HBM(shape, dtype)


def stay(t):
    return jax.tree.map(lambda v: pltpu.with_memory_space_constraint(v, pltpu.HBM), t)


VMEM = pl.BlockSpec(memory_space=pltpu.VMEM)
SMEM = pl.BlockSpec(memory_space=pltpu.SMEM)
ANY = pl.BlockSpec(memory_space=pl.ANY)
DMA = pltpu.SemaphoreType.DMA


def piece_a_kernel(s_ref, qkv_ref, out_ref, a_ref):
    n = qkv_ref.shape[2]

    @pl.when(s_ref[0] == 0)
    def _():
        a_ref[:, :n] = qkv_ref[0].astype(BF16)
        a_ref[:, n:] = qkv_ref[1].astype(BF16)

    @pl.when(s_ref[0] == 1)
    def _():
        a_ref[:, :n] = qkv_ref[2].astype(BF16)
        a_ref[:, n:] = out_ref[...].T.astype(BF16)


def piece_f_kernel(s_ref, gu_ref, down_ref, f_ref):
    half = f_ref.shape[1] // 3
    at = pl.ds(pl.multiple_of(s_ref[0] * half, half), half)
    f_ref[:, :half] = gu_ref[0, :, at].astype(BF16)
    f_ref[:, half : 2 * half] = gu_ref[1, :, at].astype(BF16)
    f_ref[:, 2 * half :] = down_ref[:, at].astype(BF16)


def whole(*shape):
    return pl.BlockSpec(shape, lambda i: (0,) * len(shape))


def one_step(kernel, name, scalars, inputs, outputs, mib=24, scratch=(), us=0.1):
    return pl.pallas_call(
        kernel,
        grid=(1,),
        in_specs=[SMEM] + [whole(*t.shape) for t in inputs],
        out_specs=[whole(*t.shape) for t in outputs],
        out_shape=outputs,
        scratch_shapes=list(scratch),
        compiler_params=params(mib),
        cost_estimate=cost(us),
        name=name,
    )(scalars, *inputs)


def join_kernel(s_ref, *refs):
    blocks, whole_ref, sems = refs[:-2], refs[-2], refs[-1]
    cols, part = len(blocks), blocks[0].shape[0]
    copies = []
    for hop, block in enumerate(blocks):
        at = pl.multiple_of((s_ref[1] ^ hop) * part, part)
        copies.append(pltpu.make_async_copy(block, whole_ref.at[pl.ds(at, part)], sems.at[hop]))
    for copy in copies:
        copy.start()
    for copy in copies:
        copy.wait()


def pick_kernel(s_ref, a0_ref, a2_ref, a3_ref, send_ref, sems):
    def move(lo, hi):
        copies = [
            pltpu.make_async_copy(lo, send_ref.at[0], sems.at[0]),
            pltpu.make_async_copy(hi, send_ref.at[1], sems.at[1]),
        ]
        for copy in copies:
            copy.start()
        for copy in copies:
            copy.wait()

    @pl.when(s_ref[0] == 0)
    def _():
        move(a2_ref, a3_ref)

    @pl.when(s_ref[0] == 1)
    def _():
        move(a0_ref, a2_ref)


def causal(scores_t, block):
    keys = scores_t.shape[0]
    row = lax.broadcasted_iota(jnp.int32, (block, block), 0)
    column = lax.broadcasted_iota(jnp.int32, (block, block), 1)
    tail = jnp.where(row <= column, scores_t[keys - block :], NEGATIVE)
    return tail if keys == block else jnp.concatenate([scores_t[: keys - block], tail], 0)


def swap_halves(t):
    lane = lax.broadcasted_iota(jnp.int32, (1, t.shape[1]), 1)
    return jnp.where(lane % HD < HD // 2, pltpu.roll(t, t.shape[1] - HD // 2, 1), pltpu.roll(t, HD // 2, 1))


def pick_weights(core, j, a0_ref, a1_ref, a3_ref, got_ref, qk_ref, vo_ref):
    @pl.when(core == 0)
    def _():
        vo_ref[...] = got_ref[0]

        @pl.when(j == 0)
        def _():
            qk_ref[...] = a0_ref[...]

        @pl.when(j == 1)
        def _():
            qk_ref[...] = a1_ref[...]

    @pl.when(core == 1)
    def _():
        qk_ref[...] = got_ref[0]

        @pl.when(j == 0)
        def _():
            vo_ref[...] = a1_ref[...]

        @pl.when(j == 1)
        def _():
            vo_ref[...] = a3_ref[...]


def attend_forward_kernel(
    s_ref, x0_ref, x1_ref, a0_ref, a1_ref, a3_ref, got_ref, cos_ref, sin_ref,
    q_ref, k_ref, v_ref, ot_ref, lse_ref, xt_ref, far_ref, near_ref,
    qk_w, vo_w, o_ref, total_ref,
):
    core, live = s_ref[0], s_ref[1]
    j = pl.program_id(0)
    length = q_ref.shape[1]
    tokens = x0_ref.shape[0]
    n = 3 * HD
    pick_weights(core, j, a0_ref, a1_ref, a3_ref, got_ref, qk_w, vo_w)
    lane = lax.broadcasted_iota(jnp.int32, (tokens, HD), 1)
    one = jnp.where(lane == 0, 1.0, 0.0).astype(BF16)
    for x_ref, which in ((x0_ref, core), (x1_ref, 1 - core)):
        start = pl.multiple_of(which * tokens, tokens)
        at = pl.ds(start, tokens)
        qk = mxu(x_ref[...], qk_w[...])
        cos = jnp.concatenate([cos_ref[at, :]] * 3, 1)
        sin = jnp.concatenate([sin_ref[at, :]] * 3, 1)
        qk = qk * cos + swap_halves(qk) * sin
        q = (qk[:, :n] * (HD ** -0.5)).astype(BF16)
        k = qk[:, n:].astype(BF16)
        v = mxu(x_ref[...], vo_w[:, :n]).astype(BF16)
        key = start + lax.broadcasted_iota(jnp.int32, (tokens, HD), 0)
        bias = jnp.where((lane == 0) & (key >= live), NEGATIVE, 0.0).astype(BF16)
        for head in range(3):
            lanes = slice(head * HD, (head + 1) * HD)
            q_ref[head, at, :] = jnp.concatenate([q[:, lanes], one], 1)
            k_ref[head, at, :] = jnp.concatenate([k[:, lanes], bias], 1)
            v_ref[head, at, :] = jnp.concatenate([v[:, lanes], one], 1)

        @pl.when(j == 0)
        def _():
            xt_ref[:, at] = x_ref[...].T

    for block in range(length // BQ):
        keys = (block + 1) * BQ
        span = slice(block * BQ, keys)
        parts = []
        for head in range(3):
            scores = causal(mxu(k_ref[head, :keys, :], q_ref[head, span, :], NT), BQ)
            top = jnp.max(scores, 0, keepdims=True)
            probs = jnp.exp(scores - top).astype(BF16)
            o = mxu(probs, v_ref[head, :keys, :], TN).T
            total = o[HD : HD + 1]
            parts.append(o[:HD] / total)
            lse_ref[0, head : head + 1, span] = top + jnp.log(total)
        o = jnp.concatenate(parts, 0)
        ot_ref[0, :, span] = o.astype(BF16)
        o_ref[span, :] = o.T.astype(BF16)
    part = mxu(o_ref[...], vo_w[:, n:], NT)

    @pl.when(j == 0)
    def _():
        total_ref[...] = part

    @pl.when(j == 1)
    def _():
        total_ref[...] += part
        near_ref[...] = total_ref[pl.ds(pl.multiple_of(core * tokens, tokens), tokens), :]
        far_ref[...] = total_ref[pl.ds(pl.multiple_of((1 - core) * tokens, tokens), tokens), :].astype(BF16)


def attend_forward(scalars, x_own, x_other, slots, got, cos, sin):
    tokens, width = x_own.shape
    wide = slots[0].shape[1]
    n = wide // 2
    by_j = lambda *shape: pl.BlockSpec(shape, lambda j: (j,) + (0,) * (len(shape) - 1))
    return pl.pallas_call(
        attend_forward_kernel,
        grid=(2,),
        in_specs=[SMEM]
        + [whole(tokens, width)] * 2
        + [whole(width, wide)] * 3
        + [by_j(1, width, wide), whole(LEN, 128), whole(LEN, 128)],
        out_specs=[by_j(3, LEN, 128)] * 3
        + [by_j(1, n, LEN), by_j(1, 8, LEN), whole(width, LEN)]
        + [whole(tokens, width)] * 2,
        out_shape=[hbm(6, LEN, 128)] * 3
        + [hbm(2, n, LEN), hbm(2, 8, LEN, dtype=F32), hbm(width, LEN)]
        + [out(tokens, width), out(tokens, width, dtype=F32)],
        scratch_shapes=[
            pltpu.VMEM((width, wide), BF16),
            pltpu.VMEM((width, wide), BF16),
            pltpu.VMEM((LEN, n), BF16),
            pltpu.VMEM((LEN, width), F32),
        ],
        compiler_params=params(44),
        cost_estimate=cost(2),
        name="attend_forward",
    )(scalars, x_own, x_other, *stay((slots[0], slots[1], slots[3])), got, *stay((cos, sin)))


def attend_backward_kernel(
    s_ref, d0_ref, d1_ref, lo_ref, hi_ref, got_ref, cos_ref, sin_ref, ot_ref, lse_ref,
    q_any, k_any, v_any, xt_any,
    dqk_ref, dv_ref, mine_ref, send_ref,
    q_ref, k_ref, v_ref, xt_ref, vo_w, do_ref, dk_acc, dv_acc, sems, *, j,
):
    core = s_ref[0]
    tokens = d0_ref.shape[0]
    n = 3 * HD
    heads = pl.ds(3 * j, 3)
    copies = [
        pltpu.make_async_copy(k_any.at[heads], k_ref, sems.at[0]),
        pltpu.make_async_copy(q_any.at[heads], q_ref, sems.at[1]),
        pltpu.make_async_copy(v_any.at[heads], v_ref, sems.at[2]),
        pltpu.make_async_copy(xt_any, xt_ref, sems.at[3]),
    ]
    for copy in copies:
        copy.start()

    @pl.when(core == 0)
    def _():
        vo_w[...] = got_ref[0, :, n:]

    @pl.when(core == 1)
    def _():
        vo_w[...] = hi_ref[:, n:]

    for d_ref, which in ((d0_ref, core), (d1_ref, 1 - core)):
        at = pl.ds(pl.multiple_of(which * tokens, tokens), tokens)
        do_ref[at, :] = mxu(d_ref[...], vo_w[...]).astype(BF16)

    length = do_ref.shape[0]
    products = do_ref[...].astype(F32).T * ot_ref[0].astype(F32)
    for copy in copies[:3]:
        copy.wait()

    def unrotate(t):
        return t * cos_ref[...] - swap_halves(t) * sin_ref[...]

    for head in range(3):
        lanes = slice(head * HD, (head + 1) * HD)
        delta = jnp.sum(products[lanes], 0, keepdims=True)
        dq_parts = []
        for block in range(length // BQ):
            keys = (block + 1) * BQ
            span = slice(block * BQ, keys)
            before = keys - BQ
            q = q_ref[head, span, :]
            scores = causal(mxu(k_ref[head, :keys, :], q, NT), BQ)
            probs = jnp.exp(scores - lse_ref[0, head : head + 1, span])
            d_out = do_ref[span, lanes]
            d_probs = mxu(v_ref[head, :keys, :HD], d_out, NT)
            d_scores = (probs * (d_probs - delta[:, span])).astype(BF16)
            dv_part = mxu(probs.astype(BF16), d_out)
            dk_part = mxu(d_scores, q)
            if block:
                dv_acc[:before, :] += dv_part[:before]
                dk_acc[:before, :] += dk_part[:before]
            dv_acc[before:keys, :] = dv_part[before:]
            dk_acc[before:keys, :] = dk_part[before:]
            dq_parts.append(mxu(d_scores, k_ref[head, :keys, :], TN))
        dq = jnp.concatenate(dq_parts, 0) * (HD ** -0.5)
        dqk_ref[:, head * HD : (head + 1) * HD] = unrotate(dq)[:, :HD].astype(BF16)
        dqk_ref[:, n + head * HD : n + (head + 1) * HD] = unrotate(dk_acc[...])[:, :HD].astype(BF16)
        dv_ref[:, lanes] = dv_acc[...].astype(BF16)

    copies[3].wait()
    own = jnp.where(core == 0, 0, tokens)
    grad_o = jnp.zeros((n, d0_ref.shape[1]), F32)
    for d_ref, which in ((d0_ref, core), (d1_ref, 1 - core)):
        at = pl.ds(pl.multiple_of(which * tokens, tokens), tokens)
        grad_o += mxu(ot_ref[0, :, at], d_ref[...])
    grad_o = grad_o.T.astype(BF16)
    grad_qk = mxu(xt_ref[...], dqk_ref[...]).astype(BF16)
    grad_v = mxu(xt_ref[...], dv_ref[...]).astype(BF16)

    @pl.when(core == 0)
    def _():
        mine_ref[...] = grad_qk
        send_ref[:, :n] = grad_v
        send_ref[:, n:] = grad_o

    @pl.when(core == 1)
    def _():
        send_ref[...] = grad_qk
        mine_ref[:, :n] = grad_v
        mine_ref[:, n:] = grad_o


def attend_backward(j, scalars, d_own, d_other, slots, got, cos, sin, q, k, v, out_t, lse, x_t):
    tokens, width = d_own.shape
    wide = slots[0].shape[1]
    n = wide // 2
    at_j = lambda *shape: pl.BlockSpec(shape, lambda i: (j,) + (0,) * (len(shape) - 1))
    lo, hi = (slots[0], slots[1]) if j == 0 else (slots[1], slots[3])
    return pl.pallas_call(
        functools.partial(attend_backward_kernel, j=j),
        grid=(1,),
        in_specs=[SMEM]
        + [whole(tokens, width)] * 2
        + [whole(width, wide)] * 2
        + [at_j(1, width, wide), whole(LEN, 128), whole(LEN, 128), at_j(1, n, LEN), at_j(1, 8, LEN)]
        + [ANY] * 4,
        out_specs=[whole(LEN, wide), whole(LEN, n), whole(width, wide), whole(width, wide)],
        out_shape=[hbm(LEN, wide), hbm(LEN, n), hbm(width, wide), hbm(width, wide)],
        scratch_shapes=[
            pltpu.VMEM((3, LEN, 128), BF16),
            pltpu.VMEM((3, LEN, 128), BF16),
            pltpu.VMEM((3, LEN, 128), BF16),
            pltpu.VMEM((width, LEN), BF16),
            pltpu.VMEM((width, n), BF16),
            pltpu.VMEM((LEN, n), BF16),
            pltpu.VMEM((LEN, 128), F32),
            pltpu.VMEM((LEN, HD), F32),
            DMA((4,)),
        ],
        compiler_params=params(44),
        cost_estimate=cost(2),
        name="attend_backward",
    )(scalars, d_own, d_other, *stay((lo, hi, got, cos, sin, out_t, lse, q, k, v, x_t)))


def input_grad_kernel(s_ref, p0_ref, p1_ref, v0_ref, v1_ref, a0_ref, a1_ref, a3_ref, got_ref, far_ref, near_ref, qk_w, vo_w):
    core = s_ref[0]
    n = v0_ref.shape[1]
    tokens = far_ref.shape[0]
    for j, (lo, hi) in enumerate(((a0_ref, a1_ref), (a1_ref, a3_ref))):

        @pl.when(core == 0)
        def _():
            qk_w[j] = lo[...]
            vo_w[j] = got_ref[j, :, :n]

        @pl.when(core == 1)
        def _():
            qk_w[j] = got_ref[j]
            vo_w[j] = hi[:, :n]

    for which, dst in ((1 - core, far_ref), (core, near_ref)):
        at = pl.ds(pl.multiple_of(which * tokens, tokens), tokens)
        total = mxu(p0_ref[at, :], qk_w[0], NT) + mxu(v0_ref[at, :], vo_w[0], NT)
        total = total + (mxu(p1_ref[at, :], qk_w[1], NT) + mxu(v1_ref[at, :], vo_w[1], NT))
        dst[...] = total.astype(dst.dtype)


def input_grad_parts(scalars, d_qk, d_v, slots, got, tokens):
    width, wide = slots[0].shape
    return one_step(
        input_grad_kernel,
        "input_grad",
        scalars,
        stay((*d_qk, *d_v, slots[0], slots[1], slots[3], got)),
        [out(tokens, width), out(tokens, width, dtype=F32)],
        40,
        [pltpu.VMEM((2, width, wide), BF16), pltpu.VMEM((2, width, wide // 2), BF16)],
    )


def first_norm_kernel(s_ref, x_ref, near_ref, far_ref, gain_ref, resid_ref, normed_ref):
    residual = x_ref[...].astype(F32) + (near_ref[...] + far_ref[...].astype(F32))
    scale = lax.rsqrt(jnp.mean(residual * residual, -1, keepdims=True) + EPSILON)
    resid_ref[...] = residual
    normed_ref[...] = (residual * scale * gain_ref[0:1, :]).astype(BF16)


def last_norm_kernel(s_ref, resid_ref, near_ref, far_ref, gain_ref, own_cot_ref, moved_cot_ref, out_ref, dsum_ref, dffn_ref, dgain_ref):
    core, live = s_ref[0], s_ref[1]
    tokens, width = resid_ref.shape
    residual = resid_ref[...]
    scale = lax.rsqrt(jnp.mean(residual * residual, -1, keepdims=True) + EPSILON)
    summed = residual * scale * gain_ref[0:1, :] + (near_ref[...] + far_ref[...].astype(F32))
    scale = lax.rsqrt(jnp.mean(summed * summed, -1, keepdims=True) + EPSILON)
    unit = summed * scale
    out_ref[...] = (unit * gain_ref[1:2, :]).astype(BF16)
    position = core * tokens + lax.broadcasted_iota(jnp.int32, (tokens, 1), 0)
    cot = jnp.where(s_ref[2] == 1, own_cot_ref[...].astype(F32), moved_cot_ref[...].astype(F32))
    cot = jnp.where(position < live, cot, 0.0)
    dgain_ref[...] = jnp.sum(cot * unit, 0, keepdims=True)
    hat = cot * gain_ref[1:2, :]
    inner = jnp.mean(hat * unit, -1, keepdims=True)
    d_summed = scale * (hat - unit * inner)
    dsum_ref[...] = d_summed
    dffn_ref[...] = d_summed.astype(BF16)


def back_norm_kernel(s_ref, resid_ref, near_ref, far_ref, dsum_ref, gain_ref, dres_ref, dbranch_ref, dgain_ref):
    residual = resid_ref[...]
    scale = lax.rsqrt(jnp.mean(residual * residual, -1, keepdims=True) + EPSILON)
    unit = residual * scale
    d_normed = dsum_ref[...] + (near_ref[...] + far_ref[...].astype(F32))
    dgain_ref[...] = jnp.sum(d_normed * unit, 0, keepdims=True)
    hat = d_normed * gain_ref[0:1, :]
    inner = jnp.mean(hat * unit, -1, keepdims=True)
    d_residual = scale * (hat - unit * inner)
    dres_ref[...] = d_residual
    dbranch_ref[...] = d_residual.astype(BF16)


def fetch_slots(step, sources, dst, sems):
    copies = [pltpu.make_async_copy(src, dst.at[i], sems.at[i]) for i, src in enumerate(sources)]

    @pl.when(step == 0)
    def _():
        for copy in copies:
            copy.start()

    for i, copy in enumerate(copies):

        @pl.when(step == i)
        def _():
            copy.wait()


def ffn_forward_kernel(y0_ref, y1_ref, *refs, slots, start, finish):
    refs = list(refs)
    carry_ref = None if start else refs.pop(0)
    sources, refs = refs[:slots], refs[slots:]
    hid_ref, silu_ref, slope_ref = refs[:3]
    results = refs[3:5]
    w_ref, total_ref, sems = refs[-3:]
    step = pl.program_id(0)
    tokens = y0_ref.shape[0]
    half = hid_ref.shape[2]
    fetch_slots(step, sources, w_ref, sems)

    @pl.when(step == 0)
    def _():
        total_ref[...] = jnp.zeros_like(total_ref) if start else carry_ref[...]
        if start:
            results[1][:, :tokens] = y0_ref[...].T
            results[1][:, tokens:] = y1_ref[...].T

    for part, y_ref in ((0, y0_ref), (1, y1_ref)):
        at = slice(part * tokens, (part + 1) * tokens)
        both = mxu(y_ref[...], w_ref[step, :, : 2 * half])
        gate, up = both[:, :half], both[:, half:]
        sig = jax.nn.sigmoid(gate)
        silu = gate * sig
        hidden = (silu * up).astype(BF16)
        hid_ref[0, at, :] = hidden
        silu_ref[0, at, :] = silu.astype(BF16)
        slope_ref[0, at, :] = (up * (sig + silu * (1.0 - sig))).astype(BF16)
        total_ref[at, :] += mxu(hidden, w_ref[step, :, 2 * half :], NT)

    @pl.when(step == slots - 1)
    def _():
        if finish:
            far_ref, near_ref = results
            near_ref[...] = total_ref[:tokens, :]
            far_ref[...] = total_ref[tokens:, :].astype(BF16)
        else:
            results[0][...] = total_ref[...]


def ffn_forward(normed, normed_other, slots, carry, finish):
    tokens, width = normed.shape
    lanes = slots[0].shape[1]
    count = len(slots)
    half = lanes // 3
    per_slot = pl.BlockSpec((1, 2 * tokens, half), lambda s: (s, 0, 0))
    if finish:
        results = [out(tokens, width), out(tokens, width, dtype=F32)]
    else:
        results = [out(2 * tokens, width, dtype=F32), hbm(width, 2 * tokens)]
    inputs = (normed, normed_other) + (() if carry is None else (carry,))
    return pl.pallas_call(
        functools.partial(ffn_forward_kernel, slots=count, start=carry is None, finish=finish),
        grid=(count,),
        in_specs=[whole(*t.shape) for t in inputs] + [ANY] * count,
        out_specs=[per_slot] * 3 + [whole(*t.shape) for t in results],
        out_shape=[hbm(count, 2 * tokens, half)] * 3 + results,
        scratch_shapes=[
            pltpu.VMEM((count, width, lanes), BF16),
            pltpu.VMEM((2 * tokens, width), F32),
            DMA((count,)),
        ],
        compiler_params=params(36),
        cost_estimate=cost(2),
        name="ffn_forward",
    )(*inputs, *slots)


def ffn_backward_kernel(d0_ref, d1_ref, silu_a, slope_a, silu_b, slope_b, *refs):
    sources, (dgu_ref, far_ref, near_ref, w_ref, total_ref, sems) = refs[:4], refs[4:]
    step = pl.program_id(0)
    tokens = d0_ref.shape[0]
    half = silu_a.shape[2]
    fetch_slots(step, sources, w_ref, sems)

    @pl.when(step == 0)
    def _():
        total_ref[...] = jnp.zeros_like(total_ref)

    def slot(silu_ref, slope_ref):
        for part, d_ref in ((0, d0_ref), (1, d1_ref)):
            at = slice(part * tokens, (part + 1) * tokens)
            d_hidden = mxu(d_ref[...], w_ref[step, :, 2 * half :])
            d_gate = (d_hidden * slope_ref[0, at, :].astype(F32)).astype(BF16)
            d_up = (d_hidden * silu_ref[0, at, :].astype(F32)).astype(BF16)
            dgu_ref[0, at, :half] = d_gate
            dgu_ref[0, at, half:] = d_up
            term = mxu(d_gate, w_ref[step, :, :half], NT) + mxu(d_up, w_ref[step, :, half : 2 * half], NT)
            total_ref[at, :] += term

    @pl.when(step < 3)
    def _():
        slot(silu_a, slope_a)

    @pl.when(step == 3)
    def _():
        slot(silu_b, slope_b)
        near_ref[...] = total_ref[:tokens, :]
        far_ref[...] = total_ref[tokens:, :].astype(BF16)


def ffn_backward(d_ffn, d_other, low, high, slots):
    tokens, width = d_ffn.shape
    lanes = slots[0].shape[1]
    half = lanes // 3
    first_three = pl.BlockSpec((1, 2 * tokens, half), lambda s: (jnp.minimum(s, 2), 0, 0))
    return pl.pallas_call(
        ffn_backward_kernel,
        grid=(4,),
        in_specs=[whole(tokens, width)] * 2
        + [first_three] * 2
        + [whole(1, 2 * tokens, half)] * 2
        + [ANY] * 4,
        out_specs=[pl.BlockSpec((1, 2 * tokens, 2 * half), lambda s: (s, 0, 0))] + [whole(tokens, width)] * 2,
        out_shape=[hbm(4, 2 * tokens, 2 * half), out(tokens, width), out(tokens, width, dtype=F32)],
        scratch_shapes=[
            pltpu.VMEM((4, width, lanes), BF16),
            pltpu.VMEM((2 * tokens, width), F32),
            DMA((4,)),
        ],
        compiler_params=params(40),
        cost_estimate=cost(2),
        name="ffn_backward",
    )(d_ffn, d_other, *stay((*low[1:], *high[1:], *slots)))


def grads_g_kernel(*refs, count, moved):
    yt_ref, refs = refs[0], refs[1:]
    dgu, refs = refs[:count], refs[count:]
    moved_ref, results = (refs[0], refs[1:]) if moved else (None, refs)
    for i, (dgu_ref, result_ref) in enumerate(zip(dgu, results)):
        grad = mxu(yt_ref[...], dgu_ref[0])
        if moved and i == 0:
            grad = grad + moved_ref[...].astype(F32)
        result_ref[...] = grad.astype(BF16)


def grads_g(y_t, d_gu, slots, moved=None):
    width, length = y_t.shape
    wide = d_gu.shape[2]
    at_slot = [pl.BlockSpec((1, length, wide), functools.partial(lambda n, i: (n, 0, 0), n)) for n in slots]
    extra = [] if moved is None else [moved]
    return pl.pallas_call(
        functools.partial(grads_g_kernel, count=len(slots), moved=moved is not None),
        grid=(1,),
        in_specs=[whole(width, length)] + at_slot + [whole(*t.shape) for t in extra],
        out_specs=[whole(width, wide)] * len(slots),
        out_shape=[out(width, wide)] * len(slots),
        compiler_params=params(32),
        cost_estimate=cost(0.1),
        name="grads_g",
    )(stay(y_t), *[stay(d_gu)] * len(slots), *extra)


def grads_d_kernel(s_ref, d0_ref, d1_ref, hid_a, hid_b, *refs):
    blocks, dt_ref, grad_ref = refs[:-2], refs[-2], refs[-1]
    tokens = d0_ref.shape[0]
    dt_ref[:, :tokens] = d0_ref[...].T
    dt_ref[:, tokens:] = d1_ref[...].T
    for slot in range(4):
        hidden = hid_a[slot] if slot < 3 else hid_b[0]
        grad_ref[slot] = mxu(dt_ref[...], hidden).astype(BF16)
    for hop, block_ref in enumerate(blocks):
        rows = block_ref.shape[1]
        place = (s_ref[1] ^ hop) if len(blocks) > 1 else 0
        at = pl.ds(pl.multiple_of(place * rows, rows), rows)
        for slot in range(4):
            block_ref[slot] = grad_ref[slot, at, :]


def first_slots_kernel(s_ref, mine1_ref, theirs1_ref, dn_ref, dn_moved_ref, s3_ref, sum_ref):
    sum_ref[...] = (dn_ref[...].astype(F32) + dn_moved_ref[...].astype(F32)).astype(BF16)

    @pl.when(s_ref[0] == 0)
    def _():
        s3_ref[...] = theirs1_ref[...]

    @pl.when(s_ref[0] == 1)
    def _():
        s3_ref[...] = mine1_ref[...]


def slots_kernel(s_ref, mine0_ref, mine1_ref, theirs0_ref, theirs1_ref, moved_ref, s1_ref, s2_ref):
    moved = moved_ref[...].astype(F32)

    @pl.when(s_ref[0] == 0)
    def _():
        s1_ref[...] = (mine1_ref[...].astype(F32) + moved).astype(BF16)
        s2_ref[...] = theirs0_ref[...]

    @pl.when(s_ref[0] == 1)
    def _():
        s1_ref[...] = (mine0_ref[...].astype(F32) + moved).astype(BF16)
        s2_ref[...] = theirs1_ref[...]


def merge_kernel(s_ref, base0_ref, base1_ref, one_ref, two_ref, *blocks):
    cols = len(blocks)
    part = blocks[0].shape[0]
    for hop, block_ref in enumerate(blocks):
        at = pl.ds(pl.multiple_of((s_ref[1] ^ hop) * part, part), part)
        moved = one_ref[at, :].astype(F32) + two_ref[at, :].astype(F32)

        @pl.when(s_ref[0] == 0)
        def _():
            block_ref[...] = (base0_ref[at, :].astype(F32) + moved).astype(BF16)

        @pl.when(s_ref[0] == 1)
        def _():
            block_ref[...] = (base1_ref[at, :].astype(F32) + moved).astype(BF16)


def merge_one_kernel(s_ref, base_ref, one_ref, two_ref, *blocks):
    part = blocks[0].shape[0]
    for hop, block_ref in enumerate(blocks):
        at = pl.ds(pl.multiple_of((s_ref[1] ^ hop) * part, part), part)
        moved = one_ref[at, :].astype(F32) + two_ref[at, :].astype(F32)
        block_ref[...] = (base_ref[at, :].astype(F32) + moved).astype(BF16)


def pack_kernel(s_ref, *refs):
    shards, gain_ref, pack_ref = refs[:-2], refs[-2], refs[-1]
    total = jnp.zeros((1, 1), F32)
    for ref in shards:
        value = ref[...].astype(F32)
        total = total + jnp.sum(jnp.sum(value * value, 0, keepdims=True), 1, keepdims=True)
    row = lax.broadcasted_iota(jnp.int32, pack_ref.shape, 0)
    gain = jnp.where(row == 0, gain_ref[0:1, :], gain_ref[1:2, :])
    pack_ref[...] = jnp.where(row < 2, gain, jnp.broadcast_to(total, pack_ref.shape))


def update(grad_full, moment, weight, average, factor):
    clipped = grad_full * factor
    new_moment = MOMENTUM * moment + clipped
    new_weight = weight - RATE * (clipped + MOMENTUM * new_moment)
    new_average = DECAY * average + (1.0 - DECAY) * new_weight
    return (new_moment, new_weight, new_average)


def fetch_kernel(*refs):
    count = (len(refs) - 1) // 2
    sems = refs[-1]
    copies = [pltpu.make_async_copy(refs[i], refs[count + i], sems.at[i]) for i in range(count)]
    for copy in copies:
        copy.start()
    for copy in copies:
        copy.wait()


def update_kernel(s_ref, pack_ref, a0_ref, a1_ref, g0_ref, g1_ref, d0_ref, d1_ref, gm_ref, gw_ref, ge_ref, *refs):
    old, refs = refs[:12], refs[12:]
    new, refs = refs[:12], refs[12:]
    gain_new, norm_ref, refs = refs[:3], refs[3], refs[4:]
    held, out_sems = refs[:12], refs[12]
    gains = pack_ref[0:2, :]
    squares = pack_ref[2:3, 0:1] + jnp.sum(jnp.sum(gains * gains, 0, keepdims=True), 1, keepdims=True)
    norm = jnp.sqrt(squares)
    norm_ref[...] = norm
    factor = jnp.minimum(1.0, CLIP / (norm + 1e-06))
    for ref, value in zip(gain_new, update(gains, gm_ref[...], gw_ref[...], ge_ref[...], factor)):
        ref[...] = value
    n = held[0].shape[2]
    half = d0_ref.shape[1]

    def put(kind, at, grad):
        moment, weight, average = (old[kind + 4 * i] for i in range(3))
        results = update(grad, moment[at], weight[at], average[at], factor)
        for i, value in enumerate(results):
            held[kind + 4 * i][at] = value

    every = slice(None)

    def parts(kind, mine, other):
        if kind == 0:
            qk, vo = mine[0], other[0]
            put(0, (0, every, every), qk[:, :n].astype(F32))
            put(0, (1, every, every), qk[:, n:].astype(F32))
            put(0, (2, every, every), vo[:, :n].astype(F32))
        elif kind == 1:
            put(1, (every, every), other[0][:, n:].astype(F32).T)
        else:
            for which, part in enumerate((mine, other)):
                lanes = slice(which * half, (which + 1) * half)
                if kind == 2:
                    put(2, (0, every, lanes), part[1][:, :half].astype(F32))
                    put(2, (1, every, lanes), part[1][:, half:].astype(F32))
                else:
                    put(3, (every, lanes), part[2][...].astype(F32))

    here, there = (a0_ref, g0_ref, d0_ref), (a1_ref, g1_ref, d1_ref)
    for kind in (2, 3, 0, 1):
        @pl.when(s_ref[0] == 0)
        def _():
            parts(kind, here, there)

        @pl.when(s_ref[0] == 1)
        def _():
            parts(kind, there, here)

        for i in (kind, kind + 4, kind + 8):
            pltpu.make_async_copy(held[i], new[i], out_sems.at[i]).start()
    for i in range(12):
        pltpu.make_async_copy(held[i], new[i], out_sems.at[i]).wait()


def body(
    rows,
    cols,
    block_input,
    out_grad,
    lengths,
    w_qkv,
    w_out,
    w_gate_up,
    w_down,
    gains,
    mom_qkv,
    mom_out,
    mom_gate_up,
    mom_down,
    mom_gains,
    ema_qkv,
    ema_out,
    ema_gate_up,
    ema_down,
    ema_gains,
):
    d = lax.axis_index("dp")
    r = lax.axis_index("row")
    c = lax.axis_index("col")
    core0 = d == 0
    stays = d == r % 2
    tokens, width = block_input.shape
    ring = cols == 4
    mesh_sizes = {"row": rows, "col": cols}
    part = width // cols
    head_cols = w_qkv.shape[2]
    half = w_gate_up.shape[2] // 2

    pairs = [(i, j) for i in range(2) for j in range(rows)]
    swap_pairs = [(i * rows + j, (j % 2) * rows + (j // 2) * 2 + i) for i, j in pairs]
    cross_pairs = [(i, j) for i, j in swap_pairs if i != j]
    first_pairs = [(i * rows + j, i * rows + (j ^ (1 if i == 0 else 2))) for i, j in pairs]
    second_pairs = [(i * rows + j, i * rows + (j ^ (2 if i == 0 else 1))) for i, j in pairs]

    def swap_tokens(t):
        return lax.ppermute(t, ("dp", "row"), swap_pairs)

    def cross_tokens(t):
        return lax.ppermute(t, ("dp", "row"), cross_pairs)

    def first(t):
        return lax.ppermute(t, ("dp", "row"), first_pairs)

    def second(t):
        return lax.ppermute(t, ("dp", "row"), second_pairs)

    def core(t):
        return lax.ppermute(t, "dp", [(0, 1), (1, 0)])

    def along(t, k):
        return lax.ppermute(t, "col", [(i, i ^ k) for i in range(cols)])

    def join_cols(*blocks):
        return pl.pallas_call(
            join_kernel,
            in_specs=[SMEM] + [ANY] * cols,
            out_specs=ANY,
            out_shape=out(width, blocks[0].shape[1]),
            scratch_shapes=[DMA((cols,))],
            compiler_params=params(16),
            cost_estimate=cost(0.1),
            name="join",
        )(ids, *blocks)

    def gather_cols(t):
        return lax.all_gather(t, "col", axis=t.ndim - 2, tiled=True)

    def add(*values):
        total = values[0].astype(F32)
        for value in values[1:]:
            total = total + value.astype(F32)
        return total.astype(BF16)

    ids = jnp.stack([d, c]).astype(jnp.int32)
    (piece_a,) = one_step(piece_a_kernel, "piece_a", ids, stay((w_qkv, w_out)), [out(part, 2 * head_cols)], 60)
    piece_a, block_input = fence(piece_a, block_input)
    a_cols = [along(piece_a, 1), along(piece_a, 2)] if ring else [gather_cols(piece_a)]
    moved_x = cross_tokens(block_input)
    (piece_f,) = one_step(piece_f_kernel, "piece_f", ids, stay((w_gate_up, w_down.T)), [out(part, 3 * half)], 60)
    a_cols, piece_f, out_grad = fence(a_cols, piece_f, out_grad)
    moved_cot = cross_tokens(out_grad)
    if ring:
        a_cols = a_cols + [along(a_cols[1], 1)]
        f_cols = [along(piece_f, 1), along(piece_f, 2)]
    else:
        f_cols = [gather_cols(piece_f)]
    a_cols, piece_a, lengths, moved_x = fence(a_cols, piece_a, lengths, moved_x)
    a0 = join_cols(piece_a, *a_cols) if ring else a_cols[0]
    a1, a2 = first(a0), second(a0)
    x_own = jnp.where(stays, block_input, moved_x)
    a0, a1, a2, f_cols, x_own, moved_cot = fence(a0, a1, a2, f_cols, x_own, moved_cot)
    a3 = second(a1)
    if ring:
        f_cols = f_cols + [along(f_cols[1], 1)]
    x_other = core(x_own)
    own_length = swap_tokens(lengths)[0, :]
    seq_ids = jnp.arange(own_length.shape[0], dtype=jnp.int32)
    own_length = jnp.sum(jnp.where(seq_ids == r // 2, own_length, 0))
    scalars = jnp.stack([d.astype(jnp.int32), own_length, stays.astype(jnp.int32)])
    a0, a1, a2, a3, f_cols, x_own, x_other, scalars = fence(a0, a1, a2, a3, f_cols, x_own, x_other, scalars)
    f0 = join_cols(piece_f, *f_cols) if ring else f_cols[0]
    f0, a0, a2, a3 = fence(f0, a0, a2, a3)
    slots_a = [a0, a1, a2, a3]
    send = pl.pallas_call(
        pick_kernel,
        in_specs=[SMEM] + [ANY] * 3,
        out_specs=ANY,
        out_shape=out(2, width, 2 * head_cols),
        scratch_shapes=[DMA((2,))],
        compiler_params=params(16),
        cost_estimate=cost(0.1),
        name="pick",
    )(ids, a0, a2, a3)
    got = core(send)
    f1, f2 = first(f0), second(f0)
    cos, sin = pair_tables()
    q, k, v, attended_t, lse, x_t, far, near = attend_forward(scalars, x_own, x_other, slots_a, got, cos, sin)
    far, near, f1, f2 = fence(far, near, f1, f2)
    f3 = second(f1)
    residual, normed = one_step(
        first_norm_kernel,
        "first_norm",
        ids,
        (x_own, near, core(far), gains),
        [out(tokens, width, dtype=F32), out(tokens, width)],
    )
    normed_other = core(normed)

    *low, carry, y_t = ffn_forward(normed, normed_other, [f0, f1, f2], None, False)
    carry, f3 = fence(carry, f3)
    slots_f = [f0, f1, f2, f3]
    *high, far, near = ffn_forward(normed, normed_other, [f3], carry, True)
    output, d_summed, d_ffn, grad_gain_two = one_step(
        last_norm_kernel,
        "last_norm",
        scalars,
        (residual, near, core(far), gains, out_grad, moved_cot),
        [out(tokens, width), out(tokens, width, dtype=F32), out(tokens, width), out(1, width, dtype=F32)],
        32,
    )
    d_ffn_other = core(d_ffn)
    moved_out = cross_tokens(output)

    d_gu, far, near = ffn_backward(d_ffn, d_ffn_other, low, high, slots_f)
    far, near, moved_out, d_gu = fence(far, near, moved_out, d_gu)
    got_far = core(far)
    (gu3,) = grads_g(y_t, d_gu, (3,))
    got_far, gu3 = fence(got_far, gu3)
    gu_moved = second(gu3)
    d_residual, d_branch, grad_gain_one = one_step(
        back_norm_kernel,
        "back_norm",
        ids,
        (residual, near, got_far, d_summed, gains),
        [out(tokens, width, dtype=F32), out(tokens, width), out(1, width, dtype=F32)],
    )
    d_branch_other = core(d_branch)
    dn = one_step(
        grads_d_kernel,
        "grads_d",
        ids,
        stay((d_ffn, d_ffn_other, low[0], high[0])),
        [hbm(4, part if ring else width, half)] * (cols if ring else 1),
        32,
        [pltpu.VMEM((width, 2 * tokens), BF16), pltpu.VMEM((4, width, half), BF16)],
    )
    d_branch_other, dn = fence(d_branch_other, dn)
    gain_pair = jnp.concatenate([grad_gain_one, grad_gain_two], 0)
    gain_pair = gain_pair + core(gain_pair)
    dn_one = along(dn[3], 1) if ring else dn[0]
    back = (scalars, d_branch, d_branch_other, slots_a, got, cos, sin, q, k, v, attended_t, lse, x_t)
    dqk1, dv1, mine1, send1 = attend_backward(1, *back)
    dqk1, dv1, mine1, send1, gu_moved, dn_one, d_branch, gain_pair = fence(
        dqk1, dv1, mine1, send1, gu_moved, dn_one, d_branch, gain_pair
    )
    theirs1 = core(send1)
    gu1, gu2, gu0 = grads_g(y_t, d_gu, (1, 2, 0), gu_moved)
    theirs1, gu1, gu2 = fence(theirs1, gu1, gu2)
    s3, dn_two = one_step(
        first_slots_kernel,
        "first_slots",
        ids,
        (mine1, theirs1, dn[2] if ring else dn[0], dn_one),
        [out(width, 2 * head_cols), out(*dn[0].shape)],
    )
    s3, dn_two, gu1, gu2, d_branch = fence(s3, dn_two, gu1, gu2, d_branch)
    a_moved = second(s3)
    gu_one, gu_two = first(gu1), second(gu2)
    dn_last = [along(dn_two, 2), along(dn[1], 1)] if ring else []
    back = (scalars, d_branch) + back[2:]
    dqk0, dv0, mine0, send0 = attend_backward(0, *back)
    dqk0, dv0, mine0, send0, a_moved, gu_one, gu_two, dn_last = fence(
        dqk0, dv0, mine0, send0, a_moved, gu_one, gu_two, dn_last
    )
    theirs0 = core(send0)
    if ring:
        own_dn = add(dn[0], *dn_last)
    else:
        own_dn = lax.psum_scatter(dn[0], "col", scatter_dimension=1, tiled=True)
    dn_moved = second(own_dn[3])

    def merge(base0, base1, one, two):
        if not ring:
            return [add(jnp.where(core0, base0, base1), one, two)]
        return one_step(merge_kernel, "merge", ids, (base0, base1, one, two), [out(part, base0.shape[1])] * cols)

    def to_owner(blocks):
        if not ring:
            return [lax.psum_scatter(blocks[0], "col", scatter_dimension=0, tiled=True)]
        return [blocks[0]] + [along(blocks[hop], hop) for hop in range(1, cols)]

    if ring:
        g_parts = one_step(
            merge_one_kernel, "merge_one", ids, (gu0, gu_one, gu_two), [out(part, gu0.shape[1])] * cols
        )
    else:
        g_parts = merge(gu0, gu0, gu_one, gu_two)
    theirs0, g_parts = fence(theirs0, g_parts)
    s1, s2 = one_step(
        slots_kernel, "slots", ids, (mine0, mine1, theirs0, theirs1, a_moved), [out(width, 2 * head_cols)] * 2
    )
    s1, s2, g_parts, dqk0, output, dn_moved = fence(s1, s2, g_parts, dqk0, output, dn_moved)
    a_one, a_two = first(s1), second(s2)
    g_parts = to_owner(g_parts)
    far, near = input_grad_parts(scalars, (dqk0, dqk1), (dv0, dv1), slots_a, got, tokens)
    output = jnp.where(stays, output.astype(F32), moved_out.astype(F32))
    a_one, a_two, g_parts, far, near, output, mom_gains = fence(
        a_one, a_two, g_parts, far, near, output, mom_gains
    )
    old = (mom_qkv, mom_out, mom_gate_up, mom_down.T) + (w_qkv, w_out, w_gate_up, w_down.T)
    old = old + (ema_qkv, ema_out, ema_gate_up, ema_down.T)
    old, a_one = fence(old, a_one)
    a_parts = to_owner(merge(mine0, theirs0, a_one, a_two))
    dn_one, dn_two = first(add(own_dn[1], dn_moved)), second(own_dn[2])
    shard_g = add(*g_parts)
    held = pl.pallas_call(
        fetch_kernel,
        in_specs=[ANY] * 12,
        out_specs=[VMEM] * 12,
        out_shape=[pltpu.VMEM(t.shape, F32) for t in old],
        scratch_shapes=[DMA((12,))],
        compiler_params=params(16),
        cost_estimate=cost(0.1),
        name="fetch",
    )(*stay(old))
    a_parts, dn_one, dn_two, shard_g, held, far = fence(a_parts, dn_one, dn_two, shard_g, held, far)
    shard_a = add(*a_parts)
    shard_d = add(own_dn[0], dn_one, dn_two)

    far_a, far_d, far_g = core(shard_a), core(shard_d), core(shard_g)
    got_far = core(far)
    far_a, far_d, far_g, got_far = fence(far_a, far_d, far_g, got_far)
    input_grad = d_residual + (near + got_far.astype(F32))
    moved_grad = cross_tokens(input_grad.astype(BF16))
    pack = one_step(
        pack_kernel,
        "pack",
        ids,
        (shard_a, far_a, shard_g, far_g, shard_d, far_d, gain_pair),
        [out(8, width, dtype=F32)],
    )[0]
    for axis, bits in (("col", (2, 1) if ring else ()), ("row", (2, 1))):
        size = mesh_sizes[axis]
        for bit in bits:
            moved = lax.ppermute(pack, axis, [(i, i ^ bit) for i in range(size)])
            if (axis, bit) == ("row", 1):
                input_grad = jnp.where(stays, input_grad, moved_grad.astype(F32))
                moved, input_grad = fence(moved, input_grad)
            pack = pack + moved
    if not ring:
        pack = lax.psum(pack, "col")

    results = pl.pallas_call(
        update_kernel,
        in_specs=[SMEM] + [VMEM] * 22,
        out_specs=[ANY] * 12 + [VMEM] * 4,
        out_shape=[out(*t.shape, dtype=F32) for t in old]
        + [out(*gains.shape, dtype=F32)] * 3
        + [out(1, 1, dtype=F32)],
        scratch_shapes=[pltpu.VMEM(t.shape, F32) for t in old] + [DMA((12,))],
        compiler_params=params(24),
        cost_estimate=cost(0.1),
        name="update",
    )(ids, pack, shard_a, far_a, shard_g, far_g, shard_d, far_d, mom_gains, gains, ema_gains, *held)
    new = results[:12]
    gain_new = results[12:15]
    grad_norm = results[15][0, 0]
    return (
        output,
        input_grad,
        grad_norm,
        *new[0:3],
        new[3].T,
        gain_new[0],
        *new[4:7],
        new[7].T,
        gain_new[1],
        *new[8:11],
        new[11].T,
        gain_new[2],
    )


def solution(mesh):
    tok = P(("dp", "col", "row"), None)
    weights = (P(None, "col", "row"), P("row", "col"), P(None, "col", "row"), P("row", "col"), P())
    in_specs = (tok, tok, P(("dp", "col"), None)) + weights * 3
    out_specs = (tok, tok, P()) + weights * 3
    fn = functools.partial(body, mesh.shape["row"], mesh.shape["col"])
    return jax.shard_map(fn, mesh=mesh, in_specs=in_specs, out_specs=out_specs, check_vma=False)
```
